32 devices in a mesh: seq: 2 (over y), dp: 16 (over z, x, core).
Axes of the slice: x: 2, y: 2, z: 4, core: 2. Of those that a mesh axis runs over, the one named last changes fastest.
Arguments:
- tokens: bfloat16 [16, 1024, 768], P('dp', 'seq'), may hold values from -6 to 6
- first_values: bfloat16 [16, 1024, 384], P('dp', 'seq'), may hold values from -6 to 6
- out_grad: bfloat16 [16, 1024, 768], P('dp', 'seq'), may hold values from -6 to 6
- block_place: int32 [16, 4], P('dp'), may hold values from 0 to 3, each once within a row
- owners: int32 [414], replicated, may hold values from 0 to 15, as said below
- masters: float32 [640, 16384], P('dp'), as said below
- moment_one: float32 [640, 16384], P('dp')
- moment_two: float32 [640, 16384], P('dp'), as said below
- vector_master: float32 [8832], replicated
- vector_moment_one: float32 [8832], replicated
- vector_moment_two: float32 [8832], replicated, as said below
Outputs:
- output: bfloat16 [16, 1024, 768], P('dp', 'seq')
- tokens_grad: float32 [16, 1024, 768], P('dp', 'seq')
- first_grad: float32 [16, 1024, 384], P('dp', 'seq')
- new_masters: float32 [640, 16384], P('dp')
- new_moment_one: float32 [640, 16384], P('dp')
- new_moment_two: float32 [640, 16384], P('dp')
- new_copies: bfloat16 [640, 16384], P('dp')
- new_vector: float32 [8832], replicated
- new_vector_one: float32 [8832], replicated
- new_vector_two: float32 [8832], replicated
The draws below stay inside these ranges and needn't reach their ends.
Inputs may be any that keep to these rules, and one draw needn't show every extreme that they name: `owners`: block t holds entries t * 16384 onward of the six weight matrices laid end to end; no index of dp keeps more than 40 blocks, and one keeps exactly 40. `block_place`: each row orders the 4 blocks of one sequence. `masters`: rows that no block is placed in are unused slots. `moment_two`: Positive. `vector_moment_two`: Positive.
All inputs are finite; a program needn't handle non-finite values.
Results may differ from the reference program's by a relative error of at most 0.011.
Values may be sent and summed in bfloat16 or wider, within the bound.
A program may use at most 256 MiB of HBM per device.

```python
import math
import jax
import jax.numpy as jnp
from jax import lax

D = 768
H = 12
HD = 64
FF = 3072
SEQ_LEN = 1024
TILE_LEN = 16384
STEP = 10
HV = 384
SEQS = 16
TOKENS = 16384
NB = 4
BL = 256
TILES = 414
CAP = 40
SLOTS = 640
VEC = 8832
N_DP = 16


GRAD_TABLE = [0.4, 0.4, 0.3, 0.1, 0.35, 0.6]


def owner_table(key):
    key = jax.random.fold_in(key, 101)
    subkeys = jax.random.split(key, 3)
    full_owner = jax.random.randint(subkeys[0], (), 0, N_DP)
    rank_order = jax.random.permutation(subkeys[1], SLOTS)
    slot_owner = jnp.arange(SLOTS, dtype=jnp.int32) // CAP
    priority = jnp.where(slot_owner == full_owner, 0, 1 + rank_order)
    chosen = jnp.argsort(priority, stable=True)[:TILES]
    chosen = chosen[jax.random.permutation(subkeys[2], TILES)]
    return (chosen // CAP).astype(jnp.int32)


def slot_scales(key, table):
    owners_drawn = owner_table(key)
    tile_order = jnp.arange(TILES, dtype=jnp.int32)
    earlier = (owners_drawn[None, :] == owners_drawn[:, None]) & (tile_order[None, :] < tile_order[:, None])
    slot_rows = owners_drawn * CAP + jnp.sum(earlier.astype(jnp.int32), axis=1)
    tile_of = jnp.full((SLOTS,), TILES, jnp.int32).at[slot_rows].set(tile_order)
    element = tile_of[:, None] * TILE_LEN + jnp.arange(TILE_LEN, dtype=jnp.int32)[None, :]
    limits = [D * D, 2 * D * D, 2 * D * D + D * HV, 3 * D * D + D * HV, 3 * D * D + D * HV + D * FF]
    scale = jnp.full((SLOTS, TILE_LEN), table[5], jnp.float32)
    for place in [4, 3, 2, 1, 0]:
        scale = jnp.where(element < limits[place], jnp.float32(table[place]), scale)
    return scale


def log_uniform(key, shape, lower, upper):
    return jnp.exp(jax.random.uniform(key, shape, jnp.float32, math.log(lower), math.log(upper)))


def signed_sizes(key, shape):
    sign_key, size_key = jax.random.split(key)
    signs = jnp.where(jax.random.bernoulli(sign_key, 0.5, shape), 1.0, -1.0)
    sizes_drawn = log_uniform(size_key, shape, 0.5, 2.0)
    return signs * sizes_drawn


def draw_owners(key, part):
    return owner_table(key)


def draw_masters(key, part):
    spread = slot_scales(key, [D ** (-0.5), D ** (-0.5), D ** (-0.5), (D // 32) ** (-0.5), D ** (-0.5), FF ** (-0.5)])
    key = jax.random.fold_in(key, 1)
    base = jnp.clip(jax.random.normal(key, (SLOTS, TILE_LEN), jnp.float32), -4.0, 4.0)
    return base * spread


def draw_moment_one(key, part):
    spread = slot_scales(key, GRAD_TABLE) * TOKENS ** 0.5
    key = jax.random.fold_in(key, 2)
    return signed_sizes(key, (SLOTS, TILE_LEN)) * spread


def draw_moment_two(key, part):
    spread = slot_scales(key, GRAD_TABLE) * TOKENS ** 0.5
    key = jax.random.fold_in(key, 3)
    factor = log_uniform(key, (SLOTS, TILE_LEN), 1.0, 4.0)
    return factor * spread * spread


def draw_vector_master(key, part):
    key = jax.random.fold_in(key, 4)
    gain_key, bias_key = jax.random.split(key)
    entry = jnp.arange(VEC, dtype=jnp.int32)
    is_gain = (entry < D) | (entry >= 2 * D) & (entry < 3 * D)
    gains = log_uniform(gain_key, (VEC,), 0.6, 1.6)
    biases = 0.3 * jnp.clip(jax.random.normal(bias_key, (VEC,), jnp.float32), -4.0, 4.0)
    return jnp.where(is_gain, gains, biases)


def draw_vector_moment_one(key, part):
    key = jax.random.fold_in(key, 5)
    return signed_sizes(key, (VEC,)) * (0.5 * TOKENS ** 0.5)


def draw_vector_moment_two(key, part):
    key = jax.random.fold_in(key, 6)
    factor = log_uniform(key, (VEC,), 1.0, 4.0)
    return factor * (0.25 * TOKENS)


def level_of(rng, extent, shards, least, top_value):
    loudness, own = 1.0, jax.random.fold_in(rng, 6)
    for axis_at, blocks in shards:
        heights = jnp.exp(jax.random.uniform(jax.random.fold_in(own, axis_at), (blocks,), jnp.float32, least / len(shards), top_value / len(shards)))
        loudness = loudness * jnp.repeat(heights, extent[axis_at] // blocks).reshape([-1 if axis == axis_at else 1 for axis in range(len(extent))])
    return loudness


def gaussian(stream_key, dims, scale, bound, cuts=(), held_as=jnp.bfloat16):
    factor_of = level_of(stream_key, dims, cuts, -0.22, 0.18) if cuts else 1.0
    drawn = jax.random.normal(stream_key, dims, jnp.float32) * scale * factor_of
    return jnp.minimum(jnp.maximum(drawn, -bound), bound).astype(held_as)


def setup_inputs(seed: int = 0) -> dict:
    arg_keys = jax.random.split(jax.random.key(seed), 12)
    tokens = gaussian(arg_keys[0], (SEQS, SEQ_LEN, D), 1.0, 6.0, ((0, 16), (1, 2)))
    first_values = gaussian(arg_keys[1], (SEQS, SEQ_LEN, HV), 1.0, 6.0, ((0, 16), (1, 2)))
    out_grad = gaussian(arg_keys[2], (SEQS, SEQ_LEN, D), 1.0, 6.0, ((0, 16), (1, 2)))
    block_place = jax.vmap(lambda own: jax.random.permutation(own, NB))(jax.random.split(arg_keys[3], SEQS)).reshape((SEQS, NB)).astype(jnp.int32)
    owners = draw_owners(jax.random.fold_in(arg_keys[11], 71), 0)
    masters = draw_masters(jax.random.fold_in(arg_keys[11], 71), 0)
    moment_one = draw_moment_one(jax.random.fold_in(arg_keys[11], 71), 0)
    moment_two = draw_moment_two(jax.random.fold_in(arg_keys[11], 71), 0)
    vector_master = draw_vector_master(jax.random.fold_in(arg_keys[11], 71), 0)
    vector_moment_one = draw_vector_moment_one(jax.random.fold_in(arg_keys[11], 71), 0)
    vector_moment_two = draw_vector_moment_two(jax.random.fold_in(arg_keys[11], 71), 0)
    return {"tokens": tokens, "first_values": first_values, "out_grad": out_grad, "block_place": block_place, "owners": owners, "masters": masters, "moment_one": moment_one, "moment_two": moment_two, "vector_master": vector_master, "vector_moment_one": vector_moment_one, "vector_moment_two": vector_moment_two}


EPS_NORM = 1e-05
EPS_ADAM = 1e-08
BETA_ONE = 0.5
BETA_TWO = 0.5
RATE_MATRIX = 0.03
RATE_VECTOR = 0.25
DECAY_MATRIX = 0.1
PRECISE = lax.Precision.HIGHEST

@jax.custom_vjp
def low(v):
    return lax.optimization_barrier(v.astype(jnp.bfloat16)).astype(jnp.float32)

@jax.custom_vjp
def low_back(v):
    return v

def low_keep(v):
    return (low(v), None)

def low_pass(kept, grad):
    return (grad,)

def back_keep(v):
    return (v, None)

def back_low(kept, grad):
    return (low(grad),)
low.defvjp(low_keep, low_pass)
low_back.defvjp(back_keep, back_low)

def dot_high(left, right):
    return jnp.dot(left, right, precision=PRECISE)

def layer_norm(values, norm_gain, norm_shift):
    center = lax.optimization_barrier(jnp.mean(values, axis=-1, keepdims=True))
    centred = values - center
    spread = lax.optimization_barrier(jnp.mean(centred * centred, axis=-1, keepdims=True))
    return centred * lax.rsqrt(spread + EPS_NORM) * norm_gain + norm_shift

def gelu_tanh(values):
    return 0.5 * values * (1.0 + jnp.tanh(0.7978845608028654 * (values + 0.044715 * values * values * values)))

def slot_numbers(owners):
    tile_order = jnp.arange(owners.shape[0], dtype=jnp.int32)
    earlier = (owners[None, :] == owners[:, None]) & (tile_order[None, :] < tile_order[:, None])
    return lax.optimization_barrier(jnp.sum(earlier.astype(jnp.int32), axis=1))

def split_weights(flat):
    lengths = [D * D, D * D, D * HV, D * D, D * FF, FF * D]
    matrix_shapes = [(D, D), (D, D), (D, HV), (D, D), (D, FF), (FF, D)]
    pieces = []
    offset = 0
    for length, matrix_shape in zip(lengths, matrix_shapes):
        pieces.append(flat[offset:offset + length].reshape(matrix_shape))
        offset = offset + length
    return pieces

def split_vector(vector):
    pieces = [vector[i * D:(i + 1) * D] for i in range(7)]
    pieces.append(vector[7 * D:7 * D + HV])
    pieces.append(vector[7 * D + HV:])
    return pieces

def adam_step(weight, first_moment, second_moment, gradient, step_rate, weight_decay):
    first_new = BETA_ONE * first_moment + (1.0 - BETA_ONE) * gradient
    second_new = BETA_TWO * second_moment + (1.0 - BETA_TWO) * gradient * gradient
    first_fix = 1.0 - BETA_ONE ** STEP
    second_fix = 1.0 - BETA_TWO ** STEP
    update = first_new / first_fix / (jnp.sqrt(second_new / second_fix) + EPS_ADAM)
    return (weight - step_rate * (update + weight_decay * weight), first_new, second_new)

def attend_sequence(packed):
    query_rows, key_rows, value_rows, positions = packed
    scores = low_back(jnp.einsum('qhd,khd->hqk', query_rows, key_rows, precision=PRECISE) * HD ** (-0.5))
    allowed = positions[None, :] <= positions[:, None]
    scores = jnp.where(allowed[None], scores, -1e+30)
    row_top = lax.optimization_barrier(jnp.max(scores, axis=-1, keepdims=True))
    exponent = jnp.exp(scores - row_top)
    weights_soft = low(exponent / lax.optimization_barrier(jnp.sum(exponent, axis=-1, keepdims=True)))
    return jnp.einsum('hqk,khd->qhd', weights_soft, value_rows, precision=PRECISE)

def forward(inputs, firsts, w_query, w_key, w_value, w_out, w_up, w_down, vector, positions):
    gain_one, shift_one, gain_two, shift_two, bias_query, bias_out, bias_down, bias_value, bias_up = split_vector(vector)
    normed_one = low(layer_norm(inputs, gain_one, shift_one))
    query_rows = low(low_back(dot_high(normed_one, w_query) + bias_query))
    key_rows = low(low_back(dot_high(normed_one, w_key)))
    fresh_rows = low(low_back(dot_high(normed_one, w_value) + bias_value))
    value_rows = jnp.concatenate([fresh_rows, firsts], axis=1)
    heads_shape = (SEQS, SEQ_LEN, H, HD)
    attended = lax.map(jax.checkpoint(attend_sequence), (query_rows.reshape(heads_shape), key_rows.reshape(heads_shape), value_rows.reshape(heads_shape), positions))
    attended = low(low_back(attended.reshape(SEQS * SEQ_LEN, D)))
    resid = inputs + low_back(dot_high(attended, w_out) + bias_out)
    normed_two = low(layer_norm(resid, gain_two, shift_two))
    hidden_pre = low_back(dot_high(normed_two, w_up) + bias_up)
    hidden_act = low(gelu_tanh(hidden_pre))
    return resid + dot_high(hidden_act, w_down) + bias_down

def reference(tokens, first_values, out_grad, block_place, owners, masters, moment_one, moment_two, vector_master, vector_moment_one, vector_moment_two):
    slot_rows = owners * CAP + slot_numbers(owners)
    flat = masters.astype(jnp.bfloat16)[slot_rows].reshape(-1).astype(jnp.float32)
    matrices = split_weights(flat)
    stored = jnp.arange(SEQ_LEN, dtype=jnp.int32)
    positions = jnp.repeat(block_place, BL, axis=1) * BL + (stored % BL)[None, :]
    inputs = tokens.reshape(SEQS * SEQ_LEN, D).astype(jnp.float32)
    firsts = first_values.reshape(SEQS * SEQ_LEN, HV).astype(jnp.float32)

    def layer(inputs, firsts, w_query, w_key, w_value, w_out, w_up, w_down, vector):
        return forward(inputs, firsts, w_query, w_key, w_value, w_out, w_up, w_down, vector, positions)
    result, pullback = jax.vjp(layer, inputs, firsts, *matrices, vector_master)
    grads = pullback(out_grad.reshape(SEQS * SEQ_LEN, D).astype(jnp.float32))
    grad_tiles = jnp.concatenate([g.reshape(-1) for g in grads[2:8]]).reshape(TILES, TILE_LEN)
    slot_grads = jnp.zeros((SLOTS, TILE_LEN), jnp.float32).at[slot_rows].set(grad_tiles)
    new_master, new_one, new_two = adam_step(masters, moment_one, moment_two, slot_grads, RATE_MATRIX, DECAY_MATRIX)
    vector_new, vector_one, vector_two = adam_step(vector_master, vector_moment_one, vector_moment_two, grads[8], RATE_VECTOR, 0.0)
    return (result.astype(jnp.bfloat16).reshape(SEQS, SEQ_LEN, D), grads[0].reshape(SEQS, SEQ_LEN, D), grads[1].reshape(SEQS, SEQ_LEN, HV), new_master, new_one, new_two, new_master.astype(jnp.bfloat16), vector_new, vector_one, vector_two)
```

```python
import jax
import jax.numpy as jnp
from jax import lax
from jax.sharding import PartitionSpec as P

D = 768
HD = 64
FF = 3072
STEP = 10
HV = 384


EPS_NORM = 1e-05
EPS_ADAM = 1e-08
BETA_ONE = 0.5
BETA_TWO = 0.5
RATE_MATRIX = 0.03
RATE_VECTOR = 0.25
DECAY_MATRIX = 0.1


def from_partner(value, axis, distance):
    mask = 2**distance
    pairs = [(source, source ^ mask) for source in range(lax.axis_size(axis))]
    return lax.ppermute(value, axis, pairs)


def layer_norm(values, norm_gain, norm_shift):
    center = jnp.mean(values, axis=-1, keepdims=True)
    centred = values - center
    spread = jnp.mean(centred * centred, axis=-1, keepdims=True)
    return centred * lax.rsqrt(spread + EPS_NORM) * norm_gain + norm_shift


def gelu_tanh(values):
    return (
        0.5
        * values
        * (1.0 + jnp.tanh(0.7978845608028654 * (values + 0.044715 * values * values * values)))
    )


def slot_numbers(owners):
    tile_order = jnp.arange(owners.shape[0], dtype=jnp.int32)
    earlier = (owners[None, :] == owners[:, None]) & (tile_order[None, :] < tile_order[:, None])
    return jnp.sum(earlier.astype(jnp.int32), axis=1)


def split_weights(flat):
    lengths = [D * D, D * D, D * HV, D * D, D * FF, FF * D]
    matrix_shapes = [(D, D), (D, D), (D, HV), (D, D), (D, FF), (FF, D)]
    pieces = []
    offset = 0
    for length, matrix_shape in zip(lengths, matrix_shapes):
        pieces.append(flat[offset : offset + length].reshape(matrix_shape))
        offset = offset + length
    return pieces


def split_vector(vector):
    pieces = [vector[i * D : (i + 1) * D] for i in range(7)]
    pieces.append(vector[7 * D : 7 * D + HV])
    pieces.append(vector[7 * D + HV :])
    return pieces


def adam_step(weight, first_moment, second_moment, gradient, step_rate, weight_decay):
    first_new = BETA_ONE * first_moment + (1.0 - BETA_ONE) * gradient
    second_new = BETA_TWO * second_moment + (1.0 - BETA_TWO) * gradient * gradient
    first_fix = 1.0 - BETA_ONE**STEP
    second_fix = 1.0 - BETA_TWO**STEP
    update = first_new / first_fix / (jnp.sqrt(second_new / second_fix) + EPS_ADAM)
    return (weight - step_rate * (update + weight_decay * weight), first_new, second_new)


def inverse_of(slot_rows, slot_total):
    tile_count = slot_rows.shape[0]
    return (
        jnp.full((slot_total,), tile_count, jnp.int32)
        .at[slot_rows]
        .set(jnp.arange(tile_count, dtype=jnp.int32))
    )


def masked_scores(query_part, key_part, near_pos, all_pos):
    scores = jnp.einsum(
        "qhd,khd->hqk", query_part, key_part, preferred_element_type=jnp.float32
    ) * HD ** (-0.5)
    allowed = all_pos[None, :] <= near_pos[:, None]
    return jnp.where(allowed[None], scores, -1e30)


def attend_block(packed):
    query_seq, key_seq, value_seq, near_pos, all_pos = packed
    value_heads = HV // HD
    outputs = []
    log_parts = []
    for head_group in range(2):
        columns = slice(head_group * HV, (head_group + 1) * HV)
        query_part = query_seq[:, columns].reshape(-1, value_heads, HD)
        key_part = key_seq[:, columns].reshape(-1, value_heads, HD)
        value_part = value_seq[:, columns].reshape(-1, value_heads, HD)
        scores = masked_scores(query_part, key_part, near_pos, all_pos)
        row_top = jnp.max(scores, axis=-1, keepdims=True)
        exponent = jnp.exp(scores - row_top)
        row_sum = jnp.sum(exponent, axis=-1, keepdims=True)
        weights_low = (exponent / row_sum).astype(jnp.bfloat16)
        mixed = jnp.einsum(
            "hqk,khd->qhd", weights_low, value_part, preferred_element_type=jnp.float32
        )
        outputs.append(mixed.reshape(-1, HV))
        log_parts.append((row_top + jnp.log(row_sum))[..., 0])
    return (jnp.concatenate(outputs, axis=1), jnp.concatenate(log_parts, axis=0))


def attend_back(packed):
    query_seq, key_seq, value_seq, near_pos, all_pos, log_total, grad_seq = packed
    value_heads = HV // HD
    query_grads = []
    key_grads = []
    value_grads = []
    for head_group in range(2):
        columns = slice(head_group * HV, (head_group + 1) * HV)
        query_part = query_seq[:, columns].reshape(-1, value_heads, HD)
        key_part = key_seq[:, columns].reshape(-1, value_heads, HD)
        value_part = value_seq[:, columns].reshape(-1, value_heads, HD)
        grad_part = grad_seq[:, columns].reshape(-1, value_heads, HD)
        scores = masked_scores(query_part, key_part, near_pos, all_pos)
        log_part = log_total[head_group * value_heads : (head_group + 1) * value_heads]
        chance = jnp.exp(scores - log_part[..., None])
        grad_chance = jnp.einsum(
            "qhd,khd->hqk", grad_part, value_part, preferred_element_type=jnp.float32
        )
        grad_value = jnp.einsum(
            "hqk,qhd->khd",
            chance.astype(jnp.bfloat16),
            grad_part,
            preferred_element_type=jnp.float32,
        )
        grad_score = (
            chance * (grad_chance - jnp.sum(chance * grad_chance, axis=-1, keepdims=True))
        ).astype(jnp.bfloat16)
        grad_query = jnp.einsum(
            "hqk,khd->qhd", grad_score, key_part, preferred_element_type=jnp.float32
        ) * HD ** (-0.5)
        grad_key = jnp.einsum(
            "hqk,qhd->khd", grad_score, query_part, preferred_element_type=jnp.float32
        ) * HD ** (-0.5)
        query_grads.append(grad_query.reshape(-1, HV))
        key_grads.append(grad_key.reshape(-1, HV))
        value_grads.append(grad_value.reshape(-1, HV))
    return (
        jnp.concatenate(query_grads, axis=1),
        jnp.concatenate(key_grads, axis=1),
        jnp.concatenate(value_grads, axis=1),
    )


def shards(
    tokens,
    first_values,
    out_grad,
    block_place,
    owners,
    masters,
    moment_one,
    moment_two,
    vector_master,
    vector_moment_one,
    vector_moment_two,
):
    capacity = masters.shape[0]
    tile_len = masters.shape[1]
    dp_count = lax.axis_size("dp")
    tile_count = owners.shape[0]
    slot_index = slot_numbers(owners)
    slot_rows = owners * capacity + slot_index
    owner_inverse = inverse_of(slot_rows, capacity * dp_count)
    gathered = lax.all_gather(masters.astype(jnp.bfloat16), "dp", axis=0, tiled=True)
    tiles = jnp.take(gathered, slot_rows, axis=0)
    w_query, w_key, w_value, w_out, w_up, w_down = split_weights(tiles.reshape(-1))
    (
        gain_one,
        shift_one,
        gain_two,
        shift_two,
        bias_query,
        bias_out,
        bias_down,
        bias_value,
        bias_up,
    ) = split_vector(vector_master)
    seq_count = lax.axis_size("seq")
    seq_here = lax.axis_index("seq")
    seqs_here, half_len, model_width = tokens.shape
    row_count = seqs_here * half_len
    per_device = block_place.shape[1] // seq_count
    block_len = half_len // per_device
    near_blocks = lax.dynamic_slice_in_dim(block_place, seq_here * per_device, per_device, 1)
    far_blocks = lax.dynamic_slice_in_dim(block_place, (1 - seq_here) * per_device, per_device, 1)
    within = jnp.arange(half_len, dtype=jnp.int32) % block_len
    near_pos = jnp.repeat(near_blocks, block_len, axis=1) * block_len + within[None, :]
    far_pos = jnp.repeat(far_blocks, block_len, axis=1) * block_len + within[None, :]
    all_pos = jnp.concatenate([near_pos, far_pos], axis=1)
    inputs = tokens.reshape(row_count, model_width).astype(jnp.float32)
    normed_one, norm_one_back = jax.vjp(layer_norm, inputs, gain_one, shift_one)
    normed_low = normed_one.astype(jnp.bfloat16)
    query_rows = (
        jnp.dot(normed_low, w_query, preferred_element_type=jnp.float32) + bias_query
    ).astype(jnp.bfloat16)
    key_rows = jnp.dot(normed_low, w_key, preferred_element_type=jnp.float32).astype(jnp.bfloat16)
    fresh_rows = (
        jnp.dot(normed_low, w_value, preferred_element_type=jnp.float32) + bias_value
    ).astype(jnp.bfloat16)
    value_rows = jnp.concatenate([fresh_rows, first_values.reshape(row_count, HV)], axis=1)
    key_far, value_far = from_partner((key_rows, value_rows), "seq", 0)
    seq_view = (seqs_here, half_len, model_width)
    key_all = jnp.concatenate([key_rows.reshape(seq_view), key_far.reshape(seq_view)], axis=1)
    value_all = jnp.concatenate([value_rows.reshape(seq_view), value_far.reshape(seq_view)], axis=1)
    query_view = query_rows.reshape(seq_view)
    attended, log_total = lax.map(attend_block, (query_view, key_all, value_all, near_pos, all_pos))
    attended_low = attended.reshape(row_count, model_width).astype(jnp.bfloat16)
    resid = inputs + jnp.dot(attended_low, w_out, preferred_element_type=jnp.float32) + bias_out
    normed_two, norm_two_back = jax.vjp(layer_norm, resid, gain_two, shift_two)
    normed_two_low = normed_two.astype(jnp.bfloat16)
    hidden_pre = jnp.dot(normed_two_low, w_up, preferred_element_type=jnp.float32) + bias_up
    hidden_act, gelu_back = jax.vjp(gelu_tanh, hidden_pre)
    hidden_low = hidden_act.astype(jnp.bfloat16)
    result = resid + jnp.dot(hidden_low, w_down, preferred_element_type=jnp.float32) + bias_down
    grad_result = out_grad.reshape(row_count, model_width)
    grad_w_down = jnp.einsum(
        "rf,rd->fd", hidden_low, grad_result, preferred_element_type=jnp.float32
    )
    grad_bias_down = jnp.sum(grad_result.astype(jnp.float32), axis=0)
    grad_act = jnp.einsum("rd,fd->rf", grad_result, w_down, preferred_element_type=jnp.float32)
    grad_pre_low = gelu_back(grad_act)[0].astype(jnp.bfloat16)
    grad_bias_up = jnp.sum(grad_pre_low.astype(jnp.float32), axis=0)
    grad_w_up = jnp.einsum(
        "rd,rf->df", normed_two_low, grad_pre_low, preferred_element_type=jnp.float32
    )
    grad_normed_two = jnp.einsum(
        "rf,df->rd", grad_pre_low, w_up, preferred_element_type=jnp.float32
    )
    grad_resid_norm, grad_gain_two, grad_shift_two = norm_two_back(grad_normed_two)
    grad_resid = grad_result.astype(jnp.float32) + grad_resid_norm
    grad_resid_low = grad_resid.astype(jnp.bfloat16)
    grad_bias_out = jnp.sum(grad_resid_low.astype(jnp.float32), axis=0)
    grad_w_out = jnp.einsum(
        "re,rd->ed", attended_low, grad_resid_low, preferred_element_type=jnp.float32
    )
    grad_attended = jnp.einsum(
        "rd,ed->re", grad_resid_low, w_out, preferred_element_type=jnp.float32
    ).astype(jnp.bfloat16)
    grad_query, grad_key_all, grad_value_all = lax.map(
        attend_back,
        (
            query_view,
            key_all,
            value_all,
            near_pos,
            all_pos,
            log_total,
            grad_attended.reshape(seq_view),
        ),
    )
    key_back, value_back = from_partner(
        (
            grad_key_all[:, half_len:].reshape(row_count, model_width),
            grad_value_all[:, half_len:].reshape(row_count, model_width),
        ),
        "seq",
        0,
    )
    grad_key = grad_key_all[:, :half_len].reshape(row_count, model_width) + key_back
    grad_value = grad_value_all[:, :half_len].reshape(row_count, model_width) + value_back
    grad_query_low = grad_query.reshape(row_count, model_width).astype(jnp.bfloat16)
    grad_key_low = grad_key.astype(jnp.bfloat16)
    grad_fresh_low = grad_value[:, :HV].astype(jnp.bfloat16)
    first_grad = grad_value[:, HV:]
    grad_bias_query = jnp.sum(grad_query_low.astype(jnp.float32), axis=0)
    grad_bias_value = jnp.sum(grad_fresh_low.astype(jnp.float32), axis=0)
    grad_w_query = jnp.einsum(
        "rd,re->de", normed_low, grad_query_low, preferred_element_type=jnp.float32
    )
    grad_w_key = jnp.einsum(
        "rd,re->de", normed_low, grad_key_low, preferred_element_type=jnp.float32
    )
    grad_w_value = jnp.einsum(
        "rd,re->de", normed_low, grad_fresh_low, preferred_element_type=jnp.float32
    )
    grad_normed_one = jnp.einsum(
        "re,de->rd", grad_query_low, w_query, preferred_element_type=jnp.float32
    )
    grad_normed_one = grad_normed_one + jnp.einsum(
        "re,de->rd", grad_key_low, w_key, preferred_element_type=jnp.float32
    )
    grad_normed_one = grad_normed_one + jnp.einsum(
        "re,de->rd", grad_fresh_low, w_value, preferred_element_type=jnp.float32
    )
    grad_input_norm, grad_gain_one, grad_shift_one = norm_one_back(grad_normed_one)
    tokens_grad = grad_resid + grad_input_norm
    grad_tiles = jnp.concatenate(
        [
            grad_w_query.reshape(-1),
            grad_w_key.reshape(-1),
            grad_w_value.reshape(-1),
            grad_w_out.reshape(-1),
            grad_w_up.reshape(-1),
            grad_w_down.reshape(-1),
        ]
    ).reshape(tile_count, tile_len)
    vector_grad = jnp.concatenate(
        [
            grad_gain_one,
            grad_shift_one,
            grad_gain_two,
            grad_shift_two,
            grad_bias_query,
            grad_bias_out,
            grad_bias_down,
            grad_bias_value,
            grad_bias_up,
        ]
    )
    vector_total = lax.psum(vector_grad, ("seq", "dp"))
    grad_low = grad_tiles.astype(jnp.bfloat16)
    picked = jnp.take(grad_low, jnp.minimum(owner_inverse, tile_count - 1), axis=0)
    slot_term = jnp.where((owner_inverse < tile_count)[:, None], picked, jnp.zeros((), jnp.bfloat16))
    owned_sum = lax.psum_scatter(slot_term, "dp", scatter_dimension=0, tiled=True)
    reduced = lax.psum(owned_sum, "seq").astype(jnp.float32)
    new_master, new_one, new_two = adam_step(
        masters, moment_one, moment_two, reduced, RATE_MATRIX, DECAY_MATRIX
    )
    vector_new, vector_one, vector_two = adam_step(
        vector_master, vector_moment_one, vector_moment_two, vector_total, RATE_VECTOR, 0.0
    )
    return (
        result.astype(jnp.bfloat16).reshape(seq_view),
        tokens_grad.reshape(seq_view),
        first_grad.reshape(seqs_here, half_len, HV),
        new_master,
        new_one,
        new_two,
        new_master.astype(jnp.bfloat16),
        vector_new,
        vector_one,
        vector_two,
    )


def solution(mesh):
    placed = (
        P("dp", "seq", None),
        P("dp", "seq", None),
        P("dp", "seq", None),
        P("dp", None),
        P(),
        P("dp", None),
        P("dp", None),
        P("dp", None),
        P(),
        P(),
        P(),
    )
    return jax.shard_map(
        shards,
        mesh=mesh,
        in_specs=placed,
        out_specs=(
            P("dp", "seq", None),
            P("dp", "seq", None),
            P("dp", "seq", None),
            P("dp", None),
            P("dp", None),
            P("dp", None),
            P("dp", None),
            P(),
            P(),
            P(),
        ),
        check_vma=False,
    )
```

```python
import functools

import jax
import jax.numpy as jnp
from jax import lax
from jax.experimental import pallas as pl
from jax.experimental.pallas import tpu as pltpu
from jax.sharding import PartitionSpec as P

D = 768
HD = 64
FF = 3072
STEP = 10
HV = 384
LANE = 128
QKV = 2 * D + HV
FF_STEP = 512
VEC = 7 * D + HV + FF
MIB = 1024 * 1024

EPS_NORM = 1e-05
EPS_ADAM = 1e-08
BETA_ONE = 0.5
BETA_TWO = 0.5
RATE_MATRIX = 0.03
RATE_VECTOR = 0.25
DECAY_MATRIX = 0.1
FAR = -1e30

BF16 = jnp.bfloat16
F32 = jnp.float32

NN = (((1,), (0,)), ((), ()))
NT = (((1,), (1,)), ((), ()))
TN = (((0,), (0,)), ((), ()))


def mm(left, right, dims=NN):
    return lax.dot_general(left, right, dims, preferred_element_type=F32)


def vec_part(vec_ref, index):
    if index < 7:
        return vec_ref[:, index * D : (index + 1) * D]
    if index == 7:
        return vec_ref[:, 7 * D : 7 * D + HV]
    return vec_ref[:, 7 * D + HV :]


def params(mib, **more):
    return pltpu.CompilerParams(vmem_limit_bytes=mib * MIB, **more)


def whole(shape):
    return pl.BlockSpec(shape, lambda *_: (0,) * len(shape))


def cost(flops, bytes_accessed, transcendentals=0):
    return pl.CostEstimate(
        flops=int(flops), bytes_accessed=int(bytes_accessed), transcendentals=int(transcendentals)
    )


def adam_step(weight, first_moment, second_moment, gradient, step_rate, weight_decay):
    first_new = BETA_ONE * first_moment + (1.0 - BETA_ONE) * gradient
    second_new = BETA_TWO * second_moment + (1.0 - BETA_TWO) * gradient * gradient
    first_fix = 1.0 - BETA_ONE**STEP
    second_fix = 1.0 - BETA_TWO**STEP
    update = first_new / first_fix / (jnp.sqrt(second_new / second_fix) + EPS_ADAM)
    return (weight - step_rate * (update + weight_decay * weight), first_new, second_new)


def slot_numbers(owners):
    tile_order = jnp.arange(owners.shape[0], dtype=jnp.int32)
    earlier = (owners[None, :] == owners[:, None]) & (tile_order[None, :] < tile_order[:, None])
    return jnp.sum(earlier.astype(jnp.int32), axis=1)


def normed(values):
    center = jnp.mean(values, axis=-1, keepdims=True)
    centred = values - center
    spread = jnp.mean(centred * centred, axis=-1, keepdims=True)
    rate = lax.rsqrt(spread + EPS_NORM)
    return centred * rate, rate


def norm_back(grad, hat, rate, gain):
    g = grad * gain
    return rate * (
        g - jnp.mean(g, axis=-1, keepdims=True) - hat * jnp.mean(g * hat, axis=-1, keepdims=True)
    )


def pack_kernel(src, dst, flat):
    rows = src.shape[0]
    for c in range(LANE):
        flat[pl.ds(c, rows, stride=LANE), :] = src[:, c * LANE : (c + 1) * LANE]
    dst[...] = flat[...].astype(BF16)


def pack_slots(masters):
    capacity, tile_len = masters.shape
    rows = 8 if capacity % 8 == 0 else capacity
    return pl.pallas_call(
        pack_kernel,
        out_shape=jax.ShapeDtypeStruct((capacity * LANE, LANE), BF16),
        grid=(capacity // rows,),
        in_specs=[pl.BlockSpec((rows, tile_len), lambda i: (i, 0))],
        out_specs=pl.BlockSpec((rows * LANE, LANE), lambda i: (i, 0)),
        scratch_shapes=[pltpu.VMEM((rows * LANE, LANE), F32)],
        compiler_params=params(32),
        cost_estimate=cost(0, capacity * tile_len * 6),
        name="pack_slots",
    )(masters)


def weight_chunks():
    chunks = [
        (0, 36, 6, 0, 0, 0),
        (36, 36, 6, 0, D, 0),
        (72, 18, 3, 0, 2 * D, 0),
        (90, 36, 6, 1, 0, 0),
    ]
    for i in range(4):
        chunks.append((126 + 36 * i, 36, 24, 2, 0, 192 * i))
    for i in range(4):
        chunks.append((270 + 36 * i, 36, 6, 3, 0, 768 * i))
    return chunks


def unpack_kernel(slot_rows, slots, w_qkv, w_out, w_up, w_down, stage, o_qkv, o_out, o_up, o_down, flat, sems, out_sems):
    chunks = weight_chunks()
    places = (o_qkv, o_out, o_up, o_down)
    ends = (w_qkv, w_out, w_up, w_down)

    for number, (first, tiles, _, _, _, _) in enumerate(chunks):

        @pl.loop(0, tiles)
        def _(i, first=first, number=number):
            t = first + i
            pltpu.make_async_copy(
                slots.at[pl.ds(pl.multiple_of(slot_rows[t] * LANE, LANE), LANE)],
                stage.at[pl.ds(pl.multiple_of(t * LANE, LANE), LANE)],
                sems.at[number],
            ).start()

    copies = []
    for number, (first, tiles, per_row, matrix, column, row) in enumerate(chunks):
        span = pl.ds(first * LANE, tiles * LANE)
        pltpu.make_async_copy(stage.at[span], stage.at[span], sems.at[number]).wait()
        place = places[matrix]
        lines = 3 * LANE // per_row

        @pl.loop(0, tiles // 6)
        def _(g, first=first, per_row=per_row, place=place, column=column, row=row, lines=lines):
            for half in range(2):
                base = pl.multiple_of(first * LANE + (2 * g + half) * 3 * LANE, LANE)
                flat[half] = stage[pl.ds(base, 3 * LANE), :].astype(F32)
            for half in range(2):
                top = pl.multiple_of(row + (2 * g + half) * lines, 16)
                for j in range(per_row):
                    place[pl.ds(top, lines), column + j * LANE : column + (j + 1) * LANE] = flat[
                        half, pl.ds(j, lines, stride=per_row), :
                    ].astype(BF16)

        rows = tiles * LANE // per_row
        columns = pl.ds(column, per_row * LANE)
        copy = pltpu.make_async_copy(
            place.at[pl.ds(row, rows), columns],
            ends[matrix].at[pl.ds(row, rows), columns],
            out_sems.at[number],
        )
        copy.start()
        copies.append(copy)
    for copy in copies:
        copy.wait()


def unpack_weights(slot_rows, slots):
    tile_count = slot_rows.shape[0]
    shapes = [(D, QKV), (D, D), (D, FF), (FF, D)]
    any_space = pl.BlockSpec(memory_space=pl.ANY)
    return pl.pallas_call(
        unpack_kernel,
        out_shape=[jax.ShapeDtypeStruct(s, BF16) for s in shapes],
        grid_spec=pltpu.PrefetchScalarGridSpec(
            num_scalar_prefetch=1,
            grid=(1,),
            in_specs=[any_space],
            out_specs=[any_space] * 4,
            scratch_shapes=[pltpu.VMEM((tile_count * LANE, LANE), BF16)]
            + [pltpu.VMEM(s, BF16) for s in shapes]
            + [
                pltpu.VMEM((2, 3 * LANE, LANE), F32),
                pltpu.SemaphoreType.DMA((12,)),
                pltpu.SemaphoreType.DMA((12,)),
            ],
        ),
        compiler_params=params(48),
        cost_estimate=cost(0, 4 * tile_count * LANE * LANE),
        name="unpack_weights",
    )(slot_rows, slots)


def project_kernel(tokens, firsts, w_qkv, vec, n1, q, k, v):
    hat, _ = normed(tokens[...].astype(F32))
    low = (hat * vec_part(vec, 0) + vec_part(vec, 1)).astype(BF16)
    n1[...] = low

    @pl.when(pl.program_id(0) < 2)
    def _():
        query = mm(low, w_qkv[:, :D]) + vec_part(vec, 4)
        q[...] = (query.astype(BF16).astype(F32) * HD ** (-0.5)).astype(BF16)

    k[...] = mm(low, w_qkv[:, D : 2 * D]).astype(BF16)
    v[:, :HV] = (mm(low, w_qkv[:, 2 * D :]) + vec_part(vec, 7)).astype(BF16)
    v[:, HV:] = firsts[...]


def project(tokens, firsts, w_qkv, vec):
    rows = tokens.shape[0]
    step = rows // 4
    by_row = lambda i: (i, 0)
    return pl.pallas_call(
        project_kernel,
        out_shape=[
            jax.ShapeDtypeStruct((rows, D), BF16),
            jax.ShapeDtypeStruct((rows // 2, D), BF16),
            jax.ShapeDtypeStruct((rows, D), BF16),
            jax.ShapeDtypeStruct((rows, D), BF16),
        ],
        grid=(4,),
        in_specs=[
            pl.BlockSpec((step, D), by_row),
            pl.BlockSpec((step, HV), by_row),
            whole((D, QKV)),
            whole((1, VEC)),
        ],
        out_specs=[
            pl.BlockSpec((step, D), by_row),
            pl.BlockSpec((step, D), lambda i: (jnp.minimum(i, 1), 0)),
            pl.BlockSpec((step, D), by_row),
            pl.BlockSpec((step, D), by_row),
        ],
        compiler_params=params(48),
        cost_estimate=cost(2 * rows * D * QKV, 2 * D * QKV + rows * D * 10),
        name="project",
    )(tokens, firsts, w_qkv, vec)


def attend_kernel(q, k, v, row_pos, column_pos, out, chance, bias):
    queries = q.shape[0]
    block = queries // 2

    @pl.when(pl.program_id(0) == 0)
    def _():
        bias[...] = jnp.where(column_pos[...] <= row_pos[...], 0.0, FAR)

    for head in range(2):
        cols = slice(head * HD, (head + 1) * HD)
        key = k[:, cols]
        value = v[:, cols]
        for part in range(2):
            near = slice(part * block, (part + 1) * block)
            scores = mm(key, q[near, cols], NT) + bias[:, near]
            top = jnp.max(scores, axis=0, keepdims=True)
            power = jnp.exp(scores - top)
            total = jnp.sum(power, axis=0, keepdims=True)
            weights = (power * (1.0 / total)).astype(BF16)
            chance[head, :, near] = weights
            mixed = mm(value, weights, TN)
            out[near, cols] = mixed.T.astype(BF16)


def attend(q, k, v, row_pos, column_pos):
    queries, keys = q.shape[0], k.shape[0]
    pairs = D // LANE
    by_column = lambda i: (0, i)
    return pl.pallas_call(
        attend_kernel,
        out_shape=[
            jax.ShapeDtypeStruct((queries, D), BF16),
            jax.ShapeDtypeStruct((2 * pairs, keys, queries), BF16),
        ],
        grid=(pairs,),
        in_specs=[
            pl.BlockSpec((queries, LANE), by_column),
            pl.BlockSpec((keys, LANE), by_column),
            pl.BlockSpec((keys, LANE), by_column),
            whole((1, queries)),
            whole((keys, 1)),
        ],
        out_specs=[
            pl.BlockSpec((queries, LANE), by_column),
            pl.BlockSpec((2, keys, queries), lambda i: (i, 0, 0)),
        ],
        scratch_shapes=[pltpu.VMEM((keys, queries), F32)],
        compiler_params=params(48),
        cost_estimate=cost(4 * queries * keys * D, 24 * queries * keys, 12 * queries * keys),
        name="attend",
    )(q, k, v, row_pos, column_pos)


def hidden_kernel(
    tokens, att, og, w_out, w_up, w_down, vec,
    result, grad_resid, resid_low, grad_att, d_up, d_down, vec_grad,
    resid, hat, n2, rate, acc, acc_grad, flat_up, flat_down,
):
    step = pl.program_id(0)
    per_row = D // LANE
    wide = FF // LANE

    @pl.when(step == 0)
    def _():
        base = tokens[...].astype(F32) + mm(att[...], w_out[...]) + vec_part(vec, 5)
        resid[...] = base
        unit, scale = normed(base)
        hat[...] = unit
        rate[...] = scale
        n2[...] = (unit * vec_part(vec, 2) + vec_part(vec, 3)).astype(BF16)
        vec_grad[...] = jnp.zeros_like(vec_grad)

    start = pl.multiple_of(7 * D + HV + step * FF_STEP, LANE)
    pre = mm(n2[...], w_up[...]) + vec[:, pl.ds(start, FF_STEP)]
    square = pre * pre
    bent = jnp.tanh(0.7978845608028654 * (pre + 0.044715 * square * pre))
    half = 0.5 * (1.0 + bent)
    act = (pre * half).astype(BF16)
    slope = half + (0.5 * 0.7978845608028654) * pre * (1.0 - bent * bent) * (1.0 + 0.134145 * square)
    grad_pre32 = mm(og[...], w_down[...], NT) * slope
    grad_pre = grad_pre32.astype(BF16)
    vec_grad[:, pl.ds(start, FF_STEP)] = jnp.sum(grad_pre.astype(F32), axis=0, keepdims=True)
    more = mm(act, w_down[...])
    more_grad = mm(grad_pre, w_up[...], NT)

    @pl.when(step == 0)
    def _():
        acc[...] = more
        acc_grad[...] = more_grad

    @pl.when(step > 0)
    def _():
        acc[...] += more
        acc_grad[...] += more_grad

    down = mm(act, og[...], TN)
    for j in range(per_row):
        flat_down[pl.ds(j, FF_STEP, stride=per_row), :] = down[:, j * LANE : (j + 1) * LANE]
    d_down[...] = flat_down[...].astype(BF16)
    up = mm(n2[...], grad_pre, TN)
    for j in range(FF_STEP // LANE):
        flat_up[pl.ds(step * (FF_STEP // LANE) + j, D, stride=wide), :] = up[
            :, j * LANE : (j + 1) * LANE
        ]

    @pl.when(step == FF // FF_STEP - 1)
    def _():
        d_up[...] = flat_up[...].astype(BF16)
        result[...] = (resid[...] + acc[...] + vec_part(vec, 6)).astype(BF16)
        grad = acc_grad[...]
        unit = hat[...]
        vec_grad[:, 2 * D : 3 * D] = jnp.sum(grad * unit, axis=0, keepdims=True)
        vec_grad[:, 3 * D : 4 * D] = jnp.sum(grad, axis=0, keepdims=True)
        given = og[...].astype(F32)
        back = given + norm_back(grad, unit, rate[...], vec_part(vec, 2))
        grad_resid[...] = back
        low = back.astype(BF16)
        resid_low[...] = low
        vec_grad[:, 5 * D : 6 * D] = jnp.sum(low.astype(F32), axis=0, keepdims=True)
        vec_grad[:, 6 * D : 7 * D] = jnp.sum(given, axis=0, keepdims=True)
        grad_att[...] = mm(low, w_out[...], NT).astype(BF16)


def hidden(tokens, att, og, w_out, w_up, w_down, vec):
    rows = tokens.shape[0]
    line = (rows, D)
    flat_rows = FF * D // LANE
    return pl.pallas_call(
        hidden_kernel,
        out_shape=[
            jax.ShapeDtypeStruct(line, BF16),
            jax.ShapeDtypeStruct(line, F32),
            jax.ShapeDtypeStruct(line, BF16),
            jax.ShapeDtypeStruct(line, BF16),
            jax.ShapeDtypeStruct((flat_rows, LANE), BF16),
            jax.ShapeDtypeStruct((flat_rows, LANE), BF16),
            jax.ShapeDtypeStruct((1, VEC), F32),
        ],
        grid=(FF // FF_STEP,),
        in_specs=[
            whole(line),
            whole(line),
            whole(line),
            whole((D, D)),
            pl.BlockSpec((D, FF_STEP), lambda i: (0, i)),
            pl.BlockSpec((FF_STEP, D), lambda i: (i, 0)),
            whole((1, VEC)),
        ],
        out_specs=[
            whole(line),
            whole(line),
            whole(line),
            whole(line),
            whole((flat_rows, LANE)),
            pl.BlockSpec((FF_STEP * D // LANE, LANE), lambda i: (i, 0)),
            whole((1, VEC)),
        ],
        scratch_shapes=[
            pltpu.VMEM(line, F32),
            pltpu.VMEM(line, F32),
            pltpu.VMEM(line, BF16),
            pltpu.VMEM((rows, 1), F32),
            pltpu.VMEM(line, F32),
            pltpu.VMEM(line, F32),
            pltpu.VMEM((flat_rows, LANE), F32),
            pltpu.VMEM((FF_STEP * D // LANE, LANE), F32),
        ],
        compiler_params=params(58),
        cost_estimate=cost(2 * rows * D * (6 * FF + 2 * D), 8 * D * FF + 20 * rows * D, rows * FF),
        name="hidden",
    )(tokens, att, og, w_out, w_up, w_down, vec)


def attend_back_kernel(q, k, v, att, grad_att, chance, d_q, d_k, d_fresh, d_first):
    pair = pl.program_id(0)
    for head in range(2):
        cols = slice(head * HD, (head + 1) * HD)
        grad = grad_att[:, cols]
        weights = chance[head]
        shared = grad.astype(F32) * att[:, cols].astype(F32)
        delta = jnp.sum(shared.T, axis=0, keepdims=True)
        grad_chance = mm(v[:, cols], grad, NT)
        grad_scores = (weights.astype(F32) * (grad_chance - delta)).astype(BF16)
        grad_value = mm(weights, grad)

        @pl.when(pair < 3)
        def _(grad_value=grad_value, cols=cols):
            d_fresh[:, cols] = grad_value.astype(BF16)

        @pl.when(pair >= 3)
        def _(grad_value=grad_value, cols=cols):
            d_first[:, cols] = grad_value

        d_k[:, cols] = mm(grad_scores, q[:, cols]).astype(BF16)
        d_q[:, cols] = (mm(k[:, cols], grad_scores, TN).T * HD ** (-0.5)).astype(BF16)


def attend_back(q, k, v, att, grad_att, chance):
    queries, keys = q.shape[0], k.shape[0]
    pairs = D // LANE
    by_column = lambda i: (0, i)
    return pl.pallas_call(
        attend_back_kernel,
        out_shape=[
            jax.ShapeDtypeStruct((queries, D), BF16),
            jax.ShapeDtypeStruct((keys, D), BF16),
            jax.ShapeDtypeStruct((keys, HV), BF16),
            jax.ShapeDtypeStruct((keys, HV), F32),
        ],
        grid=(pairs,),
        in_specs=[
            pl.BlockSpec((queries, LANE), by_column),
            pl.BlockSpec((keys, LANE), by_column),
            pl.BlockSpec((keys, LANE), by_column),
            pl.BlockSpec((queries, LANE), by_column),
            pl.BlockSpec((queries, LANE), by_column),
            pl.BlockSpec((2, keys, queries), lambda i: (i, 0, 0)),
        ],
        out_specs=[
            pl.BlockSpec((queries, LANE), by_column),
            pl.BlockSpec((keys, LANE), by_column),
            pl.BlockSpec((keys, LANE), lambda i: (0, jnp.minimum(i, 2))),
            pl.BlockSpec((keys, LANE), lambda i: (0, jnp.maximum(i - 3, 0))),
        ],
        compiler_params=params(48),
        cost_estimate=cost(8 * queries * keys * D, 24 * queries * keys),
        name="attend_back",
    )(q, k, v, att, grad_att, chance)


def project_back_kernel(
    tokens, n1, d_q, d_k, d_fresh, att, resid_low, w_qkv, vec,
    grad_near, grad_far, d_rest, vec_grad, flat,
):
    rows = n1.shape[0] // 2
    per_row = D // LANE
    grads = mm(d_k[...], w_qkv[:, D : 2 * D], NT) + mm(d_fresh[...], w_qkv[:, 2 * D :], NT)
    near = grads[:rows] + mm(d_q[...], w_qkv[:, :D], NT)
    far = grads[rows:]
    grad_near[...] = near
    grad_far[...] = far.astype(BF16)
    hat, _ = normed(tokens[...].astype(F32))
    vec_grad[...] = jnp.zeros_like(vec_grad)
    vec_grad[:, :D] = jnp.sum(near * hat[:rows], axis=0, keepdims=True) + jnp.sum(
        far * hat[rows:], axis=0, keepdims=True
    )
    vec_grad[:, D : 2 * D] = jnp.sum(near, axis=0, keepdims=True) + jnp.sum(
        far, axis=0, keepdims=True
    )
    vec_grad[:, 4 * D : 5 * D] = jnp.sum(d_q[...].astype(F32), axis=0, keepdims=True)
    vec_grad[:, 7 * D : 7 * D + HV] = jnp.sum(d_fresh[...].astype(F32), axis=0, keepdims=True)
    pieces = (
        (n1, d_q, rows, 0, per_row),
        (n1, d_k, 2 * rows, D * per_row, per_row),
        (n1, d_fresh, 2 * rows, 2 * D * per_row, HV // LANE),
        (att, resid_low, rows, 2 * D * per_row + D * HV // LANE, per_row),
    )
    for left, right, count, start, columns in pieces:
        product = mm(left[:count], right[:count], TN)
        size = D * columns
        for j in range(columns):
            flat[pl.ds(j, D, stride=columns), :] = product[:, j * LANE : (j + 1) * LANE]
        d_rest[start : start + size] = flat[:size].astype(BF16)
    used = 3 * D * per_row + D * HV // LANE
    d_rest[used:] = jnp.zeros((d_rest.shape[0] - used, LANE), BF16)


def project_back(tokens, n1, d_q, d_k, d_fresh, att, resid_low, w_qkv, vec):
    rows = n1.shape[0] // 2
    vm = pl.BlockSpec(memory_space=pltpu.VMEM)
    return pl.pallas_call(
        project_back_kernel,
        out_shape=[
            jax.ShapeDtypeStruct((rows, D), F32),
            jax.ShapeDtypeStruct((rows, D), BF16),
            jax.ShapeDtypeStruct((128 * LANE, LANE), BF16),
            jax.ShapeDtypeStruct((1, VEC), F32),
        ],
        in_specs=[vm] * 9,
        out_specs=[vm] * 4,
        scratch_shapes=[pltpu.VMEM((D * D // LANE, LANE), F32)],
        compiler_params=params(58),
        cost_estimate=cost(2 * rows * D * (7 * D), 14 * MIB),
        name="project_back",
    )(tokens, n1, d_q, d_k, d_fresh, att, resid_low, w_qkv, vec)


def adam_kernel(places, grads, used, weight, one, two, new, new_one, new_two, low, stage, flat, sems):
    step = pl.program_id(0)
    rows = weight.shape[0]
    steps = pl.num_programs(0)

    @pl.when(step == 0)
    def _():
        @pl.loop(0, steps)
        def _(s):
            @pl.loop(0, rows)
            def _(i):
                slot = s * rows + i
                pltpu.make_async_copy(
                    grads.at[pl.ds(pl.multiple_of(places[slot] * LANE, LANE), LANE)],
                    stage.at[pl.ds(pl.multiple_of(slot * LANE, LANE), LANE)],
                    sems.at[s],
                ).start()

    span = pl.ds(pl.multiple_of(step * rows * LANE, LANE), rows * LANE)
    pltpu.make_async_copy(stage.at[span], stage.at[span], sems.at[step]).wait()
    flat[...] = stage[span, :].astype(F32)
    keep = used[...] > 0.0
    for c in range(LANE):
        columns = slice(c * LANE, (c + 1) * LANE)
        gradient = jnp.where(keep, flat[pl.ds(c, rows, stride=LANE), :], 0.0)
        after, after_one, after_two = adam_step(
            weight[:, columns], one[:, columns], two[:, columns], gradient, RATE_MATRIX, DECAY_MATRIX
        )
        new[:, columns] = after
        new_one[:, columns] = after_one
        new_two[:, columns] = after_two
        low[:, columns] = after.astype(BF16)


def adam(places, grads, used, weight, one, two):
    capacity, tile_len = weight.shape
    rows = 8 if capacity % 8 == 0 else capacity
    steps = capacity // rows
    block = pl.BlockSpec((rows, tile_len), lambda i, *_: (i, 0))
    return pl.pallas_call(
        adam_kernel,
        out_shape=[jax.ShapeDtypeStruct(weight.shape, F32)] * 3
        + [jax.ShapeDtypeStruct(weight.shape, BF16)],
        grid_spec=pltpu.PrefetchScalarGridSpec(
            num_scalar_prefetch=1,
            grid=(steps,),
            in_specs=[
                pl.BlockSpec(memory_space=pl.ANY),
                pl.BlockSpec((rows, LANE), lambda i, *_: (i, 0)),
                block,
                block,
                block,
            ],
            out_specs=[block] * 4,
            scratch_shapes=[
                pltpu.VMEM((capacity * LANE, LANE), BF16),
                pltpu.VMEM((rows * LANE, LANE), F32),
                pltpu.SemaphoreType.DMA((steps,)),
            ],
        ),
        compiler_params=params(48),
        cost_estimate=cost(20 * capacity * tile_len, 28 * capacity * tile_len, 2 * capacity * tile_len),
        name="adam",
    )(places, grads, used, weight, one, two)


def swap(value):
    return lax.ppermute(value, "seq", [(0, 1), (1, 0)])


def shards(
    tokens,
    first_values,
    out_grad,
    block_place,
    owners,
    masters,
    moment_one,
    moment_two,
    vector_master,
    vector_moment_one,
    vector_moment_two,
):
    capacity = masters.shape[0]
    dp_count = lax.axis_size("dp")
    tile_count = owners.shape[0]
    dp_here = lax.axis_index("dp")
    seq_here = lax.axis_index("seq")
    _, half_len, _ = tokens.shape

    tokens = tokens.reshape(half_len, D)
    firsts = first_values.reshape(half_len, HV)
    given = out_grad.reshape(half_len, D)
    tokens_far, firsts_far = swap(tokens), swap(firsts)
    packed = pack_slots(masters)
    slots = lax.all_gather(packed, "dp", axis=0, tiled=True)

    slot_index = slot_numbers(owners)
    slot_rows = owners * capacity + slot_index
    mine = (owners == dp_here)[None, :] & (
        slot_index[None, :] == jnp.arange(capacity, dtype=jnp.int32)[:, None]
    )
    tile_order = jnp.arange(tile_count, dtype=jnp.int32)
    tile_here = jnp.sum(jnp.where(mine, tile_order[None, :], 0), axis=1)
    tile_here = tile_here + jnp.where(tile_here >= 126, 2, 0)
    used = jnp.broadcast_to(
        jnp.any(mine, axis=1).astype(F32)[:, None], (capacity, LANE)
    )

    blocks = block_place.reshape(-1)
    per_device = blocks.shape[0] // 2
    block_len = half_len // per_device
    ordered = jnp.roll(blocks, -seq_here * per_device)
    all_pos = (
        ordered[:, None] * block_len + jnp.arange(block_len, dtype=jnp.int32)[None, :]
    ).reshape(-1)
    row_pos = all_pos[:half_len].reshape(1, half_len)
    column_pos = all_pos.reshape(2 * half_len, 1)

    vec = vector_master.reshape(1, VEC)
    tokens_all = jnp.concatenate([tokens, tokens_far], axis=0)
    firsts_all = jnp.concatenate([firsts, firsts_far], axis=0)

    w_qkv, w_out, w_up, w_down = unpack_weights(slot_rows, slots)
    n1, q, k, v = project(tokens_all, firsts_all, w_qkv, vec)
    att, chance = attend(q, k, v, row_pos, column_pos)
    result, grad_resid, resid_low, grad_att, d_up, d_down, vec_one = hidden(
        tokens, att, given, w_out, w_up, w_down, vec
    )
    d_q, d_k, d_fresh, d_first = attend_back(q, k, v, att, grad_att, chance)
    grad_near, grad_far, d_rest, vec_two = project_back(
        tokens_all, n1, d_q, d_k, d_fresh, att, resid_low, w_qkv, vec
    )
    grad_back = swap(grad_far)
    first_back = swap(d_first[half_len:].astype(BF16))
    both = ("seq", "dp")
    grads = lax.psum(jnp.concatenate([d_rest, d_up, d_down], axis=0), both)
    vector_total = lax.psum((vec_one + vec_two).reshape(VEC), both)

    grad_n1 = grad_near + grad_back.astype(F32)
    hat, rate = normed(tokens.astype(F32))
    tokens_grad = grad_resid + norm_back(grad_n1, hat, rate, vec[:, :D])
    first_grad = d_first[:half_len] + first_back.astype(F32)

    new_master, new_one, new_two, new_low = adam(
        tile_here, grads, used, masters, moment_one, moment_two
    )
    vector_new, vector_one, vector_two = adam_step(
        vector_master, vector_moment_one, vector_moment_two, vector_total, RATE_VECTOR, 0.0
    )
    return (
        result.reshape(1, half_len, D),
        tokens_grad.reshape(1, half_len, D),
        first_grad.reshape(1, half_len, HV),
        new_master,
        new_one,
        new_two,
        new_low,
        vector_new,
        vector_one,
        vector_two,
    )


def solution(mesh):
    rows = P("dp", "seq", None)
    slots = P("dp", None)
    return jax.shard_map(
        shards,
        mesh=mesh,
        in_specs=(rows, rows, rows, slots, P(), slots, slots, slots, P(), P(), P()),
        out_specs=(rows, rows, rows, slots, slots, slots, slots, P(), P(), P()),
        check_vma=False,
    )
```

```python
import functools

import jax
import jax.numpy as jnp
from jax import lax
from jax.experimental import pallas as pl
from jax.experimental.pallas import tpu as pltpu
from jax.sharding import PartitionSpec as P

D = 768
HD = 64
FF = 3072
STEP = 10
HV = 384
LANE = 128
QKV = 2 * D + HV
FF_STEP = 512
VEC = 7 * D + HV + FF
MIB = 1024 * 1024
LINE = 4
REST = 126 * LANE

EPS_NORM = 1e-05
EPS_ADAM = 1e-08
BETA_ONE = 0.5
BETA_TWO = 0.5
RATE_MATRIX = 0.03
RATE_VECTOR = 0.25
DECAY_MATRIX = 0.1
FAR = -1e30

BF16 = jnp.bfloat16
F32 = jnp.float32

NN = (((1,), (0,)), ((), ()))
NT = (((1,), (1,)), ((), ()))
TN = (((0,), (0,)), ((), ()))


def mm(left, right, dims=NN):
    return lax.dot_general(left, right, dims, preferred_element_type=F32)


def vec_part(vec_ref, index):
    if index < 7:
        return vec_ref[:, index * D : (index + 1) * D]
    if index == 7:
        return vec_ref[:, 7 * D : 7 * D + HV]
    return vec_ref[:, 7 * D + HV :]


def params(mib, **more):
    return pltpu.CompilerParams(vmem_limit_bytes=mib * MIB, **more)


def whole(shape):
    return pl.BlockSpec(shape, lambda *_: (0,) * len(shape))


def cost(flops, bytes_accessed, transcendentals=0):
    return pl.CostEstimate(
        flops=int(flops), bytes_accessed=int(bytes_accessed), transcendentals=int(transcendentals)
    )


def adam_step(weight, first_moment, second_moment, gradient, step_rate, weight_decay):
    first_new = BETA_ONE * first_moment + (1.0 - BETA_ONE) * gradient
    second_new = BETA_TWO * second_moment + (1.0 - BETA_TWO) * gradient * gradient
    first_fix = 1.0 - BETA_ONE**STEP
    second_fix = 1.0 - BETA_TWO**STEP
    update = first_new / first_fix / (jnp.sqrt(second_new / second_fix) + EPS_ADAM)
    return (weight - step_rate * (update + weight_decay * weight), first_new, second_new)


def slot_numbers(owners):
    tile_order = jnp.arange(owners.shape[0], dtype=jnp.int32)
    earlier = (owners[None, :] == owners[:, None]) & (tile_order[None, :] < tile_order[:, None])
    return jnp.sum(earlier.astype(jnp.int32), axis=1)


def normed(values):
    center = jnp.mean(values, axis=-1, keepdims=True)
    centred = values - center
    spread = jnp.mean(centred * centred, axis=-1, keepdims=True)
    rate = lax.rsqrt(spread + EPS_NORM)
    return centred * rate, rate


def norm_back(grad, hat, rate, gain):
    g = grad * gain
    return rate * (
        g - jnp.mean(g, axis=-1, keepdims=True) - hat * jnp.mean(g * hat, axis=-1, keepdims=True)
    )


def pack_kernel(src, dst, flat):
    rows = src.shape[0]
    for c in range(LANE):
        flat[pl.ds(c, rows, stride=LANE), :] = src[:, c * LANE : (c + 1) * LANE]
    dst[...] = flat[...].astype(BF16)


def pack_slots(masters):
    capacity, tile_len = masters.shape
    rows = 8 if capacity % 8 == 0 else capacity
    return pl.pallas_call(
        pack_kernel,
        out_shape=jax.ShapeDtypeStruct((capacity * LANE, LANE), BF16),
        grid=(capacity // rows,),
        in_specs=[pl.BlockSpec((rows, tile_len), lambda i: (i, 0))],
        out_specs=pl.BlockSpec((rows * LANE, LANE), lambda i: (i, 0)),
        scratch_shapes=[pltpu.VMEM((rows * LANE, LANE), F32)],
        compiler_params=params(32),
        cost_estimate=cost(0, capacity * tile_len * 6),
        name="pack_slots",
    )(masters)


def weight_chunks():
    chunks = [
        (0, 36, 6, 0, 0, 0),
        (36, 36, 6, 0, D, 0),
        (72, 18, 3, 0, 2 * D, 0),
        (90, 36, 6, 1, 0, 0),
    ]
    for i in range(4):
        chunks.append((126 + 36 * i, 36, 24, 2, 0, 192 * i))
    for i in range(4):
        chunks.append((270 + 36 * i, 36, 6, 3, 0, 768 * i))
    return chunks


def unpack_kernel(slot_rows, slots, w_qkv, w_out, w_up, w_down, stage, o_qkv, o_out, o_up, o_down, flat, sems, out_sems):
    chunks = weight_chunks()
    places = (o_qkv, o_out, o_up, o_down)
    ends = (w_qkv, w_out, w_up, w_down)

    for number, (first, tiles, _, _, _, _) in enumerate(chunks):

        @pl.loop(0, tiles)
        def _(i, first=first, number=number):
            t = first + i
            pltpu.make_async_copy(
                slots.at[pl.ds(pl.multiple_of(slot_rows[t] * LANE, LANE), LANE)],
                stage.at[pl.ds(pl.multiple_of(t * LANE, LANE), LANE)],
                sems.at[number],
            ).start()

    copies = []
    for number, (first, tiles, per_row, matrix, column, row) in enumerate(chunks):
        span = pl.ds(first * LANE, tiles * LANE)
        pltpu.make_async_copy(stage.at[span], stage.at[span], sems.at[number]).wait()
        place = places[matrix]
        lines = 3 * LANE // per_row

        @pl.loop(0, tiles // 6)
        def _(g, first=first, per_row=per_row, place=place, column=column, row=row, lines=lines):
            for half in range(2):
                base = pl.multiple_of(first * LANE + (2 * g + half) * 3 * LANE, LANE)
                flat[half] = stage[pl.ds(base, 3 * LANE), :].astype(F32)
            for half in range(2):
                top = pl.multiple_of(row + (2 * g + half) * lines, 16)
                for j in range(per_row):
                    place[pl.ds(top, lines), column + j * LANE : column + (j + 1) * LANE] = flat[
                        half, pl.ds(j, lines, stride=per_row), :
                    ].astype(BF16)

        rows = tiles * LANE // per_row
        columns = pl.ds(column, per_row * LANE)
        copy = pltpu.make_async_copy(
            place.at[pl.ds(row, rows), columns],
            ends[matrix].at[pl.ds(row, rows), columns],
            out_sems.at[number],
        )
        copy.start()
        copies.append(copy)
    for copy in copies:
        copy.wait()


def unpack_weights(slot_rows, slots):
    tile_count = slot_rows.shape[0]
    shapes = [(D, QKV), (D, D), (D, FF), (FF, D)]
    any_space = pl.BlockSpec(memory_space=pl.ANY)
    return pl.pallas_call(
        unpack_kernel,
        out_shape=[jax.ShapeDtypeStruct(s, BF16) for s in shapes],
        grid_spec=pltpu.PrefetchScalarGridSpec(
            num_scalar_prefetch=1,
            grid=(1,),
            in_specs=[any_space],
            out_specs=[any_space] * 4,
            scratch_shapes=[pltpu.VMEM((tile_count * LANE, LANE), BF16)]
            + [pltpu.VMEM(s, BF16) for s in shapes]
            + [
                pltpu.VMEM((2, 3 * LANE, LANE), F32),
                pltpu.SemaphoreType.DMA((12,)),
                pltpu.SemaphoreType.DMA((12,)),
            ],
        ),
        compiler_params=params(48),
        cost_estimate=cost(0, 4 * tile_count * LANE * LANE),
        name="unpack_weights",
    )(slot_rows, slots)


def project_kernel(tokens, firsts, w_qkv, vec, n1, q, k, v):
    hat, _ = normed(tokens[...].astype(F32))
    low = (hat * vec_part(vec, 0) + vec_part(vec, 1)).astype(BF16)
    n1[...] = low

    @pl.when(pl.program_id(0) < 2)
    def _():
        query = mm(low, w_qkv[:, :D]) + vec_part(vec, 4)
        q[...] = (query.astype(BF16).astype(F32) * HD ** (-0.5)).astype(BF16)

    k[...] = mm(low, w_qkv[:, D : 2 * D]).astype(BF16)
    v[:, :HV] = (mm(low, w_qkv[:, 2 * D :]) + vec_part(vec, 7)).astype(BF16)
    v[:, HV:] = firsts[...]


def project(tokens, firsts, w_qkv, vec):
    rows = tokens.shape[0]
    step = rows // 4
    by_row = lambda i: (i, 0)
    return pl.pallas_call(
        project_kernel,
        out_shape=[
            jax.ShapeDtypeStruct((rows, D), BF16),
            jax.ShapeDtypeStruct((rows // 2, D), BF16),
            jax.ShapeDtypeStruct((rows, D), BF16),
            jax.ShapeDtypeStruct((rows, D), BF16),
        ],
        grid=(4,),
        in_specs=[
            pl.BlockSpec((step, D), by_row),
            pl.BlockSpec((step, HV), by_row),
            whole((D, QKV)),
            whole((1, VEC)),
        ],
        out_specs=[
            pl.BlockSpec((step, D), by_row),
            pl.BlockSpec((step, D), lambda i: (jnp.minimum(i, 1), 0)),
            pl.BlockSpec((step, D), by_row),
            pl.BlockSpec((step, D), by_row),
        ],
        compiler_params=params(48),
        cost_estimate=cost(2 * rows * D * QKV, 2 * D * QKV + rows * D * 10),
        name="project",
    )(tokens, firsts, w_qkv, vec)


def attend_kernel(q, k, v, row_pos, column_pos, out, chance, bias):
    queries = q.shape[0]
    block = queries // 2

    @pl.when(pl.program_id(0) == 0)
    def _():
        bias[...] = jnp.where(column_pos[...] <= row_pos[...], 0.0, FAR)

    for head in range(2):
        cols = slice(head * HD, (head + 1) * HD)
        key = k[:, cols]
        value = v[:, cols]
        for part in range(2):
            near = slice(part * block, (part + 1) * block)
            scores = mm(key, q[near, cols], NT) + bias[:, near]
            top = jnp.max(scores, axis=0, keepdims=True)
            power = jnp.exp(scores - top)
            total = jnp.sum(power, axis=0, keepdims=True)
            weights = (power * (1.0 / total)).astype(BF16)
            chance[head, :, near] = weights
            mixed = mm(value, weights, TN)
            out[near, cols] = mixed.T.astype(BF16)


def attend(q, k, v, row_pos, column_pos):
    queries, keys = q.shape[0], k.shape[0]
    pairs = D // LANE
    by_column = lambda i: (0, i)
    return pl.pallas_call(
        attend_kernel,
        out_shape=[
            jax.ShapeDtypeStruct((queries, D), BF16),
            jax.ShapeDtypeStruct((2 * pairs, keys, queries), BF16),
        ],
        grid=(pairs,),
        in_specs=[
            pl.BlockSpec((queries, LANE), by_column),
            pl.BlockSpec((keys, LANE), by_column),
            pl.BlockSpec((keys, LANE), by_column),
            whole((1, queries)),
            whole((keys, 1)),
        ],
        out_specs=[
            pl.BlockSpec((queries, LANE), by_column),
            pl.BlockSpec((2, keys, queries), lambda i: (i, 0, 0)),
        ],
        scratch_shapes=[pltpu.VMEM((keys, queries), F32)],
        compiler_params=params(48),
        cost_estimate=cost(4 * queries * keys * D, 24 * queries * keys, 12 * queries * keys),
        name="attend",
    )(q, k, v, row_pos, column_pos)


def hidden_kernel(
    tokens, att, og, w_out, w_up, w_down, vec,
    result, grad_resid, resid_low, grad_att, d_up, d_down, vec_grad,
    resid, hat, n2, rate, acc, acc_grad, flat_up, flat_down,
):
    step = pl.program_id(0)
    per_row = D // LANE
    wide = FF // LANE

    @pl.when(step == 0)
    def _():
        base = tokens[...].astype(F32) + mm(att[...], w_out[...]) + vec_part(vec, 5)
        resid[...] = base
        unit, scale = normed(base)
        hat[...] = unit
        rate[...] = scale
        n2[...] = (unit * vec_part(vec, 2) + vec_part(vec, 3)).astype(BF16)
        vec_grad[...] = jnp.zeros_like(vec_grad)

    start = pl.multiple_of(7 * D + HV + step * FF_STEP, LANE)
    pre = mm(n2[...], w_up[...]) + vec[:, pl.ds(start, FF_STEP)]
    square = pre * pre
    bent = jnp.tanh(0.7978845608028654 * (pre + 0.044715 * square * pre))
    half = 0.5 * (1.0 + bent)
    act = (pre * half).astype(BF16)
    slope = half + (0.5 * 0.7978845608028654) * pre * (1.0 - bent * bent) * (1.0 + 0.134145 * square)
    grad_pre32 = mm(og[...], w_down[...], NT) * slope
    grad_pre = grad_pre32.astype(BF16)
    vec_grad[:, pl.ds(start, FF_STEP)] = jnp.sum(grad_pre.astype(F32), axis=0, keepdims=True)
    more = mm(act, w_down[...])
    more_grad = mm(grad_pre, w_up[...], NT)

    @pl.when(step == 0)
    def _():
        acc[...] = more
        acc_grad[...] = more_grad

    @pl.when(step > 0)
    def _():
        acc[...] += more
        acc_grad[...] += more_grad

    down = mm(act, og[...], TN)
    for j in range(per_row):
        flat_down[pl.ds(j, FF_STEP, stride=per_row), :] = down[:, j * LANE : (j + 1) * LANE]
    d_down[...] = flat_down[...].astype(BF16)
    up = mm(n2[...], grad_pre, TN)
    for j in range(FF_STEP // LANE):
        flat_up[pl.ds(step * (FF_STEP // LANE) + j, D, stride=wide), :] = up[
            :, j * LANE : (j + 1) * LANE
        ]

    @pl.when(step == FF // FF_STEP - 1)
    def _():
        d_up[...] = flat_up[...].astype(BF16)
        result[...] = (resid[...] + acc[...] + vec_part(vec, 6)).astype(BF16)
        grad = acc_grad[...]
        unit = hat[...]
        vec_grad[:, 2 * D : 3 * D] = jnp.sum(grad * unit, axis=0, keepdims=True)
        vec_grad[:, 3 * D : 4 * D] = jnp.sum(grad, axis=0, keepdims=True)
        given = og[...].astype(F32)
        back = given + norm_back(grad, unit, rate[...], vec_part(vec, 2))
        grad_resid[...] = back
        low = back.astype(BF16)
        resid_low[...] = low
        vec_grad[:, 5 * D : 6 * D] = jnp.sum(low.astype(F32), axis=0, keepdims=True)
        vec_grad[:, 6 * D : 7 * D] = jnp.sum(given, axis=0, keepdims=True)
        grad_att[...] = mm(low, w_out[...], NT).astype(BF16)


def hidden(tokens, att, og, w_out, w_up, w_down, vec):
    rows = tokens.shape[0]
    line = (rows, D)
    flat_rows = FF * D // LANE
    return pl.pallas_call(
        hidden_kernel,
        out_shape=[
            jax.ShapeDtypeStruct(line, BF16),
            jax.ShapeDtypeStruct(line, F32),
            jax.ShapeDtypeStruct(line, BF16),
            jax.ShapeDtypeStruct(line, BF16),
            jax.ShapeDtypeStruct((flat_rows, LANE), BF16),
            jax.ShapeDtypeStruct((flat_rows, LANE), BF16),
            jax.ShapeDtypeStruct((1, VEC), F32),
        ],
        grid=(FF // FF_STEP,),
        in_specs=[
            whole(line),
            whole(line),
            whole(line),
            whole((D, D)),
            pl.BlockSpec((D, FF_STEP), lambda i: (0, i)),
            pl.BlockSpec((FF_STEP, D), lambda i: (i, 0)),
            whole((1, VEC)),
        ],
        out_specs=[
            whole(line),
            whole(line),
            whole(line),
            whole(line),
            whole((flat_rows, LANE)),
            pl.BlockSpec((FF_STEP * D // LANE, LANE), lambda i: (i, 0)),
            whole((1, VEC)),
        ],
        scratch_shapes=[
            pltpu.VMEM(line, F32),
            pltpu.VMEM(line, F32),
            pltpu.VMEM(line, BF16),
            pltpu.VMEM((rows, 1), F32),
            pltpu.VMEM(line, F32),
            pltpu.VMEM(line, F32),
            pltpu.VMEM((flat_rows, LANE), F32),
            pltpu.VMEM((FF_STEP * D // LANE, LANE), F32),
        ],
        compiler_params=params(58),
        cost_estimate=cost(2 * rows * D * (6 * FF + 2 * D), 8 * D * FF + 20 * rows * D, rows * FF),
        name="hidden",
    )(tokens, att, og, w_out, w_up, w_down, vec)


def attend_back_kernel(q, k, v, att, grad_att, chance, d_q, d_k, d_fresh, d_first):
    pair = pl.program_id(0)
    for head in range(2):
        cols = slice(head * HD, (head + 1) * HD)
        grad = grad_att[:, cols]
        weights = chance[head]
        shared = grad.astype(F32) * att[:, cols].astype(F32)
        delta = jnp.sum(shared.T, axis=0, keepdims=True)
        grad_chance = mm(v[:, cols], grad, NT)
        grad_scores = (weights.astype(F32) * (grad_chance - delta)).astype(BF16)
        grad_value = mm(weights, grad)

        @pl.when(pair < 3)
        def _(grad_value=grad_value, cols=cols):
            d_fresh[:, cols] = grad_value.astype(BF16)

        @pl.when(pair >= 3)
        def _(grad_value=grad_value, cols=cols):
            d_first[:, cols] = grad_value

        d_k[:, cols] = mm(grad_scores, q[:, cols]).astype(BF16)
        d_q[:, cols] = (mm(k[:, cols], grad_scores, TN).T * HD ** (-0.5)).astype(BF16)


def attend_back(q, k, v, att, grad_att, chance):
    queries, keys = q.shape[0], k.shape[0]
    pairs = D // LANE
    by_column = lambda i: (0, i)
    return pl.pallas_call(
        attend_back_kernel,
        out_shape=[
            jax.ShapeDtypeStruct((queries, D), BF16),
            jax.ShapeDtypeStruct((keys, D), BF16),
            jax.ShapeDtypeStruct((keys, HV), BF16),
            jax.ShapeDtypeStruct((keys, HV), F32),
        ],
        grid=(pairs,),
        in_specs=[
            pl.BlockSpec((queries, LANE), by_column),
            pl.BlockSpec((keys, LANE), by_column),
            pl.BlockSpec((keys, LANE), by_column),
            pl.BlockSpec((queries, LANE), by_column),
            pl.BlockSpec((queries, LANE), by_column),
            pl.BlockSpec((2, keys, queries), lambda i: (i, 0, 0)),
        ],
        out_specs=[
            pl.BlockSpec((queries, LANE), by_column),
            pl.BlockSpec((keys, LANE), by_column),
            pl.BlockSpec((keys, LANE), lambda i: (0, jnp.minimum(i, 2))),
            pl.BlockSpec((keys, LANE), lambda i: (0, jnp.maximum(i - 3, 0))),
        ],
        compiler_params=params(48),
        cost_estimate=cost(8 * queries * keys * D, 24 * queries * keys),
        name="attend_back",
    )(q, k, v, att, grad_att, chance)


def project_back_kernel(
    tokens, n1, d_q, d_k, d_fresh, att, resid_low, w_qkv, vec, vec_one,
    grad_near, grad_far, d_rest, vec_grad, flat,
):
    rows = n1.shape[0] // 2
    per_row = D // LANE
    grads = mm(d_k[...], w_qkv[:, D : 2 * D], NT) + mm(d_fresh[...], w_qkv[:, 2 * D :], NT)
    near = grads[:rows] + mm(d_q[...], w_qkv[:, :D], NT)
    far = grads[rows:]
    grad_near[...] = near
    grad_far[...] = far.astype(BF16)
    hat, _ = normed(tokens[...].astype(F32))
    vec_grad[...] = vec_one[...]
    vec_grad[:, :D] = jnp.sum(near * hat[:rows], axis=0, keepdims=True) + jnp.sum(
        far * hat[rows:], axis=0, keepdims=True
    )
    vec_grad[:, D : 2 * D] = jnp.sum(near, axis=0, keepdims=True) + jnp.sum(
        far, axis=0, keepdims=True
    )
    vec_grad[:, 4 * D : 5 * D] = jnp.sum(d_q[...].astype(F32), axis=0, keepdims=True)
    vec_grad[:, 7 * D : 7 * D + HV] = jnp.sum(d_fresh[...].astype(F32), axis=0, keepdims=True)
    pieces = (
        (n1, d_q, rows, 0, per_row),
        (n1, d_k, 2 * rows, D * per_row, per_row),
        (n1, d_fresh, 2 * rows, 2 * D * per_row, HV // LANE),
        (att, resid_low, rows, 2 * D * per_row + D * HV // LANE, per_row),
    )
    for left, right, count, start, columns in pieces:
        product = mm(left[:count], right[:count], TN)
        size = D * columns
        for j in range(columns):
            flat[pl.ds(j, D, stride=columns), :] = product[:, j * LANE : (j + 1) * LANE]
        d_rest[start : start + size] = flat[:size].astype(BF16)
    flat[: 2 * LANE] = jnp.zeros((2 * LANE, LANE), F32)
    for j in range(VEC // LANE):
        flat[j : j + 1] = vec_grad[:, j * LANE : (j + 1) * LANE]
    d_rest[REST:] = flat[: 2 * LANE].astype(BF16)


def project_back(tokens, n1, d_q, d_k, d_fresh, att, resid_low, w_qkv, vec, vec_one):
    rows = n1.shape[0] // 2
    vm = pl.BlockSpec(memory_space=pltpu.VMEM)
    return pl.pallas_call(
        project_back_kernel,
        out_shape=[
            jax.ShapeDtypeStruct((rows, D), F32),
            jax.ShapeDtypeStruct((rows, D), BF16),
            jax.ShapeDtypeStruct((128 * LANE, LANE), BF16),
        ],
        in_specs=[vm] * 10,
        out_specs=[vm] * 3,
        scratch_shapes=[pltpu.VMEM((1, VEC), F32), pltpu.VMEM((D * D // LANE, LANE), F32)],
        compiler_params=params(58),
        cost_estimate=cost(2 * rows * D * (7 * D), 14 * MIB),
        name="project_back",
    )(tokens, n1, d_q, d_k, d_fresh, att, resid_low, w_qkv, vec, vec_one)


def adam_kernel(places, grads, used, weight, one, two, new, new_one, new_two, low, stage, flat, sems):
    step = pl.program_id(0)
    rows = weight.shape[0]
    steps = pl.num_programs(0)

    @pl.when(step == 0)
    def _():
        @pl.loop(0, steps)
        def _(s):
            @pl.loop(0, rows)
            def _(i):
                slot = s * rows + i
                pltpu.make_async_copy(
                    grads.at[pl.ds(pl.multiple_of(places[slot] * LANE, LANE), LANE)],
                    stage.at[pl.ds(pl.multiple_of(slot * LANE, LANE), LANE)],
                    sems.at[s],
                ).start()

    span = pl.ds(pl.multiple_of(step * rows * LANE, LANE), rows * LANE)
    pltpu.make_async_copy(stage.at[span], stage.at[span], sems.at[step]).wait()
    flat[...] = stage[span, :].astype(F32)
    keep = used[...] > 0.0
    for c in range(LANE):
        columns = slice(c * LANE, (c + 1) * LANE)
        gradient = jnp.where(keep, flat[pl.ds(c, rows, stride=LANE), :], 0.0)
        after, after_one, after_two = adam_step(
            weight[:, columns], one[:, columns], two[:, columns], gradient, RATE_MATRIX, DECAY_MATRIX
        )
        new[:, columns] = after
        new_one[:, columns] = after_one
        new_two[:, columns] = after_two
        low[:, columns] = after.astype(BF16)


def adam(places, grads, used, weight, one, two):
    capacity, tile_len = weight.shape
    rows = 8 if capacity % 8 == 0 else capacity
    steps = capacity // rows
    block = pl.BlockSpec((rows, tile_len), lambda i, *_: (i, 0))
    return pl.pallas_call(
        adam_kernel,
        out_shape=[jax.ShapeDtypeStruct(weight.shape, F32)] * 3
        + [jax.ShapeDtypeStruct(weight.shape, BF16)],
        grid_spec=pltpu.PrefetchScalarGridSpec(
            num_scalar_prefetch=1,
            grid=(steps,),
            in_specs=[
                pl.BlockSpec(memory_space=pl.ANY),
                pl.BlockSpec((rows, LANE), lambda i, *_: (i, 0)),
                block,
                block,
                block,
            ],
            out_specs=[block] * 4,
            scratch_shapes=[
                pltpu.VMEM((capacity * LANE, LANE), BF16),
                pltpu.VMEM((rows * LANE, LANE), F32),
                pltpu.SemaphoreType.DMA((steps,)),
            ],
        ),
        compiler_params=params(48),
        cost_estimate=cost(20 * capacity * tile_len, 28 * capacity * tile_len, 2 * capacity * tile_len),
        name="adam",
    )(places, grads, used, weight, one, two)


RS_KINDS = ("core", "xa", "yb", "ya", "xb", "up", "down")
AG_KINDS = ("g_up", "g_down", "g_xa", "g_yb", "g_ya", "g_xb", "g_ya2", "g_xb2", "g_c", "g_c2", "g_c3")


class Links:
    def __init__(self, line, send_sems, recv_sems):
        dp = lax.axis_index("dp")
        self.line = line
        self.y = lax.axis_index("seq")
        self.z = dp // 4
        self.x = (dp // 2) % 2
        self.c = dp % 2
        self.send_sems, self.recv_sems = send_sems, recv_sems
        self.to = {
            "core": {"dp": self.z * 4 + self.x * 2 + (1 - self.c)},
            "x": {"dp": self.z * 4 + (1 - self.x) * 2 + self.c},
            "y": {"seq": 1 - self.y},
            "up": {"dp": dp + 4},
            "down": {"dp": dp - 4},
        }
        self.sent = []

    def greet(self):
        barrier = pltpu.get_barrier_semaphore()
        for name in ("core", "x", "y"):
            pl.semaphore_signal(barrier, inc=1, device_id=self.to[name])

        @pl.when(self.z > 0)
        def _():
            pl.semaphore_signal(barrier, inc=1, device_id=self.to["down"])

        @pl.when(self.z < self.line - 1)
        def _():
            pl.semaphore_signal(barrier, inc=1, device_id=self.to["up"])

        pl.semaphore_wait(
            barrier,
            3 + jnp.where(self.z > 0, 1, 0) + jnp.where(self.z < self.line - 1, 1, 0),
        )

    def copy(self, source, target, index, way):
        return pltpu.make_async_remote_copy(
            src_ref=source,
            dst_ref=target,
            send_sem=self.send_sems.at[index],
            recv_sem=self.recv_sems.at[index],
            device_id=self.to[way],
        )

    def send(self, source, target, index, way, when=None):
        if when is None:
            self.copy(source, target, index, way).start()
        else:

            @pl.when(when)
            def _():
                self.copy(source, target, index, way).start()

        self.sent.append((source, target, index, way, when))

    def arrive(self, target, index, way):
        self.copy(target, target, index, way).wait_recv()

    def finish(self):
        for source, target, index, way, when in self.sent:
            if when is None:
                self.copy(source, target, index, way).wait_send()
            else:

                @pl.when(when)
                def _(source=source, target=target, index=index, way=way):
                    self.copy(source, target, index, way).wait_send()


def add_into(place, *others):
    total = place[...].astype(F32)
    for other in others:
        total = total + other[...].astype(F32)
    place[...] = total.astype(BF16)


class Scatter:
    def __init__(self, links, base, source, offset, rows, held, r_core, r_xa, r_yb, r_ya, r_xb, r_up, r_down, load_sems):
        self.k, self.base, self.source, self.offset, self.rows = links, base, source, offset, rows
        self.held, self.r_core = held, r_core
        self.r_xa, self.r_yb, self.r_ya, self.r_xb = r_xa, r_yb, r_ya, r_xb
        self.r_up, self.r_down, self.load_sems = r_up, r_down, load_sems
        self.halves = (pl.ds(0, rows // 2), pl.ds(rows // 2, rows // 2))
        order = []
        low, high = 0, links.line - 1
        while low <= high:
            order.append(high)
            if low < high:
                order.append(low)
            low, high = low + 1, high - 1
        self.order = order

    def at(self, kind, z):
        return self.base + RS_KINDS.index(kind) * self.k.line + z

    def load(self, z):
        four = 4 * self.rows
        start = self.offset + (self.k.c * self.k.line + z) * four
        out = []
        for i in range(4):
            out.append(
                pltpu.make_async_copy(
                    self.source.at[pl.ds(pl.multiple_of(start + i * self.rows, 16), self.rows)],
                    self.held.at[z, i // 2, i % 2],
                    self.load_sems.at[4 * z + i],
                )
            )
        return out

    def begin(self):
        k = self.k
        for z in self.order:
            start = self.offset + ((1 - k.c) * k.line + z) * 4 * self.rows
            k.send(
                self.source.at[pl.ds(pl.multiple_of(start, 16), 4 * self.rows)],
                self.r_core.at[z],
                self.at("core", z),
                "core",
            )
            for copy in self.load(z):
                copy.start()

    def first(self, z):
        k, (a, b) = self.k, self.halves
        for copy in self.load(z):
            copy.wait()
        k.arrive(self.r_core.at[z], self.at("core", z), "core")
        for i in range(4):
            add_into(self.held.at[z, i // 2, i % 2], self.r_core.at[z, pl.ds(i * self.rows, self.rows)])
        k.send(self.held.at[z, 1 - k.x, :, a], self.r_xa.at[z], self.at("xa", z), "x")
        k.send(self.held.at[z, :, 1 - k.y, b], self.r_yb.at[z], self.at("yb", z), "y")

    def second(self, z):
        k, (a, b) = self.k, self.halves
        k.arrive(self.r_xa.at[z], self.at("xa", z), "x")
        for y in range(2):
            add_into(self.held.at[z, k.x, y, a], self.r_xa.at[z, y])
        k.send(self.held.at[z, k.x, 1 - k.y, a], self.r_ya.at[z], self.at("ya", z), "y")
        k.arrive(self.r_yb.at[z], self.at("yb", z), "y")
        for x in range(2):
            add_into(self.held.at[z, x, k.y, b], self.r_yb.at[z, x])
        k.send(self.held.at[z, 1 - k.x, k.y, b], self.r_xb.at[z], self.at("xb", z), "x")

    def third(self, z):
        k, (a, b) = self.k, self.halves
        k.arrive(self.r_ya.at[z], self.at("ya", z), "y")
        add_into(self.held.at[z, k.x, k.y, a], self.r_ya.at[z])
        k.arrive(self.r_xb.at[z], self.at("xb", z), "x")
        add_into(self.held.at[z, k.x, k.y, b], self.r_xb.at[z])
        mine = self.held.at[z, k.x, k.y]

        @pl.when((k.z < z) & (k.z > 0))
        def _():
            k.arrive(self.r_up.at[z], self.at("up", z), "up")
            add_into(mine, self.r_up.at[z])

        @pl.when((k.z > z) & (k.z < k.line - 1))
        def _():
            k.arrive(self.r_down.at[z], self.at("down", z), "down")
            add_into(mine, self.r_down.at[z])

        k.send(mine, self.r_up.at[z], self.at("up", z), "up", k.z < z)
        k.send(mine, self.r_down.at[z], self.at("down", z), "down", k.z > z)

    def last(self):
        k = self.k
        mine = self.held.at[k.z, k.x, k.y]

        @pl.when(k.z > 0)
        def _():
            k.arrive(self.r_up.at[k.z], self.at("up", k.z), "up")
            add_into(mine, self.r_up.at[k.z])

        @pl.when(k.z < k.line - 1)
        def _():
            k.arrive(self.r_down.at[k.z], self.at("down", k.z), "down")
            add_into(mine, self.r_down.at[k.z])


class Gather:
    def __init__(self, links, base, piece, out, rows, index, copy_sem):
        self.k, self.base, self.piece, self.out, self.rows = links, base, piece, out, rows
        self.index, self.copy_sem = index, copy_sem
        self.halves = (pl.ds(0, rows // 2), pl.ds(rows // 2, rows // 2))

    def at(self, kind, z):
        return self.base + AG_KINDS.index(kind) * self.k.line + z

    def spot(self, c, z, x, y, half=None):
        start = self.index(c, z, x, y)
        if half is None:
            return self.out.at[pl.ds(pl.multiple_of(start, 16), self.rows)]
        return self.out.at[pl.ds(pl.multiple_of(start + half * (self.rows // 2), 16), self.rows // 2)]

    def own_copy(self):
        k = self.k
        return pltpu.make_async_copy(self.piece, self.spot(k.c, k.z, k.x, k.y), self.copy_sem)

    def pass_on(self, z, source, when):
        k = self.k
        a, b = self.halves
        whole = self.spot(k.c, z, k.x, k.y)
        half = [self.spot(k.c, z, k.x, k.y, i) for i in range(2)]
        if source is None:
            parts = half
            source = whole
        else:
            parts = [source.at[a], source.at[b]]
        k.send(parts[0], half[0], self.at("g_xa", z), "x", when)
        k.send(parts[1], half[1], self.at("g_yb", z), "y", when)
        k.send(parts[0], half[0], self.at("g_ya", z), "y", when)
        k.send(parts[1], half[1], self.at("g_xb", z), "x", when)
        k.send(source, whole, self.at("g_c", z), "core", when)

    def begin(self):
        k = self.k
        self.own_copy().start()
        mine = self.spot(k.c, k.z, k.x, k.y)
        k.send(self.piece, mine, self.at("g_up", k.z), "up", k.z < k.line - 1)
        k.send(self.piece, mine, self.at("g_down", k.z), "down", k.z > 0)
        self.pass_on(k.z, self.piece, None)

    def along(self, r):
        k = self.k
        for sign, kind, way in ((-1, "g_up", "up"), (1, "g_down", "down")):
            z = k.z + sign * r
            here = (k.z >= r) if sign < 0 else (k.z + r < k.line)
            place = self.spot(k.c, z, k.x, k.y)

            @pl.when(here)
            def _(place=place, kind=kind, z=z, way=way):
                k.arrive(place, self.at(kind, z), way)

            more = (k.z < k.line - 1) if sign < 0 else (k.z > 0)
            k.send(place, place, self.at(kind, z), way, here & more)
            self.pass_on(z, None, here)

    def turn(self, z):
        k = self.k
        beside = self.spot(k.c, z, 1 - k.x, k.y, 0)
        k.arrive(beside, self.at("g_xa", z), "x")
        k.send(beside, beside, self.at("g_ya2", z), "y")
        across = self.spot(k.c, z, k.x, 1 - k.y, 1)
        k.arrive(across, self.at("g_yb", z), "y")
        k.send(across, across, self.at("g_xb2", z), "x")

    def share(self, z):
        k = self.k
        k.arrive(self.spot(k.c, z, k.x, 1 - k.y, 0), self.at("g_ya", z), "y")
        across = self.spot(k.c, z, k.x, 1 - k.y)
        k.send(across, across, self.at("g_c2", z), "core")
        k.arrive(self.spot(k.c, z, 1 - k.x, k.y, 1), self.at("g_xb", z), "x")
        k.arrive(self.spot(k.c, z, 1 - k.x, 1 - k.y, 0), self.at("g_ya2", z), "y")
        k.arrive(self.spot(k.c, z, 1 - k.x, 1 - k.y, 1), self.at("g_xb2", z), "x")
        for y in range(2):
            beside = self.spot(k.c, z, 1 - k.x, y)
            k.send(beside, beside, self.at("g_c3", z) if y == 0 else self.at("g_c3", z) + k.line, "core")

    def end(self):
        k = self.k
        self.own_copy().wait()
        other = 1 - k.c
        for z in range(k.line):
            k.arrive(self.spot(other, z, k.x, k.y), self.at("g_c", z), "core")
            k.arrive(self.spot(other, z, k.x, 1 - k.y), self.at("g_c2", z), "core")
            for y in range(2):
                k.arrive(self.spot(other, z, 1 - k.x, y), self.at("g_c3", z) + y * k.line, "core")


RS_SEMS = len(RS_KINDS)
AG_SEMS = len(AG_KINDS) + 1


def all_reduce_kernel(line, sizes, swaps, *refs):
    count = len(sizes)
    sources, near = refs[:count], refs[count : count + swaps]
    out, far = refs[count + swaps], refs[count + swaps + 1 : count + 2 * swaps + 1]
    scratch = refs[count + 2 * swaps + 1 :]
    send_sems, recv_sems, load_sems, copy_sems = scratch[-4:]
    links = Links(line, send_sems, recv_sems)
    links.greet()
    spare = count * (RS_SEMS + AG_SEMS) * line
    scatters, gathers = [], []
    top = 0
    per_group = (RS_SEMS + AG_SEMS) * line
    for g, size in enumerate(sizes):
        rows = size // (8 * line)
        buffers = scratch[8 * g : 8 * g + 8]
        scatters.append(
            Scatter(links, g * per_group, sources[g], 0, rows, *buffers, load_sems.at[g])
        )

        def index(c, z, x, y, top=top, rows=rows):
            return top + (((c * line + z) * 2 + x) * 2 + y) * rows

        gathers.append(
            Gather(
                links,
                g * per_group + RS_SEMS * line,
                buffers[0].at[links.z, links.x, links.y],
                out,
                rows,
                index,
                copy_sems.at[g],
            )
        )
        top += size

    def stage_first(g):
        for z in scatters[g].order:
            scatters[g].first(z)

    def stage_second(g):
        for z in scatters[g].order:
            scatters[g].second(z)

    def stage_third(g):
        for z in scatters[g].order:
            scatters[g].third(z)
        scatters[g].last()
        gathers[g].begin()

    def stage_along(g):
        for r in range(1, line):
            gathers[g].along(r)

    def stage_turn(g):
        for z in range(line):
            gathers[g].turn(z)

    def stage_share(g):
        for z in range(line):
            gathers[g].share(z)

    stages = [stage_first, stage_second, stage_third, stage_along, stage_turn, stage_share]
    for g in range(count):
        scatters[g].begin()
    for i in range(swaps):
        links.send(near[i], far[i], spare + i, "y")
    for slot in range(len(stages) + count - 1):
        for g in reversed(range(count)):
            if 0 <= slot - g < len(stages):
                stages[slot - g](g)
    for g in range(count):
        gathers[g].end()
    for i in range(swaps):
        links.arrive(far[i], spare + i, "y")
    links.finish()


def all_reduce(arrays, swaps, line, collective_id):
    sizes = [a.shape[0] for a in arrays]
    any_space = pl.BlockSpec(memory_space=pl.ANY)
    scratch = []
    for size in sizes:
        rows = size // (8 * line)
        half = rows // 2
        scratch += [
            pltpu.VMEM((line, 2, 2, rows, LANE), BF16),
            pltpu.VMEM((line, 4 * rows, LANE), BF16),
            pltpu.VMEM((line, 2, half, LANE), BF16),
            pltpu.VMEM((line, 2, half, LANE), BF16),
            pltpu.VMEM((line, half, LANE), BF16),
            pltpu.VMEM((line, half, LANE), BF16),
            pltpu.VMEM((line, rows, LANE), BF16),
            pltpu.VMEM((line, rows, LANE), BF16),
        ]
    sems = len(sizes) * (RS_SEMS + AG_SEMS) * line + len(swaps)
    scratch += [
        pltpu.SemaphoreType.DMA((sems,)),
        pltpu.SemaphoreType.DMA((sems,)),
        pltpu.SemaphoreType.DMA((len(sizes), 4 * line)),
        pltpu.SemaphoreType.DMA((len(sizes),)),
    ]
    return pl.pallas_call(
        functools.partial(all_reduce_kernel, line, sizes, len(swaps)),
        out_shape=[jax.ShapeDtypeStruct((sum(sizes), LANE), BF16)]
        + [jax.ShapeDtypeStruct(s.shape, s.dtype) for s in swaps],
        in_specs=[any_space] * (len(sizes) + len(swaps)),
        out_specs=[any_space] * (1 + len(swaps)),
        scratch_shapes=scratch,
        compiler_params=pltpu.CompilerParams(
            vmem_limit_bytes=56 * MIB, collective_id=collective_id, has_side_effects=True
        ),
        cost_estimate=pl.CostEstimate(flops=0, bytes_accessed=100 * MIB, transcendentals=0),
        name="all_reduce",
    )(*arrays, *swaps)


def all_gather_kernel(line, swaps, piece, *refs):
    near, out, far = refs[:swaps], refs[swaps], refs[swaps + 1 : 2 * swaps + 1]
    send_sems, recv_sems, copy_sem = refs[2 * swaps + 1 :]
    links = Links(line, send_sems, recv_sems)
    links.greet()
    spare = AG_SEMS * line
    for i in range(swaps):
        links.send(near[i], far[i], spare + i, "y")
    rows = piece.shape[0] // 2

    def index(c, z, x, y):
        return (((z * 2 + x) * 2 + c) * 2 + y) * rows

    mine = piece.at[pl.ds(pl.multiple_of(links.y * rows, 16), rows)]
    gather = Gather(links, 0, mine, out, rows, index, copy_sem)
    gather.begin()
    for r in range(1, line):
        gather.along(r)
    for z in range(line):
        gather.turn(z)
    for z in range(line):
        gather.share(z)
    gather.end()
    for i in range(swaps):
        links.arrive(far[i], spare + i, "y")
    links.finish()


def all_gather(piece, swaps, line, collective_id):
    any_space = pl.BlockSpec(memory_space=pl.ANY)
    sems = AG_SEMS * line + len(swaps)
    return pl.pallas_call(
        functools.partial(all_gather_kernel, line, len(swaps)),
        out_shape=[jax.ShapeDtypeStruct((4 * line * piece.shape[0], LANE), BF16)]
        + [jax.ShapeDtypeStruct(s.shape, s.dtype) for s in swaps],
        in_specs=[any_space] * (1 + len(swaps)),
        out_specs=[any_space] * (1 + len(swaps)),
        scratch_shapes=[
            pltpu.SemaphoreType.DMA((sems,)),
            pltpu.SemaphoreType.DMA((sems,)),
            pltpu.SemaphoreType.DMA,
        ],
        compiler_params=pltpu.CompilerParams(collective_id=collective_id, has_side_effects=True),
        cost_estimate=pl.CostEstimate(flops=0, bytes_accessed=100 * MIB, transcendentals=0),
        name="all_gather",
    )(piece, *swaps)


def swap(value):
    return lax.ppermute(value, "seq", [(0, 1), (1, 0)])


def shards(
    tokens,
    first_values,
    out_grad,
    block_place,
    owners,
    masters,
    moment_one,
    moment_two,
    vector_master,
    vector_moment_one,
    vector_moment_two,
):
    capacity = masters.shape[0]
    dp_count = lax.axis_size("dp")
    tile_count = owners.shape[0]
    dp_here = lax.axis_index("dp")
    seq_here = lax.axis_index("seq")
    _, half_len, _ = tokens.shape

    tokens = tokens.reshape(half_len, D)
    firsts = first_values.reshape(half_len, HV)
    given = out_grad.reshape(half_len, D)
    line = dp_count // 4
    packed = pack_slots(masters)
    if line == LINE:
        slots, tokens_far, firsts_far = all_gather(packed, [tokens, firsts], line, 1)
    else:
        tokens_far, firsts_far = swap(tokens), swap(firsts)
        slots = lax.all_gather(packed, "dp", axis=0, tiled=True)

    slot_index = slot_numbers(owners)
    slot_rows = owners * capacity + slot_index
    mine = (owners == dp_here)[None, :] & (
        slot_index[None, :] == jnp.arange(capacity, dtype=jnp.int32)[:, None]
    )
    tile_order = jnp.arange(tile_count, dtype=jnp.int32)
    tile_here = jnp.sum(jnp.where(mine, tile_order[None, :], 0), axis=1)
    tile_here = tile_here + jnp.where(tile_here >= 126, 2, 0)
    used = jnp.broadcast_to(
        jnp.any(mine, axis=1).astype(F32)[:, None], (capacity, LANE)
    )

    blocks = block_place.reshape(-1)
    per_device = blocks.shape[0] // 2
    block_len = half_len // per_device
    ordered = jnp.roll(blocks, -seq_here * per_device)
    all_pos = (
        ordered[:, None] * block_len + jnp.arange(block_len, dtype=jnp.int32)[None, :]
    ).reshape(-1)
    row_pos = all_pos[:half_len].reshape(1, half_len)
    column_pos = all_pos.reshape(2 * half_len, 1)

    vec = vector_master.reshape(1, VEC)
    tokens_all = jnp.concatenate([tokens, tokens_far], axis=0)
    firsts_all = jnp.concatenate([firsts, firsts_far], axis=0)

    w_qkv, w_out, w_up, w_down = unpack_weights(slot_rows, slots)
    n1, q, k, v = project(tokens_all, firsts_all, w_qkv, vec)
    att, chance = attend(q, k, v, row_pos, column_pos)
    result, grad_resid, resid_low, grad_att, d_up, d_down, vec_one = hidden(
        tokens, att, given, w_out, w_up, w_down, vec
    )
    d_q, d_k, d_fresh, d_first = attend_back(q, k, v, att, grad_att, chance)
    grad_near, grad_far, d_rest = project_back(
        tokens_all, n1, d_q, d_k, d_fresh, att, resid_low, w_qkv, vec, vec_one
    )
    first_far = d_first[half_len:].astype(BF16)
    if line == LINE:
        grads, grad_back, first_back = all_reduce([d_rest, d_up, d_down], [grad_far, first_far], line, 0)
    else:
        grad_back, first_back = swap(grad_far), swap(first_far)
        grads = lax.psum(jnp.concatenate([d_rest, d_up, d_down], axis=0), ("seq", "dp"))
    vector_total = grads[REST : REST + VEC // LANE].reshape(VEC).astype(F32)

    grad_n1 = grad_near + grad_back.astype(F32)
    hat, rate = normed(tokens.astype(F32))
    tokens_grad = grad_resid + norm_back(grad_n1, hat, rate, vec[:, :D])
    first_grad = d_first[:half_len] + first_back.astype(F32)

    new_master, new_one, new_two, new_low = adam(
        tile_here, grads, used, masters, moment_one, moment_two
    )
    vector_new, vector_one, vector_two = adam_step(
        vector_master, vector_moment_one, vector_moment_two, vector_total, RATE_VECTOR, 0.0
    )
    return (
        result.reshape(1, half_len, D),
        tokens_grad.reshape(1, half_len, D),
        first_grad.reshape(1, half_len, HV),
        new_master,
        new_one,
        new_two,
        new_low,
        vector_new,
        vector_one,
        vector_two,
    )


def solution(mesh):
    rows = P("dp", "seq", None)
    slots = P("dp", None)
    return jax.shard_map(
        shards,
        mesh=mesh,
        in_specs=(rows, rows, rows, slots, P(), slots, slots, slots, P(), P(), P()),
        out_specs=(rows, rows, rows, slots, slots, slots, slots, P(), P(), P()),
        check_vma=False,
    )
```

```python
import functools

import jax
import jax.numpy as jnp
from jax import lax
from jax.experimental import pallas as pl
from jax.experimental.pallas import tpu as pltpu
from jax.sharding import PartitionSpec as P

D = 768
HD = 64
FF = 3072
STEP = 10
HV = 384
LANE = 128
QKV = 2 * D + HV
FF_STEP = 512
VEC = 7 * D + HV + FF
MIB = 1024 * 1024
LINE = 4
REST = 126 * LANE

EPS_NORM = 1e-05
EPS_ADAM = 1e-08
BETA_ONE = 0.5
BETA_TWO = 0.5
RATE_MATRIX = 0.03
RATE_VECTOR = 0.25
DECAY_MATRIX = 0.1
FAR = -1e30

BF16 = jnp.bfloat16
F32 = jnp.float32

NN = (((1,), (0,)), ((), ()))
NT = (((1,), (1,)), ((), ()))
TN = (((0,), (0,)), ((), ()))


def mm(left, right, dims=NN):
    return lax.dot_general(left, right, dims, preferred_element_type=F32)


def vec_part(vec_ref, index):
    if index < 7:
        return vec_ref[:, index * D : (index + 1) * D]
    if index == 7:
        return vec_ref[:, 7 * D : 7 * D + HV]
    return vec_ref[:, 7 * D + HV :]


def params(mib, **more):
    return pltpu.CompilerParams(vmem_limit_bytes=mib * MIB, **more)


def whole(shape):
    return pl.BlockSpec(shape, lambda *_: (0,) * len(shape))


def cost(flops, bytes_accessed, transcendentals=0):
    return pl.CostEstimate(
        flops=int(flops), bytes_accessed=int(bytes_accessed), transcendentals=int(transcendentals)
    )


def adam_step(weight, first_moment, second_moment, gradient, step_rate, weight_decay):
    first_new = BETA_ONE * first_moment + (1.0 - BETA_ONE) * gradient
    second_new = BETA_TWO * second_moment + (1.0 - BETA_TWO) * gradient * gradient
    first_fix = 1.0 - BETA_ONE**STEP
    second_fix = 1.0 - BETA_TWO**STEP
    update = first_new / first_fix / (jnp.sqrt(second_new / second_fix) + EPS_ADAM)
    return (weight - step_rate * (update + weight_decay * weight), first_new, second_new)


def slot_numbers(owners):
    tile_order = jnp.arange(owners.shape[0], dtype=jnp.int32)
    earlier = (owners[None, :] == owners[:, None]) & (tile_order[None, :] < tile_order[:, None])
    return jnp.sum(earlier.astype(jnp.int32), axis=1)


def normed(values):
    center = jnp.mean(values, axis=-1, keepdims=True)
    centred = values - center
    spread = jnp.mean(centred * centred, axis=-1, keepdims=True)
    rate = lax.rsqrt(spread + EPS_NORM)
    return centred * rate, rate


def norm_back(grad, hat, rate, gain):
    g = grad * gain
    return rate * (
        g - jnp.mean(g, axis=-1, keepdims=True) - hat * jnp.mean(g * hat, axis=-1, keepdims=True)
    )


def pack_kernel(src, dst, flat):
    rows = src.shape[0]
    for c in range(LANE):
        flat[pl.ds(c, rows, stride=LANE), :] = src[:, c * LANE : (c + 1) * LANE]
    dst[...] = flat[...].astype(BF16)


def pack_slots(masters):
    capacity, tile_len = masters.shape
    rows = 8 if capacity % 8 == 0 else capacity
    return pl.pallas_call(
        pack_kernel,
        out_shape=jax.ShapeDtypeStruct((capacity * LANE, LANE), BF16),
        grid=(capacity // rows,),
        in_specs=[pl.BlockSpec((rows, tile_len), lambda i: (i, 0))],
        out_specs=pl.BlockSpec((rows * LANE, LANE), lambda i: (i, 0)),
        scratch_shapes=[pltpu.VMEM((rows * LANE, LANE), F32)],
        compiler_params=params(32),
        cost_estimate=cost(0, capacity * tile_len * 6),
        name="pack_slots",
    )(masters)


def weight_chunks():
    chunks = [
        (0, 36, 6, 0, 0, 0),
        (36, 36, 6, 0, D, 0),
        (72, 18, 3, 0, 2 * D, 0),
        (90, 36, 6, 1, 0, 0),
    ]
    for i in range(4):
        chunks.append((126 + 36 * i, 36, 24, 2, 0, 192 * i))
    for i in range(4):
        chunks.append((270 + 36 * i, 36, 6, 3, 0, 768 * i))
    return chunks


def unpack_kernel(slot_rows, slots, w_qkv, w_out, w_up, w_down, stage, o_qkv, o_out, o_up, o_down, flat, sems, out_sems):
    chunks = weight_chunks()
    places = (o_qkv, o_out, o_up, o_down)
    ends = (w_qkv, w_out, w_up, w_down)

    for number, (first, tiles, _, _, _, _) in enumerate(chunks):

        @pl.loop(0, tiles)
        def _(i, first=first, number=number):
            t = first + i
            pltpu.make_async_copy(
                slots.at[pl.ds(pl.multiple_of(slot_rows[t] * LANE, LANE), LANE)],
                stage.at[pl.ds(pl.multiple_of(t * LANE, LANE), LANE)],
                sems.at[number],
            ).start()

    copies = []
    for number, (first, tiles, per_row, matrix, column, row) in enumerate(chunks):
        span = pl.ds(first * LANE, tiles * LANE)
        pltpu.make_async_copy(stage.at[span], stage.at[span], sems.at[number]).wait()
        place = places[matrix]
        lines = 3 * LANE // per_row

        @pl.loop(0, tiles // 6)
        def _(g, first=first, per_row=per_row, place=place, column=column, row=row, lines=lines):
            for half in range(2):
                base = pl.multiple_of(first * LANE + (2 * g + half) * 3 * LANE, LANE)
                flat[half] = stage[pl.ds(base, 3 * LANE), :].astype(F32)
            for half in range(2):
                top = pl.multiple_of(row + (2 * g + half) * lines, 16)
                for j in range(per_row):
                    place[pl.ds(top, lines), column + j * LANE : column + (j + 1) * LANE] = flat[
                        half, pl.ds(j, lines, stride=per_row), :
                    ].astype(BF16)

        rows = tiles * LANE // per_row
        columns = pl.ds(column, per_row * LANE)
        copy = pltpu.make_async_copy(
            place.at[pl.ds(row, rows), columns],
            ends[matrix].at[pl.ds(row, rows), columns],
            out_sems.at[number],
        )
        copy.start()
        copies.append(copy)
    for copy in copies:
        copy.wait()


def unpack_weights(slot_rows, slots):
    tile_count = slot_rows.shape[0]
    shapes = [(D, QKV), (D, D), (D, FF), (FF, D)]
    any_space = pl.BlockSpec(memory_space=pl.ANY)
    return pl.pallas_call(
        unpack_kernel,
        out_shape=[jax.ShapeDtypeStruct(s, BF16) for s in shapes],
        grid_spec=pltpu.PrefetchScalarGridSpec(
            num_scalar_prefetch=1,
            grid=(1,),
            in_specs=[any_space],
            out_specs=[any_space] * 4,
            scratch_shapes=[pltpu.VMEM((tile_count * LANE, LANE), BF16)]
            + [pltpu.VMEM(s, BF16) for s in shapes]
            + [
                pltpu.VMEM((2, 3 * LANE, LANE), F32),
                pltpu.SemaphoreType.DMA((12,)),
                pltpu.SemaphoreType.DMA((12,)),
            ],
        ),
        compiler_params=params(48),
        cost_estimate=cost(0, 4 * tile_count * LANE * LANE),
        name="unpack_weights",
    )(slot_rows, slots)


def project_kernel(tokens, firsts, w_qkv, vec, n1, q, k, v):
    hat, _ = normed(tokens[...].astype(F32))
    low = (hat * vec_part(vec, 0) + vec_part(vec, 1)).astype(BF16)
    n1[...] = low

    @pl.when(pl.program_id(0) < 2)
    def _():
        query = mm(low, w_qkv[:, :D]) + vec_part(vec, 4)
        q[...] = (query.astype(BF16).astype(F32) * HD ** (-0.5)).astype(BF16)

    k[...] = mm(low, w_qkv[:, D : 2 * D]).astype(BF16)
    v[:, :HV] = (mm(low, w_qkv[:, 2 * D :]) + vec_part(vec, 7)).astype(BF16)
    v[:, HV:] = firsts[...]


def project(tokens, firsts, w_qkv, vec):
    rows = tokens.shape[0]
    step = rows // 4
    by_row = lambda i: (i, 0)
    return pl.pallas_call(
        project_kernel,
        out_shape=[
            jax.ShapeDtypeStruct((rows, D), BF16),
            jax.ShapeDtypeStruct((rows // 2, D), BF16),
            jax.ShapeDtypeStruct((rows, D), BF16),
            jax.ShapeDtypeStruct((rows, D), BF16),
        ],
        grid=(4,),
        in_specs=[
            pl.BlockSpec((step, D), by_row),
            pl.BlockSpec((step, HV), by_row),
            whole((D, QKV)),
            whole((1, VEC)),
        ],
        out_specs=[
            pl.BlockSpec((step, D), by_row),
            pl.BlockSpec((step, D), lambda i: (jnp.minimum(i, 1), 0)),
            pl.BlockSpec((step, D), by_row),
            pl.BlockSpec((step, D), by_row),
        ],
        compiler_params=params(48),
        cost_estimate=cost(2 * rows * D * QKV, 2 * D * QKV + rows * D * 10),
        name="project",
    )(tokens, firsts, w_qkv, vec)


def attend_kernel(q, k, v, row_pos, column_pos, out, chance, bias):
    queries = q.shape[0]
    block = queries // 2

    @pl.when(pl.program_id(0) == 0)
    def _():
        bias[...] = jnp.where(column_pos[...] <= row_pos[...], 0.0, FAR)

    for head in range(2):
        cols = slice(head * HD, (head + 1) * HD)
        key = k[:, cols]
        value = v[:, cols]
        for part in range(2):
            near = slice(part * block, (part + 1) * block)
            scores = mm(key, q[near, cols], NT) + bias[:, near]
            top = jnp.max(scores, axis=0, keepdims=True)
            power = jnp.exp(scores - top)
            total = jnp.sum(power, axis=0, keepdims=True)
            weights = (power * (1.0 / total)).astype(BF16)
            chance[head, :, near] = weights
            mixed = mm(value, weights, TN)
            out[near, cols] = mixed.T.astype(BF16)


def attend(q, k, v, row_pos, column_pos):
    queries, keys = q.shape[0], k.shape[0]
    pairs = D // LANE
    by_column = lambda i: (0, i)
    return pl.pallas_call(
        attend_kernel,
        out_shape=[
            jax.ShapeDtypeStruct((queries, D), BF16),
            jax.ShapeDtypeStruct((2 * pairs, keys, queries), BF16),
        ],
        grid=(pairs,),
        in_specs=[
            pl.BlockSpec((queries, LANE), by_column),
            pl.BlockSpec((keys, LANE), by_column),
            pl.BlockSpec((keys, LANE), by_column),
            whole((1, queries)),
            whole((keys, 1)),
        ],
        out_specs=[
            pl.BlockSpec((queries, LANE), by_column),
            pl.BlockSpec((2, keys, queries), lambda i: (i, 0, 0)),
        ],
        scratch_shapes=[pltpu.VMEM((keys, queries), F32)],
        compiler_params=params(48),
        cost_estimate=cost(4 * queries * keys * D, 24 * queries * keys, 12 * queries * keys),
        name="attend",
    )(q, k, v, row_pos, column_pos)


def hidden_kernel(
    tokens, att, og, w_out, w_up, w_down, vec,
    result, grad_resid, resid_low, grad_att, d_up, d_down, vec_grad,
    resid, hat, n2, rate, acc, acc_grad, flat_up, flat_down,
):
    step = pl.program_id(0)
    per_row = D // LANE
    wide = FF // LANE

    @pl.when(step == 0)
    def _():
        base = tokens[...].astype(F32) + mm(att[...], w_out[...]) + vec_part(vec, 5)
        resid[...] = base
        unit, scale = normed(base)
        hat[...] = unit
        rate[...] = scale
        n2[...] = (unit * vec_part(vec, 2) + vec_part(vec, 3)).astype(BF16)
        vec_grad[...] = jnp.zeros_like(vec_grad)

    start = pl.multiple_of(7 * D + HV + step * FF_STEP, LANE)
    pre = mm(n2[...], w_up[...]) + vec[:, pl.ds(start, FF_STEP)]
    square = pre * pre
    bent = jnp.tanh(0.7978845608028654 * (pre + 0.044715 * square * pre))
    half = 0.5 * (1.0 + bent)
    act = (pre * half).astype(BF16)
    slope = half + (0.5 * 0.7978845608028654) * pre * (1.0 - bent * bent) * (1.0 + 0.134145 * square)
    grad_pre32 = mm(og[...], w_down[...], NT) * slope
    grad_pre = grad_pre32.astype(BF16)
    vec_grad[:, pl.ds(start, FF_STEP)] = jnp.sum(grad_pre.astype(F32), axis=0, keepdims=True)
    more = mm(act, w_down[...])
    more_grad = mm(grad_pre, w_up[...], NT)

    @pl.when(step == 0)
    def _():
        acc[...] = more
        acc_grad[...] = more_grad

    @pl.when(step > 0)
    def _():
        acc[...] += more
        acc_grad[...] += more_grad

    down = mm(act, og[...], TN)
    for j in range(per_row):
        flat_down[pl.ds(j, FF_STEP, stride=per_row), :] = down[:, j * LANE : (j + 1) * LANE]
    d_down[...] = flat_down[...].astype(BF16)
    up = mm(n2[...], grad_pre, TN)
    for j in range(FF_STEP // LANE):
        flat_up[pl.ds(step * (FF_STEP // LANE) + j, D, stride=wide), :] = up[
            :, j * LANE : (j + 1) * LANE
        ]

    @pl.when(step == FF // FF_STEP - 1)
    def _():
        d_up[...] = flat_up[...].astype(BF16)
        result[...] = (resid[...] + acc[...] + vec_part(vec, 6)).astype(BF16)
        grad = acc_grad[...]
        unit = hat[...]
        vec_grad[:, 2 * D : 3 * D] = jnp.sum(grad * unit, axis=0, keepdims=True)
        vec_grad[:, 3 * D : 4 * D] = jnp.sum(grad, axis=0, keepdims=True)
        given = og[...].astype(F32)
        back = given + norm_back(grad, unit, rate[...], vec_part(vec, 2))
        grad_resid[...] = back
        low = back.astype(BF16)
        resid_low[...] = low
        vec_grad[:, 5 * D : 6 * D] = jnp.sum(low.astype(F32), axis=0, keepdims=True)
        vec_grad[:, 6 * D : 7 * D] = jnp.sum(given, axis=0, keepdims=True)
        grad_att[...] = mm(low, w_out[...], NT).astype(BF16)


def hidden(tokens, att, og, w_out, w_up, w_down, vec):
    rows = tokens.shape[0]
    line = (rows, D)
    flat_rows = FF * D // LANE
    return pl.pallas_call(
        hidden_kernel,
        out_shape=[
            jax.ShapeDtypeStruct(line, BF16),
            jax.ShapeDtypeStruct(line, F32),
            jax.ShapeDtypeStruct(line, BF16),
            jax.ShapeDtypeStruct(line, BF16),
            jax.ShapeDtypeStruct((flat_rows, LANE), BF16),
            jax.ShapeDtypeStruct((flat_rows, LANE), BF16),
            jax.ShapeDtypeStruct((1, VEC), F32),
        ],
        grid=(FF // FF_STEP,),
        in_specs=[
            whole(line),
            whole(line),
            whole(line),
            whole((D, D)),
            pl.BlockSpec((D, FF_STEP), lambda i: (0, i)),
            pl.BlockSpec((FF_STEP, D), lambda i: (i, 0)),
            whole((1, VEC)),
        ],
        out_specs=[
            whole(line),
            whole(line),
            whole(line),
            whole(line),
            whole((flat_rows, LANE)),
            pl.BlockSpec((FF_STEP * D // LANE, LANE), lambda i: (i, 0)),
            whole((1, VEC)),
        ],
        scratch_shapes=[
            pltpu.VMEM(line, F32),
            pltpu.VMEM(line, F32),
            pltpu.VMEM(line, BF16),
            pltpu.VMEM((rows, 1), F32),
            pltpu.VMEM(line, F32),
            pltpu.VMEM(line, F32),
            pltpu.VMEM((flat_rows, LANE), F32),
            pltpu.VMEM((FF_STEP * D // LANE, LANE), F32),
        ],
        compiler_params=params(58),
        cost_estimate=cost(2 * rows * D * (6 * FF + 2 * D), 8 * D * FF + 20 * rows * D, rows * FF),
        name="hidden",
    )(tokens, att, og, w_out, w_up, w_down, vec)


def attend_back_kernel(q, k, v, att, grad_att, chance, d_q, d_k, d_fresh, d_first):
    pair = pl.program_id(0)
    for head in range(2):
        cols = slice(head * HD, (head + 1) * HD)
        grad = grad_att[:, cols]
        weights = chance[head]
        shared = grad.astype(F32) * att[:, cols].astype(F32)
        delta = jnp.sum(shared.T, axis=0, keepdims=True)
        grad_chance = mm(v[:, cols], grad, NT)
        grad_scores = (weights.astype(F32) * (grad_chance - delta)).astype(BF16)
        grad_value = mm(weights, grad)

        @pl.when(pair < 3)
        def _(grad_value=grad_value, cols=cols):
            d_fresh[:, cols] = grad_value.astype(BF16)

        @pl.when(pair >= 3)
        def _(grad_value=grad_value, cols=cols):
            d_first[:, cols] = grad_value

        d_k[:, cols] = mm(grad_scores, q[:, cols]).astype(BF16)
        d_q[:, cols] = (mm(k[:, cols], grad_scores, TN).T * HD ** (-0.5)).astype(BF16)


def attend_back(q, k, v, att, grad_att, chance):
    queries, keys = q.shape[0], k.shape[0]
    pairs = D // LANE
    by_column = lambda i: (0, i)
    return pl.pallas_call(
        attend_back_kernel,
        out_shape=[
            jax.ShapeDtypeStruct((queries, D), BF16),
            jax.ShapeDtypeStruct((keys, D), BF16),
            jax.ShapeDtypeStruct((keys, HV), BF16),
            jax.ShapeDtypeStruct((keys, HV), F32),
        ],
        grid=(pairs,),
        in_specs=[
            pl.BlockSpec((queries, LANE), by_column),
            pl.BlockSpec((keys, LANE), by_column),
            pl.BlockSpec((keys, LANE), by_column),
            pl.BlockSpec((queries, LANE), by_column),
            pl.BlockSpec((queries, LANE), by_column),
            pl.BlockSpec((2, keys, queries), lambda i: (i, 0, 0)),
        ],
        out_specs=[
            pl.BlockSpec((queries, LANE), by_column),
            pl.BlockSpec((keys, LANE), by_column),
            pl.BlockSpec((keys, LANE), lambda i: (0, jnp.minimum(i, 2))),
            pl.BlockSpec((keys, LANE), lambda i: (0, jnp.maximum(i - 3, 0))),
        ],
        compiler_params=params(48),
        cost_estimate=cost(8 * queries * keys * D, 24 * queries * keys),
        name="attend_back",
    )(q, k, v, att, grad_att, chance)


def project_back_kernel(
    tokens, n1, d_q, d_k, d_fresh, att, resid_low, w_qkv, vec, vec_one,
    grad_near, grad_far, d_rest, vec_grad, flat,
):
    rows = n1.shape[0] // 2
    per_row = D // LANE
    grads = mm(d_k[...], w_qkv[:, D : 2 * D], NT) + mm(d_fresh[...], w_qkv[:, 2 * D :], NT)
    near = grads[:rows] + mm(d_q[...], w_qkv[:, :D], NT)
    far = grads[rows:]
    grad_near[...] = near
    grad_far[...] = far.astype(BF16)
    hat, _ = normed(tokens[...].astype(F32))
    vec_grad[...] = vec_one[...]
    vec_grad[:, :D] = jnp.sum(near * hat[:rows], axis=0, keepdims=True) + jnp.sum(
        far * hat[rows:], axis=0, keepdims=True
    )
    vec_grad[:, D : 2 * D] = jnp.sum(near, axis=0, keepdims=True) + jnp.sum(
        far, axis=0, keepdims=True
    )
    vec_grad[:, 4 * D : 5 * D] = jnp.sum(d_q[...].astype(F32), axis=0, keepdims=True)
    vec_grad[:, 7 * D : 7 * D + HV] = jnp.sum(d_fresh[...].astype(F32), axis=0, keepdims=True)
    pieces = (
        (n1, d_q, rows, 0, per_row),
        (n1, d_k, 2 * rows, D * per_row, per_row),
        (n1, d_fresh, 2 * rows, 2 * D * per_row, HV // LANE),
        (att, resid_low, rows, 2 * D * per_row + D * HV // LANE, per_row),
    )
    for left, right, count, start, columns in pieces:
        product = mm(left[:count], right[:count], TN)
        size = D * columns
        for j in range(columns):
            flat[pl.ds(j, D, stride=columns), :] = product[:, j * LANE : (j + 1) * LANE]
        d_rest[start : start + size] = flat[:size].astype(BF16)
    flat[: 2 * LANE] = jnp.zeros((2 * LANE, LANE), F32)
    for j in range(VEC // LANE):
        flat[j : j + 1] = vec_grad[:, j * LANE : (j + 1) * LANE]
    d_rest[REST:] = flat[: 2 * LANE].astype(BF16)


def project_back(tokens, n1, d_q, d_k, d_fresh, att, resid_low, w_qkv, vec, vec_one):
    rows = n1.shape[0] // 2
    vm = pl.BlockSpec(memory_space=pltpu.VMEM)
    return pl.pallas_call(
        project_back_kernel,
        out_shape=[
            jax.ShapeDtypeStruct((rows, D), F32),
            jax.ShapeDtypeStruct((rows, D), BF16),
            jax.ShapeDtypeStruct((128 * LANE, LANE), BF16),
        ],
        in_specs=[vm] * 10,
        out_specs=[vm] * 3,
        scratch_shapes=[pltpu.VMEM((1, VEC), F32), pltpu.VMEM((D * D // LANE, LANE), F32)],
        compiler_params=params(58),
        cost_estimate=cost(2 * rows * D * (7 * D), 14 * MIB),
        name="project_back",
    )(tokens, n1, d_q, d_k, d_fresh, att, resid_low, w_qkv, vec, vec_one)


def adam_kernel(places, grads, used, weight, one, two, new, new_one, new_two, low, stage, flat, sems):
    step = pl.program_id(0)
    rows = weight.shape[0]
    steps = pl.num_programs(0)

    @pl.when(step == 0)
    def _():
        @pl.loop(0, steps)
        def _(s):
            @pl.loop(0, rows)
            def _(i):
                slot = s * rows + i
                pltpu.make_async_copy(
                    grads.at[pl.ds(pl.multiple_of(places[slot] * LANE, LANE), LANE)],
                    stage.at[pl.ds(pl.multiple_of(slot * LANE, LANE), LANE)],
                    sems.at[s],
                ).start()

    span = pl.ds(pl.multiple_of(step * rows * LANE, LANE), rows * LANE)
    pltpu.make_async_copy(stage.at[span], stage.at[span], sems.at[step]).wait()
    flat[...] = stage[span, :].astype(F32)
    keep = used[...] > 0.0
    for c in range(LANE):
        columns = slice(c * LANE, (c + 1) * LANE)
        gradient = jnp.where(keep, flat[pl.ds(c, rows, stride=LANE), :], 0.0)
        after, after_one, after_two = adam_step(
            weight[:, columns], one[:, columns], two[:, columns], gradient, RATE_MATRIX, DECAY_MATRIX
        )
        new[:, columns] = after
        new_one[:, columns] = after_one
        new_two[:, columns] = after_two
        low[:, columns] = after.astype(BF16)


def adam(places, grads, used, weight, one, two):
    capacity, tile_len = weight.shape
    rows = 8 if capacity % 8 == 0 else capacity
    steps = capacity // rows
    block = pl.BlockSpec((rows, tile_len), lambda i, *_: (i, 0))
    return pl.pallas_call(
        adam_kernel,
        out_shape=[jax.ShapeDtypeStruct(weight.shape, F32)] * 3
        + [jax.ShapeDtypeStruct(weight.shape, BF16)],
        grid_spec=pltpu.PrefetchScalarGridSpec(
            num_scalar_prefetch=1,
            grid=(steps,),
            in_specs=[
                pl.BlockSpec(memory_space=pl.ANY),
                pl.BlockSpec((rows, LANE), lambda i, *_: (i, 0)),
                block,
                block,
                block,
            ],
            out_specs=[block] * 4,
            scratch_shapes=[
                pltpu.VMEM((capacity * LANE, LANE), BF16),
                pltpu.VMEM((rows * LANE, LANE), F32),
                pltpu.SemaphoreType.DMA((steps,)),
            ],
        ),
        compiler_params=params(48),
        cost_estimate=cost(20 * capacity * tile_len, 28 * capacity * tile_len, 2 * capacity * tile_len),
        name="adam",
    )(places, grads, used, weight, one, two)


class Links:
    def __init__(self, line, send_sems, recv_sems):
        dp = lax.axis_index("dp")
        self.line = line
        self.y = lax.axis_index("seq")
        self.z = dp // 4
        self.x = (dp // 2) % 2
        self.c = dp % 2
        self.send_sems, self.recv_sems = send_sems, recv_sems
        self.to = {
            "core": {"dp": self.z * 4 + self.x * 2 + (1 - self.c)},
            "x": {"dp": self.z * 4 + (1 - self.x) * 2 + self.c},
            "y": {"seq": 1 - self.y},
            "up": {"dp": dp + 4},
            "down": {"dp": dp - 4},
        }
        self.sent = []

    def greet(self, whole_line):
        barrier = pltpu.get_barrier_semaphore()
        for name in ("core", "x", "y"):
            pl.semaphore_signal(barrier, inc=1, device_id=self.to[name])
        if whole_line:
            for d in range(1, self.line):
                z = (self.z + d) % self.line
                pl.semaphore_signal(barrier, inc=1, device_id={"dp": z * 4 + self.x * 2 + self.c})
            pl.semaphore_wait(barrier, 2 + self.line)
            return

        @pl.when(self.z > 0)
        def _():
            pl.semaphore_signal(barrier, inc=1, device_id=self.to["down"])

        @pl.when(self.z < self.line - 1)
        def _():
            pl.semaphore_signal(barrier, inc=1, device_id=self.to["up"])

        pl.semaphore_wait(
            barrier,
            3 + jnp.where(self.z > 0, 1, 0) + jnp.where(self.z < self.line - 1, 1, 0),
        )

    def copy(self, source, target, index, way):
        sender, receiver = index if isinstance(index, tuple) else (index, index)
        to = self.to[way] if isinstance(way, str) else {"dp": way * 4 + self.x * 2 + self.c}
        return pltpu.make_async_remote_copy(
            src_ref=source,
            dst_ref=target,
            send_sem=self.send_sems.at[sender],
            recv_sem=self.recv_sems.at[receiver],
            device_id=to,
        )

    def send(self, describe):
        source, target, index, way, when = describe()
        if when is None:
            self.copy(source, target, index, way).start()
        else:

            @pl.when(when)
            def _():
                self.copy(source, target, index, way).start()

        self.sent.append(describe)

    def arrive(self, target, index, way):
        self.copy(target, target, index, way).wait_recv()

    def finish(self):
        for describe in self.sent:
            source, target, index, way, when = describe()
            if when is None:
                self.copy(source, target, index, way).wait_send()
            else:

                @pl.when(when)
                def _(source=source, target=target, index=index, way=way):
                    self.copy(source, target, index, way).wait_send()


def add_into(place, *others):
    total = place[...].astype(F32)
    for other in others:
        total = total + other[...].astype(F32)
    place[...] = total.astype(BF16)


class Scatter:
    KINDS = ("core", "xa", "yb", "ya", "xb", "to", "from")

    def __init__(self, links, base, source, offset, rows, cut, buffers, load_sems):
        self.k, self.base, self.source, self.offset, self.rows = links, base, source, offset, rows
        self.held, self.r_core, self.r_xa, self.r_yb, self.r_ya, self.r_xb, self.r_line = buffers
        self.load_sems = load_sems
        self.halves = (pl.ds(0, cut), pl.ds(cut, rows - cut))

    @staticmethod
    def buffers_of(rows, cut, line):
        return [
            pltpu.VMEM((line, 2, 2, rows, LANE), BF16),
            pltpu.VMEM((line, 4 * rows, LANE), BF16),
            pltpu.VMEM((line, 2, cut, LANE), BF16),
            pltpu.VMEM((line, 2, rows - cut, LANE), BF16),
            pltpu.VMEM((line, cut, LANE), BF16),
            pltpu.VMEM((line, rows - cut, LANE), BF16),
            pltpu.VMEM((line, rows, LANE), BF16),
        ]

    def at(self, kind, z):
        return self.base + self.KINDS.index(kind) * self.k.line + z

    def load(self, z):
        start = self.offset + (self.k.c * self.k.line + z) * 4 * self.rows
        return [
            pltpu.make_async_copy(
                self.source.at[pl.ds(pl.multiple_of(start + i * self.rows, 16), self.rows)],
                self.held.at[z, i // 2, i % 2],
                self.load_sems.at[4 * z + i],
            )
            for i in range(4)
        ]

    def begin(self):
        k = self.k

        def describe(z):
            start = self.offset + ((1 - k.c) * k.line + z) * 4 * self.rows
            source = self.source.at[pl.ds(pl.multiple_of(start, 16), 4 * self.rows)]
            return source, self.r_core.at[z], self.at("core", z), "core", None

        for z in range(k.line):
            k.send(functools.partial(describe, z))
            for copy in self.load(z):
                copy.start()

    def first(self, z):
        k, (a, b) = self.k, self.halves
        for copy in self.load(z):
            copy.wait()
        k.arrive(self.r_core.at[z], self.at("core", z), "core")
        for i in range(4):
            add_into(self.held.at[z, i // 2, i % 2], self.r_core.at[z, pl.ds(i * self.rows, self.rows)])
        k.send(lambda: (self.held.at[z, 1 - k.x, :, a], self.r_xa.at[z], self.at("xa", z), "x", None))
        k.send(lambda: (self.held.at[z, :, 1 - k.y, b], self.r_yb.at[z], self.at("yb", z), "y", None))

    def second(self, z):
        k, (a, b) = self.k, self.halves
        k.arrive(self.r_xa.at[z], self.at("xa", z), "x")
        for y in range(2):
            add_into(self.held.at[z, k.x, y, a], self.r_xa.at[z, y])
        k.send(lambda: (self.held.at[z, k.x, 1 - k.y, a], self.r_ya.at[z], self.at("ya", z), "y", None))
        k.arrive(self.r_yb.at[z], self.at("yb", z), "y")
        for x in range(2):
            add_into(self.held.at[z, x, k.y, b], self.r_yb.at[z, x])
        k.send(lambda: (self.held.at[z, 1 - k.x, k.y, b], self.r_xb.at[z], self.at("xb", z), "x", None))

    def third(self, z):
        k, (a, b) = self.k, self.halves
        k.arrive(self.r_ya.at[z], self.at("ya", z), "y")
        add_into(self.held.at[z, k.x, k.y, a], self.r_ya.at[z])
        k.arrive(self.r_xb.at[z], self.at("xb", z), "x")
        add_into(self.held.at[z, k.x, k.y, b], self.r_xb.at[z])

        def describe():
            index = (self.at("to", z), self.at("from", k.z))
            return self.held.at[z, k.x, k.y], self.r_line.at[k.z], index, z, k.z != z

        k.send(describe)

    def last(self):
        k = self.k
        others = [(k.z + d) % k.line for d in range(1, k.line)]
        for z in others:
            k.arrive(self.r_line.at[z], (self.at("to", z), self.at("from", z)), z)
        add_into(self.held.at[k.z, k.x, k.y], *[self.r_line.at[z] for z in others])


class Spread:
    KINDS = ("to", "from", "xa", "yb", "ya", "xb", "ya2", "xb2", "c0", "c1", "c2", "c3")

    def __init__(self, links, base, own, out, index, rows, cut):
        self.k, self.base, self.own, self.out, self.index = links, base, own, out, index
        self.parts = {None: (0, rows), 0: (0, cut), 1: (cut, rows - cut)}

    def at(self, kind, z):
        return self.base + self.KINDS.index(kind) * self.k.line + z

    def spot(self, z, other_x, other_y, half=None, core=None):
        k = self.k
        c = k.c if core is None else core
        x = 1 - k.x if other_x else k.x
        y = 1 - k.y if other_y else k.y
        first, count = self.parts[half]
        return self.out.at[pl.ds(pl.multiple_of(self.index(c, z, x, y) + first, 16), count)]

    def place(self, d):
        return (self.k.z + d) % self.k.line

    def give(self, kind, way, d, other_x=False, other_y=False, half=None, own=False):
        def describe():
            z = self.place(d)
            target = self.spot(z, other_x, other_y, half)
            source = self.own(half) if own else target
            return source, target, self.at(kind, z), way, None

        self.k.send(describe)

    def get(self, kind, way, d, other_x=False, other_y=False, half=None):
        z = self.place(d)
        self.k.arrive(self.spot(z, other_x, other_y, half), self.at(kind, z), way)

    def cross(self, d):
        own = d == 0
        self.give("xa", "x", d, half=0, own=own)
        self.give("yb", "y", d, half=1, own=own)
        self.give("ya", "y", d, half=0, own=own)
        self.give("xb", "x", d, half=1, own=own)
        self.give("c0", "core", d, own=own)

    def start(self):
        k = self.k

        def describe(d):
            z = self.place(d)
            return self.own(None), self.spot(k.z, False, False), (self.at("to", z), self.at("from", k.z)), z, None

        for d in (k.line - 1, 1, 2):
            k.send(functools.partial(describe, d))
        self.cross(0)

    def along(self, d):
        z = self.place(d)
        self.k.arrive(self.spot(z, False, False), (self.at("to", z), self.at("from", z)), z)
        self.cross(d)

    def turn(self, d):
        self.get("xa", "x", d, other_x=True, half=0)
        self.give("ya2", "y", d, other_x=True, half=0)
        self.get("yb", "y", d, other_y=True, half=1)
        self.give("xb2", "x", d, other_y=True, half=1)

    def share(self, d):
        self.get("ya", "y", d, other_y=True, half=0)
        self.give("c1", "core", d, other_y=True)
        self.get("xb", "x", d, other_x=True, half=1)
        self.give("c2", "core", d, other_x=True)
        self.get("ya2", "y", d, other_x=True, other_y=True, half=0)
        self.get("xb2", "x", d, other_x=True, other_y=True, half=1)
        self.give("c3", "core", d, other_x=True, other_y=True)

    def end(self):
        k = self.k
        for z in range(k.line):
            for i in range(4):
                k.arrive(self.spot(z, i >= 2, i % 2 == 1, core=1 - k.c), self.at(f"c{i}", z), "core")


RS_SEMS = len(Scatter.KINDS)
AR_SEMS = RS_SEMS + len(Spread.KINDS)


class Total:
    def __init__(self, links, base, source, offset, kind, out, top, buffers, load_sems, copy_sem):
        line = links.line
        size, cut, turn = kind
        rows = size // (8 * line)
        held = buffers[0]

        def index(c, z, x, y):
            return top + (((c * line + z) * 2 + x) * 2 + y) * rows

        def own(half):
            first, count = {None: (0, rows), 0: (0, turn), 1: (turn, rows - turn)}[half]
            return held.at[links.z, links.x, links.y, pl.ds(first, count)]

        self.line = line
        self.scatter = Scatter(links, base, source, offset, rows, cut, buffers, load_sems)
        self.spread = Spread(links, base + RS_SEMS * line, own, out, index, rows, turn)
        self.copy_sem = copy_sem

    def keep(self):
        g = self.spread
        return pltpu.make_async_copy(g.own(None), g.spot(g.k.z, False, False), self.copy_sem)

    def run(self, stage, part):
        scatter, spread = self.scatter, self.spread
        if stage == 0:
            scatter.begin()
        elif stage < 4:
            (scatter.first, scatter.second, scatter.third)[stage - 1](part)
        elif stage == 4:
            scatter.last()
            self.keep().start()
            spread.start()
        elif stage == 5:
            spread.along(part + 1)
        elif stage < 8:
            (spread.turn, spread.share)[stage - 6](part)
        else:
            self.keep().wait()
            spread.end()

    def parts(self, stage):
        return (1, 4, 4, 4, 1, 3, 4, 4, 1)[stage]


class Gather:
    KINDS = ("up", "down", "xa", "yb", "ya", "xb", "ya2", "xb2", "x2") + tuple(
        f"{way}{i}" for way in ("u", "d", "c") for i in range(4)
    )

    def __init__(self, links, base, own, out, index, first, rows, cut, z_first, twice):
        self.k, self.base, self.own, self.out, self.index = links, base, own, out, index
        self.parts = {None: (first, rows), 0: (first, cut), 1: (first + cut, rows - cut)}
        self.z_first, self.twice = z_first, twice

    def at(self, kind, z):
        return self.base + self.KINDS.index(kind) * self.k.line + z

    def spot(self, z, other_x, other_y, half=None, core=None):
        k = self.k
        c = k.c if core is None else core
        x = 1 - k.x if other_x else k.x
        y = 1 - k.y if other_y else k.y
        first, count = self.parts[half]
        return self.out.at[pl.ds(pl.multiple_of(self.index(c, z, x, y) + first, 16), count)]

    def give(self, kind, way, z, other_x=False, other_y=False, half=None, when=None, own=False):
        def describe():
            place = self.spot(z(), other_x, other_y, half)
            source = self.own(other_y, half) if own else place
            return source, place, self.at(kind, z()), way, None if when is None else when()

        self.k.send(describe)

    def get(self, kind, way, z, other_x=False, other_y=False, half=None):
        self.k.arrive(self.spot(z, other_x, other_y, half), self.at(kind, z), way)

    def near(self):
        k = self.k
        found = []
        for r in range(1, k.line):
            found.append(
                (
                    lambda r=r: k.z - r,
                    lambda r=r: k.z >= r,
                    "u",
                    "up",
                    lambda r=r: (k.z >= r) & (k.z < k.line - 1),
                )
            )
            found.append(
                (
                    lambda r=r: k.z + r,
                    lambda r=r: k.z + r < k.line,
                    "d",
                    "down",
                    lambda r=r: (k.z + r < k.line) & (k.z > 0),
                )
            )
        return found

    def here(self):
        return self.k.z

    def lower(self):
        return self.k.z < self.k.line - 1

    def upper(self):
        return self.k.z > 0

    def cross(self, z, when, own):
        self.give("xa", "x", z, half=0, when=when, own=own)
        self.give("yb", "y", z, half=1, when=when, own=own)
        self.give("ya", "y", z, half=0, when=when, own=own)
        self.give("xb", "x", z, half=1, when=when, own=own)
        self.give("c0", "core", z, when=when, own=own)

    def start(self):
        self.give("up", "up", self.here, when=self.lower, own=True)
        self.give("down", "down", self.here, when=self.upper, own=True)
        if self.twice:
            for other, kind in ((False, "xa"), (True, "x2")):
                self.give(kind, "x", self.here, other_y=other, own=True)
                self.give("c1" if other else "c0", "core", self.here, other_y=other, own=True)
        else:
            self.cross(self.here, None, True)

    def along(self, number):
        z, exists, _, way, goes_on = self.near()[number]

        @pl.when(exists())
        def _():
            self.get(way, way, z())

        self.give(way, way, z, when=goes_on)
        self.cross(z, exists, False)

    def turn(self, z, when):
        def waits():
            self.get("xa", "x", z(), other_x=True, half=0)

        def waits_too():
            self.get("yb", "y", z(), other_y=True, half=1)

        waits() if when is None else pl.when(when())(waits)
        self.give("ya2", "y", z, other_x=True, half=0, when=when)
        waits_too() if when is None else pl.when(when())(waits_too)
        self.give("xb2", "x", z, other_y=True, half=1, when=when)

    def share(self, z, when):
        def waits(kind, way, **place):
            def wait():
                self.get(kind, way, z(), **place)

            wait() if when is None else pl.when(when())(wait)

        waits("ya", "y", other_y=True, half=0)
        self.give("c1", "core", z, other_y=True, when=when)
        waits("xb", "x", other_x=True, half=1)
        self.give("c2", "core", z, other_x=True, when=when)
        waits("ya2", "y", other_x=True, other_y=True, half=0)
        waits("xb2", "x", other_x=True, other_y=True, half=1)
        self.give("c3", "core", z, other_x=True, other_y=True, when=when)

    def share_twice(self):
        for other, kind in ((False, "xa"), (True, "x2")):
            self.get(kind, "x", self.k.z, other_x=True, other_y=other)
            self.give("c3" if other else "c2", "core", self.here, other_x=True, other_y=other)

    def lift(self, i, own=False):
        place = dict(other_x=i >= 2, other_y=i % 2 == 1)
        self.give(f"u{i}", "up", self.here, when=self.lower, own=own, **place)
        self.give(f"d{i}", "down", self.here, when=self.upper, own=own, **place)
        self.give(f"c{i}", "core", self.here, own=own, **place)

    def start_plane(self):
        if self.twice:
            for other, kind in ((False, "xa"), (True, "x2")):
                self.give(kind, "x", self.here, other_y=other, own=True)
            self.lift(0, True)
            self.lift(1, True)
        else:
            self.give("xa", "x", self.here, half=0, own=True)
            self.give("yb", "y", self.here, half=1, own=True)
            self.give("ya", "y", self.here, half=0, own=True)
            self.give("xb", "x", self.here, half=1, own=True)
            self.lift(0, True)

    def turn_plane(self):
        if self.twice:
            for other, kind in ((False, "xa"), (True, "x2")):
                self.get(kind, "x", self.k.z, other_x=True, other_y=other)
                self.lift(3 if other else 2)
        else:
            self.turn(self.here, None)

    def lift_plane(self):
        if not self.twice:
            z = self.k.z
            self.get("ya", "y", z, other_y=True, half=0)
            self.lift(1)
            self.get("xb", "x", z, other_x=True, half=1)
            self.lift(2)
            self.get("ya2", "y", z, other_x=True, other_y=True, half=0)
            self.get("xb2", "x", z, other_x=True, other_y=True, half=1)
            self.lift(3)

    def along_plane(self, number, i):
        z, exists, letter, way, goes_on = self.near()[number]
        place = dict(other_x=i >= 2, other_y=i % 2 == 1)

        @pl.when(exists())
        def _():
            self.get(f"{letter}{i}", way, z(), **place)

        self.give(f"{letter}{i}", way, z, when=goes_on, **place)
        self.give(f"c{i}", "core", z, when=exists, **place)

    def steps(self):
        count = 2 * (self.k.line - 1)
        if self.z_first:
            one = [self.start]
            two = [lambda n=n: self.along(n) for n in range(count)]
            spots = [(z, exists) for z, exists, _, _, _ in self.near()]
            if not self.twice:
                spots = [(self.here, None)] + spots
            three = [lambda z=z, e=e: self.turn(z, e) for z, e in spots]
            four = [lambda z=z, e=e: self.share(z, e) for z, e in spots]
            if self.twice:
                four = [self.share_twice] + four
            return [one, two, three, four]
        one = [self.start_plane]
        two = [self.turn_plane]
        three = [self.lift_plane]
        four = [lambda n=n, i=i: self.along_plane(n, i) for n in range(count) for i in range(4)]
        return [one, two, three, four]

    def end(self):
        k = self.k
        for z in range(k.line):
            for i in range(4):
                k.arrive(
                    self.spot(z, i >= 2, i % 2 == 1, core=1 - k.c), self.at(f"c{i}", z), "core"
                )


AG_SEMS = len(Gather.KINDS)


def all_gather_kernel(line, swaps, cuts, piece, *refs):
    near, out, far = refs[:swaps], refs[swaps], refs[swaps + 1 : 2 * swaps + 1]
    send_sems, recv_sems, copy_sem = refs[2 * swaps + 1 :]
    links = Links(line, send_sems, recv_sems)
    links.greet(False)
    rows = piece.shape[0] // 2
    first_rows, second_rows = cuts
    spare = 2 * AG_SEMS * line

    def index(c, z, x, y):
        return (((z * 2 + x) * 2 + c) * 2 + y) * rows

    def keep():
        start = index(links.c, links.z, links.x, 0)
        return pltpu.make_async_copy(
            piece, out.at[pl.ds(pl.multiple_of(start, 16), 2 * rows)], copy_sem
        )

    gathers = []

    def own_of(first, count, cut):
        def own(other, half):
            begin, size = {None: (0, count), 0: (0, cut), 1: (cut, count - cut)}[half]
            y = 1 - links.y if other else links.y
            return piece.at[pl.ds(pl.multiple_of(y * rows + first + begin, 16), size)]

        return own

    last = rows - first_rows - second_rows
    spans = ((0, first_rows + second_rows, first_rows, True), (first_rows + second_rows, last, last // 32 * 16, False))
    for number, (first, count, cut, z_first) in enumerate(spans):
        gathers.append(
            Gather(
                links, number * AG_SEMS * line, own_of(first, count, cut), out, index,
                first, count, cut, z_first, True,
            )
        )
    flat, tall = gathers[0].steps(), gathers[1].steps()
    for step in flat[0] + tall[0]:
        step()
    keep().start()
    for i in range(swaps):
        links.send(lambda i=i: (near[i], far[i], spare + i, "y", None))
    along, rise = flat[1], tall[1] + tall[2]
    turn, share, climb = flat[2], flat[3], tall[3]
    for step in along[:2] + rise + turn[:2] + along[2:4] + climb[:8] + turn[2:4] + along[4:]:
        step()
    for step in climb[8:16] + turn[4:] + share[:3] + climb[16:] + share[3:]:
        step()
    for gather in gathers:
        gather.end()
    keep().wait()
    for i in range(swaps):
        links.arrive(far[i], spare + i, "y")
    links.finish()


def all_gather(piece, swaps, line, collective_id):
    any_space = pl.BlockSpec(memory_space=pl.ANY)
    sems = 2 * AG_SEMS * line + len(swaps)
    rows = piece.shape[0] // 2
    cuts = (rows * 2 // 5 // 16 * 16, rows * 7 // 20 // 16 * 16)
    return pl.pallas_call(
        functools.partial(all_gather_kernel, line, len(swaps), cuts),
        out_shape=[jax.ShapeDtypeStruct((4 * line * piece.shape[0], LANE), BF16)]
        + [jax.ShapeDtypeStruct(s.shape, s.dtype) for s in swaps],
        in_specs=[any_space] * (1 + len(swaps)),
        out_specs=[any_space] * (1 + len(swaps)),
        scratch_shapes=[
            pltpu.SemaphoreType.DMA((sems,)),
            pltpu.SemaphoreType.DMA((sems,)),
            pltpu.SemaphoreType.DMA,
        ],
        compiler_params=params(32, collective_id=collective_id, has_side_effects=True),
        cost_estimate=cost(0, 100 * MIB),
        name="all_gather",
    )(piece, *swaps)


PAIRS = D // LANE
UP_ROWS = FF * D // LANE
REST_ROWS = 128 * LANE
HEAD, NORM, LAST = 900, 901, 902
ORDER = (
    0, HEAD, 10, 100, 11, HEAD, HEAD, 12, 13, 20, 110, 111, 112, 113, HEAD, HEAD, HEAD, HEAD,
    21, 22, 23, HEAD, HEAD, HEAD, HEAD, HEAD, NORM, LAST, 200, 210, 211, 212, 213, 30, 31, 32,
    33, 40, 50, 60, 61, 220, 221, 222, 223, 51, 52, 70, 120, 121, 122, 123, 230, 231, 232, 233,
    240, 250, 130, 62, 63, 131, 132, 133, 260, 261, 71, 72, 73, 251, 262, 252, 263, 140, 150,
    160, 161, 151, 152, 162, 170, 163, 270, 271, 171, 272, 273, 172, 173, 80, 280, 180,
)


def segments():
    found = [[]]
    for step in ORDER:
        if step >= HEAD:
            found.append([])
        else:
            found[-1].append((step // 100, step // 10 % 10, step % 10))
    return found


def total_kinds(line):
    kinds = []
    for size in (UP_ROWS, UP_ROWS, REST_ROWS):
        rows = size // (8 * line)
        kinds.append((size, rows * 68 // 100 // 16 * 16, rows * 33 // 100 // 16 * 16))
    return kinds


def back_kernel(
    line,
    q, k, v, att, grad_att, chance, tokens, n1, att_all, resid_low, w_qkv, vec, vec_one, d_up, d_down,
    d_first, grad_near, out, grad_back, first_back,
    d_q, d_k, d_fresh, first_far, far, d_rest, vec_grad, flat, *scratch,
):
    step = pl.program_id(0)
    buffers, (send_sems, recv_sems, load_sems, copy_sems) = scratch[:-4], scratch[-4:]
    links = Links(line, send_sems, recv_sems)
    tops = (REST_ROWS + UP_ROWS, REST_ROWS, 0)
    totals = [
        Total(
            links, g * AR_SEMS * line, source, 0, kind, out, top,
            buffers[7 * g : 7 * g + 7], load_sems.at[g], copy_sems.at[g],
        )
        for g, (source, kind, top) in enumerate(zip((d_down, d_up, d_rest), total_kinds(line), tops))
    ]
    spare = len(totals) * AR_SEMS * line
    plan = segments()

    def run(number):
        for g, stage, part in plan[number]:
            totals[g].run(stage, part)

    queries = q.shape[0]
    for head in range(2):
        for s in range(PAIRS):

            @pl.when(step == s)
            def _(s=s, head=head):
                if s == 0 and head == 0:
                    links.greet(True)
                run(2 * s + head)

        @pl.when(step < PAIRS)
        def _(head=head):
            cols = slice(head * HD, (head + 1) * HD)
            grad = grad_att[:, cols]
            weights = chance[head]
            shared = grad.astype(F32) * att[:, cols].astype(F32)
            delta = jnp.sum(shared.T, axis=0, keepdims=True)
            grad_chance = mm(v[:, cols], grad, NT)
            grad_scores = (weights.astype(F32) * (grad_chance - delta)).astype(BF16)
            grad_value = mm(weights, grad)

            @pl.when(step < 3)
            def _():
                d_fresh[jnp.minimum(step, 2), :, cols] = grad_value.astype(BF16)

            @pl.when(step >= 3)
            def _():
                d_first[:, cols] = grad_value[:queries]
                first_far[jnp.maximum(step - 3, 0), :, cols] = grad_value[queries:].astype(BF16)

            d_k[step, :, cols] = mm(grad_scores, q[:, cols]).astype(BF16)
            d_q[step, :, cols] = (mm(k[:, cols], grad_scores, TN).T * HD ** (-0.5)).astype(BF16)

    @pl.when(step == PAIRS)
    def _():
        rows = n1.shape[0] // 2
        per_row = D // LANE
        run(2 * PAIRS)
        links.send(lambda: (first_far, first_back, spare, "y", None))
        dq = jnp.concatenate([d_q[i] for i in range(PAIRS)], axis=1)
        dk = jnp.concatenate([d_k[i] for i in range(PAIRS)], axis=1)
        dv = jnp.concatenate([d_fresh[i] for i in range(PAIRS // 2)], axis=1)
        grads = mm(dk, w_qkv[:, D : 2 * D], NT) + mm(dv, w_qkv[:, 2 * D :], NT)
        beside = grads[rows:]
        far[...] = beside.astype(BF16)
        links.send(lambda: (far, grad_back, spare + 1, "y", None))
        near = grads[:rows] + mm(dq, w_qkv[:, :D], NT)
        grad_near[...] = near
        hat, _ = normed(tokens[...].astype(F32))
        vec_grad[...] = vec_one[...]
        vec_grad[:, :D] = jnp.sum(near * hat[:rows], axis=0, keepdims=True) + jnp.sum(
            beside * hat[rows:], axis=0, keepdims=True
        )
        vec_grad[:, D : 2 * D] = jnp.sum(near, axis=0, keepdims=True) + jnp.sum(
            beside, axis=0, keepdims=True
        )
        vec_grad[:, 4 * D : 5 * D] = jnp.sum(dq.astype(F32), axis=0, keepdims=True)
        vec_grad[:, 7 * D : 7 * D + HV] = jnp.sum(dv.astype(F32), axis=0, keepdims=True)
        run(2 * PAIRS + 1)
        pieces = (
            (n1[:rows], dq, 0, per_row),
            (n1[...], dk, D * per_row, per_row),
            (n1[...], dv, 2 * D * per_row, HV // LANE),
            (att_all[...], resid_low[...], 2 * D * per_row + D * HV // LANE, per_row),
        )
        for left, right, start, columns in pieces:
            product = mm(left, right, TN)
            size = D * columns
            for j in range(columns):
                flat[pl.ds(j, D, stride=columns), :] = product[:, j * LANE : (j + 1) * LANE]
            d_rest[start : start + size] = flat[:size].astype(BF16)
        flat[: 2 * LANE] = jnp.zeros((2 * LANE, LANE), F32)
        for j in range(VEC // LANE):
            flat[j : j + 1] = vec_grad[:, j * LANE : (j + 1) * LANE]
        d_rest[REST:] = flat[: 2 * LANE].astype(BF16)
        run(2 * PAIRS + 2)
        links.arrive(first_back, spare, "y")
        links.arrive(grad_back, spare + 1, "y")
        links.finish()


def back(q, k, v, att, grad_att, chance, tokens, n1, resid_low, w_qkv, vec, vec_one, d_up, d_down, line):
    rows, keys = q.shape[0], k.shape[0]
    any_space = pl.BlockSpec(memory_space=pl.ANY)

    def column(count):
        return pl.BlockSpec((count, LANE), lambda i: (0, jnp.minimum(i, PAIRS - 1)))

    def once(array):
        return pl.BlockSpec(array.shape, lambda i: (0,) * array.ndim, pipeline_mode=pl.Buffered(1))

    kinds = total_kinds(line)
    scratch = []
    for size, cut, _ in kinds:
        scratch += Scatter.buffers_of(size // (8 * line), cut, line)
    sems = len(kinds) * AR_SEMS * line + 2
    return pl.pallas_call(
        functools.partial(back_kernel, line),
        out_shape=[
            jax.ShapeDtypeStruct((rows, HV), F32),
            jax.ShapeDtypeStruct((rows, D), F32),
            jax.ShapeDtypeStruct((REST_ROWS + 2 * UP_ROWS, LANE), BF16),
            jax.ShapeDtypeStruct((rows, D), BF16),
            jax.ShapeDtypeStruct((PAIRS // 2, rows, LANE), BF16),
        ],
        grid=(PAIRS + 1,),
        in_specs=[
            column(rows),
            column(keys),
            column(keys),
            column(rows),
            column(rows),
            pl.BlockSpec((2, keys, rows), lambda i: (jnp.minimum(i, PAIRS - 1), 0, 0)),
            once(tokens),
            once(n1),
            once(att),
            once(resid_low),
            once(w_qkv),
            once(vec),
            once(vec_one),
            any_space,
            any_space,
        ],
        out_specs=[
            pl.BlockSpec((rows, LANE), lambda i: (0, jnp.clip(i - 3, 0, 2))),
            pl.BlockSpec((rows, D), lambda i: (0, 0), pipeline_mode=pl.Buffered(1)),
            any_space,
            any_space,
            any_space,
        ],
        scratch_shapes=[
            pltpu.VMEM((PAIRS, rows, LANE), BF16),
            pltpu.VMEM((PAIRS, keys, LANE), BF16),
            pltpu.VMEM((PAIRS // 2, keys, LANE), BF16),
            pltpu.VMEM((PAIRS // 2, rows, LANE), BF16),
            pltpu.VMEM((rows, D), BF16),
            pltpu.VMEM((REST_ROWS, LANE), BF16),
            pltpu.VMEM((1, VEC), F32),
            pltpu.VMEM((D * D // LANE, LANE), F32),
        ]
        + scratch
        + [
            pltpu.SemaphoreType.DMA((sems,)),
            pltpu.SemaphoreType.DMA((sems,)),
            pltpu.SemaphoreType.DMA((len(kinds), 4 * line)),
            pltpu.SemaphoreType.DMA((len(kinds),)),
        ],
        compiler_params=params(62, collective_id=0, has_side_effects=True),
        cost_estimate=cost(8 * rows * keys * D + 14 * rows * D * D, 100 * MIB),
        name="back",
    )(q, k, v, att, grad_att, chance, tokens, n1, att, resid_low, w_qkv, vec, vec_one, d_up, d_down)


def swap(value):
    return lax.ppermute(value, "seq", [(0, 1), (1, 0)])


def shards(
    tokens,
    first_values,
    out_grad,
    block_place,
    owners,
    masters,
    moment_one,
    moment_two,
    vector_master,
    vector_moment_one,
    vector_moment_two,
):
    capacity = masters.shape[0]
    dp_count = lax.axis_size("dp")
    tile_count = owners.shape[0]
    dp_here = lax.axis_index("dp")
    seq_here = lax.axis_index("seq")
    _, half_len, _ = tokens.shape

    tokens = tokens.reshape(half_len, D)
    firsts = first_values.reshape(half_len, HV)
    given = out_grad.reshape(half_len, D)
    line = dp_count // 4
    packed = pack_slots(masters)
    if line == LINE:
        slots, tokens_far, firsts_far = all_gather(packed, [tokens, firsts], line, 1)
    else:
        tokens_far, firsts_far = swap(tokens), swap(firsts)
        slots = lax.all_gather(packed, "dp", axis=0, tiled=True)

    slot_index = slot_numbers(owners)
    slot_rows = owners * capacity + slot_index
    mine = (owners == dp_here)[None, :] & (
        slot_index[None, :] == jnp.arange(capacity, dtype=jnp.int32)[:, None]
    )
    tile_order = jnp.arange(tile_count, dtype=jnp.int32)
    tile_here = jnp.sum(jnp.where(mine, tile_order[None, :], 0), axis=1)
    tile_here = tile_here + jnp.where(tile_here >= 126, 2, 0)
    used = jnp.broadcast_to(
        jnp.any(mine, axis=1).astype(F32)[:, None], (capacity, LANE)
    )

    blocks = block_place.reshape(-1)
    per_device = blocks.shape[0] // 2
    block_len = half_len // per_device
    ordered = jnp.roll(blocks, -seq_here * per_device)
    all_pos = (
        ordered[:, None] * block_len + jnp.arange(block_len, dtype=jnp.int32)[None, :]
    ).reshape(-1)
    row_pos = all_pos[:half_len].reshape(1, half_len)
    column_pos = all_pos.reshape(2 * half_len, 1)

    vec = vector_master.reshape(1, VEC)
    tokens_all = jnp.concatenate([tokens, tokens_far], axis=0)
    firsts_all = jnp.concatenate([firsts, firsts_far], axis=0)

    w_qkv, w_out, w_up, w_down = unpack_weights(slot_rows, slots)
    n1, q, k, v = project(tokens_all, firsts_all, w_qkv, vec)
    att, chance = attend(q, k, v, row_pos, column_pos)
    result, grad_resid, resid_low, grad_att, d_up, d_down, vec_one = hidden(
        tokens, att, given, w_out, w_up, w_down, vec
    )
    if line == LINE:
        first_near, grad_near, grads, grad_back, first_back = back(
            q, k, v, att, grad_att, chance, tokens_all, n1, resid_low, w_qkv, vec, vec_one, d_up, d_down, line
        )
        first_back = first_back.transpose(1, 0, 2).reshape(half_len, HV)
    else:
        d_q, d_k, d_fresh, d_first = attend_back(q, k, v, att, grad_att, chance)
        grad_near, grad_far, d_rest = project_back(
            tokens_all, n1, d_q, d_k, d_fresh, att, resid_low, w_qkv, vec, vec_one
        )
        first_near = d_first[:half_len]
        grad_back, first_back = swap(grad_far), swap(d_first[half_len:].astype(BF16))
        grads = lax.psum(jnp.concatenate([d_rest, d_up, d_down], axis=0), ("seq", "dp"))
    vector_total = grads[REST : REST + VEC // LANE].reshape(VEC).astype(F32)

    grad_n1 = grad_near + grad_back.astype(F32)
    hat, rate = normed(tokens.astype(F32))
    tokens_grad = grad_resid + norm_back(grad_n1, hat, rate, vec[:, :D])
    first_grad = first_near + first_back.astype(F32)

    new_master, new_one, new_two, new_low = adam(
        tile_here, grads, used, masters, moment_one, moment_two
    )
    vector_new, vector_one, vector_two = adam_step(
        vector_master, vector_moment_one, vector_moment_two, vector_total, RATE_VECTOR, 0.0
    )
    return (
        result.reshape(1, half_len, D),
        tokens_grad.reshape(1, half_len, D),
        first_grad.reshape(1, half_len, HV),
        new_master,
        new_one,
        new_two,
        new_low,
        vector_new,
        vector_one,
        vector_two,
    )


def solution(mesh):
    rows = P("dp", "seq", None)
    slots = P("dp", None)
    return jax.shard_map(
        shards,
        mesh=mesh,
        in_specs=(rows, rows, rows, slots, P(), slots, slots, slots, P(), P(), P()),
        out_specs=(rows, rows, rows, slots, slots, slots, slots, P(), P(), P()),
        check_vma=False,
    )
```

```python
import functools

import jax
import jax.numpy as jnp
from jax import lax
from jax.experimental import pallas as pl
from jax.experimental.pallas import tpu as pltpu
from jax.sharding import PartitionSpec as P

D = 768
HD = 64
FF = 3072
STEP = 10
HV = 384
LANE = 128
QKV = 2 * D + HV
FF_STEP = 768
VEC = 7 * D + HV + FF
MIB = 1024 * 1024
LINE = 4
REST = 126 * LANE

EPS_NORM = 1e-05
EPS_ADAM = 1e-08
BETA_ONE = 0.5
BETA_TWO = 0.5
RATE_MATRIX = 0.03
RATE_VECTOR = 0.25
DECAY_MATRIX = 0.1
FAR = -1e30

BF16 = jnp.bfloat16
F32 = jnp.float32

NN = (((1,), (0,)), ((), ()))
NT = (((1,), (1,)), ((), ()))
TN = (((0,), (0,)), ((), ()))


def mm(left, right, dims=NN):
    return lax.dot_general(left, right, dims, preferred_element_type=F32)


def vec_part(vec_ref, index):
    if index < 7:
        return vec_ref[:, index * D : (index + 1) * D]
    if index == 7:
        return vec_ref[:, 7 * D : 7 * D + HV]
    return vec_ref[:, 7 * D + HV :]


def params(mib, **more):
    return pltpu.CompilerParams(vmem_limit_bytes=mib * MIB, **more)


def whole(shape):
    return pl.BlockSpec(shape, lambda *_: (0,) * len(shape))


def cost(flops, bytes_accessed, transcendentals=0):
    return pl.CostEstimate(
        flops=int(flops), bytes_accessed=int(bytes_accessed), transcendentals=int(transcendentals)
    )


def adam_step(weight, first_moment, second_moment, gradient, step_rate, weight_decay):
    first_new = BETA_ONE * first_moment + (1.0 - BETA_ONE) * gradient
    second_new = BETA_TWO * second_moment + (1.0 - BETA_TWO) * gradient * gradient
    first_fix = 1.0 - BETA_ONE**STEP
    second_fix = 1.0 - BETA_TWO**STEP
    update = (first_new * (1.0 / first_fix)) / (jnp.sqrt(second_new * (1.0 / second_fix)) + EPS_ADAM)
    return (weight - step_rate * (update + weight_decay * weight), first_new, second_new)


def slot_numbers(owners):
    tile_order = jnp.arange(owners.shape[0], dtype=jnp.int32)
    earlier = (owners[None, :] == owners[:, None]) & (tile_order[None, :] < tile_order[:, None])
    return jnp.sum(earlier.astype(jnp.int32), axis=1)


def normed(values):
    center = jnp.mean(values, axis=-1, keepdims=True)
    centred = values - center
    spread = jnp.mean(centred * centred, axis=-1, keepdims=True)
    rate = lax.rsqrt(spread + EPS_NORM)
    return centred * rate, rate


def norm_back(grad, hat, rate, gain):
    g = grad * gain
    return rate * (
        g - jnp.mean(g, axis=-1, keepdims=True) - hat * jnp.mean(g * hat, axis=-1, keepdims=True)
    )


def pack_kernel(src, dst, flat):
    rows = src.shape[0]
    for c in range(LANE):
        flat[pl.ds(c, rows, stride=LANE), :] = src[:, c * LANE : (c + 1) * LANE]
    dst[...] = flat[...].astype(BF16)


def pack_slots(masters):
    capacity, tile_len = masters.shape
    rows = 8 if capacity % 8 == 0 else capacity
    return pl.pallas_call(
        pack_kernel,
        out_shape=jax.ShapeDtypeStruct((capacity * LANE, LANE), BF16),
        grid=(capacity // rows,),
        in_specs=[pl.BlockSpec((rows, tile_len), lambda i: (i, 0))],
        out_specs=pl.BlockSpec((rows * LANE, LANE), lambda i: (i, 0)),
        scratch_shapes=[pltpu.VMEM((rows * LANE, LANE), F32)],
        compiler_params=params(60),
        cost_estimate=cost(0, capacity * tile_len * 6),
        name="pack_slots",
    )(masters)


def weight_chunks():
    chunks = [
        (0, 36, 6, 0, 0, 0),
        (36, 36, 6, 0, D, 0),
        (72, 18, 3, 0, 2 * D, 0),
        (90, 36, 6, 1, 0, 0),
    ]
    for i in range(4):
        chunks.append((126 + 36 * i, 36, 24, 2, 0, 192 * i))
    for i in range(4):
        chunks.append((270 + 36 * i, 36, 6, 3, 0, 768 * i))
    return chunks


def unpack_kernel(slot_rows, slots, w_qkv, w_out, w_up, w_down, stage, o_qkv, o_out, o_up, o_down, flat, sems, out_sems):
    chunks = weight_chunks()
    places = (o_qkv, o_out, o_up, o_down)
    ends = (w_qkv, w_out, w_up, w_down)

    for number, (first, tiles, _, _, _, _) in enumerate(chunks):

        @pl.loop(0, tiles)
        def _(i, first=first, number=number):
            t = first + i
            pltpu.make_async_copy(
                slots.at[pl.ds(pl.multiple_of(slot_rows[t] * LANE, LANE), LANE)],
                stage.at[pl.ds(pl.multiple_of(t * LANE, LANE), LANE)],
                sems.at[number],
            ).start()

    copies = []
    for number, (first, tiles, per_row, matrix, column, row) in enumerate(chunks):
        span = pl.ds(first * LANE, tiles * LANE)
        pltpu.make_async_copy(stage.at[span], stage.at[span], sems.at[number]).wait()
        place = places[matrix]
        lines = 3 * LANE // per_row

        @pl.loop(0, tiles // 6)
        def _(g, first=first, per_row=per_row, place=place, column=column, row=row, lines=lines):
            for half in range(2):
                base = pl.multiple_of(first * LANE + (2 * g + half) * 3 * LANE, LANE)
                flat[half] = stage[pl.ds(base, 3 * LANE), :].astype(F32)
            for half in range(2):
                top = pl.multiple_of(row + (2 * g + half) * lines, 16)
                for j in range(per_row):
                    place[pl.ds(top, lines), column + j * LANE : column + (j + 1) * LANE] = flat[
                        half, pl.ds(j, lines, stride=per_row), :
                    ].astype(BF16)

        rows = tiles * LANE // per_row
        columns = pl.ds(column, per_row * LANE)
        copy = pltpu.make_async_copy(
            place.at[pl.ds(row, rows), columns],
            ends[matrix].at[pl.ds(row, rows), columns],
            out_sems.at[number],
        )
        copy.start()
        copies.append(copy)
    for copy in copies:
        copy.wait()


def unpack_weights(slot_rows, slots):
    tile_count = slot_rows.shape[0]
    shapes = [(D, QKV), (D, D), (D, FF), (FF, D)]
    any_space = pl.BlockSpec(memory_space=pl.ANY)
    return pl.pallas_call(
        unpack_kernel,
        out_shape=[jax.ShapeDtypeStruct(s, BF16) for s in shapes],
        grid_spec=pltpu.PrefetchScalarGridSpec(
            num_scalar_prefetch=1,
            grid=(1,),
            in_specs=[any_space],
            out_specs=[any_space] * 4,
            scratch_shapes=[pltpu.VMEM((tile_count * LANE, LANE), BF16)]
            + [pltpu.VMEM(s, BF16) for s in shapes]
            + [
                pltpu.VMEM((2, 3 * LANE, LANE), F32),
                pltpu.SemaphoreType.DMA((12,)),
                pltpu.SemaphoreType.DMA((12,)),
            ],
        ),
        compiler_params=params(60),
        cost_estimate=cost(0, 4 * tile_count * LANE * LANE),
        name="unpack_weights",
    )(slot_rows, slots)


def project_kernel(near, far, firsts, firsts_far, w_qkv, vec, n1, q, k, v):
    first = pl.program_id(0) == 0
    tokens = jnp.where(first, near[...], far[...])
    hat, _ = normed(tokens.astype(F32))
    low = (hat * vec_part(vec, 0) + vec_part(vec, 1)).astype(BF16)
    n1[...] = low
    k[...] = mm(low, w_qkv[:, D : 2 * D]).astype(BF16)
    v[:, :HV] = (mm(low, w_qkv[:, 2 * D :]) + vec_part(vec, 7)).astype(BF16)
    v[:, HV:] = jnp.where(first, firsts[...], firsts_far[...])

    @pl.when(first)
    def _():
        query = mm(low, w_qkv[:, :D]) + vec_part(vec, 4)
        q[...] = (query.astype(BF16).astype(F32) * HD ** (-0.5)).astype(BF16)


def project(near, far, firsts, firsts_far, w_qkv, vec):
    rows = near.shape[0]
    by_row = pl.BlockSpec((rows, D), lambda i: (i, 0))
    return pl.pallas_call(
        project_kernel,
        out_shape=[
            jax.ShapeDtypeStruct((2 * rows, D), BF16),
            jax.ShapeDtypeStruct((rows, D), BF16),
            jax.ShapeDtypeStruct((2 * rows, D), BF16),
            jax.ShapeDtypeStruct((2 * rows, D), BF16),
        ],
        grid=(2,),
        in_specs=[
            whole((rows, D)),
            whole((rows, D)),
            whole((rows, HV)),
            whole((rows, HV)),
            whole((D, QKV)),
            whole((1, VEC)),
        ],
        out_specs=[by_row, whole((rows, D)), by_row, by_row],
        compiler_params=params(60),
        cost_estimate=cost(4 * rows * D * QKV, 2 * D * QKV + rows * D * 20),
        name="project",
    )(near, far, firsts, firsts_far, w_qkv, vec)


def attend_kernel(q, k, v, row_pos, column_pos, out, chance, bias):
    @pl.when(pl.program_id(0) == 0)
    def _():
        bias[...] = jnp.where(column_pos[...] <= row_pos[...], 0.0, FAR)

    heads = [slice(head * HD, (head + 1) * HD) for head in range(2)]
    scores = [mm(k[:, cols], q[:, cols], NT) + bias[...] for cols in heads]
    for head in range(2):
        top = jnp.max(scores[head], axis=0, keepdims=True)
        power = jnp.exp(scores[head] - top)
        total = jnp.sum(power, axis=0, keepdims=True)
        chance[head] = (power * (1.0 / total)).astype(BF16)
    for head, cols in enumerate(heads):
        out[:, cols] = mm(v[:, cols], chance[head], TN).T.astype(BF16)


def attend(q, k, v, row_pos, column_pos):
    queries, keys = q.shape[0], k.shape[0]
    pairs = D // LANE
    by_column = lambda i: (0, i)
    return pl.pallas_call(
        attend_kernel,
        out_shape=[
            jax.ShapeDtypeStruct((queries, D), BF16),
            jax.ShapeDtypeStruct((2 * pairs, keys, queries), BF16),
        ],
        grid=(pairs,),
        in_specs=[
            pl.BlockSpec((queries, LANE), by_column),
            pl.BlockSpec((keys, LANE), by_column),
            pl.BlockSpec((keys, LANE), by_column),
            whole((1, queries)),
            whole((keys, 1)),
        ],
        out_specs=[
            pl.BlockSpec((queries, LANE), by_column),
            pl.BlockSpec((2, keys, queries), lambda i: (i, 0, 0)),
        ],
        scratch_shapes=[pltpu.VMEM((keys, queries), F32)],
        compiler_params=params(60),
        cost_estimate=cost(4 * queries * keys * D, 24 * queries * keys, 12 * queries * keys),
        name="attend",
    )(q, k, v, row_pos, column_pos)


def hidden_kernel(
    tokens, att, og, w_out, w_up, w_down, vec,
    result, grad_resid, resid_low, grad_att, d_up, d_down, vec_grad,
    resid, hat, n2, rate, acc, acc_grad, flat_up, flat_down,
):
    step = pl.program_id(0)
    per_row = D // LANE
    wide = FF // LANE

    @pl.when(step == 0)
    def _():
        base = tokens[...].astype(F32) + mm(att[...], w_out[...]) + vec_part(vec, 5)
        resid[...] = base
        unit, scale = normed(base)
        hat[...] = unit
        rate[...] = scale
        n2[...] = (unit * vec_part(vec, 2) + vec_part(vec, 3)).astype(BF16)
        vec_grad[...] = jnp.zeros_like(vec_grad)
        acc[...] = jnp.zeros_like(acc)
        acc_grad[...] = jnp.zeros_like(acc_grad)

    start = pl.multiple_of(7 * D + HV + step * FF_STEP, LANE)
    pre = mm(n2[...], w_up[...]) + vec[:, pl.ds(start, FF_STEP)]
    square = pre * pre
    bent = jnp.tanh(0.7978845608028654 * (pre + 0.044715 * square * pre))
    half = 0.5 * (1.0 + bent)
    act = (pre * half).astype(BF16)
    slope = half + (0.5 * 0.7978845608028654) * pre * (1.0 - bent * bent) * (1.0 + 0.134145 * square)
    grad_pre32 = mm(og[...], w_down[...], NT) * slope
    grad_pre = grad_pre32.astype(BF16)
    vec_grad[:, pl.ds(start, FF_STEP)] = jnp.sum(grad_pre.astype(F32), axis=0, keepdims=True)
    acc[...] += mm(act, w_down[...])
    acc_grad[...] += mm(grad_pre, w_up[...], NT)
    down = mm(act, og[...], TN)
    for j in range(per_row):
        flat_down[pl.ds(j, FF_STEP, stride=per_row), :] = down[:, j * LANE : (j + 1) * LANE]
    d_down[...] = flat_down[...].astype(BF16)
    up = mm(n2[...], grad_pre, TN)
    for j in range(FF_STEP // LANE):
        flat_up[pl.ds(step * (FF_STEP // LANE) + j, D, stride=wide), :] = up[
            :, j * LANE : (j + 1) * LANE
        ]

    @pl.when(step == FF // FF_STEP - 1)
    def _():
        d_up[...] = flat_up[...].astype(BF16)
        result[...] = (resid[...] + acc[...] + vec_part(vec, 6)).astype(BF16)
        grad = acc_grad[...]
        unit = hat[...]
        vec_grad[:, 2 * D : 3 * D] = jnp.sum(grad * unit, axis=0, keepdims=True)
        vec_grad[:, 3 * D : 4 * D] = jnp.sum(grad, axis=0, keepdims=True)
        given = og[...].astype(F32)
        back = given + norm_back(grad, unit, rate[...], vec_part(vec, 2))
        grad_resid[...] = back
        low = back.astype(BF16)
        resid_low[...] = low
        vec_grad[:, 5 * D : 6 * D] = jnp.sum(low.astype(F32), axis=0, keepdims=True)
        vec_grad[:, 6 * D : 7 * D] = jnp.sum(given, axis=0, keepdims=True)
        grad_att[...] = mm(low, w_out[...], NT).astype(BF16)


def hidden(tokens, att, og, w_out, w_up, w_down, vec):
    rows = tokens.shape[0]
    line = (rows, D)
    flat_rows = FF * D // LANE
    return pl.pallas_call(
        hidden_kernel,
        out_shape=[
            jax.ShapeDtypeStruct(line, BF16),
            jax.ShapeDtypeStruct(line, F32),
            jax.ShapeDtypeStruct(line, BF16),
            jax.ShapeDtypeStruct(line, BF16),
            jax.ShapeDtypeStruct((flat_rows, LANE), BF16),
            jax.ShapeDtypeStruct((flat_rows, LANE), BF16),
            jax.ShapeDtypeStruct((1, VEC), F32),
        ],
        grid=(FF // FF_STEP,),
        in_specs=[
            whole(line),
            whole(line),
            whole(line),
            whole((D, D)),
            pl.BlockSpec((D, FF_STEP), lambda i: (0, i)),
            pl.BlockSpec((FF_STEP, D), lambda i: (i, 0)),
            whole((1, VEC)),
        ],
        out_specs=[
            whole(line),
            whole(line),
            whole(line),
            whole(line),
            whole((flat_rows, LANE)),
            pl.BlockSpec((FF_STEP * D // LANE, LANE), lambda i: (i, 0)),
            whole((1, VEC)),
        ],
        scratch_shapes=[
            pltpu.VMEM(line, F32),
            pltpu.VMEM(line, F32),
            pltpu.VMEM(line, BF16),
            pltpu.VMEM((rows, 1), F32),
            pltpu.VMEM(line, F32),
            pltpu.VMEM(line, F32),
            pltpu.VMEM((flat_rows, LANE), F32),
            pltpu.VMEM((FF_STEP * D // LANE, LANE), F32),
        ],
        compiler_params=params(62),
        cost_estimate=cost(2 * rows * D * (6 * FF + 2 * D), 8 * D * FF + 20 * rows * D, rows * FF),
        name="hidden",
    )(tokens, att, og, w_out, w_up, w_down, vec)


def attend_back_kernel(q, k, v, att, grad_att, chance, d_q, d_k, d_fresh, d_first):
    pair = pl.program_id(0)
    for head in range(2):
        cols = slice(head * HD, (head + 1) * HD)
        grad = grad_att[:, cols]
        weights = chance[head]
        shared = grad.astype(F32) * att[:, cols].astype(F32)
        delta = jnp.sum(shared.T, axis=0, keepdims=True)
        grad_chance = mm(v[:, cols], grad, NT)
        grad_scores = (weights.astype(F32) * (grad_chance - delta)).astype(BF16)
        grad_value = mm(weights, grad)

        @pl.when(pair < 3)
        def _(grad_value=grad_value, cols=cols):
            d_fresh[:, cols] = grad_value.astype(BF16)

        @pl.when(pair >= 3)
        def _(grad_value=grad_value, cols=cols):
            d_first[:, cols] = grad_value

        d_k[:, cols] = mm(grad_scores, q[:, cols]).astype(BF16)
        d_q[:, cols] = (mm(k[:, cols], grad_scores, TN).T * HD ** (-0.5)).astype(BF16)


def attend_back(q, k, v, att, grad_att, chance):
    queries, keys = q.shape[0], k.shape[0]
    pairs = D // LANE
    by_column = lambda i: (0, i)
    return pl.pallas_call(
        attend_back_kernel,
        out_shape=[
            jax.ShapeDtypeStruct((queries, D), BF16),
            jax.ShapeDtypeStruct((keys, D), BF16),
            jax.ShapeDtypeStruct((keys, HV), BF16),
            jax.ShapeDtypeStruct((keys, HV), F32),
        ],
        grid=(pairs,),
        in_specs=[
            pl.BlockSpec((queries, LANE), by_column),
            pl.BlockSpec((keys, LANE), by_column),
            pl.BlockSpec((keys, LANE), by_column),
            pl.BlockSpec((queries, LANE), by_column),
            pl.BlockSpec((queries, LANE), by_column),
            pl.BlockSpec((2, keys, queries), lambda i: (i, 0, 0)),
        ],
        out_specs=[
            pl.BlockSpec((queries, LANE), by_column),
            pl.BlockSpec((keys, LANE), by_column),
            pl.BlockSpec((keys, LANE), lambda i: (0, jnp.minimum(i, 2))),
            pl.BlockSpec((keys, LANE), lambda i: (0, jnp.maximum(i - 3, 0))),
        ],
        compiler_params=params(60),
        cost_estimate=cost(8 * queries * keys * D, 24 * queries * keys),
        name="attend_back",
    )(q, k, v, att, grad_att, chance)


def project_back_kernel(
    tokens, n1, d_q, d_k, d_fresh, att, resid_low, w_qkv, vec, vec_one,
    grad_near, grad_far, d_rest, vec_grad, flat,
):
    rows = n1.shape[0] // 2
    per_row = D // LANE
    grads = mm(d_k[...], w_qkv[:, D : 2 * D], NT) + mm(d_fresh[...], w_qkv[:, 2 * D :], NT)
    near = grads[:rows] + mm(d_q[...], w_qkv[:, :D], NT)
    far = grads[rows:]
    grad_near[...] = near
    grad_far[...] = far.astype(BF16)
    hat, _ = normed(tokens[...].astype(F32))
    vec_grad[...] = vec_one[...]
    vec_grad[:, :D] = jnp.sum(near * hat[:rows], axis=0, keepdims=True) + jnp.sum(
        far * hat[rows:], axis=0, keepdims=True
    )
    vec_grad[:, D : 2 * D] = jnp.sum(near, axis=0, keepdims=True) + jnp.sum(
        far, axis=0, keepdims=True
    )
    vec_grad[:, 4 * D : 5 * D] = jnp.sum(d_q[...].astype(F32), axis=0, keepdims=True)
    vec_grad[:, 7 * D : 7 * D + HV] = jnp.sum(d_fresh[...].astype(F32), axis=0, keepdims=True)
    pieces = (
        (n1, d_q, rows, 0, per_row),
        (n1, d_k, 2 * rows, D * per_row, per_row),
        (n1, d_fresh, 2 * rows, 2 * D * per_row, HV // LANE),
        (att, resid_low, rows, 2 * D * per_row + D * HV // LANE, per_row),
    )
    for left, right, count, start, columns in pieces:
        product = mm(left[:count], right[:count], TN)
        size = D * columns
        for j in range(columns):
            flat[pl.ds(j, D, stride=columns), :] = product[:, j * LANE : (j + 1) * LANE]
        d_rest[start : start + size] = flat[:size].astype(BF16)
    flat[: 2 * LANE] = jnp.zeros((2 * LANE, LANE), F32)
    for j in range(VEC // LANE):
        flat[j : j + 1] = vec_grad[:, j * LANE : (j + 1) * LANE]
    d_rest[REST:] = flat[: 2 * LANE].astype(BF16)


def project_back(tokens, n1, d_q, d_k, d_fresh, att, resid_low, w_qkv, vec, vec_one):
    rows = n1.shape[0] // 2
    vm = pl.BlockSpec(memory_space=pltpu.VMEM)
    return pl.pallas_call(
        project_back_kernel,
        out_shape=[
            jax.ShapeDtypeStruct((rows, D), F32),
            jax.ShapeDtypeStruct((rows, D), BF16),
            jax.ShapeDtypeStruct((128 * LANE, LANE), BF16),
        ],
        in_specs=[vm] * 10,
        out_specs=[vm] * 3,
        scratch_shapes=[pltpu.VMEM((1, VEC), F32), pltpu.VMEM((D * D // LANE, LANE), F32)],
        compiler_params=params(58),
        cost_estimate=cost(2 * rows * D * (7 * D), 14 * MIB),
        name="project_back",
    )(tokens, n1, d_q, d_k, d_fresh, att, resid_low, w_qkv, vec, vec_one)


def finish_kernel(
    places, grads, used, weight, one, two,
    resid, near, far, tokens, vec, firsts, firsts_far, vec_weight, vec_one, vec_two,
    new, new_one, new_two, low, tokens_grad, first_grad, new_vec, new_vec_one, new_vec_two,
    stage, flat, vec_stage, v_weight, v_one, v_two, v_low,
    v_resid, v_near, v_far, v_tokens, v_firsts, v_firsts_far,
    slot_sems, in_sems, out_sems, side_sems, vec_sem,
):
    capacity = weight.shape[0]
    rows = flat.shape[0] // LANE
    steps = capacity // rows

    def span(s):
        return pl.ds(s * rows, rows)

    vec_copy = pltpu.make_async_copy(grads.at[pl.ds(REST, vec_stage.shape[0])], vec_stage, vec_sem)
    vec_copy.start()
    brought = []
    for s in range(steps):
        for i, (source, target) in enumerate(((weight, v_weight), (one, v_one), (two, v_two))):
            brought.append(
                pltpu.make_async_copy(source.at[span(s)], target.at[span(s)], in_sems.at[3 * s + i])
            )
            brought[-1].start()

        @pl.loop(0, rows)
        def _(i, s=s):
            slot = s * rows + i
            pltpu.make_async_copy(
                grads.at[pl.ds(pl.multiple_of(places[slot] * LANE, LANE), LANE)],
                stage.at[pl.ds(pl.multiple_of(slot * LANE, LANE), LANE)],
                slot_sems.at[s],
            ).start()

    sides = [
        pltpu.make_async_copy(source, target, side_sems.at[i])
        for i, (source, target) in enumerate(
            (
                (resid, v_resid),
                (near, v_near),
                (far, v_far),
                (tokens, v_tokens),
                (firsts, v_firsts),
                (firsts_far, v_firsts_far),
            )
        )
    ]
    for copy in sides:
        copy.start()
    sent = []
    for s in range(steps):
        for copy in brought[3 * s : 3 * s + 3]:
            copy.wait()
        tile = pl.ds(s * rows * LANE, rows * LANE)
        pltpu.make_async_copy(stage.at[tile], stage.at[tile], slot_sems.at[s]).wait()
        flat[...] = stage[tile, :].astype(F32)
        keep = used[span(s), :] > 0.0
        for c in range(LANE):
            columns = slice(c * LANE, (c + 1) * LANE)
            gradient = jnp.where(keep, flat[pl.ds(c, rows, stride=LANE), :], 0.0)
            after, after_one, after_two = adam_step(
                v_weight[span(s), columns], v_one[span(s), columns], v_two[span(s), columns],
                gradient, RATE_MATRIX, DECAY_MATRIX,
            )
            v_weight[span(s), columns] = after
            v_one[span(s), columns] = after_one
            v_two[span(s), columns] = after_two
            v_low[s, :, columns] = after.astype(BF16)
        for i, (source, target) in enumerate(
            (
                (v_weight.at[span(s)], new.at[span(s)]),
                (v_one.at[span(s)], new_one.at[span(s)]),
                (v_two.at[span(s)], new_two.at[span(s)]),
            )
        ):
            sent.append(pltpu.make_async_copy(source, target, out_sems.at[3 * s + i]))
            sent[-1].start()
    for s in range(steps):
        low[span(s), :] = v_low[s]
    vec_copy.wait()
    count = vec_weight.shape[0]
    after, after_one, after_two = adam_step(
        vec_weight[...], vec_one[...], vec_two[...],
        vec_stage[...].astype(F32)[:count], RATE_VECTOR, 0.0,
    )
    new_vec[...] = after
    new_vec_one[...] = after_one
    new_vec_two[...] = after_two
    for copy in sides:
        copy.wait()
    grad = v_near[...] + v_far[...].astype(F32)
    hat, rate = normed(v_tokens[...].astype(F32))
    v_resid[...] += norm_back(grad, hat, rate, vec_part(vec, 0))
    for i in range(HV // LANE):
        columns = slice(i * LANE, (i + 1) * LANE)
        v_firsts[:, columns] += v_firsts_far[i].astype(F32)
    for i, (source, target) in enumerate(((v_resid, tokens_grad), (v_firsts, first_grad))):
        sent.append(pltpu.make_async_copy(source, target, side_sems.at[i]))
        sent[-1].start()
    for copy in sent:
        copy.wait()


def finish(places, grads, used, weight, one, two, resid, near, far, tokens, vec, firsts, firsts_far, vectors):
    capacity, tile_len = weight.shape
    rows = 8 if capacity % 8 == 0 else capacity
    steps = capacity // rows
    flat_vec = vectors[0].shape
    any_space = pl.BlockSpec(memory_space=pl.ANY)
    sides = [resid, near, far, tokens, firsts, firsts_far]
    return pl.pallas_call(
        finish_kernel,
        out_shape=[jax.ShapeDtypeStruct(weight.shape, F32)] * 3
        + [jax.ShapeDtypeStruct(weight.shape, BF16)]
        + [jax.ShapeDtypeStruct(resid.shape, F32), jax.ShapeDtypeStruct(firsts.shape, F32)]
        + [jax.ShapeDtypeStruct(flat_vec, F32)] * 3,
        grid_spec=pltpu.PrefetchScalarGridSpec(
            num_scalar_prefetch=1,
            grid=(1,),
            in_specs=[any_space, whole((capacity, LANE))]
            + [any_space] * 7
            + [whole((1, VEC))]
            + [any_space] * 2
            + [whole(flat_vec)] * 3,
            out_specs=[any_space] * 3 + [whole(weight.shape)] + [any_space] * 2 + [whole(flat_vec)] * 3,
            scratch_shapes=[
                pltpu.VMEM((capacity * LANE, LANE), BF16),
                pltpu.VMEM((rows * LANE, LANE), F32),
                pltpu.VMEM((80, LANE), BF16),
                pltpu.VMEM(weight.shape, F32),
                pltpu.VMEM(weight.shape, F32),
                pltpu.VMEM(weight.shape, F32),
                pltpu.VMEM((steps, rows, tile_len), BF16),
            ]
            + [pltpu.VMEM(side.shape, side.dtype) for side in sides]
            + [
                pltpu.SemaphoreType.DMA((steps,)),
                pltpu.SemaphoreType.DMA((3 * steps,)),
                pltpu.SemaphoreType.DMA((3 * steps,)),
                pltpu.SemaphoreType.DMA((len(sides),)),
                pltpu.SemaphoreType.DMA,
            ],
        ),
        compiler_params=params(60),
        cost_estimate=cost(20 * capacity * tile_len, 28 * capacity * tile_len, 2 * capacity * tile_len),
        name="finish",
    )(places, grads, used, weight, one, two, resid, near, far, tokens, vec, firsts, firsts_far, *vectors)


class Links:
    def __init__(self, line, send_sems, recv_sems):
        dp = lax.axis_index("dp")
        self.line = line
        self.y = lax.axis_index("seq")
        self.z = dp // 4
        self.x = (dp // 2) % 2
        self.c = dp % 2
        self.send_sems, self.recv_sems = send_sems, recv_sems
        self.to = {
            "core": {"dp": self.z * 4 + self.x * 2 + (1 - self.c)},
            "x": {"dp": self.z * 4 + (1 - self.x) * 2 + self.c},
            "y": {"seq": 1 - self.y},
            "up": {"dp": dp + 4},
            "down": {"dp": dp - 4},
        }
        self.sent = []

    def greet(self, whole_line):
        barrier = pltpu.get_barrier_semaphore()
        for name in ("core", "x", "y"):
            pl.semaphore_signal(barrier, inc=1, device_id=self.to[name])
        if whole_line:
            for d in range(1, self.line):
                z = (self.z + d) % self.line
                pl.semaphore_signal(barrier, inc=1, device_id={"dp": z * 4 + self.x * 2 + self.c})
            pl.semaphore_wait(barrier, 2 + self.line)
            return

        @pl.when(self.z > 0)
        def _():
            pl.semaphore_signal(barrier, inc=1, device_id=self.to["down"])

        @pl.when(self.z < self.line - 1)
        def _():
            pl.semaphore_signal(barrier, inc=1, device_id=self.to["up"])

        pl.semaphore_wait(
            barrier,
            3 + jnp.where(self.z > 0, 1, 0) + jnp.where(self.z < self.line - 1, 1, 0),
        )

    def copy(self, source, target, index, way):
        sender, receiver = index if isinstance(index, tuple) else (index, index)
        to = self.to[way] if isinstance(way, str) else {"dp": way * 4 + self.x * 2 + self.c}
        return pltpu.make_async_remote_copy(
            src_ref=source,
            dst_ref=target,
            send_sem=self.send_sems.at[sender],
            recv_sem=self.recv_sems.at[receiver],
            device_id=to,
        )

    def send(self, describe):
        source, target, index, way, when = describe()
        if when is None:
            self.copy(source, target, index, way).start()
        else:

            @pl.when(when)
            def _():
                self.copy(source, target, index, way).start()

        self.sent.append(describe)

    def arrive(self, target, index, way):
        self.copy(target, target, index, way).wait_recv()

    def finish(self):
        for describe in self.sent:
            source, target, index, way, when = describe()
            if when is None:
                self.copy(source, target, index, way).wait_send()
            else:

                @pl.when(when)
                def _(source=source, target=target, index=index, way=way):
                    self.copy(source, target, index, way).wait_send()


def add_into(place, *others):
    total = place[...].astype(F32)
    for other in others:
        total = total + other[...].astype(F32)
    place[...] = total.astype(BF16)


class Scatter:
    KINDS = ("core", "xa", "yb", "ya", "xb", "to", "from")

    def __init__(self, links, base, source, offset, rows, cut, buffers, load_sems):
        self.k, self.base, self.source, self.offset, self.rows = links, base, source, offset, rows
        self.held, self.r_core, self.r_xa, self.r_yb, self.r_ya, self.r_xb, self.r_line = buffers
        self.load_sems = load_sems
        self.halves = (pl.ds(0, cut), pl.ds(cut, rows - cut))

    @staticmethod
    def buffers_of(rows, cut, line):
        return [
            pltpu.VMEM((line, 2, 2, rows, LANE), BF16),
            pltpu.VMEM((line, 4 * rows, LANE), BF16),
            pltpu.VMEM((line, 2, cut, LANE), BF16),
            pltpu.VMEM((line, 2, rows - cut, LANE), BF16),
            pltpu.VMEM((line, cut, LANE), BF16),
            pltpu.VMEM((line, rows - cut, LANE), BF16),
            pltpu.VMEM((line, rows, LANE), BF16),
        ]

    def at(self, kind, z):
        return self.base + self.KINDS.index(kind) * self.k.line + z

    def load(self, z):
        start = self.offset + (self.k.c * self.k.line + z) * 4 * self.rows
        return [
            pltpu.make_async_copy(
                self.source.at[pl.ds(pl.multiple_of(start + i * self.rows, 16), self.rows)],
                self.held.at[z, i // 2, i % 2],
                self.load_sems.at[4 * z + i],
            )
            for i in range(4)
        ]

    def begin(self):
        k = self.k

        def describe(z):
            start = self.offset + ((1 - k.c) * k.line + z) * 4 * self.rows
            source = self.source.at[pl.ds(pl.multiple_of(start, 16), 4 * self.rows)]
            return source, self.r_core.at[z], self.at("core", z), "core", None

        for z in range(k.line):
            k.send(functools.partial(describe, z))
            for copy in self.load(z):
                copy.start()

    def first(self, z):
        k, (a, b) = self.k, self.halves
        for copy in self.load(z):
            copy.wait()
        k.arrive(self.r_core.at[z], self.at("core", z), "core")
        for i in range(4):
            add_into(self.held.at[z, i // 2, i % 2], self.r_core.at[z, pl.ds(i * self.rows, self.rows)])
        k.send(lambda: (self.held.at[z, 1 - k.x, :, a], self.r_xa.at[z], self.at("xa", z), "x", None))
        k.send(lambda: (self.held.at[z, :, 1 - k.y, b], self.r_yb.at[z], self.at("yb", z), "y", None))

    def second(self, z):
        k, (a, b) = self.k, self.halves
        k.arrive(self.r_xa.at[z], self.at("xa", z), "x")
        for y in range(2):
            add_into(self.held.at[z, k.x, y, a], self.r_xa.at[z, y])
        k.send(lambda: (self.held.at[z, k.x, 1 - k.y, a], self.r_ya.at[z], self.at("ya", z), "y", None))
        k.arrive(self.r_yb.at[z], self.at("yb", z), "y")
        for x in range(2):
            add_into(self.held.at[z, x, k.y, b], self.r_yb.at[z, x])
        k.send(lambda: (self.held.at[z, 1 - k.x, k.y, b], self.r_xb.at[z], self.at("xb", z), "x", None))

    def third(self, z):
        k, (a, b) = self.k, self.halves
        k.arrive(self.r_ya.at[z], self.at("ya", z), "y")
        add_into(self.held.at[z, k.x, k.y, a], self.r_ya.at[z])
        k.arrive(self.r_xb.at[z], self.at("xb", z), "x")
        add_into(self.held.at[z, k.x, k.y, b], self.r_xb.at[z])

        def describe():
            index = (self.at("to", z), self.at("from", k.z))
            return self.held.at[z, k.x, k.y], self.r_line.at[k.z], index, z, k.z != z

        k.send(describe)

    def last(self):
        k = self.k
        others = [(k.z + d) % k.line for d in range(1, k.line)]
        for z in others:
            k.arrive(self.r_line.at[z], (self.at("to", z), self.at("from", z)), z)
        add_into(self.held.at[k.z, k.x, k.y], *[self.r_line.at[z] for z in others])


class Spread:
    KINDS = ("xa", "yb", "ya", "xb", "ya2", "xb2") + tuple(
        f"{way}{i}" for way in ("to", "from", "c") for i in range(4)
    )

    def __init__(self, links, base, piece, out, index, first, rows, cut):
        self.k, self.base, self.piece, self.out, self.index = links, base, piece, out, index
        self.parts = {None: (first, rows), 0: (first, cut), 1: (first + cut, rows - cut)}

    def own(self, half):
        first, count = self.parts[half]
        return self.piece(pl.ds(first, count))

    def at(self, kind, z):
        return self.base + self.KINDS.index(kind) * self.k.line + z

    def spot(self, z, other_x, other_y, half=None, core=None):
        k = self.k
        c = k.c if core is None else core
        x = 1 - k.x if other_x else k.x
        y = 1 - k.y if other_y else k.y
        first, count = self.parts[half]
        return self.out.at[pl.ds(pl.multiple_of(self.index(c, z, x, y) + first, 16), count)]

    def place(self, d):
        return (self.k.z + d) % self.k.line

    def give(self, kind, way, d, other_x=False, other_y=False, half=None, own=False):
        def describe():
            z = self.place(d)
            target = self.spot(z, other_x, other_y, half)
            source = self.own(half) if own else target
            return source, target, self.at(kind, z), way, None

        self.k.send(describe)

    def get(self, kind, way, d, other_x=False, other_y=False, half=None):
        z = self.place(d)
        self.k.arrive(self.spot(z, other_x, other_y, half), self.at(kind, z), way)

    def lift(self, i, own=False):
        k = self.k
        place = dict(other_x=i >= 2, other_y=i % 2 == 1)

        def describe(d):
            z = self.place(d)
            target = self.spot(k.z, **place)
            source = self.own(None) if own else target
            return source, target, (self.at(f"to{i}", z), self.at(f"from{i}", k.z)), z, None

        for d in (k.line - 1, 1, 2):
            k.send(functools.partial(describe, d))

    def land(self, d, i):
        z = self.place(d)
        place = dict(other_x=i >= 2, other_y=i % 2 == 1)
        self.k.arrive(self.spot(z, **place), (self.at(f"to{i}", z), self.at(f"from{i}", z)), z)

    def cross(self, d):
        own = d == 0
        self.give("xa", "x", d, half=0, own=own)
        self.give("yb", "y", d, half=1, own=own)
        self.give("ya", "y", d, half=0, own=own)
        self.give("xb", "x", d, half=1, own=own)
        self.give("c0", "core", d, own=own)

    def start(self):
        self.lift(0, True)
        self.cross(0)

    def along(self, d):
        self.land(d, 0)
        self.cross(d)

    def turn(self, d):
        self.get("xa", "x", d, other_x=True, half=0)
        self.give("ya2", "y", d, other_x=True, half=0)
        self.get("yb", "y", d, other_y=True, half=1)
        self.give("xb2", "x", d, other_y=True, half=1)

    def share(self, d, late=False):
        self.get("ya", "y", d, other_y=True, half=0)
        self.give("c1", "core", d, other_y=True)
        if late:
            self.lift(1)
        self.get("xb", "x", d, other_x=True, half=1)
        self.give("c2", "core", d, other_x=True)
        if late:
            self.lift(2)
        self.get("ya2", "y", d, other_x=True, other_y=True, half=0)
        self.get("xb2", "x", d, other_x=True, other_y=True, half=1)
        self.give("c3", "core", d, other_x=True, other_y=True)
        if late:
            self.lift(3)

    def along_late(self, d):
        for i in range(4):
            self.land(d, i)
            self.give(f"c{i}", "core", d, other_x=i >= 2, other_y=i % 2 == 1)

    def end(self):
        k = self.k
        for z in range(k.line):
            for i in range(4):
                k.arrive(self.spot(z, i >= 2, i % 2 == 1, core=1 - k.c), self.at(f"c{i}", z), "core")


RS_SEMS = len(Scatter.KINDS)
AR_SEMS = RS_SEMS + 2 * len(Spread.KINDS)


class Total:
    def __init__(self, links, base, source, offset, kind, out, top, buffers, load_sems, copy_sem):
        line = links.line
        size, cut, turn, plain = kind
        rows = size // (8 * line)
        held = buffers[0]

        def index(c, z, x, y):
            return top + (((c * line + z) * 2 + x) * 2 + y) * rows

        def piece(span):
            return held.at[links.z, links.x, links.y, span]

        self.k, self.piece, self.out, self.index, self.rows = links, piece, out, index, rows
        self.scatter = Scatter(links, base, source, offset, rows, cut, buffers, load_sems)
        base = base + RS_SEMS * line
        self.spread = Spread(links, base, piece, out, index, 0, plain, turn)
        self.late = None
        if plain < rows:
            base = base + len(Spread.KINDS) * line
            rest = rows - plain
            self.late = Spread(links, base, piece, out, index, plain, rest, rest // 32 * 16)
        self.copy_sem = copy_sem

    def keep(self):
        k = self.k
        start = pl.multiple_of(self.index(k.c, k.z, k.x, k.y), 16)
        return pltpu.make_async_copy(
            self.piece(pl.ds(0, self.rows)), self.out.at[pl.ds(start, self.rows)], self.copy_sem
        )

    def run(self, stage, part):
        scatter, spread, late = self.scatter, self.spread, self.late
        if stage == 0:
            scatter.begin()
        elif stage < 4:
            (scatter.first, scatter.second, scatter.third)[stage - 1](part)
        elif stage == 4:
            scatter.last()
            self.keep().start()
            spread.start()
            if late is not None:
                late.start()
        elif stage == 5 and part < 3:
            spread.along(part + 1)
        elif stage == 5 and part == 3:
            late.turn(0)
        elif stage == 5 and part == 4:
            late.share(0, True)
        elif stage == 5:
            late.along_late(part - 4)
        elif stage < 8:
            (spread.turn, spread.share)[stage - 6](part)
        else:
            self.keep().wait()
            spread.end()
            if late is not None:
                late.end()


class Gather:
    KINDS = ("up", "down", "xa", "yb", "ya", "xb", "ya2", "xb2", "x2") + tuple(
        f"{way}{i}" for way in ("u", "d", "c") for i in range(4)
    )

    def __init__(self, links, base, own, out, index, first, rows, cut, z_first, twice):
        self.k, self.base, self.own, self.out, self.index = links, base, own, out, index
        self.parts = {None: (first, rows), 0: (first, cut), 1: (first + cut, rows - cut)}
        self.z_first, self.twice = z_first, twice

    def at(self, kind, z):
        return self.base + self.KINDS.index(kind) * self.k.line + z

    def spot(self, z, other_x, other_y, half=None, core=None):
        k = self.k
        c = k.c if core is None else core
        x = 1 - k.x if other_x else k.x
        y = 1 - k.y if other_y else k.y
        first, count = self.parts[half]
        return self.out.at[pl.ds(pl.multiple_of(self.index(c, z, x, y) + first, 16), count)]

    def give(self, kind, way, z, other_x=False, other_y=False, half=None, when=None, own=False):
        def describe():
            place = self.spot(z(), other_x, other_y, half)
            source = self.own(other_y, half) if own else place
            return source, place, self.at(kind, z()), way, None if when is None else when()

        self.k.send(describe)

    def get(self, kind, way, z, other_x=False, other_y=False, half=None):
        self.k.arrive(self.spot(z, other_x, other_y, half), self.at(kind, z), way)

    def near(self):
        k = self.k
        found = []
        for r in range(1, k.line):
            found.append(
                (
                    lambda r=r: k.z - r,
                    lambda r=r: k.z >= r,
                    "u",
                    "up",
                    lambda r=r: (k.z >= r) & (k.z < k.line - 1),
                )
            )
            found.append(
                (
                    lambda r=r: k.z + r,
                    lambda r=r: k.z + r < k.line,
                    "d",
                    "down",
                    lambda r=r: (k.z + r < k.line) & (k.z > 0),
                )
            )
        return found

    def here(self):
        return self.k.z

    def lower(self):
        return self.k.z < self.k.line - 1

    def upper(self):
        return self.k.z > 0

    def cross(self, z, when, own):
        self.give("xa", "x", z, half=0, when=when, own=own)
        self.give("yb", "y", z, half=1, when=when, own=own)
        self.give("ya", "y", z, half=0, when=when, own=own)
        self.give("xb", "x", z, half=1, when=when, own=own)
        self.give("c0", "core", z, when=when, own=own)

    def start(self):
        self.give("up", "up", self.here, when=self.lower, own=True)
        self.give("down", "down", self.here, when=self.upper, own=True)
        if self.twice:
            for other, kind in ((False, "xa"), (True, "x2")):
                self.give(kind, "x", self.here, other_y=other, own=True)
                self.give("c1" if other else "c0", "core", self.here, other_y=other, own=True)
        else:
            self.cross(self.here, None, True)

    def along(self, number):
        z, exists, _, way, goes_on = self.near()[number]

        @pl.when(exists())
        def _():
            self.get(way, way, z())

        self.give(way, way, z, when=goes_on)
        self.cross(z, exists, False)

    def turn(self, z, when):
        def waits():
            self.get("xa", "x", z(), other_x=True, half=0)

        def waits_too():
            self.get("yb", "y", z(), other_y=True, half=1)

        waits() if when is None else pl.when(when())(waits)
        self.give("ya2", "y", z, other_x=True, half=0, when=when)
        waits_too() if when is None else pl.when(when())(waits_too)
        self.give("xb2", "x", z, other_y=True, half=1, when=when)

    def share(self, z, when):
        def waits(kind, way, **place):
            def wait():
                self.get(kind, way, z(), **place)

            wait() if when is None else pl.when(when())(wait)

        waits("ya", "y", other_y=True, half=0)
        self.give("c1", "core", z, other_y=True, when=when)
        waits("xb", "x", other_x=True, half=1)
        self.give("c2", "core", z, other_x=True, when=when)
        waits("ya2", "y", other_x=True, other_y=True, half=0)
        waits("xb2", "x", other_x=True, other_y=True, half=1)
        self.give("c3", "core", z, other_x=True, other_y=True, when=when)

    def share_twice(self):
        for other, kind in ((False, "xa"), (True, "x2")):
            self.get(kind, "x", self.k.z, other_x=True, other_y=other)
            self.give("c3" if other else "c2", "core", self.here, other_x=True, other_y=other)

    def lift(self, i, own=False):
        place = dict(other_x=i >= 2, other_y=i % 2 == 1)
        self.give(f"u{i}", "up", self.here, when=self.lower, own=own, **place)
        self.give(f"d{i}", "down", self.here, when=self.upper, own=own, **place)
        self.give(f"c{i}", "core", self.here, own=own, **place)

    def start_plane(self):
        if self.twice:
            for other, kind in ((False, "xa"), (True, "x2")):
                self.give(kind, "x", self.here, other_y=other, own=True)
            self.lift(0, True)
            self.lift(1, True)
        else:
            self.give("xa", "x", self.here, half=0, own=True)
            self.give("yb", "y", self.here, half=1, own=True)
            self.give("ya", "y", self.here, half=0, own=True)
            self.give("xb", "x", self.here, half=1, own=True)
            self.lift(0, True)

    def turn_plane(self):
        if self.twice:
            for other, kind in ((False, "xa"), (True, "x2")):
                self.get(kind, "x", self.k.z, other_x=True, other_y=other)
                self.lift(3 if other else 2)
        else:
            self.turn(self.here, None)

    def lift_plane(self):
        if not self.twice:
            z = self.k.z
            self.get("ya", "y", z, other_y=True, half=0)
            self.lift(1)
            self.get("xb", "x", z, other_x=True, half=1)
            self.lift(2)
            self.get("ya2", "y", z, other_x=True, other_y=True, half=0)
            self.get("xb2", "x", z, other_x=True, other_y=True, half=1)
            self.lift(3)

    def along_plane(self, number, i):
        z, exists, letter, way, goes_on = self.near()[number]
        place = dict(other_x=i >= 2, other_y=i % 2 == 1)

        @pl.when(exists())
        def _():
            self.get(f"{letter}{i}", way, z(), **place)

        self.give(f"{letter}{i}", way, z, when=goes_on, **place)
        self.give(f"c{i}", "core", z, when=exists, **place)

    def steps(self):
        count = 2 * (self.k.line - 1)
        if self.z_first:
            one = [self.start]
            two = [lambda n=n: self.along(n) for n in range(count)]
            spots = [(z, exists) for z, exists, _, _, _ in self.near()]
            if not self.twice:
                spots = [(self.here, None)] + spots
            three = [lambda z=z, e=e: self.turn(z, e) for z, e in spots]
            four = [lambda z=z, e=e: self.share(z, e) for z, e in spots]
            if self.twice:
                four = [self.share_twice] + four
            return [one, two, three, four]
        one = [self.start_plane]
        two = [self.turn_plane]
        three = [self.lift_plane]
        four = [lambda n=n, i=i: self.along_plane(n, i) for n in range(count) for i in range(4)]
        return [one, two, three, four]

    def end(self):
        k = self.k
        for z in range(k.line):
            for i in range(4):
                k.arrive(
                    self.spot(z, i >= 2, i % 2 == 1, core=1 - k.c), self.at(f"c{i}", z), "core"
                )


AG_SEMS = len(Gather.KINDS)


def all_gather_kernel(line, swaps, cuts, piece, *refs):
    near, out, far = refs[:swaps], refs[swaps], refs[swaps + 1 : 2 * swaps + 1]
    send_sems, recv_sems, copy_sem = refs[2 * swaps + 1 :]
    links = Links(line, send_sems, recv_sems)
    links.greet(False)
    rows = piece.shape[0] // 2
    first_rows, second_rows = cuts
    spare = 2 * AG_SEMS * line

    def index(c, z, x, y):
        return (((z * 2 + x) * 2 + c) * 2 + y) * rows

    def keep():
        start = index(links.c, links.z, links.x, 0)
        return pltpu.make_async_copy(
            piece, out.at[pl.ds(pl.multiple_of(start, 16), 2 * rows)], copy_sem
        )

    gathers = []

    def own_of(first, count, cut):
        def own(other, half):
            begin, size = {None: (0, count), 0: (0, cut), 1: (cut, count - cut)}[half]
            y = 1 - links.y if other else links.y
            return piece.at[pl.ds(pl.multiple_of(y * rows + first + begin, 16), size)]

        return own

    last = rows - first_rows - second_rows
    spans = ((0, first_rows + second_rows, first_rows, True), (first_rows + second_rows, last, last // 32 * 16, False))
    for number, (first, count, cut, z_first) in enumerate(spans):
        gathers.append(
            Gather(
                links, number * AG_SEMS * line, own_of(first, count, cut), out, index,
                first, count, cut, z_first, True,
            )
        )
    flat, tall = gathers[0].steps(), gathers[1].steps()
    for step in flat[0] + tall[0]:
        step()
    keep().start()
    for i in range(swaps):
        links.send(lambda i=i: (near[i], far[i], spare + i, "y", None))
    along, rise = flat[1], tall[1] + tall[2]
    turn, share, climb = flat[2], flat[3], tall[3]
    for step in along[:2] + rise + turn[:2] + along[2:4] + climb[:8] + turn[2:4] + along[4:]:
        step()
    for step in climb[8:16] + turn[4:] + share[:3] + climb[16:] + share[3:]:
        step()
    for gather in gathers:
        gather.end()
    keep().wait()
    for i in range(swaps):
        links.arrive(far[i], spare + i, "y")
    links.finish()


def all_gather(piece, swaps, line, collective_id):
    any_space = pl.BlockSpec(memory_space=pl.ANY)
    sems = 2 * AG_SEMS * line + len(swaps)
    rows = piece.shape[0] // 2
    cuts = (rows * 2 // 5 // 16 * 16, rows * 7 // 20 // 16 * 16)
    return pl.pallas_call(
        functools.partial(all_gather_kernel, line, len(swaps), cuts),
        out_shape=[jax.ShapeDtypeStruct((4 * line * piece.shape[0], LANE), BF16)]
        + [jax.ShapeDtypeStruct(s.shape, s.dtype) for s in swaps],
        in_specs=[any_space] * (1 + len(swaps)),
        out_specs=[any_space] * (1 + len(swaps)),
        scratch_shapes=[
            pltpu.SemaphoreType.DMA((sems,)),
            pltpu.SemaphoreType.DMA((sems,)),
            pltpu.SemaphoreType.DMA,
        ],
        compiler_params=params(32, collective_id=collective_id, has_side_effects=True),
        cost_estimate=cost(0, 100 * MIB),
        name="all_gather",
    )(piece, *swaps)


PAIRS = D // LANE
UP_ROWS = FF * D // LANE
REST_ROWS = 128 * LANE
HEAD, NORM, LAST = 900, 901, 902
ORDER = (
    100, 0, HEAD, HEAD, 110, 111, 112, 113, 10, 11, 120, HEAD, HEAD, 121, HEAD, HEAD, 122, HEAD,
    HEAD, 123, 12, 13, HEAD, HEAD, HEAD, HEAD, NORM, 130, 20, 21, 131, 132, 133, LAST, 200, 22,
    23, 210, 211, 212, 213, 140, 150, 30, 31, 32, 33, 220, 221, 222, 40, 223, 160, 161, 153, 50,
    51, 52, 230, 231, 232, 233, 53, 170, 171, 154, 151, 152, 60, 61, 240, 155, 54, 62, 63, 250,
    156, 157, 162, 163, 70, 253, 251, 252, 260, 71, 72, 73, 172, 173, 180, 55, 254, 56, 261,
    262, 57, 80, 270, 271, 263, 272, 273, 255, 256, 257, 280,
)


def segments():
    found = [[]]
    for step in ORDER:
        if step >= HEAD:
            found.append([])
        else:
            found[-1].append((step // 100, step // 10 % 10, step % 10))
    return found


def total_kinds(line):
    kinds = []
    for size, late in ((UP_ROWS, 20), (UP_ROWS, 20), (REST_ROWS, 30)):
        rows = size // (8 * line)
        plain = rows - rows * late // 100 // 32 * 32
        kinds.append((size, rows * 68 // 100 // 16 * 16, plain * 33 // 100 // 16 * 16, plain))
    return kinds


def back_kernel(
    line,
    q, k, v, att, grad_att, chance, tokens, tokens_far, n1, att_all, resid_low, w_qkv, vec, vec_one, d_up, d_down,
    d_first, grad_near, out, grad_back, first_back,
    d_q, d_k, d_v, far, d_rest, vec_grad, flat, *scratch,
):
    step = pl.program_id(0)
    buffers, (send_sems, recv_sems, load_sems, copy_sems) = scratch[:-4], scratch[-4:]
    links = Links(line, send_sems, recv_sems)
    tops = (REST_ROWS + UP_ROWS, REST_ROWS, 0)
    totals = [
        Total(
            links, g * AR_SEMS * line, source, 0, kind, out, top,
            buffers[7 * g : 7 * g + 7], load_sems.at[g], copy_sems.at[g],
        )
        for g, (source, kind, top) in enumerate(zip((d_down, d_up, d_rest), total_kinds(line), tops))
    ]
    spare = len(totals) * AR_SEMS * line
    plan = segments()

    def run(number):
        for g, stage, part in plan[number]:
            totals[g].run(stage, part)

    queries = q.shape[0]
    for head in range(2):
        for s in range(PAIRS):

            @pl.when(step == s)
            def _(s=s, head=head):
                if s == 0 and head == 0:
                    links.greet(True)
                run(2 * s + head)

        @pl.when(step < PAIRS)
        def _(head=head):
            cols = slice(head * HD, (head + 1) * HD)
            grad = grad_att[:, cols]
            weights = chance[head]
            shared = grad.astype(F32) * att[:, cols].astype(F32)
            delta = jnp.sum(shared.T, axis=0, keepdims=True)
            grad_chance = mm(v[:, cols], grad, NT)
            grad_scores = (weights.astype(F32) * (grad_chance - delta)).astype(BF16)
            grad_value = mm(weights, grad)

            d_v[step, :, cols] = grad_value.astype(BF16)
            d_first[:, cols] = grad_value[:queries]
            d_k[step, :, cols] = mm(grad_scores, q[:, cols]).astype(BF16)
            d_q[step, :, cols] = (mm(k[:, cols], grad_scores, TN).T * HD ** (-0.5)).astype(BF16)

    @pl.when(step == PAIRS)
    def _():
        rows = n1.shape[0] // 2
        per_row = D // LANE
        run(2 * PAIRS)
        rows = n1.shape[0] // 2
        first_far = d_v.at[pl.ds(PAIRS // 2, PAIRS // 2), pl.ds(rows, rows)]
        links.send(lambda: (first_far, first_back, spare, "y", None))
        dq = jnp.concatenate([d_q[i] for i in range(PAIRS)], axis=1)
        dk = jnp.concatenate([d_k[i] for i in range(PAIRS)], axis=1)
        dv = jnp.concatenate([d_v[i] for i in range(PAIRS // 2)], axis=1)
        grads = mm(dk, w_qkv[:, D : 2 * D], NT) + mm(dv, w_qkv[:, 2 * D :], NT)
        beside = grads[rows:]
        far[...] = beside.astype(BF16)
        links.send(lambda: (far, grad_back, spare + 1, "y", None))
        near = grads[:rows] + mm(dq, w_qkv[:, :D], NT)
        grad_near[...] = near
        hat, _ = normed(tokens[...].astype(F32))
        hat_far, _ = normed(tokens_far[...].astype(F32))
        vec_grad[...] = vec_one[...]
        vec_grad[:, :D] = jnp.sum(near * hat, axis=0, keepdims=True) + jnp.sum(
            beside * hat_far, axis=0, keepdims=True
        )
        vec_grad[:, D : 2 * D] = jnp.sum(near, axis=0, keepdims=True) + jnp.sum(
            beside, axis=0, keepdims=True
        )
        vec_grad[:, 4 * D : 5 * D] = jnp.sum(dq.astype(F32), axis=0, keepdims=True)
        vec_grad[:, 7 * D : 7 * D + HV] = jnp.sum(dv.astype(F32), axis=0, keepdims=True)
        run(2 * PAIRS + 1)
        pieces = (
            (n1[:rows], dq, 0, per_row),
            (n1[...], dk, D * per_row, per_row),
            (n1[...], dv, 2 * D * per_row, HV // LANE),
            (att_all[...], resid_low[...], 2 * D * per_row + D * HV // LANE, per_row),
        )
        for left, right, start, columns in pieces:
            product = mm(left, right, TN)
            size = D * columns
            for j in range(columns):
                flat[pl.ds(j, D, stride=columns), :] = product[:, j * LANE : (j + 1) * LANE]
            d_rest[start : start + size] = flat[:size].astype(BF16)
        flat[: 2 * LANE] = jnp.zeros((2 * LANE, LANE), F32)
        for j in range(VEC // LANE):
            flat[j : j + 1] = vec_grad[:, j * LANE : (j + 1) * LANE]
        d_rest[REST:] = flat[: 2 * LANE].astype(BF16)
        run(2 * PAIRS + 2)
        links.arrive(first_back, spare, "y")
        links.arrive(grad_back, spare + 1, "y")
        links.finish()


def back(q, k, v, att, grad_att, chance, tokens, tokens_far, n1, resid_low, w_qkv, vec, vec_one, d_up, d_down, line):
    rows, keys = q.shape[0], k.shape[0]
    any_space = pl.BlockSpec(memory_space=pl.ANY)

    def column(count):
        return pl.BlockSpec((count, LANE), lambda i: (0, jnp.minimum(i, PAIRS - 1)))

    def once(array):
        return pl.BlockSpec(array.shape, lambda i: (0,) * array.ndim, pipeline_mode=pl.Buffered(1))

    kinds = total_kinds(line)
    scratch = []
    for size, cut, _, _ in kinds:
        scratch += Scatter.buffers_of(size // (8 * line), cut, line)
    sems = len(kinds) * AR_SEMS * line + 2
    return pl.pallas_call(
        functools.partial(back_kernel, line),
        out_shape=[
            jax.ShapeDtypeStruct((rows, HV), F32),
            jax.ShapeDtypeStruct((rows, D), F32),
            jax.ShapeDtypeStruct((REST_ROWS + 2 * UP_ROWS, LANE), BF16),
            jax.ShapeDtypeStruct((rows, D), BF16),
            jax.ShapeDtypeStruct((PAIRS // 2, rows, LANE), BF16),
        ],
        grid=(PAIRS + 1,),
        in_specs=[
            column(rows),
            column(keys),
            column(keys),
            column(rows),
            column(rows),
            pl.BlockSpec((2, keys, rows), lambda i: (jnp.minimum(i, PAIRS - 1), 0, 0)),
            once(tokens),
            once(tokens_far),
            once(n1),
            once(att),
            once(resid_low),
            once(w_qkv),
            once(vec),
            once(vec_one),
            any_space,
            any_space,
        ],
        out_specs=[
            pl.BlockSpec((rows, LANE), lambda i: (0, jnp.clip(i - 3, 0, 2))),
            pl.BlockSpec((rows, D), lambda i: (0, 0), pipeline_mode=pl.Buffered(1)),
            any_space,
            any_space,
            any_space,
        ],
        scratch_shapes=[
            pltpu.VMEM((PAIRS, rows, LANE), BF16),
            pltpu.VMEM((PAIRS, keys, LANE), BF16),
            pltpu.VMEM((PAIRS, keys, LANE), BF16),
            pltpu.VMEM((rows, D), BF16),
            pltpu.VMEM((REST_ROWS, LANE), BF16),
            pltpu.VMEM((1, VEC), F32),
            pltpu.VMEM((D * D // LANE, LANE), F32),
        ]
        + scratch
        + [
            pltpu.SemaphoreType.DMA((sems,)),
            pltpu.SemaphoreType.DMA((sems,)),
            pltpu.SemaphoreType.DMA((len(kinds), 4 * line)),
            pltpu.SemaphoreType.DMA((len(kinds),)),
        ],
        compiler_params=params(62, collective_id=0, has_side_effects=True),
        cost_estimate=cost(8 * rows * keys * D + 14 * rows * D * D, 100 * MIB),
        name="back",
    )(q, k, v, att, grad_att, chance, tokens, tokens_far, n1, att, resid_low, w_qkv, vec, vec_one, d_up, d_down)


def swap(value):
    return lax.ppermute(value, "seq", [(0, 1), (1, 0)])


def shards(
    tokens,
    first_values,
    out_grad,
    block_place,
    owners,
    masters,
    moment_one,
    moment_two,
    vector_master,
    vector_moment_one,
    vector_moment_two,
):
    capacity = masters.shape[0]
    dp_count = lax.axis_size("dp")
    tile_count = owners.shape[0]
    dp_here = lax.axis_index("dp")
    seq_here = lax.axis_index("seq")
    _, half_len, _ = tokens.shape

    tokens = tokens.reshape(half_len, D)
    firsts = first_values.reshape(half_len, HV)
    given = out_grad.reshape(half_len, D)
    line = dp_count // 4
    packed = pack_slots(masters)
    if line == LINE:
        slots, tokens_far, firsts_far = all_gather(packed, [tokens, firsts], line, 1)
    else:
        tokens_far, firsts_far = swap(tokens), swap(firsts)
        slots = lax.all_gather(packed, "dp", axis=0, tiled=True)

    slot_index = slot_numbers(owners)
    slot_rows = owners * capacity + slot_index
    mine = (owners == dp_here)[None, :] & (
        slot_index[None, :] == jnp.arange(capacity, dtype=jnp.int32)[:, None]
    )
    tile_order = jnp.arange(tile_count, dtype=jnp.int32)
    tile_here = jnp.sum(jnp.where(mine, tile_order[None, :], 0), axis=1)
    tile_here = tile_here + jnp.where(tile_here >= 126, 2, 0)
    used = jnp.broadcast_to(
        jnp.any(mine, axis=1).astype(F32)[:, None], (capacity, LANE)
    )

    blocks = block_place.reshape(-1)
    per_device = blocks.shape[0] // 2
    block_len = half_len // per_device
    ordered = jnp.roll(blocks, -seq_here * per_device)
    all_pos = (
        ordered[:, None] * block_len + jnp.arange(block_len, dtype=jnp.int32)[None, :]
    ).reshape(-1)
    row_pos = all_pos[:half_len].reshape(1, half_len)
    column_pos = all_pos.reshape(2 * half_len, 1)

    vec = vector_master.reshape(1, VEC)
    w_qkv, w_out, w_up, w_down = unpack_weights(slot_rows, slots)
    n1, q, k, v = project(tokens, tokens_far, firsts, firsts_far, w_qkv, vec)
    att, chance = attend(q, k, v, row_pos, column_pos)
    result, grad_resid, resid_low, grad_att, d_up, d_down, vec_one = hidden(
        tokens, att, given, w_out, w_up, w_down, vec
    )
    if line == LINE:
        first_near, grad_near, grads, grad_back, first_back = back(
            q, k, v, att, grad_att, chance, tokens, tokens_far, n1, resid_low, w_qkv, vec, vec_one, d_up, d_down, line
        )
    else:
        d_q, d_k, d_fresh, d_first = attend_back(q, k, v, att, grad_att, chance)
        grad_near, grad_far, d_rest = project_back(
            jnp.concatenate([tokens, tokens_far], axis=0), n1, d_q, d_k, d_fresh, att, resid_low, w_qkv, vec, vec_one
        )
        first_near = d_first[:half_len]
        grad_back, first_back = swap(grad_far), swap(d_first[half_len:].astype(BF16))
        first_back = first_back.reshape(half_len, HV // LANE, LANE).transpose(1, 0, 2)
        grads = lax.psum(jnp.concatenate([d_rest, d_up, d_down], axis=0), ("seq", "dp"))
    vectors = [
        v.reshape(VEC // LANE, LANE) for v in (vector_master, vector_moment_one, vector_moment_two)
    ]
    new_master, new_one, new_two, new_low, tokens_grad, first_grad, *new_vectors = finish(
        tile_here, grads, used, masters, moment_one, moment_two,
        grad_resid, grad_near, grad_back, tokens, vec, first_near, first_back, vectors,
    )
    return (
        result.reshape(1, half_len, D),
        tokens_grad.reshape(1, half_len, D),
        first_grad.reshape(1, half_len, HV),
        new_master,
        new_one,
        new_two,
        new_low,
        *(v.reshape(VEC) for v in new_vectors),
    )


def solution(mesh):
    rows = P("dp", "seq", None)
    slots = P("dp", None)
    return jax.shard_map(
        shards,
        mesh=mesh,
        in_specs=(rows, rows, rows, slots, P(), slots, slots, slots, P(), P(), P()),
        out_specs=(rows, rows, rows, slots, slots, slots, slots, P(), P(), P()),
        check_vma=False,
    )
```

```python
import functools

import jax
import jax.numpy as jnp
from jax import lax
from jax.experimental import pallas as pl
from jax.experimental.pallas import tpu as pltpu
from jax.sharding import PartitionSpec as P

D = 768
HD = 64
FF = 3072
STEP = 10
HV = 384
LANE = 128
QKV = 2 * D + HV
FF_STEP = 768
VEC = 7 * D + HV + FF
MIB = 1024 * 1024
LINE = 4
REST = 126 * LANE

EPS_NORM = 1e-05
EPS_ADAM = 1e-08
BETA_ONE = 0.5
BETA_TWO = 0.5
RATE_MATRIX = 0.03
RATE_VECTOR = 0.25
DECAY_MATRIX = 0.1
FAR = -1e30

BF16 = jnp.bfloat16
F32 = jnp.float32

NN = (((1,), (0,)), ((), ()))
NT = (((1,), (1,)), ((), ()))
TN = (((0,), (0,)), ((), ()))


def mm(left, right, dims=NN):
    return lax.dot_general(left, right, dims, preferred_element_type=F32)


def vec_part(vec_ref, index):
    if index < 7:
        return vec_ref[:, index * D : (index + 1) * D]
    if index == 7:
        return vec_ref[:, 7 * D : 7 * D + HV]
    return vec_ref[:, 7 * D + HV :]


def params(mib, **more):
    return pltpu.CompilerParams(vmem_limit_bytes=mib * MIB, **more)


def whole(shape):
    return pl.BlockSpec(shape, lambda *_: (0,) * len(shape))


def cost(flops, bytes_accessed, transcendentals=0):
    return pl.CostEstimate(
        flops=int(flops), bytes_accessed=int(bytes_accessed), transcendentals=int(transcendentals)
    )


def adam_step(weight, first_moment, second_moment, gradient, step_rate, weight_decay):
    first_new = BETA_ONE * first_moment + (1.0 - BETA_ONE) * gradient
    second_new = BETA_TWO * second_moment + (1.0 - BETA_TWO) * gradient * gradient
    first_fix = 1.0 - BETA_ONE**STEP
    second_fix = 1.0 - BETA_TWO**STEP
    update = (first_new * (1.0 / first_fix)) / (jnp.sqrt(second_new * (1.0 / second_fix)) + EPS_ADAM)
    return (weight - step_rate * (update + weight_decay * weight), first_new, second_new)


def slot_numbers(owners):
    tile_order = jnp.arange(owners.shape[0], dtype=jnp.int32)
    earlier = (owners[None, :] == owners[:, None]) & (tile_order[None, :] < tile_order[:, None])
    return jnp.sum(earlier.astype(jnp.int32), axis=1)


def normed(values):
    center = jnp.mean(values, axis=-1, keepdims=True)
    centred = values - center
    spread = jnp.mean(centred * centred, axis=-1, keepdims=True)
    rate = lax.rsqrt(spread + EPS_NORM)
    return centred * rate, rate


def norm_back(grad, hat, rate, gain):
    g = grad * gain
    return rate * (
        g - jnp.mean(g, axis=-1, keepdims=True) - hat * jnp.mean(g * hat, axis=-1, keepdims=True)
    )


def pack_rows(src, flat):
    rows = src.shape[0]
    for c in range(LANE):
        flat[pl.ds(c, rows, stride=LANE), :] = src[:, c * LANE : (c + 1) * LANE]


def pack_kernel(src, dst, flat):
    pack_rows(src, flat)
    dst[...] = flat[...].astype(BF16)


def pack_slots(masters):
    capacity, tile_len = masters.shape
    rows = 8 if capacity % 8 == 0 else capacity
    return pl.pallas_call(
        pack_kernel,
        out_shape=jax.ShapeDtypeStruct((capacity * LANE, LANE), BF16),
        grid=(capacity // rows,),
        in_specs=[pl.BlockSpec((rows, tile_len), lambda i: (i, 0))],
        out_specs=pl.BlockSpec((rows * LANE, LANE), lambda i: (i, 0)),
        scratch_shapes=[pltpu.VMEM((rows * LANE, LANE), F32)],
        compiler_params=params(60),
        cost_estimate=cost(0, capacity * tile_len * 6),
        name="pack_slots",
    )(masters)


def weight_chunks():
    chunks = [
        (0, 36, 6, 0, 0, 0),
        (36, 36, 6, 0, D, 0),
        (72, 18, 3, 0, 2 * D, 0),
        (90, 36, 6, 1, 0, 0),
    ]
    for i in range(4):
        chunks.append((126 + 36 * i, 36, 24, 2, 0, 192 * i))
    for i in range(4):
        chunks.append((270 + 36 * i, 36, 6, 3, 0, 768 * i))
    return chunks


def unpack_kernel(slot_rows, slots, w_qkv, w_out, w_up, w_down, stage, o_qkv, o_out, o_up, o_down, flat, sems, out_sems):
    chunks = weight_chunks()
    places = (o_qkv, o_out, o_up, o_down)
    ends = (w_qkv, w_out, w_up, w_down)

    for number, (first, tiles, _, _, _, _) in enumerate(chunks):

        @pl.loop(0, tiles)
        def _(i, first=first, number=number):
            t = first + i
            pltpu.make_async_copy(
                slots.at[pl.ds(pl.multiple_of(slot_rows[t] * LANE, LANE), LANE)],
                stage.at[pl.ds(pl.multiple_of(t * LANE, LANE), LANE)],
                sems.at[number],
            ).start()

    copies = []
    for number, (first, tiles, per_row, matrix, column, row) in enumerate(chunks):
        span = pl.ds(first * LANE, tiles * LANE)
        pltpu.make_async_copy(stage.at[span], stage.at[span], sems.at[number]).wait()
        place = places[matrix]
        lines = 3 * LANE // per_row

        @pl.loop(0, tiles // 6)
        def _(g, first=first, per_row=per_row, place=place, column=column, row=row, lines=lines):
            for half in range(2):
                base = pl.multiple_of(first * LANE + (2 * g + half) * 3 * LANE, LANE)
                flat[half] = stage[pl.ds(base, 3 * LANE), :].astype(F32)
            for half in range(2):
                top = pl.multiple_of(row + (2 * g + half) * lines, 16)
                for j in range(per_row):
                    place[pl.ds(top, lines), column + j * LANE : column + (j + 1) * LANE] = flat[
                        half, pl.ds(j, lines, stride=per_row), :
                    ].astype(BF16)

        rows = tiles * LANE // per_row
        columns = pl.ds(column, per_row * LANE)
        copy = pltpu.make_async_copy(
            place.at[pl.ds(row, rows), columns],
            ends[matrix].at[pl.ds(row, rows), columns],
            out_sems.at[number],
        )
        copy.start()
        copies.append(copy)
    for copy in copies:
        copy.wait()


def unpack_weights(slot_rows, slots):
    tile_count = slot_rows.shape[0]
    shapes = [(D, QKV), (D, D), (D, FF), (FF, D)]
    any_space = pl.BlockSpec(memory_space=pl.ANY)
    return pl.pallas_call(
        unpack_kernel,
        out_shape=[jax.ShapeDtypeStruct(s, BF16) for s in shapes],
        grid_spec=pltpu.PrefetchScalarGridSpec(
            num_scalar_prefetch=1,
            grid=(1,),
            in_specs=[any_space],
            out_specs=[any_space] * 4,
            scratch_shapes=[pltpu.VMEM((tile_count * LANE, LANE), BF16)]
            + [pltpu.VMEM(s, BF16) for s in shapes]
            + [
                pltpu.VMEM((2, 3 * LANE, LANE), F32),
                pltpu.SemaphoreType.DMA((12,)),
                pltpu.SemaphoreType.DMA((12,)),
            ],
        ),
        compiler_params=params(60),
        cost_estimate=cost(0, 4 * tile_count * LANE * LANE),
        name="unpack_weights",
    )(slot_rows, slots)


def project_kernel(near, far, firsts, firsts_far, w_qkv, vec, n1, q, k, v):
    first = pl.program_id(0) == 0
    tokens = jnp.where(first, near[...], far[...])
    hat, _ = normed(tokens.astype(F32))
    low = (hat * vec_part(vec, 0) + vec_part(vec, 1)).astype(BF16)
    n1[...] = low
    k[...] = mm(low, w_qkv[:, D : 2 * D]).astype(BF16)
    v[:, :HV] = (mm(low, w_qkv[:, 2 * D :]) + vec_part(vec, 7)).astype(BF16)
    v[:, HV:] = jnp.where(first, firsts[...], firsts_far[...])

    @pl.when(first)
    def _():
        query = mm(low, w_qkv[:, :D]) + vec_part(vec, 4)
        q[...] = (query.astype(BF16).astype(F32) * HD ** (-0.5)).astype(BF16)


def project(near, far, firsts, firsts_far, w_qkv, vec):
    rows = near.shape[0]
    by_row = pl.BlockSpec((rows, D), lambda i: (i, 0))
    return pl.pallas_call(
        project_kernel,
        out_shape=[
            jax.ShapeDtypeStruct((2 * rows, D), BF16),
            jax.ShapeDtypeStruct((rows, D), BF16),
            jax.ShapeDtypeStruct((2 * rows, D), BF16),
            jax.ShapeDtypeStruct((2 * rows, D), BF16),
        ],
        grid=(2,),
        in_specs=[
            whole((rows, D)),
            whole((rows, D)),
            whole((rows, HV)),
            whole((rows, HV)),
            whole((D, QKV)),
            whole((1, VEC)),
        ],
        out_specs=[by_row, whole((rows, D)), by_row, by_row],
        compiler_params=params(60),
        cost_estimate=cost(4 * rows * D * QKV, 2 * D * QKV + rows * D * 20),
        name="project",
    )(near, far, firsts, firsts_far, w_qkv, vec)


def attend_kernel(q, k, v, row_pos, column_pos, out, chance, bias):
    @pl.when(pl.program_id(0) == 0)
    def _():
        bias[...] = jnp.where(column_pos[...] <= row_pos[...], 0.0, FAR)

    heads = [slice(head * HD, (head + 1) * HD) for head in range(2)]
    scores = [mm(k[:, cols], q[:, cols], NT) + bias[...] for cols in heads]
    for head in range(2):
        top = jnp.max(scores[head], axis=0, keepdims=True)
        power = jnp.exp(scores[head] - top)
        total = jnp.sum(power, axis=0, keepdims=True)
        chance[head] = (power * (1.0 / total)).astype(BF16)
    for head, cols in enumerate(heads):
        out[:, cols] = mm(v[:, cols], chance[head], TN).T.astype(BF16)


def attend(q, k, v, row_pos, column_pos):
    queries, keys = q.shape[0], k.shape[0]
    pairs = D // LANE
    by_column = lambda i: (0, i)
    return pl.pallas_call(
        attend_kernel,
        out_shape=[
            jax.ShapeDtypeStruct((queries, D), BF16),
            jax.ShapeDtypeStruct((2 * pairs, keys, queries), BF16),
        ],
        grid=(pairs,),
        in_specs=[
            pl.BlockSpec((queries, LANE), by_column),
            pl.BlockSpec((keys, LANE), by_column),
            pl.BlockSpec((keys, LANE), by_column),
            whole((1, queries)),
            whole((keys, 1)),
        ],
        out_specs=[
            pl.BlockSpec((queries, LANE), by_column),
            pl.BlockSpec((2, keys, queries), lambda i: (i, 0, 0)),
        ],
        scratch_shapes=[pltpu.VMEM((keys, queries), F32)],
        compiler_params=params(60),
        cost_estimate=cost(4 * queries * keys * D, 24 * queries * keys, 12 * queries * keys),
        name="attend",
    )(q, k, v, row_pos, column_pos)


def hidden_kernel(
    tokens, att, og, w_out, w_up, w_down, vec,
    result, grad_resid, resid_low, grad_att, d_up, d_down, vec_grad,
    resid, hat, n2, rate, acc, acc_grad, flat_up, flat_down,
):
    step = pl.program_id(0)
    per_row = D // LANE
    wide = FF // LANE

    @pl.when(step == 0)
    def _():
        base = tokens[...].astype(F32) + mm(att[...], w_out[...]) + vec_part(vec, 5)
        resid[...] = base
        unit, scale = normed(base)
        hat[...] = unit
        rate[...] = scale
        n2[...] = (unit * vec_part(vec, 2) + vec_part(vec, 3)).astype(BF16)
        vec_grad[...] = jnp.zeros_like(vec_grad)
        acc[...] = jnp.zeros_like(acc)
        acc_grad[...] = jnp.zeros_like(acc_grad)

    start = pl.multiple_of(7 * D + HV + step * FF_STEP, LANE)
    pre = mm(n2[...], w_up[...]) + vec[:, pl.ds(start, FF_STEP)]
    square = pre * pre
    bent = jnp.tanh(0.7978845608028654 * (pre + 0.044715 * square * pre))
    half = 0.5 * (1.0 + bent)
    act = (pre * half).astype(BF16)
    slope = half + (0.5 * 0.7978845608028654) * pre * (1.0 - bent * bent) * (1.0 + 0.134145 * square)
    grad_pre32 = mm(og[...], w_down[...], NT) * slope
    grad_pre = grad_pre32.astype(BF16)
    vec_grad[:, pl.ds(start, FF_STEP)] = jnp.sum(grad_pre.astype(F32), axis=0, keepdims=True)
    acc[...] += mm(act, w_down[...])
    acc_grad[...] += mm(grad_pre, w_up[...], NT)
    down = mm(act, og[...], TN)
    for j in range(per_row):
        flat_down[pl.ds(j, FF_STEP, stride=per_row), :] = down[:, j * LANE : (j + 1) * LANE]
    d_down[...] = flat_down[...].astype(BF16)
    up = mm(n2[...], grad_pre, TN)
    for j in range(FF_STEP // LANE):
        flat_up[pl.ds(step * (FF_STEP // LANE) + j, D, stride=wide), :] = up[
            :, j * LANE : (j + 1) * LANE
        ]

    @pl.when(step == FF // FF_STEP - 1)
    def _():
        d_up[...] = flat_up[...].astype(BF16)
        result[...] = (resid[...] + acc[...] + vec_part(vec, 6)).astype(BF16)
        grad = acc_grad[...]
        unit = hat[...]
        vec_grad[:, 2 * D : 3 * D] = jnp.sum(grad * unit, axis=0, keepdims=True)
        vec_grad[:, 3 * D : 4 * D] = jnp.sum(grad, axis=0, keepdims=True)
        given = og[...].astype(F32)
        back = given + norm_back(grad, unit, rate[...], vec_part(vec, 2))
        grad_resid[...] = back
        low = back.astype(BF16)
        resid_low[...] = low
        vec_grad[:, 5 * D : 6 * D] = jnp.sum(low.astype(F32), axis=0, keepdims=True)
        vec_grad[:, 6 * D : 7 * D] = jnp.sum(given, axis=0, keepdims=True)
        grad_att[...] = mm(low, w_out[...], NT).astype(BF16)


def hidden(tokens, att, og, w_out, w_up, w_down, vec):
    rows = tokens.shape[0]
    line = (rows, D)
    flat_rows = FF * D // LANE
    return pl.pallas_call(
        hidden_kernel,
        out_shape=[
            jax.ShapeDtypeStruct(line, BF16),
            jax.ShapeDtypeStruct(line, F32),
            jax.ShapeDtypeStruct(line, BF16),
            jax.ShapeDtypeStruct(line, BF16),
            jax.ShapeDtypeStruct((flat_rows, LANE), BF16),
            jax.ShapeDtypeStruct((flat_rows, LANE), BF16),
            jax.ShapeDtypeStruct((1, VEC), F32),
        ],
        grid=(FF // FF_STEP,),
        in_specs=[
            whole(line),
            whole(line),
            whole(line),
            whole((D, D)),
            pl.BlockSpec((D, FF_STEP), lambda i: (0, i)),
            pl.BlockSpec((FF_STEP, D), lambda i: (i, 0)),
            whole((1, VEC)),
        ],
        out_specs=[
            whole(line),
            whole(line),
            whole(line),
            whole(line),
            whole((flat_rows, LANE)),
            pl.BlockSpec((FF_STEP * D // LANE, LANE), lambda i: (i, 0)),
            whole((1, VEC)),
        ],
        scratch_shapes=[
            pltpu.VMEM(line, F32),
            pltpu.VMEM(line, F32),
            pltpu.VMEM(line, BF16),
            pltpu.VMEM((rows, 1), F32),
            pltpu.VMEM(line, F32),
            pltpu.VMEM(line, F32),
            pltpu.VMEM((flat_rows, LANE), F32),
            pltpu.VMEM((FF_STEP * D // LANE, LANE), F32),
        ],
        compiler_params=params(62),
        cost_estimate=cost(2 * rows * D * (6 * FF + 2 * D), 8 * D * FF + 20 * rows * D, rows * FF),
        name="hidden",
    )(tokens, att, og, w_out, w_up, w_down, vec)


def attend_back_kernel(q, k, v, att, grad_att, chance, d_q, d_k, d_fresh, d_first):
    pair = pl.program_id(0)
    for head in range(2):
        cols = slice(head * HD, (head + 1) * HD)
        grad = grad_att[:, cols]
        weights = chance[head]
        shared = grad.astype(F32) * att[:, cols].astype(F32)
        delta = jnp.sum(shared.T, axis=0, keepdims=True)
        grad_chance = mm(v[:, cols], grad, NT)
        grad_scores = (weights.astype(F32) * (grad_chance - delta)).astype(BF16)
        grad_value = mm(weights, grad)

        @pl.when(pair < 3)
        def _(grad_value=grad_value, cols=cols):
            d_fresh[:, cols] = grad_value.astype(BF16)

        @pl.when(pair >= 3)
        def _(grad_value=grad_value, cols=cols):
            d_first[:, cols] = grad_value

        d_k[:, cols] = mm(grad_scores, q[:, cols]).astype(BF16)
        d_q[:, cols] = (mm(k[:, cols], grad_scores, TN).T * HD ** (-0.5)).astype(BF16)


def attend_back(q, k, v, att, grad_att, chance):
    queries, keys = q.shape[0], k.shape[0]
    pairs = D // LANE
    by_column = lambda i: (0, i)
    return pl.pallas_call(
        attend_back_kernel,
        out_shape=[
            jax.ShapeDtypeStruct((queries, D), BF16),
            jax.ShapeDtypeStruct((keys, D), BF16),
            jax.ShapeDtypeStruct((keys, HV), BF16),
            jax.ShapeDtypeStruct((keys, HV), F32),
        ],
        grid=(pairs,),
        in_specs=[
            pl.BlockSpec((queries, LANE), by_column),
            pl.BlockSpec((keys, LANE), by_column),
            pl.BlockSpec((keys, LANE), by_column),
            pl.BlockSpec((queries, LANE), by_column),
            pl.BlockSpec((queries, LANE), by_column),
            pl.BlockSpec((2, keys, queries), lambda i: (i, 0, 0)),
        ],
        out_specs=[
            pl.BlockSpec((queries, LANE), by_column),
            pl.BlockSpec((keys, LANE), by_column),
            pl.BlockSpec((keys, LANE), lambda i: (0, jnp.minimum(i, 2))),
            pl.BlockSpec((keys, LANE), lambda i: (0, jnp.maximum(i - 3, 0))),
        ],
        compiler_params=params(60),
        cost_estimate=cost(8 * queries * keys * D, 24 * queries * keys),
        name="attend_back",
    )(q, k, v, att, grad_att, chance)


def project_back_kernel(
    tokens, n1, d_q, d_k, d_fresh, att, resid_low, w_qkv, vec, vec_one,
    grad_near, grad_far, d_rest, vec_grad, flat,
):
    rows = n1.shape[0] // 2
    per_row = D // LANE
    grads = mm(d_k[...], w_qkv[:, D : 2 * D], NT) + mm(d_fresh[...], w_qkv[:, 2 * D :], NT)
    near = grads[:rows] + mm(d_q[...], w_qkv[:, :D], NT)
    far = grads[rows:]
    grad_near[...] = near
    grad_far[...] = far.astype(BF16)
    hat, _ = normed(tokens[...].astype(F32))
    vec_grad[...] = vec_one[...]
    vec_grad[:, :D] = jnp.sum(near * hat[:rows], axis=0, keepdims=True) + jnp.sum(
        far * hat[rows:], axis=0, keepdims=True
    )
    vec_grad[:, D : 2 * D] = jnp.sum(near, axis=0, keepdims=True) + jnp.sum(
        far, axis=0, keepdims=True
    )
    vec_grad[:, 4 * D : 5 * D] = jnp.sum(d_q[...].astype(F32), axis=0, keepdims=True)
    vec_grad[:, 7 * D : 7 * D + HV] = jnp.sum(d_fresh[...].astype(F32), axis=0, keepdims=True)
    pieces = (
        (n1, d_q, rows, 0, per_row),
        (n1, d_k, 2 * rows, D * per_row, per_row),
        (n1, d_fresh, 2 * rows, 2 * D * per_row, HV // LANE),
        (att, resid_low, rows, 2 * D * per_row + D * HV // LANE, per_row),
    )
    for left, right, count, start, columns in pieces:
        product = mm(left[:count], right[:count], TN)
        size = D * columns
        for j in range(columns):
            flat[pl.ds(j, D, stride=columns), :] = product[:, j * LANE : (j + 1) * LANE]
        d_rest[start : start + size] = flat[:size].astype(BF16)
    flat[: 2 * LANE] = jnp.zeros((2 * LANE, LANE), F32)
    for j in range(VEC // LANE):
        flat[j : j + 1] = vec_grad[:, j * LANE : (j + 1) * LANE]
    d_rest[REST:] = flat[: 2 * LANE].astype(BF16)


def project_back(tokens, n1, d_q, d_k, d_fresh, att, resid_low, w_qkv, vec, vec_one):
    rows = n1.shape[0] // 2
    vm = pl.BlockSpec(memory_space=pltpu.VMEM)
    return pl.pallas_call(
        project_back_kernel,
        out_shape=[
            jax.ShapeDtypeStruct((rows, D), F32),
            jax.ShapeDtypeStruct((rows, D), BF16),
            jax.ShapeDtypeStruct((128 * LANE, LANE), BF16),
        ],
        in_specs=[vm] * 10,
        out_specs=[vm] * 3,
        scratch_shapes=[pltpu.VMEM((1, VEC), F32), pltpu.VMEM((D * D // LANE, LANE), F32)],
        compiler_params=params(58),
        cost_estimate=cost(2 * rows * D * (7 * D), 14 * MIB),
        name="project_back",
    )(tokens, n1, d_q, d_k, d_fresh, att, resid_low, w_qkv, vec, vec_one)


def finish_kernel(
    places, grads, used, weight, one, two,
    resid, near, far, tokens, vec, firsts, firsts_far, vec_weight, vec_one, vec_two,
    new, new_one, new_two, low, tokens_grad, first_grad, new_vec, new_vec_one, new_vec_two,
    stage, flat, vec_stage, v_weight, v_one, v_two, v_low,
    v_resid, v_near, v_far, v_tokens, v_firsts, v_firsts_far,
    slot_sems, in_sems, out_sems, side_sems, vec_sem,
):
    capacity = weight.shape[0]
    rows = flat.shape[0] // LANE
    steps = capacity // rows

    def span(s):
        return pl.ds(s * rows, rows)

    vec_copy = pltpu.make_async_copy(grads.at[pl.ds(REST, vec_stage.shape[0])], vec_stage, vec_sem)
    vec_copy.start()
    brought = []
    for s in range(steps):
        for i, (source, target) in enumerate(((weight, v_weight), (one, v_one), (two, v_two))):
            brought.append(
                pltpu.make_async_copy(source.at[span(s)], target.at[span(s)], in_sems.at[3 * s + i])
            )
            brought[-1].start()

        @pl.loop(0, rows)
        def _(i, s=s):
            slot = s * rows + i
            pltpu.make_async_copy(
                grads.at[pl.ds(pl.multiple_of(places[slot] * LANE, LANE), LANE)],
                stage.at[pl.ds(pl.multiple_of(slot * LANE, LANE), LANE)],
                slot_sems.at[s],
            ).start()

    sides = [
        pltpu.make_async_copy(source, target, side_sems.at[i])
        for i, (source, target) in enumerate(
            (
                (resid, v_resid),
                (near, v_near),
                (far, v_far),
                (tokens, v_tokens),
                (firsts, v_firsts),
                (firsts_far, v_firsts_far),
            )
        )
    ]
    for copy in sides:
        copy.start()
    sent = []
    for s in range(steps):
        for copy in brought[3 * s : 3 * s + 3]:
            copy.wait()
        tile = pl.ds(s * rows * LANE, rows * LANE)
        pltpu.make_async_copy(stage.at[tile], stage.at[tile], slot_sems.at[s]).wait()
        flat[...] = stage[tile, :].astype(F32)
        keep = used[span(s), :] > 0.0
        for c in range(LANE):
            columns = slice(c * LANE, (c + 1) * LANE)
            gradient = jnp.where(keep, flat[pl.ds(c, rows, stride=LANE), :], 0.0)
            after, after_one, after_two = adam_step(
                v_weight[span(s), columns], v_one[span(s), columns], v_two[span(s), columns],
                gradient, RATE_MATRIX, DECAY_MATRIX,
            )
            v_weight[span(s), columns] = after
            v_one[span(s), columns] = after_one
            v_two[span(s), columns] = after_two
            v_low[s, :, columns] = after.astype(BF16)
        for i, (source, target) in enumerate(
            (
                (v_weight.at[span(s)], new.at[span(s)]),
                (v_one.at[span(s)], new_one.at[span(s)]),
                (v_two.at[span(s)], new_two.at[span(s)]),
            )
        ):
            sent.append(pltpu.make_async_copy(source, target, out_sems.at[3 * s + i]))
            sent[-1].start()
    for s in range(steps):
        low[span(s), :] = v_low[s]
    vec_copy.wait()
    count = vec_weight.shape[0]
    after, after_one, after_two = adam_step(
        vec_weight[...], vec_one[...], vec_two[...],
        vec_stage[...].astype(F32)[:count], RATE_VECTOR, 0.0,
    )
    new_vec[...] = after
    new_vec_one[...] = after_one
    new_vec_two[...] = after_two
    for copy in sides:
        copy.wait()
    grad = v_near[...] + v_far[...].astype(F32)
    hat, rate = normed(v_tokens[...].astype(F32))
    v_resid[...] += norm_back(grad, hat, rate, vec_part(vec, 0))
    for i in range(HV // LANE):
        columns = slice(i * LANE, (i + 1) * LANE)
        v_firsts[:, columns] += v_firsts_far[i].astype(F32)
    for i, (source, target) in enumerate(((v_resid, tokens_grad), (v_firsts, first_grad))):
        sent.append(pltpu.make_async_copy(source, target, side_sems.at[i]))
        sent[-1].start()
    for copy in sent:
        copy.wait()


def finish(places, grads, used, weight, one, two, resid, near, far, tokens, vec, firsts, firsts_far, vectors):
    capacity, tile_len = weight.shape
    rows = 8 if capacity % 8 == 0 else capacity
    steps = capacity // rows
    flat_vec = vectors[0].shape
    any_space = pl.BlockSpec(memory_space=pl.ANY)
    sides = [resid, near, far, tokens, firsts, firsts_far]
    return pl.pallas_call(
        finish_kernel,
        out_shape=[jax.ShapeDtypeStruct(weight.shape, F32)] * 3
        + [jax.ShapeDtypeStruct(weight.shape, BF16)]
        + [jax.ShapeDtypeStruct(resid.shape, F32), jax.ShapeDtypeStruct(firsts.shape, F32)]
        + [jax.ShapeDtypeStruct(flat_vec, F32)] * 3,
        grid_spec=pltpu.PrefetchScalarGridSpec(
            num_scalar_prefetch=1,
            grid=(1,),
            in_specs=[any_space, whole((capacity, LANE))]
            + [any_space] * 7
            + [whole((1, VEC))]
            + [any_space] * 2
            + [whole(flat_vec)] * 3,
            out_specs=[any_space] * 3 + [whole(weight.shape)] + [any_space] * 2 + [whole(flat_vec)] * 3,
            scratch_shapes=[
                pltpu.VMEM((capacity * LANE, LANE), BF16),
                pltpu.VMEM((rows * LANE, LANE), F32),
                pltpu.VMEM((80, LANE), BF16),
                pltpu.VMEM(weight.shape, F32),
                pltpu.VMEM(weight.shape, F32),
                pltpu.VMEM(weight.shape, F32),
                pltpu.VMEM((steps, rows, tile_len), BF16),
            ]
            + [pltpu.VMEM(side.shape, side.dtype) for side in sides]
            + [
                pltpu.SemaphoreType.DMA((steps,)),
                pltpu.SemaphoreType.DMA((3 * steps,)),
                pltpu.SemaphoreType.DMA((3 * steps,)),
                pltpu.SemaphoreType.DMA((len(sides),)),
                pltpu.SemaphoreType.DMA,
            ],
        ),
        compiler_params=params(60),
        cost_estimate=cost(20 * capacity * tile_len, 28 * capacity * tile_len, 2 * capacity * tile_len),
        name="finish",
    )(places, grads, used, weight, one, two, resid, near, far, tokens, vec, firsts, firsts_far, *vectors)


class Links:
    def __init__(self, line, send_sems, recv_sems):
        dp = lax.axis_index("dp")
        self.line = line
        self.y = lax.axis_index("seq")
        self.z = dp // 4
        self.x = (dp // 2) % 2
        self.c = dp % 2
        self.send_sems, self.recv_sems = send_sems, recv_sems
        self.to = {
            "core": {"dp": self.z * 4 + self.x * 2 + (1 - self.c)},
            "x": {"dp": self.z * 4 + (1 - self.x) * 2 + self.c},
            "y": {"seq": 1 - self.y},
            "up": {"dp": dp + 4},
            "down": {"dp": dp - 4},
        }
        self.sent = []

    def greet(self, whole_line, meanwhile=lambda: None):
        barrier = pltpu.get_barrier_semaphore()
        for name in ("core", "x", "y"):
            pl.semaphore_signal(barrier, inc=1, device_id=self.to[name])
        if whole_line:
            for d in range(1, self.line):
                z = (self.z + d) % self.line
                pl.semaphore_signal(barrier, inc=1, device_id={"dp": z * 4 + self.x * 2 + self.c})
            meanwhile()
            pl.semaphore_wait(barrier, 2 + self.line)
            return

        @pl.when(self.z > 0)
        def _():
            pl.semaphore_signal(barrier, inc=1, device_id=self.to["down"])

        @pl.when(self.z < self.line - 1)
        def _():
            pl.semaphore_signal(barrier, inc=1, device_id=self.to["up"])

        meanwhile()
        pl.semaphore_wait(
            barrier,
            3 + jnp.where(self.z > 0, 1, 0) + jnp.where(self.z < self.line - 1, 1, 0),
        )

    def copy(self, source, target, index, way):
        sender, receiver = index if isinstance(index, tuple) else (index, index)
        to = self.to[way] if isinstance(way, str) else {"dp": way * 4 + self.x * 2 + self.c}
        return pltpu.make_async_remote_copy(
            src_ref=source,
            dst_ref=target,
            send_sem=self.send_sems.at[sender],
            recv_sem=self.recv_sems.at[receiver],
            device_id=to,
        )

    def send(self, describe):
        source, target, index, way, when = describe()
        if when is None:
            self.copy(source, target, index, way).start()
        else:

            @pl.when(when)
            def _():
                self.copy(source, target, index, way).start()

        self.sent.append(describe)

    def arrive(self, target, index, way):
        self.copy(target, target, index, way).wait_recv()

    def finish(self):
        for describe in self.sent:
            source, target, index, way, when = describe()
            if when is None:
                self.copy(source, target, index, way).wait_send()
            else:

                @pl.when(when)
                def _(source=source, target=target, index=index, way=way):
                    self.copy(source, target, index, way).wait_send()


def add_into(place, *others):
    total = place[...].astype(F32)
    for other in others:
        total = total + other[...].astype(F32)
    place[...] = total.astype(BF16)


class Scatter:
    KINDS = ("core", "xa", "yb", "ya", "xb", "to", "from")

    def __init__(self, links, base, source, offset, rows, cut, buffers, load_sems):
        self.k, self.base, self.source, self.offset, self.rows = links, base, source, offset, rows
        self.held, self.r_core, self.r_xa, self.r_yb, self.r_ya, self.r_xb, self.r_line = buffers
        self.load_sems = load_sems
        self.halves = (pl.ds(0, cut), pl.ds(cut, rows - cut))

    @staticmethod
    def buffers_of(rows, cut, line):
        return [
            pltpu.VMEM((line, 2, 2, rows, LANE), BF16),
            pltpu.VMEM((line, 4 * rows, LANE), BF16),
            pltpu.VMEM((line, 2, cut, LANE), BF16),
            pltpu.VMEM((line, 2, rows - cut, LANE), BF16),
            pltpu.VMEM((line, cut, LANE), BF16),
            pltpu.VMEM((line, rows - cut, LANE), BF16),
            pltpu.VMEM((line, rows, LANE), BF16),
        ]

    def at(self, kind, z):
        return self.base + self.KINDS.index(kind) * self.k.line + z

    def load(self, z):
        start = self.offset + (self.k.c * self.k.line + z) * 4 * self.rows
        return [
            pltpu.make_async_copy(
                self.source.at[pl.ds(pl.multiple_of(start + i * self.rows, 16), self.rows)],
                self.held.at[z, i // 2, i % 2],
                self.load_sems.at[4 * z + i],
            )
            for i in range(4)
        ]

    def begin(self):
        k = self.k

        def describe(z):
            start = self.offset + ((1 - k.c) * k.line + z) * 4 * self.rows
            source = self.source.at[pl.ds(pl.multiple_of(start, 16), 4 * self.rows)]
            return source, self.r_core.at[z], self.at("core", z), "core", None

        for z in range(k.line):
            k.send(functools.partial(describe, z))
            for copy in self.load(z):
                copy.start()

    def first(self, z):
        k, (a, b) = self.k, self.halves
        for copy in self.load(z):
            copy.wait()
        k.arrive(self.r_core.at[z], self.at("core", z), "core")
        for i in range(4):
            add_into(self.held.at[z, i // 2, i % 2], self.r_core.at[z, pl.ds(i * self.rows, self.rows)])
        k.send(lambda: (self.held.at[z, 1 - k.x, :, a], self.r_xa.at[z], self.at("xa", z), "x", None))
        k.send(lambda: (self.held.at[z, :, 1 - k.y, b], self.r_yb.at[z], self.at("yb", z), "y", None))

    def second(self, z):
        k, (a, b) = self.k, self.halves
        k.arrive(self.r_xa.at[z], self.at("xa", z), "x")
        for y in range(2):
            add_into(self.held.at[z, k.x, y, a], self.r_xa.at[z, y])
        k.send(lambda: (self.held.at[z, k.x, 1 - k.y, a], self.r_ya.at[z], self.at("ya", z), "y", None))
        k.arrive(self.r_yb.at[z], self.at("yb", z), "y")
        for x in range(2):
            add_into(self.held.at[z, x, k.y, b], self.r_yb.at[z, x])
        k.send(lambda: (self.held.at[z, 1 - k.x, k.y, b], self.r_xb.at[z], self.at("xb", z), "x", None))

    def third(self, z):
        k, (a, b) = self.k, self.halves
        k.arrive(self.r_ya.at[z], self.at("ya", z), "y")
        add_into(self.held.at[z, k.x, k.y, a], self.r_ya.at[z])
        k.arrive(self.r_xb.at[z], self.at("xb", z), "x")
        add_into(self.held.at[z, k.x, k.y, b], self.r_xb.at[z])

        def describe():
            index = (self.at("to", z), self.at("from", k.z))
            return self.held.at[z, k.x, k.y], self.r_line.at[k.z], index, z, k.z != z

        k.send(describe)

    def last(self):
        k = self.k
        others = [(k.z + d) % k.line for d in range(1, k.line)]
        for z in others:
            k.arrive(self.r_line.at[z], (self.at("to", z), self.at("from", z)), z)
        add_into(self.held.at[k.z, k.x, k.y], *[self.r_line.at[z] for z in others])


class Spread:
    KINDS = ("xa", "yb", "ya", "xb", "ya2", "xb2") + tuple(
        f"{way}{i}" for way in ("to", "from", "c") for i in range(4)
    )

    def __init__(self, links, base, piece, out, index, first, rows, cut):
        self.k, self.base, self.piece, self.out, self.index = links, base, piece, out, index
        self.parts = {None: (first, rows), 0: (first, cut), 1: (first + cut, rows - cut)}

    def own(self, half):
        first, count = self.parts[half]
        return self.piece(pl.ds(first, count))

    def at(self, kind, z):
        return self.base + self.KINDS.index(kind) * self.k.line + z

    def spot(self, z, other_x, other_y, half=None, core=None):
        k = self.k
        c = k.c if core is None else core
        x = 1 - k.x if other_x else k.x
        y = 1 - k.y if other_y else k.y
        first, count = self.parts[half]
        return self.out.at[pl.ds(pl.multiple_of(self.index(c, z, x, y) + first, 16), count)]

    def place(self, d):
        return (self.k.z + d) % self.k.line

    def give(self, kind, way, d, other_x=False, other_y=False, half=None, own=False):
        def describe():
            z = self.place(d)
            target = self.spot(z, other_x, other_y, half)
            source = self.own(half) if own else target
            return source, target, self.at(kind, z), way, None

        self.k.send(describe)

    def get(self, kind, way, d, other_x=False, other_y=False, half=None):
        z = self.place(d)
        self.k.arrive(self.spot(z, other_x, other_y, half), self.at(kind, z), way)

    def lift(self, i, own=False):
        k = self.k
        place = dict(other_x=i >= 2, other_y=i % 2 == 1)

        def describe(d):
            z = self.place(d)
            target = self.spot(k.z, **place)
            source = self.own(None) if own else target
            return source, target, (self.at(f"to{i}", z), self.at(f"from{i}", k.z)), z, None

        for d in (k.line - 1, 1, 2):
            k.send(functools.partial(describe, d))

    def land(self, d, i):
        z = self.place(d)
        place = dict(other_x=i >= 2, other_y=i % 2 == 1)
        self.k.arrive(self.spot(z, **place), (self.at(f"to{i}", z), self.at(f"from{i}", z)), z)

    def cross(self, d):
        own = d == 0
        self.give("xa", "x", d, half=0, own=own)
        self.give("yb", "y", d, half=1, own=own)
        self.give("ya", "y", d, half=0, own=own)
        self.give("xb", "x", d, half=1, own=own)
        self.give("c0", "core", d, own=own)

    def start(self):
        self.lift(0, True)
        self.cross(0)

    def along(self, d):
        self.land(d, 0)
        self.cross(d)

    def turn(self, d):
        self.get("xa", "x", d, other_x=True, half=0)
        self.give("ya2", "y", d, other_x=True, half=0)
        self.get("yb", "y", d, other_y=True, half=1)
        self.give("xb2", "x", d, other_y=True, half=1)

    def share(self, d, late=False):
        self.get("ya", "y", d, other_y=True, half=0)
        self.give("c1", "core", d, other_y=True)
        if late:
            self.lift(1)
        self.get("xb", "x", d, other_x=True, half=1)
        self.give("c2", "core", d, other_x=True)
        if late:
            self.lift(2)
        self.get("ya2", "y", d, other_x=True, other_y=True, half=0)
        self.get("xb2", "x", d, other_x=True, other_y=True, half=1)
        self.give("c3", "core", d, other_x=True, other_y=True)
        if late:
            self.lift(3)

    def along_late(self, d):
        for i in range(4):
            self.land(d, i)
            self.give(f"c{i}", "core", d, other_x=i >= 2, other_y=i % 2 == 1)

    def end(self):
        k = self.k
        for z in range(k.line):
            for i in range(4):
                k.arrive(self.spot(z, i >= 2, i % 2 == 1, core=1 - k.c), self.at(f"c{i}", z), "core")


RS_SEMS = len(Scatter.KINDS)
AR_SEMS = RS_SEMS + 2 * len(Spread.KINDS)


class Total:
    def __init__(self, links, base, source, offset, kind, out, top, buffers, load_sems, copy_sem):
        line = links.line
        size, cut, turn, plain = kind
        rows = size // (8 * line)
        held = buffers[0]

        def index(c, z, x, y):
            return top + (((c * line + z) * 2 + x) * 2 + y) * rows

        def piece(span):
            return held.at[links.z, links.x, links.y, span]

        self.k, self.piece, self.out, self.index, self.rows = links, piece, out, index, rows
        self.scatter = Scatter(links, base, source, offset, rows, cut, buffers, load_sems)
        base = base + RS_SEMS * line
        self.spread = Spread(links, base, piece, out, index, 0, plain, turn)
        self.late = None
        if plain < rows:
            base = base + len(Spread.KINDS) * line
            rest = rows - plain
            self.late = Spread(links, base, piece, out, index, plain, rest, rest // 32 * 16)
        self.copy_sem = copy_sem

    def keep(self):
        k = self.k
        start = pl.multiple_of(self.index(k.c, k.z, k.x, k.y), 16)
        return pltpu.make_async_copy(
            self.piece(pl.ds(0, self.rows)), self.out.at[pl.ds(start, self.rows)], self.copy_sem
        )

    def run(self, stage, part):
        scatter, spread, late = self.scatter, self.spread, self.late
        if stage == 0:
            scatter.begin()
        elif stage < 4:
            (scatter.first, scatter.second, scatter.third)[stage - 1](part)
        elif stage == 4:
            scatter.last()
            self.keep().start()
            spread.start()
            if late is not None:
                late.start()
        elif stage == 5 and part < 3:
            spread.along(part + 1)
        elif stage == 5 and part == 3:
            late.turn(0)
        elif stage == 5 and part == 4:
            late.share(0, True)
        elif stage == 5:
            late.along_late(part - 4)
        elif stage < 8:
            (spread.turn, spread.share)[stage - 6](part)
        else:
            self.keep().wait()
            spread.end()
            if late is not None:
                late.end()


class Gather:
    KINDS = ("up", "down", "xa", "yb", "ya", "xb", "ya2", "xb2", "x2") + tuple(
        f"{way}{i}" for way in ("u", "d", "c") for i in range(4)
    )

    def __init__(self, links, base, own, out, index, first, rows, cut, z_first, twice):
        self.k, self.base, self.own, self.out, self.index = links, base, own, out, index
        self.parts = {None: (first, rows), 0: (first, cut), 1: (first + cut, rows - cut)}
        self.z_first, self.twice = z_first, twice

    def at(self, kind, z):
        return self.base + self.KINDS.index(kind) * self.k.line + z

    def spot(self, z, other_x, other_y, half=None, core=None):
        k = self.k
        c = k.c if core is None else core
        x = 1 - k.x if other_x else k.x
        y = 1 - k.y if other_y else k.y
        first, count = self.parts[half]
        return self.out.at[pl.ds(pl.multiple_of(self.index(c, z, x, y) + first, 16), count)]

    def give(self, kind, way, z, other_x=False, other_y=False, half=None, when=None, own=False):
        def describe():
            place = self.spot(z(), other_x, other_y, half)
            source = self.own(other_y, half) if own else place
            return source, place, self.at(kind, z()), way, None if when is None else when()

        self.k.send(describe)

    def get(self, kind, way, z, other_x=False, other_y=False, half=None):
        self.k.arrive(self.spot(z, other_x, other_y, half), self.at(kind, z), way)

    def near(self):
        k = self.k
        found = []
        for r in range(1, k.line):
            found.append(
                (
                    lambda r=r: k.z - r,
                    lambda r=r: k.z >= r,
                    "u",
                    "up",
                    lambda r=r: (k.z >= r) & (k.z < k.line - 1),
                )
            )
            found.append(
                (
                    lambda r=r: k.z + r,
                    lambda r=r: k.z + r < k.line,
                    "d",
                    "down",
                    lambda r=r: (k.z + r < k.line) & (k.z > 0),
                )
            )
        return found

    def here(self):
        return self.k.z

    def lower(self):
        return self.k.z < self.k.line - 1

    def upper(self):
        return self.k.z > 0

    def cross(self, z, when, own):
        self.give("xa", "x", z, half=0, when=when, own=own)
        self.give("yb", "y", z, half=1, when=when, own=own)
        self.give("ya", "y", z, half=0, when=when, own=own)
        self.give("xb", "x", z, half=1, when=when, own=own)
        self.give("c0", "core", z, when=when, own=own)

    def start(self):
        self.give("up", "up", self.here, when=self.lower, own=True)
        self.give("down", "down", self.here, when=self.upper, own=True)
        if self.twice:
            for other, kind in ((False, "xa"), (True, "x2")):
                self.give(kind, "x", self.here, other_y=other, own=True)
                self.give("c1" if other else "c0", "core", self.here, other_y=other, own=True)
        else:
            self.cross(self.here, None, True)

    def along(self, number):
        z, exists, _, way, goes_on = self.near()[number]

        @pl.when(exists())
        def _():
            self.get(way, way, z())

        self.give(way, way, z, when=goes_on)
        self.cross(z, exists, False)

    def turn(self, z, when):
        def waits():
            self.get("xa", "x", z(), other_x=True, half=0)

        def waits_too():
            self.get("yb", "y", z(), other_y=True, half=1)

        waits() if when is None else pl.when(when())(waits)
        self.give("ya2", "y", z, other_x=True, half=0, when=when)
        waits_too() if when is None else pl.when(when())(waits_too)
        self.give("xb2", "x", z, other_y=True, half=1, when=when)

    def share(self, z, when):
        def waits(kind, way, **place):
            def wait():
                self.get(kind, way, z(), **place)

            wait() if when is None else pl.when(when())(wait)

        waits("ya", "y", other_y=True, half=0)
        self.give("c1", "core", z, other_y=True, when=when)
        waits("xb", "x", other_x=True, half=1)
        self.give("c2", "core", z, other_x=True, when=when)
        waits("ya2", "y", other_x=True, other_y=True, half=0)
        waits("xb2", "x", other_x=True, other_y=True, half=1)
        self.give("c3", "core", z, other_x=True, other_y=True, when=when)

    def share_twice(self):
        for other, kind in ((False, "xa"), (True, "x2")):
            self.get(kind, "x", self.k.z, other_x=True, other_y=other)
            self.give("c3" if other else "c2", "core", self.here, other_x=True, other_y=other)

    def lift(self, i, own=False):
        place = dict(other_x=i >= 2, other_y=i % 2 == 1)
        self.give(f"u{i}", "up", self.here, when=self.lower, own=own, **place)
        self.give(f"d{i}", "down", self.here, when=self.upper, own=own, **place)
        self.give(f"c{i}", "core", self.here, own=own, **place)

    def start_plane(self):
        if self.twice:
            for other, kind in ((False, "xa"), (True, "x2")):
                self.give(kind, "x", self.here, other_y=other, own=True)
            self.lift(0, True)
            self.lift(1, True)
        else:
            self.give("xa", "x", self.here, half=0, own=True)
            self.give("yb", "y", self.here, half=1, own=True)
            self.give("ya", "y", self.here, half=0, own=True)
            self.give("xb", "x", self.here, half=1, own=True)
            self.lift(0, True)

    def turn_plane(self):
        if self.twice:
            for other, kind in ((False, "xa"), (True, "x2")):
                self.get(kind, "x", self.k.z, other_x=True, other_y=other)
                self.lift(3 if other else 2)
        else:
            self.turn(self.here, None)

    def lift_plane(self):
        if not self.twice:
            z = self.k.z
            self.get("ya", "y", z, other_y=True, half=0)
            self.lift(1)
            self.get("xb", "x", z, other_x=True, half=1)
            self.lift(2)
            self.get("ya2", "y", z, other_x=True, other_y=True, half=0)
            self.get("xb2", "x", z, other_x=True, other_y=True, half=1)
            self.lift(3)

    def along_plane(self, number, i):
        z, exists, letter, way, goes_on = self.near()[number]
        place = dict(other_x=i >= 2, other_y=i % 2 == 1)

        @pl.when(exists())
        def _():
            self.get(f"{letter}{i}", way, z(), **place)

        self.give(f"{letter}{i}", way, z, when=goes_on, **place)
        self.give(f"c{i}", "core", z, when=exists, **place)

    def steps(self):
        count = 2 * (self.k.line - 1)
        if self.z_first:
            one = [self.start]
            two = [lambda n=n: self.along(n) for n in range(count)]
            spots = [(z, exists) for z, exists, _, _, _ in self.near()]
            if not self.twice:
                spots = [(self.here, None)] + spots
            three = [lambda z=z, e=e: self.turn(z, e) for z, e in spots]
            four = [lambda z=z, e=e: self.share(z, e) for z, e in spots]
            if self.twice:
                four = [self.share_twice] + four
            return [one, two, three, four]
        one = [self.start_plane]
        two = [self.turn_plane]
        three = [self.lift_plane]
        four = [lambda n=n, i=i: self.along_plane(n, i) for n in range(count) for i in range(4)]
        return [one, two, three, four]

    def end(self):
        k = self.k
        for z in range(k.line):
            for i in range(4):
                k.arrive(
                    self.spot(z, i >= 2, i % 2 == 1, core=1 - k.c), self.at(f"c{i}", z), "core"
                )


AG_SEMS = len(Gather.KINDS)


def all_gather_kernel(line, swaps, cuts, masters, *refs):
    near, out, far = refs[:swaps], refs[swaps], refs[swaps + 1 : 2 * swaps + 1]
    piece, flat, send_sems, recv_sems, copy_sem = refs[2 * swaps + 1 :]
    links = Links(line, send_sems, recv_sems)

    def pack():
        rows = flat.shape[0] // LANE
        for top in range(0, masters.shape[0], rows):
            pack_rows(masters.at[pl.ds(top, rows)], flat)
            piece[top * LANE : (top + rows) * LANE] = flat[...].astype(BF16)

    links.greet(False, pack)
    rows = piece.shape[0] // 2
    first_rows, second_rows = cuts
    spare = 2 * AG_SEMS * line

    def index(c, z, x, y):
        return (((z * 2 + x) * 2 + c) * 2 + y) * rows

    def keep():
        start = index(links.c, links.z, links.x, 0)
        return pltpu.make_async_copy(
            piece, out.at[pl.ds(pl.multiple_of(start, 16), 2 * rows)], copy_sem
        )

    gathers = []

    def own_of(first, count, cut):
        def own(other, half):
            begin, size = {None: (0, count), 0: (0, cut), 1: (cut, count - cut)}[half]
            y = 1 - links.y if other else links.y
            return piece.at[pl.ds(pl.multiple_of(y * rows + first + begin, 16), size)]

        return own

    last = rows - first_rows - second_rows
    spans = ((0, first_rows + second_rows, first_rows, True), (first_rows + second_rows, last, last // 32 * 16, False))
    for number, (first, count, cut, z_first) in enumerate(spans):
        gathers.append(
            Gather(
                links, number * AG_SEMS * line, own_of(first, count, cut), out, index,
                first, count, cut, z_first, True,
            )
        )
    flat, tall = gathers[0].steps(), gathers[1].steps()
    for step in flat[0] + tall[0]:
        step()
    keep().start()
    for i in range(swaps):
        links.send(lambda i=i: (near[i], far[i], spare + i, "y", None))
    along, rise = flat[1], tall[1] + tall[2]
    turn, share, climb = flat[2], flat[3], tall[3]
    for step in along[:2] + rise + turn[:2] + along[2:4] + climb[:8] + turn[2:4] + along[4:]:
        step()
    for step in climb[8:16] + turn[4:] + share[:3] + climb[16:] + share[3:]:
        step()
    for gather in gathers:
        gather.end()
    keep().wait()
    for i in range(swaps):
        links.arrive(far[i], spare + i, "y")
    links.finish()


def all_gather(masters, swaps, line, collective_id):
    any_space = pl.BlockSpec(memory_space=pl.ANY)
    sems = 2 * AG_SEMS * line + len(swaps)
    count = masters.shape[0] * LANE
    rows = count // 2
    cuts = (rows * 2 // 5 // 16 * 16, rows * 7 // 20 // 16 * 16)
    return pl.pallas_call(
        functools.partial(all_gather_kernel, line, len(swaps), cuts),
        out_shape=[jax.ShapeDtypeStruct((4 * line * count, LANE), BF16)]
        + [jax.ShapeDtypeStruct(s.shape, s.dtype) for s in swaps],
        in_specs=[pl.BlockSpec(memory_space=pltpu.VMEM)] + [any_space] * len(swaps),
        out_specs=[any_space] * (1 + len(swaps)),
        scratch_shapes=[
            pltpu.VMEM((count, LANE), BF16),
            pltpu.VMEM((8 * LANE, LANE), F32),
            pltpu.SemaphoreType.DMA((sems,)),
            pltpu.SemaphoreType.DMA((sems,)),
            pltpu.SemaphoreType.DMA,
        ],
        compiler_params=params(60, collective_id=collective_id, has_side_effects=True),
        cost_estimate=cost(0, 100 * MIB),
        name="all_gather",
    )(masters, *swaps)


PAIRS = D // LANE
UP_ROWS = FF * D // LANE
REST_ROWS = 128 * LANE
HEAD, NORM, LAST = 900, 901, 902
ORDER = (
    100, 0, HEAD, HEAD, 110, 111, 112, 113, 10, 11, 120, HEAD, HEAD, 121, HEAD, HEAD, 122, HEAD,
    HEAD, 123, 12, 13, HEAD, HEAD, HEAD, HEAD, NORM, 130, 20, 21, 131, 132, 133, LAST, 200, 22,
    23, 210, 211, 212, 213, 140, 150, 30, 31, 32, 33, 220, 221, 222, 40, 223, 160, 161, 153, 50,
    51, 52, 230, 231, 232, 233, 53, 170, 171, 154, 151, 152, 60, 61, 240, 155, 54, 62, 63, 250,
    156, 157, 162, 163, 70, 253, 251, 252, 260, 71, 72, 73, 172, 173, 180, 55, 254, 56, 261,
    262, 57, 80, 270, 271, 263, 272, 273, 255, 256, 257, 280,
)


def segments():
    found = [[]]
    for step in ORDER:
        if step >= HEAD:
            found.append([])
        else:
            found[-1].append((step // 100, step // 10 % 10, step % 10))
    return found


def total_kinds(line):
    kinds = []
    for size, late in ((UP_ROWS, 20), (UP_ROWS, 20), (REST_ROWS, 30)):
        rows = size // (8 * line)
        plain = rows - rows * late // 100 // 32 * 32
        kinds.append((size, rows * 68 // 100 // 16 * 16, plain * 33 // 100 // 16 * 16, plain))
    return kinds


def back_kernel(
    line,
    q, k, v, att, grad_att, chance, tokens, tokens_far, n1, att_all, resid_low, w_qkv, vec, vec_one, d_up, d_down,
    d_first, grad_near, out, grad_back, first_back,
    d_q, d_k, d_v, far, d_rest, vec_grad, flat, *scratch,
):
    step = pl.program_id(0)
    sources = (tokens, tokens_far, n1, att_all, resid_low, w_qkv)
    late, late_sems, scratch = scratch[:6], scratch[6], scratch[7:]
    copies = [
        pltpu.make_async_copy(source, target, late_sems.at[i])
        for i, (source, target) in enumerate(zip(sources, late))
    ]
    buffers, (send_sems, recv_sems, load_sems, copy_sems) = scratch[:-4], scratch[-4:]
    links = Links(line, send_sems, recv_sems)
    tops = (REST_ROWS + UP_ROWS, REST_ROWS, 0)
    totals = [
        Total(
            links, g * AR_SEMS * line, source, 0, kind, out, top,
            buffers[7 * g : 7 * g + 7], load_sems.at[g], copy_sems.at[g],
        )
        for g, (source, kind, top) in enumerate(zip((d_down, d_up, d_rest), total_kinds(line), tops))
    ]
    spare = len(totals) * AR_SEMS * line
    plan = segments()

    def run(number):
        for g, stage, part in plan[number]:
            totals[g].run(stage, part)

    queries = q.shape[0]
    for head in range(2):
        for s in range(PAIRS):

            @pl.when(step == s)
            def _(s=s, head=head):
                if s == 0 and head == 0:
                    links.greet(True)
                    for copy in copies:
                        copy.start()
                run(2 * s + head)

        @pl.when(step < PAIRS)
        def _(head=head):
            cols = slice(head * HD, (head + 1) * HD)
            grad = grad_att[:, cols]
            weights = chance[head]
            shared = grad.astype(F32) * att[:, cols].astype(F32)
            delta = jnp.sum(shared.T, axis=0, keepdims=True)
            grad_chance = mm(v[:, cols], grad, NT)
            grad_scores = (weights.astype(F32) * (grad_chance - delta)).astype(BF16)
            grad_value = mm(weights, grad)

            d_v[step, :, cols] = grad_value.astype(BF16)
            d_first[:, cols] = grad_value[:queries]
            d_k[step, :, cols] = mm(grad_scores, q[:, cols]).astype(BF16)
            d_q[step, :, cols] = (mm(k[:, cols], grad_scores, TN).T * HD ** (-0.5)).astype(BF16)

    @pl.when(step == PAIRS)
    def _():
        for copy in copies:
            copy.wait()
        tokens, tokens_far, n1, att_all, resid_low, w_qkv = late
        rows = n1.shape[0] // 2
        per_row = D // LANE
        run(2 * PAIRS)
        rows = n1.shape[0] // 2
        first_far = d_v.at[pl.ds(PAIRS // 2, PAIRS // 2), pl.ds(rows, rows)]
        links.send(lambda: (first_far, first_back, spare, "y", None))
        dq = jnp.concatenate([d_q[i] for i in range(PAIRS)], axis=1)
        dk = jnp.concatenate([d_k[i] for i in range(PAIRS)], axis=1)
        dv = jnp.concatenate([d_v[i] for i in range(PAIRS // 2)], axis=1)
        grads = mm(dk, w_qkv[:, D : 2 * D], NT) + mm(dv, w_qkv[:, 2 * D :], NT)
        beside = grads[rows:]
        far[...] = beside.astype(BF16)
        links.send(lambda: (far, grad_back, spare + 1, "y", None))
        near = grads[:rows] + mm(dq, w_qkv[:, :D], NT)
        grad_near[...] = near
        hat, _ = normed(tokens[...].astype(F32))
        hat_far, _ = normed(tokens_far[...].astype(F32))
        vec_grad[...] = vec_one[...]
        vec_grad[:, :D] = jnp.sum(near * hat, axis=0, keepdims=True) + jnp.sum(
            beside * hat_far, axis=0, keepdims=True
        )
        vec_grad[:, D : 2 * D] = jnp.sum(near, axis=0, keepdims=True) + jnp.sum(
            beside, axis=0, keepdims=True
        )
        vec_grad[:, 4 * D : 5 * D] = jnp.sum(dq.astype(F32), axis=0, keepdims=True)
        vec_grad[:, 7 * D : 7 * D + HV] = jnp.sum(dv.astype(F32), axis=0, keepdims=True)
        run(2 * PAIRS + 1)
        pieces = (
            (n1[:rows], dq, 0, per_row),
            (n1[...], dk, D * per_row, per_row),
            (n1[...], dv, 2 * D * per_row, HV // LANE),
            (att_all[...], resid_low[...], 2 * D * per_row + D * HV // LANE, per_row),
        )
        for left, right, start, columns in pieces:
            product = mm(left, right, TN)
            size = D * columns
            for j in range(columns):
                flat[pl.ds(j, D, stride=columns), :] = product[:, j * LANE : (j + 1) * LANE]
            d_rest[start : start + size] = flat[:size].astype(BF16)
        flat[: 2 * LANE] = jnp.zeros((2 * LANE, LANE), F32)
        for j in range(VEC // LANE):
            flat[j : j + 1] = vec_grad[:, j * LANE : (j + 1) * LANE]
        d_rest[REST:] = flat[: 2 * LANE].astype(BF16)
        run(2 * PAIRS + 2)
        links.arrive(first_back, spare, "y")
        links.arrive(grad_back, spare + 1, "y")
        links.finish()


def back(q, k, v, att, grad_att, chance, tokens, tokens_far, n1, resid_low, w_qkv, vec, vec_one, d_up, d_down, line):
    rows, keys = q.shape[0], k.shape[0]
    any_space = pl.BlockSpec(memory_space=pl.ANY)

    def column(count):
        return pl.BlockSpec((count, LANE), lambda i: (0, jnp.minimum(i, PAIRS - 1)))

    def once(array):
        return pl.BlockSpec(array.shape, lambda i: (0,) * array.ndim, pipeline_mode=pl.Buffered(1))

    kinds = total_kinds(line)
    scratch = []
    for size, cut, _, _ in kinds:
        scratch += Scatter.buffers_of(size // (8 * line), cut, line)
    sems = len(kinds) * AR_SEMS * line + 2
    return pl.pallas_call(
        functools.partial(back_kernel, line),
        out_shape=[
            jax.ShapeDtypeStruct((rows, HV), F32),
            jax.ShapeDtypeStruct((rows, D), F32),
            jax.ShapeDtypeStruct((REST_ROWS + 2 * UP_ROWS, LANE), BF16),
            jax.ShapeDtypeStruct((rows, D), BF16),
            jax.ShapeDtypeStruct((PAIRS // 2, rows, LANE), BF16),
        ],
        grid=(PAIRS + 1,),
        in_specs=[
            column(rows),
            column(keys),
            column(keys),
            column(rows),
            column(rows),
            pl.BlockSpec((2, keys, rows), lambda i: (jnp.minimum(i, PAIRS - 1), 0, 0)),
            any_space,
            any_space,
            any_space,
            any_space,
            any_space,
            any_space,
            once(vec),
            once(vec_one),
            any_space,
            any_space,
        ],
        out_specs=[
            pl.BlockSpec((rows, LANE), lambda i: (0, jnp.clip(i - 3, 0, 2))),
            pl.BlockSpec((rows, D), lambda i: (0, 0), pipeline_mode=pl.Buffered(1)),
            any_space,
            any_space,
            any_space,
        ],
        scratch_shapes=[
            pltpu.VMEM((PAIRS, rows, LANE), BF16),
            pltpu.VMEM((PAIRS, keys, LANE), BF16),
            pltpu.VMEM((PAIRS, keys, LANE), BF16),
            pltpu.VMEM((rows, D), BF16),
            pltpu.VMEM((REST_ROWS, LANE), BF16),
            pltpu.VMEM((1, VEC), F32),
            pltpu.VMEM((D * D // LANE, LANE), F32),
        ]
        + [pltpu.VMEM(a.shape, a.dtype) for a in (tokens, tokens_far, n1, att, resid_low, w_qkv)]
        + [pltpu.SemaphoreType.DMA((6,))]
        + scratch
        + [
            pltpu.SemaphoreType.DMA((sems,)),
            pltpu.SemaphoreType.DMA((sems,)),
            pltpu.SemaphoreType.DMA((len(kinds), 4 * line)),
            pltpu.SemaphoreType.DMA((len(kinds),)),
        ],
        compiler_params=params(62, collective_id=0, has_side_effects=True),
        cost_estimate=cost(8 * rows * keys * D + 14 * rows * D * D, 100 * MIB),
        name="back",
    )(q, k, v, att, grad_att, chance, tokens, tokens_far, n1, att, resid_low, w_qkv, vec, vec_one, d_up, d_down)


def swap(value):
    return lax.ppermute(value, "seq", [(0, 1), (1, 0)])


def shards(
    tokens,
    first_values,
    out_grad,
    block_place,
    owners,
    masters,
    moment_one,
    moment_two,
    vector_master,
    vector_moment_one,
    vector_moment_two,
):
    capacity = masters.shape[0]
    dp_count = lax.axis_size("dp")
    tile_count = owners.shape[0]
    dp_here = lax.axis_index("dp")
    seq_here = lax.axis_index("seq")
    _, half_len, _ = tokens.shape

    tokens = tokens.reshape(half_len, D)
    firsts = first_values.reshape(half_len, HV)
    given = out_grad.reshape(half_len, D)
    line = dp_count // 4
    if line == LINE and capacity % 8 == 0:
        slots, tokens_far, firsts_far = all_gather(masters, [tokens, firsts], line, 1)
    else:
        tokens_far, firsts_far = swap(tokens), swap(firsts)
        slots = lax.all_gather(pack_slots(masters), "dp", axis=0, tiled=True)

    slot_index = slot_numbers(owners)
    slot_rows = owners * capacity + slot_index
    mine = (owners == dp_here)[None, :] & (
        slot_index[None, :] == jnp.arange(capacity, dtype=jnp.int32)[:, None]
    )
    tile_order = jnp.arange(tile_count, dtype=jnp.int32)
    tile_here = jnp.sum(jnp.where(mine, tile_order[None, :], 0), axis=1)
    tile_here = tile_here + jnp.where(tile_here >= 126, 2, 0)
    used = jnp.broadcast_to(
        jnp.any(mine, axis=1).astype(F32)[:, None], (capacity, LANE)
    )

    blocks = block_place.reshape(-1)
    per_device = blocks.shape[0] // 2
    block_len = half_len // per_device
    ordered = jnp.roll(blocks, -seq_here * per_device)
    all_pos = (
        ordered[:, None] * block_len + jnp.arange(block_len, dtype=jnp.int32)[None, :]
    ).reshape(-1)
    row_pos = all_pos[:half_len].reshape(1, half_len)
    column_pos = all_pos.reshape(2 * half_len, 1)

    vec = vector_master.reshape(1, VEC)
    w_qkv, w_out, w_up, w_down = unpack_weights(slot_rows, slots)
    n1, q, k, v = project(tokens, tokens_far, firsts, firsts_far, w_qkv, vec)
    att, chance = attend(q, k, v, row_pos, column_pos)
    result, grad_resid, resid_low, grad_att, d_up, d_down, vec_one = hidden(
        tokens, att, given, w_out, w_up, w_down, vec
    )
    if line == LINE:
        first_near, grad_near, grads, grad_back, first_back = back(
            q, k, v, att, grad_att, chance, tokens, tokens_far, n1, resid_low, w_qkv, vec, vec_one, d_up, d_down, line
        )
    else:
        d_q, d_k, d_fresh, d_first = attend_back(q, k, v, att, grad_att, chance)
        grad_near, grad_far, d_rest = project_back(
            jnp.concatenate([tokens, tokens_far], axis=0), n1, d_q, d_k, d_fresh, att, resid_low, w_qkv, vec, vec_one
        )
        first_near = d_first[:half_len]
        grad_back, first_back = swap(grad_far), swap(d_first[half_len:].astype(BF16))
        first_back = first_back.reshape(half_len, HV // LANE, LANE).transpose(1, 0, 2)
        grads = lax.psum(jnp.concatenate([d_rest, d_up, d_down], axis=0), ("seq", "dp"))
    vectors = [
        v.reshape(VEC // LANE, LANE) for v in (vector_master, vector_moment_one, vector_moment_two)
    ]
    new_master, new_one, new_two, new_low, tokens_grad, first_grad, *new_vectors = finish(
        tile_here, grads, used, masters, moment_one, moment_two,
        grad_resid, grad_near, grad_back, tokens, vec, first_near, first_back, vectors,
    )
    return (
        result.reshape(1, half_len, D),
        tokens_grad.reshape(1, half_len, D),
        first_grad.reshape(1, half_len, HV),
        new_master,
        new_one,
        new_two,
        new_low,
        *(v.reshape(VEC) for v in new_vectors),
    )


def solution(mesh):
    rows = P("dp", "seq", None)
    slots = P("dp", None)
    return jax.shard_map(
        shards,
        mesh=mesh,
        in_specs=(rows, rows, rows, slots, P(), slots, slots, slots, P(), P(), P()),
        out_specs=(rows, rows, rows, slots, slots, slots, slots, P(), P(), P()),
        check_vma=False,
    )
```

```python
import functools

import jax
import jax.numpy as jnp
from jax import lax
from jax.experimental import pallas as pl
from jax.experimental.pallas import tpu as pltpu
from jax.sharding import PartitionSpec as P

D = 768
HD = 64
FF = 3072
STEP = 10
HV = 384
LANE = 128
QKV = 2 * D + HV
FF_STEP = 768
VEC = 7 * D + HV + FF
MIB = 1024 * 1024
LINE = 4
REST = 126 * LANE

EPS_NORM = 1e-05
EPS_ADAM = 1e-08
BETA_ONE = 0.5
BETA_TWO = 0.5
RATE_MATRIX = 0.03
RATE_VECTOR = 0.25
DECAY_MATRIX = 0.1
FAR = -1e30

BF16 = jnp.bfloat16
F32 = jnp.float32

NN = (((1,), (0,)), ((), ()))
NT = (((1,), (1,)), ((), ()))
TN = (((0,), (0,)), ((), ()))


def mm(left, right, dims=NN):
    return lax.dot_general(left, right, dims, preferred_element_type=F32)


def vec_part(vec_ref, index):
    if index < 7:
        return vec_ref[:, index * D : (index + 1) * D]
    if index == 7:
        return vec_ref[:, 7 * D : 7 * D + HV]
    return vec_ref[:, 7 * D + HV :]


def params(mib, **more):
    return pltpu.CompilerParams(vmem_limit_bytes=mib * MIB, **more)


def whole(shape):
    return pl.BlockSpec(shape, lambda *_: (0,) * len(shape))


def cost(flops, bytes_accessed, transcendentals=0):
    return pl.CostEstimate(
        flops=int(flops), bytes_accessed=int(bytes_accessed), transcendentals=int(transcendentals)
    )


def adam_step(weight, first_moment, second_moment, gradient, step_rate, weight_decay):
    first_new = BETA_ONE * first_moment + (1.0 - BETA_ONE) * gradient
    second_new = BETA_TWO * second_moment + (1.0 - BETA_TWO) * gradient * gradient
    first_fix = 1.0 - BETA_ONE**STEP
    second_fix = 1.0 - BETA_TWO**STEP
    update = (first_new * (1.0 / first_fix)) / (jnp.sqrt(second_new * (1.0 / second_fix)) + EPS_ADAM)
    return (weight - step_rate * (update + weight_decay * weight), first_new, second_new)


def slot_numbers(owners):
    tile_order = jnp.arange(owners.shape[0], dtype=jnp.int32)
    earlier = (owners[None, :] == owners[:, None]) & (tile_order[None, :] < tile_order[:, None])
    return jnp.sum(earlier.astype(jnp.int32), axis=1)


def normed(values):
    center = jnp.mean(values, axis=-1, keepdims=True)
    centred = values - center
    spread = jnp.mean(centred * centred, axis=-1, keepdims=True)
    rate = lax.rsqrt(spread + EPS_NORM)
    return centred * rate, rate


def norm_back(grad, hat, rate, gain):
    g = grad * gain
    return rate * (
        g - jnp.mean(g, axis=-1, keepdims=True) - hat * jnp.mean(g * hat, axis=-1, keepdims=True)
    )


def pack_rows(src, flat):
    rows = src.shape[0]
    for c in range(LANE):
        flat[pl.ds(c, rows, stride=LANE), :] = src[:, c * LANE : (c + 1) * LANE]


def pack_kernel(src, dst, flat):
    pack_rows(src, flat)
    dst[...] = flat[...].astype(BF16)


def pack_slots(masters):
    capacity, tile_len = masters.shape
    rows = 8 if capacity % 8 == 0 else capacity
    return pl.pallas_call(
        pack_kernel,
        out_shape=jax.ShapeDtypeStruct((capacity * LANE, LANE), BF16),
        grid=(capacity // rows,),
        in_specs=[pl.BlockSpec((rows, tile_len), lambda i: (i, 0))],
        out_specs=pl.BlockSpec((rows * LANE, LANE), lambda i: (i, 0)),
        scratch_shapes=[pltpu.VMEM((rows * LANE, LANE), F32)],
        compiler_params=params(60),
        cost_estimate=cost(0, capacity * tile_len * 6),
        name="pack_slots",
    )(masters)


def weight_chunks():
    chunks = [
        (0, 36, 6, 0, 0, 0),
        (36, 36, 6, 0, D, 0),
        (72, 18, 3, 0, 2 * D, 0),
        (90, 36, 6, 1, 0, 0),
    ]
    for i in range(4):
        chunks.append((126 + 36 * i, 36, 24, 2, 0, 192 * i))
    for i in range(4):
        chunks.append((270 + 36 * i, 36, 6, 3, 0, 768 * i))
    return chunks


def unpack_kernel(slot_rows, slots, w_qkv, w_out, w_up, w_down, stage, o_qkv, o_out, o_up, o_down, flat, sems, out_sems):
    chunks = weight_chunks()
    places = (o_qkv, o_out, o_up, o_down)
    ends = (w_qkv, w_out, w_up, w_down)

    for number, (first, tiles, _, _, _, _) in enumerate(chunks):

        @pl.loop(0, tiles)
        def _(i, first=first, number=number):
            t = first + i
            pltpu.make_async_copy(
                slots.at[pl.ds(pl.multiple_of(slot_rows[t] * LANE, LANE), LANE)],
                stage.at[pl.ds(pl.multiple_of(t * LANE, LANE), LANE)],
                sems.at[number],
            ).start()

    copies = []
    for number, (first, tiles, per_row, matrix, column, row) in enumerate(chunks):
        span = pl.ds(first * LANE, tiles * LANE)
        pltpu.make_async_copy(stage.at[span], stage.at[span], sems.at[number]).wait()
        place = places[matrix]
        lines = 3 * LANE // per_row

        @pl.loop(0, tiles // 6)
        def _(g, first=first, per_row=per_row, place=place, column=column, row=row, lines=lines):
            for half in range(2):
                base = pl.multiple_of(first * LANE + (2 * g + half) * 3 * LANE, LANE)
                flat[half] = stage[pl.ds(base, 3 * LANE), :].astype(F32)
            for half in range(2):
                top = pl.multiple_of(row + (2 * g + half) * lines, 16)
                for j in range(per_row):
                    place[pl.ds(top, lines), column + j * LANE : column + (j + 1) * LANE] = flat[
                        half, pl.ds(j, lines, stride=per_row), :
                    ].astype(BF16)

        rows = tiles * LANE // per_row
        columns = pl.ds(column, per_row * LANE)
        copy = pltpu.make_async_copy(
            place.at[pl.ds(row, rows), columns],
            ends[matrix].at[pl.ds(row, rows), columns],
            out_sems.at[number],
        )
        copy.start()
        copies.append(copy)
    for copy in copies:
        copy.wait()


def unpack_weights(slot_rows, slots):
    tile_count = slot_rows.shape[0]
    shapes = [(D, QKV), (D, D), (D, FF), (FF, D)]
    any_space = pl.BlockSpec(memory_space=pl.ANY)
    return pl.pallas_call(
        unpack_kernel,
        out_shape=[jax.ShapeDtypeStruct(s, BF16) for s in shapes],
        grid_spec=pltpu.PrefetchScalarGridSpec(
            num_scalar_prefetch=1,
            grid=(1,),
            in_specs=[any_space],
            out_specs=[any_space] * 4,
            scratch_shapes=[pltpu.VMEM((tile_count * LANE, LANE), BF16)]
            + [pltpu.VMEM(s, BF16) for s in shapes]
            + [
                pltpu.VMEM((2, 3 * LANE, LANE), F32),
                pltpu.SemaphoreType.DMA((12,)),
                pltpu.SemaphoreType.DMA((12,)),
            ],
        ),
        compiler_params=params(60),
        cost_estimate=cost(0, 4 * tile_count * LANE * LANE),
        name="unpack_weights",
    )(slot_rows, slots)


def project_kernel(near, far, firsts, firsts_far, w_qkv, vec, n1, q, k, v):
    first = pl.program_id(0) == 0
    tokens = jnp.where(first, near[...], far[...])
    hat, _ = normed(tokens.astype(F32))
    low = (hat * vec_part(vec, 0) + vec_part(vec, 1)).astype(BF16)
    n1[...] = low
    k[...] = mm(low, w_qkv[:, D : 2 * D]).astype(BF16)
    v[:, :HV] = (mm(low, w_qkv[:, 2 * D :]) + vec_part(vec, 7)).astype(BF16)
    v[:, HV:] = jnp.where(first, firsts[...], firsts_far[...])

    @pl.when(first)
    def _():
        query = mm(low, w_qkv[:, :D]) + vec_part(vec, 4)
        q[...] = (query.astype(BF16).astype(F32) * HD ** (-0.5)).astype(BF16)


def project(near, far, firsts, firsts_far, w_qkv, vec):
    rows = near.shape[0]
    by_row = pl.BlockSpec((rows, D), lambda i: (i, 0))
    return pl.pallas_call(
        project_kernel,
        out_shape=[
            jax.ShapeDtypeStruct((2 * rows, D), BF16),
            jax.ShapeDtypeStruct((rows, D), BF16),
            jax.ShapeDtypeStruct((2 * rows, D), BF16),
            jax.ShapeDtypeStruct((2 * rows, D), BF16),
        ],
        grid=(2,),
        in_specs=[
            whole((rows, D)),
            whole((rows, D)),
            whole((rows, HV)),
            whole((rows, HV)),
            whole((D, QKV)),
            whole((1, VEC)),
        ],
        out_specs=[by_row, whole((rows, D)), by_row, by_row],
        compiler_params=params(60),
        cost_estimate=cost(4 * rows * D * QKV, 2 * D * QKV + rows * D * 20),
        name="project",
    )(near, far, firsts, firsts_far, w_qkv, vec)


def attend_kernel(places, q, k, v, out, chance, bias):
    @pl.when(pl.program_id(0) == 0)
    def _():
        here = lax.axis_index("seq")
        count = places.shape[1] // 2
        size = q.shape[0] // count
        ahead = lax.broadcasted_iota(jnp.int32, (size, size), 0) - lax.broadcasted_iota(
            jnp.int32, (size, size), 1
        )
        for i in range(2 * count):
            side = here if i < count else 1 - here
            key_place = places[0, side * count + i % count]
            for j in range(count):
                shift = (places[0, here * count + j] - key_place) * size
                bias[i * size : (i + 1) * size, j * size : (j + 1) * size] = jnp.where(
                    ahead <= shift, 0.0, FAR
                )

    heads = [slice(head * HD, (head + 1) * HD) for head in range(2)]
    scores = [mm(k[:, cols], q[:, cols], NT) + bias[...] for cols in heads]
    for head in range(2):
        top = jnp.max(scores[head], axis=0, keepdims=True)
        power = jnp.exp(scores[head] - top)
        total = jnp.sum(power, axis=0, keepdims=True)
        chance[head] = (power * (1.0 / total)).astype(BF16)
    for head, cols in enumerate(heads):
        out[:, cols] = mm(v[:, cols], chance[head], TN).T.astype(BF16)


def attend(places, q, k, v):
    queries, keys = q.shape[0], k.shape[0]
    pairs = D // LANE
    by_column = lambda i, *_: (0, i)
    return pl.pallas_call(
        attend_kernel,
        out_shape=[
            jax.ShapeDtypeStruct((queries, D), BF16),
            jax.ShapeDtypeStruct((2 * pairs, keys, queries), BF16),
        ],
        grid_spec=pltpu.PrefetchScalarGridSpec(
            num_scalar_prefetch=1,
            grid=(pairs,),
            in_specs=[
                pl.BlockSpec((queries, LANE), by_column),
                pl.BlockSpec((keys, LANE), by_column),
                pl.BlockSpec((keys, LANE), by_column),
            ],
            out_specs=[
                pl.BlockSpec((queries, LANE), by_column),
                pl.BlockSpec((2, keys, queries), lambda i, *_: (i, 0, 0)),
            ],
            scratch_shapes=[pltpu.VMEM((keys, queries), F32)],
        ),
        compiler_params=params(60),
        cost_estimate=cost(4 * queries * keys * D, 24 * queries * keys, 12 * queries * keys),
        name="attend",
    )(places, q, k, v)


def hidden_kernel(
    tokens, att, og, w_out, w_up, w_down, vec,
    result, grad_resid, resid_low, grad_att, d_up, d_down, vec_grad,
    resid, hat, n2, rate, acc, acc_grad, flat_up, flat_down,
):
    step = pl.program_id(0)
    per_row = D // LANE
    wide = FF // LANE

    @pl.when(step == 0)
    def _():
        base = tokens[...].astype(F32) + mm(att[...], w_out[...]) + vec_part(vec, 5)
        resid[...] = base
        unit, scale = normed(base)
        hat[...] = unit
        rate[...] = scale
        n2[...] = (unit * vec_part(vec, 2) + vec_part(vec, 3)).astype(BF16)
        vec_grad[...] = jnp.zeros_like(vec_grad)
        acc[...] = jnp.zeros_like(acc)
        acc_grad[...] = jnp.zeros_like(acc_grad)

    start = pl.multiple_of(7 * D + HV + step * FF_STEP, LANE)
    pre = mm(n2[...], w_up[...]) + vec[:, pl.ds(start, FF_STEP)]
    square = pre * pre
    bent = jnp.tanh(0.7978845608028654 * (pre + 0.044715 * square * pre))
    half = 0.5 * (1.0 + bent)
    act = (pre * half).astype(BF16)
    slope = half + (0.5 * 0.7978845608028654) * pre * (1.0 - bent * bent) * (1.0 + 0.134145 * square)
    grad_pre32 = mm(og[...], w_down[...], NT) * slope
    grad_pre = grad_pre32.astype(BF16)
    vec_grad[:, pl.ds(start, FF_STEP)] = jnp.sum(grad_pre.astype(F32), axis=0, keepdims=True)
    acc[...] += mm(act, w_down[...])
    acc_grad[...] += mm(grad_pre, w_up[...], NT)
    down = mm(act, og[...], TN)
    for j in range(per_row):
        flat_down[pl.ds(j, FF_STEP, stride=per_row), :] = down[:, j * LANE : (j + 1) * LANE]
    d_down[...] = flat_down[...].astype(BF16)
    up = mm(n2[...], grad_pre, TN)
    for j in range(FF_STEP // LANE):
        flat_up[pl.ds(step * (FF_STEP // LANE) + j, D, stride=wide), :] = up[
            :, j * LANE : (j + 1) * LANE
        ]

    @pl.when(step == FF // FF_STEP - 1)
    def _():
        d_up[...] = flat_up[...].astype(BF16)
        result[...] = (resid[...] + acc[...] + vec_part(vec, 6)).astype(BF16)
        grad = acc_grad[...]
        unit = hat[...]
        vec_grad[:, 2 * D : 3 * D] = jnp.sum(grad * unit, axis=0, keepdims=True)
        vec_grad[:, 3 * D : 4 * D] = jnp.sum(grad, axis=0, keepdims=True)
        given = og[...].astype(F32)
        back = given + norm_back(grad, unit, rate[...], vec_part(vec, 2))
        grad_resid[...] = back
        low = back.astype(BF16)
        resid_low[...] = low
        vec_grad[:, 5 * D : 6 * D] = jnp.sum(low.astype(F32), axis=0, keepdims=True)
        vec_grad[:, 6 * D : 7 * D] = jnp.sum(given, axis=0, keepdims=True)
        grad_att[...] = mm(low, w_out[...], NT).astype(BF16)


def hidden(tokens, att, og, w_out, w_up, w_down, vec):
    rows = tokens.shape[0]
    line = (rows, D)
    flat_rows = FF * D // LANE
    return pl.pallas_call(
        hidden_kernel,
        out_shape=[
            jax.ShapeDtypeStruct(line, BF16),
            jax.ShapeDtypeStruct(line, F32),
            jax.ShapeDtypeStruct(line, BF16),
            jax.ShapeDtypeStruct(line, BF16),
            jax.ShapeDtypeStruct((flat_rows, LANE), BF16),
            jax.ShapeDtypeStruct((flat_rows, LANE), BF16),
            jax.ShapeDtypeStruct((1, VEC), F32),
        ],
        grid=(FF // FF_STEP,),
        in_specs=[
            whole(line),
            whole(line),
            whole(line),
            whole((D, D)),
            pl.BlockSpec((D, FF_STEP), lambda i: (0, i)),
            pl.BlockSpec((FF_STEP, D), lambda i: (i, 0)),
            whole((1, VEC)),
        ],
        out_specs=[
            whole(line),
            whole(line),
            whole(line),
            whole(line),
            whole((flat_rows, LANE)),
            pl.BlockSpec((FF_STEP * D // LANE, LANE), lambda i: (i, 0)),
            whole((1, VEC)),
        ],
        scratch_shapes=[
            pltpu.VMEM(line, F32),
            pltpu.VMEM(line, F32),
            pltpu.VMEM(line, BF16),
            pltpu.VMEM((rows, 1), F32),
            pltpu.VMEM(line, F32),
            pltpu.VMEM(line, F32),
            pltpu.VMEM((flat_rows, LANE), F32),
            pltpu.VMEM((FF_STEP * D // LANE, LANE), F32),
        ],
        compiler_params=params(62),
        cost_estimate=cost(2 * rows * D * (6 * FF + 2 * D), 8 * D * FF + 20 * rows * D, rows * FF),
        name="hidden",
    )(tokens, att, og, w_out, w_up, w_down, vec)


def attend_back_kernel(q, k, v, att, grad_att, chance, d_q, d_k, d_fresh, d_first):
    pair = pl.program_id(0)
    for head in range(2):
        cols = slice(head * HD, (head + 1) * HD)
        grad = grad_att[:, cols]
        weights = chance[head]
        shared = grad.astype(F32) * att[:, cols].astype(F32)
        delta = jnp.sum(shared.T, axis=0, keepdims=True)
        grad_chance = mm(v[:, cols], grad, NT)
        grad_scores = (weights.astype(F32) * (grad_chance - delta)).astype(BF16)
        grad_value = mm(weights, grad)

        @pl.when(pair < 3)
        def _(grad_value=grad_value, cols=cols):
            d_fresh[:, cols] = grad_value.astype(BF16)

        @pl.when(pair >= 3)
        def _(grad_value=grad_value, cols=cols):
            d_first[:, cols] = grad_value

        d_k[:, cols] = mm(grad_scores, q[:, cols]).astype(BF16)
        d_q[:, cols] = (mm(k[:, cols], grad_scores, TN).T * HD ** (-0.5)).astype(BF16)


def attend_back(q, k, v, att, grad_att, chance):
    queries, keys = q.shape[0], k.shape[0]
    pairs = D // LANE
    by_column = lambda i: (0, i)
    return pl.pallas_call(
        attend_back_kernel,
        out_shape=[
            jax.ShapeDtypeStruct((queries, D), BF16),
            jax.ShapeDtypeStruct((keys, D), BF16),
            jax.ShapeDtypeStruct((keys, HV), BF16),
            jax.ShapeDtypeStruct((keys, HV), F32),
        ],
        grid=(pairs,),
        in_specs=[
            pl.BlockSpec((queries, LANE), by_column),
            pl.BlockSpec((keys, LANE), by_column),
            pl.BlockSpec((keys, LANE), by_column),
            pl.BlockSpec((queries, LANE), by_column),
            pl.BlockSpec((queries, LANE), by_column),
            pl.BlockSpec((2, keys, queries), lambda i: (i, 0, 0)),
        ],
        out_specs=[
            pl.BlockSpec((queries, LANE), by_column),
            pl.BlockSpec((keys, LANE), by_column),
            pl.BlockSpec((keys, LANE), lambda i: (0, jnp.minimum(i, 2))),
            pl.BlockSpec((keys, LANE), lambda i: (0, jnp.maximum(i - 3, 0))),
        ],
        compiler_params=params(60),
        cost_estimate=cost(8 * queries * keys * D, 24 * queries * keys),
        name="attend_back",
    )(q, k, v, att, grad_att, chance)


def project_back_kernel(
    tokens, n1, d_q, d_k, d_fresh, att, resid_low, w_qkv, vec, vec_one,
    grad_near, grad_far, d_rest, vec_grad, flat,
):
    rows = n1.shape[0] // 2
    per_row = D // LANE
    grads = mm(d_k[...], w_qkv[:, D : 2 * D], NT) + mm(d_fresh[...], w_qkv[:, 2 * D :], NT)
    near = grads[:rows] + mm(d_q[...], w_qkv[:, :D], NT)
    far = grads[rows:]
    grad_near[...] = near
    grad_far[...] = far.astype(BF16)
    hat, _ = normed(tokens[...].astype(F32))
    vec_grad[...] = vec_one[...]
    vec_grad[:, :D] = jnp.sum(near * hat[:rows], axis=0, keepdims=True) + jnp.sum(
        far * hat[rows:], axis=0, keepdims=True
    )
    vec_grad[:, D : 2 * D] = jnp.sum(near, axis=0, keepdims=True) + jnp.sum(
        far, axis=0, keepdims=True
    )
    vec_grad[:, 4 * D : 5 * D] = jnp.sum(d_q[...].astype(F32), axis=0, keepdims=True)
    vec_grad[:, 7 * D : 7 * D + HV] = jnp.sum(d_fresh[...].astype(F32), axis=0, keepdims=True)
    pieces = (
        (n1, d_q, rows, 0, per_row),
        (n1, d_k, 2 * rows, D * per_row, per_row),
        (n1, d_fresh, 2 * rows, 2 * D * per_row, HV // LANE),
        (att, resid_low, rows, 2 * D * per_row + D * HV // LANE, per_row),
    )
    for left, right, count, start, columns in pieces:
        product = mm(left[:count], right[:count], TN)
        size = D * columns
        for j in range(columns):
            flat[pl.ds(j, D, stride=columns), :] = product[:, j * LANE : (j + 1) * LANE]
        d_rest[start : start + size] = flat[:size].astype(BF16)
    flat[: 2 * LANE] = jnp.zeros((2 * LANE, LANE), F32)
    for j in range(VEC // LANE):
        flat[j : j + 1] = vec_grad[:, j * LANE : (j + 1) * LANE]
    d_rest[REST:] = flat[: 2 * LANE].astype(BF16)


def project_back(tokens, n1, d_q, d_k, d_fresh, att, resid_low, w_qkv, vec, vec_one):
    rows = n1.shape[0] // 2
    vm = pl.BlockSpec(memory_space=pltpu.VMEM)
    return pl.pallas_call(
        project_back_kernel,
        out_shape=[
            jax.ShapeDtypeStruct((rows, D), F32),
            jax.ShapeDtypeStruct((rows, D), BF16),
            jax.ShapeDtypeStruct((128 * LANE, LANE), BF16),
        ],
        in_specs=[vm] * 10,
        out_specs=[vm] * 3,
        scratch_shapes=[pltpu.VMEM((1, VEC), F32), pltpu.VMEM((D * D // LANE, LANE), F32)],
        compiler_params=params(58),
        cost_estimate=cost(2 * rows * D * (7 * D), 14 * MIB),
        name="project_back",
    )(tokens, n1, d_q, d_k, d_fresh, att, resid_low, w_qkv, vec, vec_one)


def finish_kernel(
    places, grads, weight, one, two,
    resid, near, far, tokens, vec, firsts, firsts_far, vec_weight, vec_one, vec_two,
    new, new_one, new_two, low, tokens_grad, first_grad, new_vec, new_vec_one, new_vec_two,
    stage, flat, vec_stage, v_weight, v_one, v_two, v_low,
    v_resid, v_near, v_far, v_tokens, v_firsts, v_firsts_far,
    slot_sems, in_sems, out_sems, side_sems, vec_sem,
):
    capacity = weight.shape[0]
    rows = flat.shape[0] // LANE
    steps = capacity // rows

    def span(s):
        return pl.ds(s * rows, rows)

    vec_copy = pltpu.make_async_copy(grads.at[pl.ds(REST, vec_stage.shape[0])], vec_stage, vec_sem)
    vec_copy.start()
    brought = []
    for s in range(steps):
        for i, (source, target) in enumerate(((weight, v_weight), (one, v_one), (two, v_two))):
            brought.append(
                pltpu.make_async_copy(source.at[span(s)], target.at[span(s)], in_sems.at[3 * s + i])
            )
            brought[-1].start()

        @pl.loop(0, rows)
        def _(i, s=s):
            slot = s * rows + i
            pltpu.make_async_copy(
                grads.at[pl.ds(pl.multiple_of(jnp.maximum(places[slot], 0) * LANE, LANE), LANE)],
                stage.at[pl.ds(pl.multiple_of(slot * LANE, LANE), LANE)],
                slot_sems.at[s],
            ).start()

    sides = [
        pltpu.make_async_copy(source, target, side_sems.at[i])
        for i, (source, target) in enumerate(
            (
                (resid, v_resid),
                (near, v_near),
                (far, v_far),
                (tokens, v_tokens),
                (firsts, v_firsts),
                (firsts_far, v_firsts_far),
            )
        )
    ]
    for copy in sides:
        copy.start()
    sent = []
    for s in range(steps):
        for copy in brought[3 * s : 3 * s + 3]:
            copy.wait()
        tile = pl.ds(s * rows * LANE, rows * LANE)
        pltpu.make_async_copy(stage.at[tile], stage.at[tile], slot_sems.at[s]).wait()
        flat[...] = stage[tile, :].astype(F32)
        line = lax.broadcasted_iota(jnp.int32, (rows, LANE), 0)
        taken = jnp.zeros((rows, LANE), jnp.int32)
        for i in range(rows):
            taken = jnp.where(line == i, places[s * rows + i], taken)
        keep = taken >= 0
        for c in range(LANE):
            columns = slice(c * LANE, (c + 1) * LANE)
            gradient = jnp.where(keep, flat[pl.ds(c, rows, stride=LANE), :], 0.0)
            after, after_one, after_two = adam_step(
                v_weight[span(s), columns], v_one[span(s), columns], v_two[span(s), columns],
                gradient, RATE_MATRIX, DECAY_MATRIX,
            )
            v_weight[span(s), columns] = after
            v_one[span(s), columns] = after_one
            v_two[span(s), columns] = after_two
            v_low[s, :, columns] = after.astype(BF16)
        for i, (source, target) in enumerate(
            (
                (v_weight.at[span(s)], new.at[span(s)]),
                (v_one.at[span(s)], new_one.at[span(s)]),
                (v_two.at[span(s)], new_two.at[span(s)]),
            )
        ):
            sent.append(pltpu.make_async_copy(source, target, out_sems.at[3 * s + i]))
            sent[-1].start()
    for s in range(steps):
        low[span(s), :] = v_low[s]
    vec_copy.wait()
    count = vec_weight.shape[0]
    after, after_one, after_two = adam_step(
        vec_weight[...], vec_one[...], vec_two[...],
        vec_stage[...].astype(F32)[:count], RATE_VECTOR, 0.0,
    )
    new_vec[...] = after
    new_vec_one[...] = after_one
    new_vec_two[...] = after_two
    for copy in sides:
        copy.wait()
    grad = v_near[...] + v_far[...].astype(F32)
    hat, rate = normed(v_tokens[...].astype(F32))
    v_resid[...] += norm_back(grad, hat, rate, vec_part(vec, 0))
    for i in range(HV // LANE):
        columns = slice(i * LANE, (i + 1) * LANE)
        v_firsts[:, columns] += v_firsts_far[i].astype(F32)
    for i, (source, target) in enumerate(((v_resid, tokens_grad), (v_firsts, first_grad))):
        sent.append(pltpu.make_async_copy(source, target, side_sems.at[i]))
        sent[-1].start()
    for copy in sent:
        copy.wait()


def finish(places, grads, weight, one, two, resid, near, far, tokens, vec, firsts, firsts_far, vectors):
    capacity, tile_len = weight.shape
    rows = 8 if capacity % 8 == 0 else capacity
    steps = capacity // rows
    flat_vec = vectors[0].shape
    any_space = pl.BlockSpec(memory_space=pl.ANY)
    sides = [resid, near, far, tokens, firsts, firsts_far]
    return pl.pallas_call(
        finish_kernel,
        out_shape=[jax.ShapeDtypeStruct(weight.shape, F32)] * 3
        + [jax.ShapeDtypeStruct(weight.shape, BF16)]
        + [jax.ShapeDtypeStruct(resid.shape, F32), jax.ShapeDtypeStruct(firsts.shape, F32)]
        + [jax.ShapeDtypeStruct(flat_vec, F32)] * 3,
        grid_spec=pltpu.PrefetchScalarGridSpec(
            num_scalar_prefetch=1,
            grid=(1,),
            in_specs=[any_space] * 8
            + [whole((1, VEC))]
            + [any_space] * 2
            + [whole(flat_vec)] * 3,
            out_specs=[any_space] * 3 + [whole(weight.shape)] + [any_space] * 2 + [whole(flat_vec)] * 3,
            scratch_shapes=[
                pltpu.VMEM((capacity * LANE, LANE), BF16),
                pltpu.VMEM((rows * LANE, LANE), F32),
                pltpu.VMEM((80, LANE), BF16),
                pltpu.VMEM(weight.shape, F32),
                pltpu.VMEM(weight.shape, F32),
                pltpu.VMEM(weight.shape, F32),
                pltpu.VMEM((steps, rows, tile_len), BF16),
            ]
            + [pltpu.VMEM(side.shape, side.dtype) for side in sides]
            + [
                pltpu.SemaphoreType.DMA((steps,)),
                pltpu.SemaphoreType.DMA((3 * steps,)),
                pltpu.SemaphoreType.DMA((3 * steps,)),
                pltpu.SemaphoreType.DMA((len(sides),)),
                pltpu.SemaphoreType.DMA,
            ],
        ),
        compiler_params=params(60),
        cost_estimate=cost(20 * capacity * tile_len, 28 * capacity * tile_len, 2 * capacity * tile_len),
        name="finish",
    )(places, grads, weight, one, two, resid, near, far, tokens, vec, firsts, firsts_far, *vectors)


class Links:
    def __init__(self, line, send_sems, recv_sems):
        dp = lax.axis_index("dp")
        self.line = line
        self.y = lax.axis_index("seq")
        self.z = dp // 4
        self.x = (dp // 2) % 2
        self.c = dp % 2
        self.send_sems, self.recv_sems = send_sems, recv_sems
        self.to = {
            "core": {"dp": self.z * 4 + self.x * 2 + (1 - self.c)},
            "x": {"dp": self.z * 4 + (1 - self.x) * 2 + self.c},
            "y": {"seq": 1 - self.y},
            "up": {"dp": dp + 4},
            "down": {"dp": dp - 4},
        }
        self.sent = []

    def greet(self, whole_line, meanwhile=lambda: None):
        barrier = pltpu.get_barrier_semaphore()
        for name in ("core", "x", "y"):
            pl.semaphore_signal(barrier, inc=1, device_id=self.to[name])
        if whole_line:
            for d in range(1, self.line):
                z = (self.z + d) % self.line
                pl.semaphore_signal(barrier, inc=1, device_id={"dp": z * 4 + self.x * 2 + self.c})
            meanwhile()
            pl.semaphore_wait(barrier, 2 + self.line)
            return

        @pl.when(self.z > 0)
        def _():
            pl.semaphore_signal(barrier, inc=1, device_id=self.to["down"])

        @pl.when(self.z < self.line - 1)
        def _():
            pl.semaphore_signal(barrier, inc=1, device_id=self.to["up"])

        meanwhile()
        pl.semaphore_wait(
            barrier,
            3 + jnp.where(self.z > 0, 1, 0) + jnp.where(self.z < self.line - 1, 1, 0),
        )

    def copy(self, source, target, index, way):
        sender, receiver = index if isinstance(index, tuple) else (index, index)
        to = self.to[way] if isinstance(way, str) else {"dp": way * 4 + self.x * 2 + self.c}
        return pltpu.make_async_remote_copy(
            src_ref=source,
            dst_ref=target,
            send_sem=self.send_sems.at[sender],
            recv_sem=self.recv_sems.at[receiver],
            device_id=to,
        )

    def send(self, describe):
        source, target, index, way, when = describe()
        if when is None:
            self.copy(source, target, index, way).start()
        else:

            @pl.when(when)
            def _():
                self.copy(source, target, index, way).start()

        self.sent.append(describe)

    def arrive(self, target, index, way):
        self.copy(target, target, index, way).wait_recv()

    def finish(self):
        for describe in self.sent:
            source, target, index, way, when = describe()
            if when is None:
                self.copy(source, target, index, way).wait_send()
            else:

                @pl.when(when)
                def _(source=source, target=target, index=index, way=way):
                    self.copy(source, target, index, way).wait_send()


def add_into(place, *others):
    total = place[...].astype(F32)
    for other in others:
        total = total + other[...].astype(F32)
    place[...] = total.astype(BF16)


class Scatter:
    KINDS = ("core", "xa", "yb", "ya", "xb", "to", "from")

    def __init__(self, links, base, source, offset, rows, cut, buffers, load_sems):
        self.k, self.base, self.source, self.offset, self.rows = links, base, source, offset, rows
        self.held, self.r_core, self.r_xa, self.r_yb, self.r_ya, self.r_xb, self.r_line = buffers
        self.load_sems = load_sems
        self.halves = (pl.ds(0, cut), pl.ds(cut, rows - cut))

    @staticmethod
    def buffers_of(rows, cut, line):
        return [
            pltpu.VMEM((line, 2, 2, rows, LANE), BF16),
            pltpu.VMEM((line, 4 * rows, LANE), BF16),
            pltpu.VMEM((line, 2, cut, LANE), BF16),
            pltpu.VMEM((line, 2, rows - cut, LANE), BF16),
            pltpu.VMEM((line, cut, LANE), BF16),
            pltpu.VMEM((line, rows - cut, LANE), BF16),
            pltpu.VMEM((line, rows, LANE), BF16),
        ]

    def at(self, kind, z):
        return self.base + self.KINDS.index(kind) * self.k.line + z

    def load(self, z):
        start = self.offset + (self.k.c * self.k.line + z) * 4 * self.rows
        return [
            pltpu.make_async_copy(
                self.source.at[pl.ds(pl.multiple_of(start + i * self.rows, 16), self.rows)],
                self.held.at[z, i // 2, i % 2],
                self.load_sems.at[4 * z + i],
            )
            for i in range(4)
        ]

    def begin(self):
        k = self.k

        def describe(z):
            start = self.offset + ((1 - k.c) * k.line + z) * 4 * self.rows
            source = self.source.at[pl.ds(pl.multiple_of(start, 16), 4 * self.rows)]
            return source, self.r_core.at[z], self.at("core", z), "core", None

        for z in range(k.line):
            k.send(functools.partial(describe, z))
            for copy in self.load(z):
                copy.start()

    def first(self, z):
        k, (a, b) = self.k, self.halves
        for copy in self.load(z):
            copy.wait()
        k.arrive(self.r_core.at[z], self.at("core", z), "core")
        for i in range(4):
            add_into(self.held.at[z, i // 2, i % 2], self.r_core.at[z, pl.ds(i * self.rows, self.rows)])
        k.send(lambda: (self.held.at[z, 1 - k.x, :, a], self.r_xa.at[z], self.at("xa", z), "x", None))
        k.send(lambda: (self.held.at[z, :, 1 - k.y, b], self.r_yb.at[z], self.at("yb", z), "y", None))

    def second(self, z):
        k, (a, b) = self.k, self.halves
        k.arrive(self.r_xa.at[z], self.at("xa", z), "x")
        for y in range(2):
            add_into(self.held.at[z, k.x, y, a], self.r_xa.at[z, y])
        k.send(lambda: (self.held.at[z, k.x, 1 - k.y, a], self.r_ya.at[z], self.at("ya", z), "y", None))
        k.arrive(self.r_yb.at[z], self.at("yb", z), "y")
        for x in range(2):
            add_into(self.held.at[z, x, k.y, b], self.r_yb.at[z, x])
        k.send(lambda: (self.held.at[z, 1 - k.x, k.y, b], self.r_xb.at[z], self.at("xb", z), "x", None))

    def third(self, z):
        k, (a, b) = self.k, self.halves
        k.arrive(self.r_ya.at[z], self.at("ya", z), "y")
        add_into(self.held.at[z, k.x, k.y, a], self.r_ya.at[z])
        k.arrive(self.r_xb.at[z], self.at("xb", z), "x")
        add_into(self.held.at[z, k.x, k.y, b], self.r_xb.at[z])

        def describe():
            index = (self.at("to", z), self.at("from", k.z))
            return self.held.at[z, k.x, k.y], self.r_line.at[k.z], index, z, k.z != z

        k.send(describe)

    def last(self):
        k = self.k
        others = [(k.z + d) % k.line for d in range(1, k.line)]
        for z in others:
            k.arrive(self.r_line.at[z], (self.at("to", z), self.at("from", z)), z)
        add_into(self.held.at[k.z, k.x, k.y], *[self.r_line.at[z] for z in others])


class Spread:
    KINDS = ("xa", "yb", "ya", "xb", "ya2", "xb2") + tuple(
        f"{way}{i}" for way in ("to", "from", "c") for i in range(4)
    )

    def __init__(self, links, base, piece, out, index, first, rows, cut):
        self.k, self.base, self.piece, self.out, self.index = links, base, piece, out, index
        self.parts = {None: (first, rows), 0: (first, cut), 1: (first + cut, rows - cut)}

    def own(self, half):
        first, count = self.parts[half]
        return self.piece(pl.ds(first, count))

    def at(self, kind, z):
        return self.base + self.KINDS.index(kind) * self.k.line + z

    def spot(self, z, other_x, other_y, half=None, core=None):
        k = self.k
        c = k.c if core is None else core
        x = 1 - k.x if other_x else k.x
        y = 1 - k.y if other_y else k.y
        first, count = self.parts[half]
        return self.out.at[pl.ds(pl.multiple_of(self.index(c, z, x, y) + first, 16), count)]

    def place(self, d):
        return (self.k.z + d) % self.k.line

    def give(self, kind, way, d, other_x=False, other_y=False, half=None, own=False):
        def describe():
            z = self.place(d)
            target = self.spot(z, other_x, other_y, half)
            source = self.own(half) if own else target
            return source, target, self.at(kind, z), way, None

        self.k.send(describe)

    def get(self, kind, way, d, other_x=False, other_y=False, half=None):
        z = self.place(d)
        self.k.arrive(self.spot(z, other_x, other_y, half), self.at(kind, z), way)

    def lift(self, i, own=False):
        k = self.k
        place = dict(other_x=i >= 2, other_y=i % 2 == 1)

        def describe(d):
            z = self.place(d)
            target = self.spot(k.z, **place)
            source = self.own(None) if own else target
            return source, target, (self.at(f"to{i}", z), self.at(f"from{i}", k.z)), z, None

        for d in (k.line - 1, 1, 2):
            k.send(functools.partial(describe, d))

    def land(self, d, i):
        z = self.place(d)
        place = dict(other_x=i >= 2, other_y=i % 2 == 1)
        self.k.arrive(self.spot(z, **place), (self.at(f"to{i}", z), self.at(f"from{i}", z)), z)

    def cross(self, d):
        own = d == 0
        self.give("xa", "x", d, half=0, own=own)
        self.give("yb", "y", d, half=1, own=own)
        self.give("ya", "y", d, half=0, own=own)
        self.give("xb", "x", d, half=1, own=own)
        self.give("c0", "core", d, own=own)

    def start(self):
        self.lift(0, True)
        self.cross(0)

    def along(self, d):
        self.land(d, 0)
        self.cross(d)

    def turn(self, d):
        self.get("xa", "x", d, other_x=True, half=0)
        self.give("ya2", "y", d, other_x=True, half=0)
        self.get("yb", "y", d, other_y=True, half=1)
        self.give("xb2", "x", d, other_y=True, half=1)

    def share(self, d, late=False):
        self.get("ya", "y", d, other_y=True, half=0)
        self.give("c1", "core", d, other_y=True)
        if late:
            self.lift(1)
        self.get("xb", "x", d, other_x=True, half=1)
        self.give("c2", "core", d, other_x=True)
        if late:
            self.lift(2)
        self.get("ya2", "y", d, other_x=True, other_y=True, half=0)
        self.get("xb2", "x", d, other_x=True, other_y=True, half=1)
        self.give("c3", "core", d, other_x=True, other_y=True)
        if late:
            self.lift(3)

    def along_late(self, d):
        for i in range(4):
            self.land(d, i)
            self.give(f"c{i}", "core", d, other_x=i >= 2, other_y=i % 2 == 1)

    def end(self):
        k = self.k
        for z in range(k.line):
            for i in range(4):
                k.arrive(self.spot(z, i >= 2, i % 2 == 1, core=1 - k.c), self.at(f"c{i}", z), "core")


RS_SEMS = len(Scatter.KINDS)
AR_SEMS = RS_SEMS + 2 * len(Spread.KINDS)


class Total:
    def __init__(self, links, base, source, offset, kind, out, top, buffers, load_sems, copy_sem):
        line = links.line
        size, cut, turn, plain = kind
        rows = size // (8 * line)
        held = buffers[0]

        def index(c, z, x, y):
            return top + (((c * line + z) * 2 + x) * 2 + y) * rows

        def piece(span):
            return held.at[links.z, links.x, links.y, span]

        self.k, self.piece, self.out, self.index, self.rows = links, piece, out, index, rows
        self.scatter = Scatter(links, base, source, offset, rows, cut, buffers, load_sems)
        base = base + RS_SEMS * line
        self.spread = Spread(links, base, piece, out, index, 0, plain, turn)
        self.late = None
        if plain < rows:
            base = base + len(Spread.KINDS) * line
            rest = rows - plain
            self.late = Spread(links, base, piece, out, index, plain, rest, rest // 32 * 16)
        self.copy_sem = copy_sem

    def keep(self):
        k = self.k
        start = pl.multiple_of(self.index(k.c, k.z, k.x, k.y), 16)
        return pltpu.make_async_copy(
            self.piece(pl.ds(0, self.rows)), self.out.at[pl.ds(start, self.rows)], self.copy_sem
        )

    def run(self, stage, part):
        scatter, spread, late = self.scatter, self.spread, self.late
        if stage == 0:
            scatter.begin()
        elif stage < 4:
            (scatter.first, scatter.second, scatter.third)[stage - 1](part)
        elif stage == 4:
            scatter.last()
            self.keep().start()
            spread.start()
            if late is not None:
                late.start()
        elif stage == 5 and part < 3:
            spread.along(part + 1)
        elif stage == 5 and part == 3:
            late.turn(0)
        elif stage == 5 and part == 4:
            late.share(0, True)
        elif stage == 5:
            late.along_late(part - 4)
        elif stage < 8:
            (spread.turn, spread.share)[stage - 6](part)
        else:
            self.keep().wait()
            spread.end()
            if late is not None:
                late.end()


class Gather:
    KINDS = ("up", "down", "xa", "yb", "ya", "xb", "ya2", "xb2", "x2") + tuple(
        f"{way}{i}" for way in ("u", "d", "c") for i in range(4)
    )

    def __init__(self, links, base, own, out, index, first, rows, cut, z_first, twice):
        self.k, self.base, self.own, self.out, self.index = links, base, own, out, index
        self.parts = {None: (first, rows), 0: (first, cut), 1: (first + cut, rows - cut)}
        self.z_first, self.twice = z_first, twice

    def at(self, kind, z):
        return self.base + self.KINDS.index(kind) * self.k.line + z

    def spot(self, z, other_x, other_y, half=None, core=None):
        k = self.k
        c = k.c if core is None else core
        x = 1 - k.x if other_x else k.x
        y = 1 - k.y if other_y else k.y
        first, count = self.parts[half]
        return self.out.at[pl.ds(pl.multiple_of(self.index(c, z, x, y) + first, 16), count)]

    def give(self, kind, way, z, other_x=False, other_y=False, half=None, when=None, own=False):
        def describe():
            place = self.spot(z(), other_x, other_y, half)
            source = self.own(other_y, half) if own else place
            return source, place, self.at(kind, z()), way, None if when is None else when()

        self.k.send(describe)

    def get(self, kind, way, z, other_x=False, other_y=False, half=None):
        self.k.arrive(self.spot(z, other_x, other_y, half), self.at(kind, z), way)

    def near(self):
        k = self.k
        found = []
        for r in range(1, k.line):
            found.append(
                (
                    lambda r=r: k.z - r,
                    lambda r=r: k.z >= r,
                    "u",
                    "up",
                    lambda r=r: (k.z >= r) & (k.z < k.line - 1),
                )
            )
            found.append(
                (
                    lambda r=r: k.z + r,
                    lambda r=r: k.z + r < k.line,
                    "d",
                    "down",
                    lambda r=r: (k.z + r < k.line) & (k.z > 0),
                )
            )
        return found

    def here(self):
        return self.k.z

    def lower(self):
        return self.k.z < self.k.line - 1

    def upper(self):
        return self.k.z > 0

    def cross(self, z, when, own):
        self.give("xa", "x", z, half=0, when=when, own=own)
        self.give("yb", "y", z, half=1, when=when, own=own)
        self.give("ya", "y", z, half=0, when=when, own=own)
        self.give("xb", "x", z, half=1, when=when, own=own)
        self.give("c0", "core", z, when=when, own=own)

    def start(self):
        self.give("up", "up", self.here, when=self.lower, own=True)
        self.give("down", "down", self.here, when=self.upper, own=True)
        if self.twice:
            for other, kind in ((False, "xa"), (True, "x2")):
                self.give(kind, "x", self.here, other_y=other, own=True)
                self.give("c1" if other else "c0", "core", self.here, other_y=other, own=True)
        else:
            self.cross(self.here, None, True)

    def along(self, number):
        z, exists, _, way, goes_on = self.near()[number]

        @pl.when(exists())
        def _():
            self.get(way, way, z())

        self.give(way, way, z, when=goes_on)
        self.cross(z, exists, False)

    def turn(self, z, when):
        def waits():
            self.get("xa", "x", z(), other_x=True, half=0)

        def waits_too():
            self.get("yb", "y", z(), other_y=True, half=1)

        waits() if when is None else pl.when(when())(waits)
        self.give("ya2", "y", z, other_x=True, half=0, when=when)
        waits_too() if when is None else pl.when(when())(waits_too)
        self.give("xb2", "x", z, other_y=True, half=1, when=when)

    def share(self, z, when):
        def waits(kind, way, **place):
            def wait():
                self.get(kind, way, z(), **place)

            wait() if when is None else pl.when(when())(wait)

        waits("ya", "y", other_y=True, half=0)
        self.give("c1", "core", z, other_y=True, when=when)
        waits("xb", "x", other_x=True, half=1)
        self.give("c2", "core", z, other_x=True, when=when)
        waits("ya2", "y", other_x=True, other_y=True, half=0)
        waits("xb2", "x", other_x=True, other_y=True, half=1)
        self.give("c3", "core", z, other_x=True, other_y=True, when=when)

    def share_twice(self):
        for other, kind in ((False, "xa"), (True, "x2")):
            self.get(kind, "x", self.k.z, other_x=True, other_y=other)
            self.give("c3" if other else "c2", "core", self.here, other_x=True, other_y=other)

    def lift(self, i, own=False):
        place = dict(other_x=i >= 2, other_y=i % 2 == 1)
        self.give(f"u{i}", "up", self.here, when=self.lower, own=own, **place)
        self.give(f"d{i}", "down", self.here, when=self.upper, own=own, **place)
        self.give(f"c{i}", "core", self.here, own=own, **place)

    def start_plane(self):
        if self.twice:
            for other, kind in ((False, "xa"), (True, "x2")):
                self.give(kind, "x", self.here, other_y=other, own=True)
            self.lift(0, True)
            self.lift(1, True)
        else:
            self.give("xa", "x", self.here, half=0, own=True)
            self.give("yb", "y", self.here, half=1, own=True)
            self.give("ya", "y", self.here, half=0, own=True)
            self.give("xb", "x", self.here, half=1, own=True)
            self.lift(0, True)

    def turn_plane(self):
        if self.twice:
            for other, kind in ((False, "xa"), (True, "x2")):
                self.get(kind, "x", self.k.z, other_x=True, other_y=other)
                self.lift(3 if other else 2)
        else:
            self.turn(self.here, None)

    def lift_plane(self):
        if not self.twice:
            z = self.k.z
            self.get("ya", "y", z, other_y=True, half=0)
            self.lift(1)
            self.get("xb", "x", z, other_x=True, half=1)
            self.lift(2)
            self.get("ya2", "y", z, other_x=True, other_y=True, half=0)
            self.get("xb2", "x", z, other_x=True, other_y=True, half=1)
            self.lift(3)

    def along_plane(self, number, i):
        z, exists, letter, way, goes_on = self.near()[number]
        place = dict(other_x=i >= 2, other_y=i % 2 == 1)

        @pl.when(exists())
        def _():
            self.get(f"{letter}{i}", way, z(), **place)

        self.give(f"{letter}{i}", way, z, when=goes_on, **place)
        self.give(f"c{i}", "core", z, when=exists, **place)

    def steps(self):
        count = 2 * (self.k.line - 1)
        if self.z_first:
            one = [self.start]
            two = [lambda n=n: self.along(n) for n in range(count)]
            spots = [(z, exists) for z, exists, _, _, _ in self.near()]
            if not self.twice:
                spots = [(self.here, None)] + spots
            three = [lambda z=z, e=e: self.turn(z, e) for z, e in spots]
            four = [lambda z=z, e=e: self.share(z, e) for z, e in spots]
            if self.twice:
                four = [self.share_twice] + four
            return [one, two, three, four]
        one = [self.start_plane]
        two = [self.turn_plane]
        three = [self.lift_plane]
        four = [lambda n=n, i=i: self.along_plane(n, i) for n in range(count) for i in range(4)]
        return [one, two, three, four]

    def end(self):
        k = self.k
        for z in range(k.line):
            for i in range(4):
                k.arrive(
                    self.spot(z, i >= 2, i % 2 == 1, core=1 - k.c), self.at(f"c{i}", z), "core"
                )


AG_SEMS = len(Gather.KINDS)


def all_gather_kernel(line, swaps, cuts, masters, *refs):
    near, out, far = refs[:swaps], refs[swaps], refs[swaps + 1 : 2 * swaps + 1]
    piece, flat, send_sems, recv_sems, copy_sem = refs[2 * swaps + 1 :]
    links = Links(line, send_sems, recv_sems)

    def pack():
        rows = flat.shape[0] // LANE
        for top in range(0, masters.shape[0], rows):
            pack_rows(masters.at[pl.ds(top, rows)], flat)
            piece[top * LANE : (top + rows) * LANE] = flat[...].astype(BF16)

    links.greet(False, pack)
    rows = piece.shape[0] // 2
    first_rows, second_rows = cuts
    spare = 2 * AG_SEMS * line

    def index(c, z, x, y):
        return (((z * 2 + x) * 2 + c) * 2 + y) * rows

    def keep():
        start = index(links.c, links.z, links.x, 0)
        return pltpu.make_async_copy(
            piece, out.at[pl.ds(pl.multiple_of(start, 16), 2 * rows)], copy_sem
        )

    gathers = []

    def own_of(first, count, cut):
        def own(other, half):
            begin, size = {None: (0, count), 0: (0, cut), 1: (cut, count - cut)}[half]
            y = 1 - links.y if other else links.y
            return piece.at[pl.ds(pl.multiple_of(y * rows + first + begin, 16), size)]

        return own

    last = rows - first_rows - second_rows
    spans = ((0, first_rows + second_rows, first_rows, True), (first_rows + second_rows, last, last // 32 * 16, False))
    for number, (first, count, cut, z_first) in enumerate(spans):
        gathers.append(
            Gather(
                links, number * AG_SEMS * line, own_of(first, count, cut), out, index,
                first, count, cut, z_first, True,
            )
        )
    flat, tall = gathers[0].steps(), gathers[1].steps()
    for step in flat[0] + tall[0]:
        step()
    keep().start()
    for i in range(swaps):
        links.send(lambda i=i: (near[i], far[i], spare + i, "y", None))
    along, rise = flat[1], tall[1] + tall[2]
    turn, share, climb = flat[2], flat[3], tall[3]
    for step in along[:2] + rise + turn[:2] + along[2:4] + climb[:8] + turn[2:4] + along[4:]:
        step()
    for step in climb[8:16] + turn[4:] + share[:3] + climb[16:] + share[3:]:
        step()
    for gather in gathers:
        gather.end()
    keep().wait()
    for i in range(swaps):
        links.arrive(far[i], spare + i, "y")
    links.finish()


def all_gather(masters, swaps, line, collective_id):
    any_space = pl.BlockSpec(memory_space=pl.ANY)
    sems = 2 * AG_SEMS * line + len(swaps)
    count = masters.shape[0] * LANE
    rows = count // 2
    cuts = (rows * 2 // 5 // 16 * 16, rows * 2 // 5 // 16 * 16)
    return pl.pallas_call(
        functools.partial(all_gather_kernel, line, len(swaps), cuts),
        out_shape=[jax.ShapeDtypeStruct((4 * line * count, LANE), BF16)]
        + [jax.ShapeDtypeStruct(s.shape, s.dtype) for s in swaps],
        in_specs=[pl.BlockSpec(memory_space=pltpu.VMEM)] + [any_space] * len(swaps),
        out_specs=[any_space] * (1 + len(swaps)),
        scratch_shapes=[
            pltpu.VMEM((count, LANE), BF16),
            pltpu.VMEM((8 * LANE, LANE), F32),
            pltpu.SemaphoreType.DMA((sems,)),
            pltpu.SemaphoreType.DMA((sems,)),
            pltpu.SemaphoreType.DMA,
        ],
        compiler_params=params(60, collective_id=collective_id, has_side_effects=True),
        cost_estimate=cost(0, 100 * MIB),
        name="all_gather",
    )(masters, *swaps)


PAIRS = D // LANE
UP_ROWS = FF * D // LANE
REST_ROWS = 128 * LANE
HEAD, NORM, LAST = 900, 901, 902
ORDER = (
    100, 0, HEAD, HEAD, 110, 111, 112, 113, 10, 11, 120, HEAD, HEAD, 121, HEAD, HEAD, 122, HEAD,
    HEAD, 123, 12, 13, HEAD, HEAD, HEAD, HEAD, NORM, 130, 20, 21, 131, 132, 133, LAST, 200, 22,
    23, 210, 211, 212, 213, 140, 150, 30, 31, 32, 33, 220, 221, 222, 40, 223, 160, 161, 153, 50,
    51, 52, 230, 231, 232, 233, 53, 170, 171, 154, 151, 152, 60, 61, 240, 155, 54, 62, 63, 250,
    156, 157, 162, 163, 70, 253, 251, 252, 260, 71, 72, 73, 172, 173, 180, 55, 254, 56, 261,
    262, 57, 80, 270, 271, 263, 272, 273, 255, 256, 257, 280,
)


def segments():
    found = [[]]
    for step in ORDER:
        if step >= HEAD:
            found.append([])
        else:
            found[-1].append((step // 100, step // 10 % 10, step % 10))
    return found


def total_kinds(line):
    kinds = []
    for size, late in ((UP_ROWS, 20), (UP_ROWS, 20), (REST_ROWS, 30)):
        rows = size // (8 * line)
        plain = rows - rows * late // 100 // 32 * 32
        kinds.append((size, rows * 72 // 100 // 16 * 16, plain * 30 // 100 // 16 * 16, plain))
    return kinds


def back_kernel(
    line,
    q, k, v, att, grad_att, chance, tokens, tokens_far, n1, att_all, resid_low, w_qkv, vec, vec_one, d_up, d_down,
    d_first, grad_near, out, grad_back, first_back,
    d_q, d_k, d_v, far, d_rest, vec_grad, flat, *scratch,
):
    step = pl.program_id(0)
    sources = (tokens, tokens_far, n1, att_all, resid_low, w_qkv)
    late, late_sems, scratch = scratch[:6], scratch[6], scratch[7:]
    copies = [
        pltpu.make_async_copy(source, target, late_sems.at[i])
        for i, (source, target) in enumerate(zip(sources, late))
    ]
    buffers, (send_sems, recv_sems, load_sems, copy_sems) = scratch[:-4], scratch[-4:]
    links = Links(line, send_sems, recv_sems)
    tops = (REST_ROWS + UP_ROWS, REST_ROWS, 0)
    totals = [
        Total(
            links, g * AR_SEMS * line, source, 0, kind, out, top,
            buffers[7 * g : 7 * g + 7], load_sems.at[g], copy_sems.at[g],
        )
        for g, (source, kind, top) in enumerate(zip((d_down, d_up, d_rest), total_kinds(line), tops))
    ]
    spare = len(totals) * AR_SEMS * line
    plan = segments()

    def run(number):
        for g, stage, part in plan[number]:
            totals[g].run(stage, part)

    queries = q.shape[0]
    for head in range(2):
        for s in range(PAIRS):

            @pl.when(step == s)
            def _(s=s, head=head):
                if s == 0 and head == 0:
                    links.greet(True)
                    for copy in copies:
                        copy.start()
                run(2 * s + head)

        @pl.when(step < PAIRS)
        def _(head=head):
            cols = slice(head * HD, (head + 1) * HD)
            grad = grad_att[:, cols]
            weights = chance[head]
            shared = grad.astype(F32) * att[:, cols].astype(F32)
            delta = jnp.sum(shared.T, axis=0, keepdims=True)
            grad_chance = mm(v[:, cols], grad, NT)
            grad_scores = (weights.astype(F32) * (grad_chance - delta)).astype(BF16)
            grad_value = mm(weights, grad)

            d_v[step, :, cols] = grad_value.astype(BF16)
            d_first[:, cols] = grad_value[:queries]
            d_k[step, :, cols] = mm(grad_scores, q[:, cols]).astype(BF16)
            d_q[step, :, cols] = (mm(k[:, cols], grad_scores, TN).T * HD ** (-0.5)).astype(BF16)

    @pl.when(step == PAIRS)
    def _():
        for copy in copies:
            copy.wait()
        tokens, tokens_far, n1, att_all, resid_low, w_qkv = late
        rows = n1.shape[0] // 2
        per_row = D // LANE
        rows = n1.shape[0] // 2
        first_far = d_v.at[pl.ds(PAIRS // 2, PAIRS // 2), pl.ds(rows, rows)]
        links.send(lambda: (first_far, first_back, spare, "y", None))
        run(2 * PAIRS)
        dq = jnp.concatenate([d_q[i] for i in range(PAIRS)], axis=1)
        dk = jnp.concatenate([d_k[i] for i in range(PAIRS)], axis=1)
        dv = jnp.concatenate([d_v[i] for i in range(PAIRS // 2)], axis=1)
        grads = mm(dk, w_qkv[:, D : 2 * D], NT) + mm(dv, w_qkv[:, 2 * D :], NT)
        beside = grads[rows:]
        far[...] = beside.astype(BF16)
        links.send(lambda: (far, grad_back, spare + 1, "y", None))
        near = grads[:rows] + mm(dq, w_qkv[:, :D], NT)
        grad_near[...] = near
        hat, _ = normed(tokens[...].astype(F32))
        hat_far, _ = normed(tokens_far[...].astype(F32))
        vec_grad[...] = vec_one[...]
        vec_grad[:, :D] = jnp.sum(near * hat, axis=0, keepdims=True) + jnp.sum(
            beside * hat_far, axis=0, keepdims=True
        )
        vec_grad[:, D : 2 * D] = jnp.sum(near, axis=0, keepdims=True) + jnp.sum(
            beside, axis=0, keepdims=True
        )
        vec_grad[:, 4 * D : 5 * D] = jnp.sum(dq.astype(F32), axis=0, keepdims=True)
        vec_grad[:, 7 * D : 7 * D + HV] = jnp.sum(dv.astype(F32), axis=0, keepdims=True)
        run(2 * PAIRS + 1)
        pieces = (
            (n1[:rows], dq, 0, per_row),
            (n1[...], dk, D * per_row, per_row),
            (n1[...], dv, 2 * D * per_row, HV // LANE),
            (att_all[...], resid_low[...], 2 * D * per_row + D * HV // LANE, per_row),
        )
        for left, right, start, columns in pieces:
            product = mm(left, right, TN)
            size = D * columns
            for j in range(columns):
                flat[pl.ds(j, D, stride=columns), :] = product[:, j * LANE : (j + 1) * LANE]
            d_rest[start : start + size] = flat[:size].astype(BF16)
        flat[: 2 * LANE] = jnp.zeros((2 * LANE, LANE), F32)
        for j in range(VEC // LANE):
            flat[j : j + 1] = vec_grad[:, j * LANE : (j + 1) * LANE]
        d_rest[REST:] = flat[: 2 * LANE].astype(BF16)
        run(2 * PAIRS + 2)
        links.arrive(first_back, spare, "y")
        links.arrive(grad_back, spare + 1, "y")
        links.finish()


def back(q, k, v, att, grad_att, chance, tokens, tokens_far, n1, resid_low, w_qkv, vec, vec_one, d_up, d_down, line):
    rows, keys = q.shape[0], k.shape[0]
    any_space = pl.BlockSpec(memory_space=pl.ANY)

    def column(count):
        return pl.BlockSpec((count, LANE), lambda i: (0, jnp.minimum(i, PAIRS - 1)))

    def once(array):
        return pl.BlockSpec(array.shape, lambda i: (0,) * array.ndim, pipeline_mode=pl.Buffered(1))

    kinds = total_kinds(line)
    scratch = []
    for size, cut, _, _ in kinds:
        scratch += Scatter.buffers_of(size // (8 * line), cut, line)
    sems = len(kinds) * AR_SEMS * line + 2
    return pl.pallas_call(
        functools.partial(back_kernel, line),
        out_shape=[
            jax.ShapeDtypeStruct((rows, HV), F32),
            jax.ShapeDtypeStruct((rows, D), F32),
            jax.ShapeDtypeStruct((REST_ROWS + 2 * UP_ROWS, LANE), BF16),
            jax.ShapeDtypeStruct((rows, D), BF16),
            jax.ShapeDtypeStruct((PAIRS // 2, rows, LANE), BF16),
        ],
        grid=(PAIRS + 1,),
        in_specs=[
            column(rows),
            column(keys),
            column(keys),
            column(rows),
            column(rows),
            pl.BlockSpec((2, keys, rows), lambda i: (jnp.minimum(i, PAIRS - 1), 0, 0)),
            any_space,
            any_space,
            any_space,
            any_space,
            any_space,
            any_space,
            once(vec),
            once(vec_one),
            any_space,
            any_space,
        ],
        out_specs=[
            pl.BlockSpec((rows, LANE), lambda i: (0, jnp.clip(i - 3, 0, 2))),
            pl.BlockSpec((rows, D), lambda i: (0, 0), pipeline_mode=pl.Buffered(1)),
            any_space,
            any_space,
            any_space,
        ],
        scratch_shapes=[
            pltpu.VMEM((PAIRS, rows, LANE), BF16),
            pltpu.VMEM((PAIRS, keys, LANE), BF16),
            pltpu.VMEM((PAIRS, keys, LANE), BF16),
            pltpu.VMEM((rows, D), BF16),
            pltpu.VMEM((REST_ROWS, LANE), BF16),
            pltpu.VMEM((1, VEC), F32),
            pltpu.VMEM((D * D // LANE, LANE), F32),
        ]
        + [pltpu.VMEM(a.shape, a.dtype) for a in (tokens, tokens_far, n1, att, resid_low, w_qkv)]
        + [pltpu.SemaphoreType.DMA((6,))]
        + scratch
        + [
            pltpu.SemaphoreType.DMA((sems,)),
            pltpu.SemaphoreType.DMA((sems,)),
            pltpu.SemaphoreType.DMA((len(kinds), 4 * line)),
            pltpu.SemaphoreType.DMA((len(kinds),)),
        ],
        compiler_params=params(62, collective_id=0, has_side_effects=True),
        cost_estimate=cost(8 * rows * keys * D + 14 * rows * D * D, 100 * MIB),
        name="back",
    )(q, k, v, att, grad_att, chance, tokens, tokens_far, n1, att, resid_low, w_qkv, vec, vec_one, d_up, d_down)


def swap(value):
    return lax.ppermute(value, "seq", [(0, 1), (1, 0)])


def shards(
    tokens,
    first_values,
    out_grad,
    block_place,
    owners,
    masters,
    moment_one,
    moment_two,
    vector_master,
    vector_moment_one,
    vector_moment_two,
):
    capacity = masters.shape[0]
    dp_count = lax.axis_size("dp")
    tile_count = owners.shape[0]
    dp_here = lax.axis_index("dp")
    seq_here = lax.axis_index("seq")
    _, half_len, _ = tokens.shape

    tokens = tokens.reshape(half_len, D)
    firsts = first_values.reshape(half_len, HV)
    given = out_grad.reshape(half_len, D)
    line = dp_count // 4
    if line == LINE and capacity % 8 == 0:
        slots, tokens_far, firsts_far = all_gather(masters, [tokens, firsts], line, 1)
    else:
        tokens_far, firsts_far = swap(tokens), swap(firsts)
        slots = lax.all_gather(pack_slots(masters), "dp", axis=0, tiled=True)

    slot_index = slot_numbers(owners)
    slot_rows = owners * capacity + slot_index
    mine = (owners == dp_here)[None, :] & (
        slot_index[None, :] == jnp.arange(capacity, dtype=jnp.int32)[:, None]
    )
    tile_order = jnp.arange(tile_count, dtype=jnp.int32)
    gap = REST_ROWS // LANE - 126
    tile_place = tile_order + jnp.where(tile_order >= 126, gap, 0)
    places = jnp.sum(jnp.where(mine, tile_place[None, :] + 1, 0), axis=1) - 1

    vec = vector_master.reshape(1, VEC)
    w_qkv, w_out, w_up, w_down = unpack_weights(slot_rows, slots)
    n1, q, k, v = project(tokens, tokens_far, firsts, firsts_far, w_qkv, vec)
    att, chance = attend(block_place, q, k, v)
    result, grad_resid, resid_low, grad_att, d_up, d_down, vec_one = hidden(
        tokens, att, given, w_out, w_up, w_down, vec
    )
    if line == LINE:
        first_near, grad_near, grads, grad_back, first_back = back(
            q, k, v, att, grad_att, chance, tokens, tokens_far, n1, resid_low, w_qkv, vec, vec_one, d_up, d_down, line
        )
    else:
        d_q, d_k, d_fresh, d_first = attend_back(q, k, v, att, grad_att, chance)
        grad_near, grad_far, d_rest = project_back(
            jnp.concatenate([tokens, tokens_far], axis=0), n1, d_q, d_k, d_fresh, att, resid_low, w_qkv, vec, vec_one
        )
        first_near = d_first[:half_len]
        grad_back, first_back = swap(grad_far), swap(d_first[half_len:].astype(BF16))
        first_back = first_back.reshape(half_len, HV // LANE, LANE).transpose(1, 0, 2)
        grads = lax.psum(jnp.concatenate([d_rest, d_up, d_down], axis=0), ("seq", "dp"))
    vectors = [
        v.reshape(VEC // LANE, LANE) for v in (vector_master, vector_moment_one, vector_moment_two)
    ]
    new_master, new_one, new_two, new_low, tokens_grad, first_grad, *new_vectors = finish(
        places, grads, masters, moment_one, moment_two,
        grad_resid, grad_near, grad_back, tokens, vec, first_near, first_back, vectors,
    )
    return (
        result.reshape(1, half_len, D),
        tokens_grad.reshape(1, half_len, D),
        first_grad.reshape(1, half_len, HV),
        new_master,
        new_one,
        new_two,
        new_low,
        *(v.reshape(VEC) for v in new_vectors),
    )


def solution(mesh):
    rows = P("dp", "seq", None)
    slots = P("dp", None)
    return jax.shard_map(
        shards,
        mesh=mesh,
        in_specs=(rows, rows, rows, slots, P(), slots, slots, slots, P(), P(), P()),
        out_specs=(rows, rows, rows, slots, slots, slots, slots, P(), P(), P()),
        check_vma=False,
    )
```

```python
import functools

import jax
import jax.numpy as jnp
from jax import lax
from jax.experimental import pallas as pl
from jax.experimental.pallas import tpu as pltpu
from jax.sharding import PartitionSpec as P

D = 768
HD = 64
FF = 3072
STEP = 10
HV = 384
LANE = 128
QKV = 2 * D + HV
FF_STEP = 768
VEC = 7 * D + HV + FF
MIB = 1024 * 1024
LINE = 4
REST = 126 * LANE

EPS_NORM = 1e-05
EPS_ADAM = 1e-08
BETA_ONE = 0.5
BETA_TWO = 0.5
RATE_MATRIX = 0.03
RATE_VECTOR = 0.25
DECAY_MATRIX = 0.1
FAR = -1e30

BF16 = jnp.bfloat16
F32 = jnp.float32

NN = (((1,), (0,)), ((), ()))
NT = (((1,), (1,)), ((), ()))
TN = (((0,), (0,)), ((), ()))


def mm(left, right, dims=NN):
    return lax.dot_general(left, right, dims, preferred_element_type=F32)


def vec_part(vec_ref, index):
    if index < 7:
        return vec_ref[:, index * D : (index + 1) * D]
    if index == 7:
        return vec_ref[:, 7 * D : 7 * D + HV]
    return vec_ref[:, 7 * D + HV :]


def params(mib, **more):
    return pltpu.CompilerParams(vmem_limit_bytes=mib * MIB, **more)


def whole(shape):
    return pl.BlockSpec(shape, lambda *_: (0,) * len(shape))


def cost(flops, bytes_accessed, transcendentals=0):
    return pl.CostEstimate(
        flops=int(flops), bytes_accessed=int(bytes_accessed), transcendentals=int(transcendentals)
    )


def adam_step(weight, first_moment, second_moment, gradient, step_rate, weight_decay):
    first_new = BETA_ONE * first_moment + (1.0 - BETA_ONE) * gradient
    second_new = BETA_TWO * second_moment + (1.0 - BETA_TWO) * gradient * gradient
    first_fix = 1.0 - BETA_ONE**STEP
    second_fix = 1.0 - BETA_TWO**STEP
    update = (first_new * (1.0 / first_fix)) / (jnp.sqrt(second_new * (1.0 / second_fix)) + EPS_ADAM)
    return (weight - step_rate * (update + weight_decay * weight), first_new, second_new)


def slot_numbers(owners):
    tile_order = jnp.arange(owners.shape[0], dtype=jnp.int32)
    earlier = (owners[None, :] == owners[:, None]) & (tile_order[None, :] < tile_order[:, None])
    return jnp.sum(earlier.astype(jnp.int32), axis=1)


def normed(values):
    center = jnp.mean(values, axis=-1, keepdims=True)
    centred = values - center
    spread = jnp.mean(centred * centred, axis=-1, keepdims=True)
    rate = lax.rsqrt(spread + EPS_NORM)
    return centred * rate, rate


def norm_back(grad, hat, rate, gain):
    g = grad * gain
    return rate * (
        g - jnp.mean(g, axis=-1, keepdims=True) - hat * jnp.mean(g * hat, axis=-1, keepdims=True)
    )


def pack_rows(src, flat):
    rows = src.shape[0]
    for c in range(LANE):
        flat[pl.ds(c, rows, stride=LANE), :] = src[:, c * LANE : (c + 1) * LANE]


def pack_kernel(src, dst, flat):
    pack_rows(src, flat)
    dst[...] = flat[...].astype(BF16)


def pack_slots(masters):
    capacity, tile_len = masters.shape
    rows = 8 if capacity % 8 == 0 else capacity
    return pl.pallas_call(
        pack_kernel,
        out_shape=jax.ShapeDtypeStruct((capacity * LANE, LANE), BF16),
        grid=(capacity // rows,),
        in_specs=[pl.BlockSpec((rows, tile_len), lambda i: (i, 0))],
        out_specs=pl.BlockSpec((rows * LANE, LANE), lambda i: (i, 0)),
        scratch_shapes=[pltpu.VMEM((rows * LANE, LANE), F32)],
        compiler_params=params(60),
        cost_estimate=cost(0, capacity * tile_len * 6),
        name="pack_slots",
    )(masters)


def weight_chunks():
    chunks = [
        (0, 36, 6, 0, 0, 0),
        (36, 36, 6, 0, D, 0),
        (72, 18, 3, 0, 2 * D, 0),
        (90, 36, 6, 1, 0, 0),
    ]
    for i in range(4):
        chunks.append((126 + 36 * i, 36, 24, 2, 0, 192 * i))
    for i in range(4):
        chunks.append((270 + 36 * i, 36, 6, 3, 0, 768 * i))
    return chunks


def unpack_kernel(slot_rows, slots, w_qkv, w_out, w_up, w_down, stage, o_qkv, o_out, o_up, o_down, flat, sems, out_sems):
    chunks = weight_chunks()
    places = (o_qkv, o_out, o_up, o_down)
    ends = (w_qkv, w_out, w_up, w_down)

    for number, (first, tiles, _, _, _, _) in enumerate(chunks):

        @pl.loop(0, tiles)
        def _(i, first=first, number=number):
            t = first + i
            pltpu.make_async_copy(
                slots.at[pl.ds(pl.multiple_of(slot_rows[t] * LANE, LANE), LANE)],
                stage.at[pl.ds(pl.multiple_of(t * LANE, LANE), LANE)],
                sems.at[number],
            ).start()

    copies = []
    for number, (first, tiles, per_row, matrix, column, row) in enumerate(chunks):
        span = pl.ds(first * LANE, tiles * LANE)
        pltpu.make_async_copy(stage.at[span], stage.at[span], sems.at[number]).wait()
        place = places[matrix]
        lines = 3 * LANE // per_row

        @pl.loop(0, tiles // 6)
        def _(g, first=first, per_row=per_row, place=place, column=column, row=row, lines=lines):
            for half in range(2):
                base = pl.multiple_of(first * LANE + (2 * g + half) * 3 * LANE, LANE)
                flat[half] = stage[pl.ds(base, 3 * LANE), :].astype(F32)
            for half in range(2):
                top = pl.multiple_of(row + (2 * g + half) * lines, 16)
                for j in range(per_row):
                    place[pl.ds(top, lines), column + j * LANE : column + (j + 1) * LANE] = flat[
                        half, pl.ds(j, lines, stride=per_row), :
                    ].astype(BF16)

        rows = tiles * LANE // per_row
        columns = pl.ds(column, per_row * LANE)
        copy = pltpu.make_async_copy(
            place.at[pl.ds(row, rows), columns],
            ends[matrix].at[pl.ds(row, rows), columns],
            out_sems.at[number],
        )
        copy.start()
        copies.append(copy)
    for copy in copies:
        copy.wait()


def unpack_weights(slot_rows, slots):
    tile_count = slot_rows.shape[0]
    shapes = [(D, QKV), (D, D), (D, FF), (FF, D)]
    any_space = pl.BlockSpec(memory_space=pl.ANY)
    return pl.pallas_call(
        unpack_kernel,
        out_shape=[jax.ShapeDtypeStruct(s, BF16) for s in shapes],
        grid_spec=pltpu.PrefetchScalarGridSpec(
            num_scalar_prefetch=1,
            grid=(1,),
            in_specs=[any_space],
            out_specs=[any_space] * 4,
            scratch_shapes=[pltpu.VMEM((tile_count * LANE, LANE), BF16)]
            + [pltpu.VMEM(s, BF16) for s in shapes]
            + [
                pltpu.VMEM((2, 3 * LANE, LANE), F32),
                pltpu.SemaphoreType.DMA((12,)),
                pltpu.SemaphoreType.DMA((12,)),
            ],
        ),
        compiler_params=params(60),
        cost_estimate=cost(0, 4 * tile_count * LANE * LANE),
        name="unpack_weights",
    )(slot_rows, slots)


def project_kernel(near, far, firsts, firsts_far, w_qkv, vec, n1, q, k, v):
    first = pl.program_id(0) == 0
    tokens = jnp.where(first, near[...], far[...])
    hat, _ = normed(tokens.astype(F32))
    low = (hat * vec_part(vec, 0) + vec_part(vec, 1)).astype(BF16)
    n1[...] = low
    k[...] = mm(low, w_qkv[:, D : 2 * D]).astype(BF16)
    v[:, :HV] = (mm(low, w_qkv[:, 2 * D :]) + vec_part(vec, 7)).astype(BF16)
    v[:, HV:] = jnp.where(first, firsts[...], firsts_far[...])

    @pl.when(first)
    def _():
        query = mm(low, w_qkv[:, :D]) + vec_part(vec, 4)
        q[...] = (query.astype(BF16).astype(F32) * HD ** (-0.5)).astype(BF16)


def project(near, far, firsts, firsts_far, w_qkv, vec):
    rows = near.shape[0]
    by_row = pl.BlockSpec((rows, D), lambda i: (i, 0))
    return pl.pallas_call(
        project_kernel,
        out_shape=[
            jax.ShapeDtypeStruct((2 * rows, D), BF16),
            jax.ShapeDtypeStruct((rows, D), BF16),
            jax.ShapeDtypeStruct((2 * rows, D), BF16),
            jax.ShapeDtypeStruct((2 * rows, D), BF16),
        ],
        grid=(2,),
        in_specs=[
            whole((rows, D)),
            whole((rows, D)),
            whole((rows, HV)),
            whole((rows, HV)),
            whole((D, QKV)),
            whole((1, VEC)),
        ],
        out_specs=[by_row, whole((rows, D)), by_row, by_row],
        compiler_params=params(60),
        cost_estimate=cost(4 * rows * D * QKV, 2 * D * QKV + rows * D * 20),
        name="project",
    )(near, far, firsts, firsts_far, w_qkv, vec)


def attend_kernel(places, q, k, v, out, chance, bias):
    @pl.when(pl.program_id(0) == 0)
    def _():
        here = lax.axis_index("seq")
        count = places.shape[1] // 2
        size = q.shape[0] // count
        ahead = lax.broadcasted_iota(jnp.int32, (size, size), 0) - lax.broadcasted_iota(
            jnp.int32, (size, size), 1
        )
        for i in range(2 * count):
            side = here if i < count else 1 - here
            key_place = places[0, side * count + i % count]
            for j in range(count):
                shift = (places[0, here * count + j] - key_place) * size
                bias[i * size : (i + 1) * size, j * size : (j + 1) * size] = jnp.where(
                    ahead <= shift, 0.0, FAR
                )

    heads = [slice(head * HD, (head + 1) * HD) for head in range(2)]
    scores = [mm(k[:, cols], q[:, cols], NT) + bias[...] for cols in heads]
    for head in range(2):
        top = jnp.max(scores[head], axis=0, keepdims=True)
        power = jnp.exp(scores[head] - top)
        total = jnp.sum(power, axis=0, keepdims=True)
        chance[head] = (power * (1.0 / total)).astype(BF16)
    for head, cols in enumerate(heads):
        out[:, cols] = mm(v[:, cols], chance[head], TN).T.astype(BF16)


def attend(places, q, k, v):
    queries, keys = q.shape[0], k.shape[0]
    pairs = D // LANE
    by_column = lambda i, *_: (0, i)
    return pl.pallas_call(
        attend_kernel,
        out_shape=[
            jax.ShapeDtypeStruct((queries, D), BF16),
            jax.ShapeDtypeStruct((2 * pairs, keys, queries), BF16),
        ],
        grid_spec=pltpu.PrefetchScalarGridSpec(
            num_scalar_prefetch=1,
            grid=(pairs,),
            in_specs=[
                pl.BlockSpec((queries, LANE), by_column),
                pl.BlockSpec((keys, LANE), by_column),
                pl.BlockSpec((keys, LANE), by_column),
            ],
            out_specs=[
                pl.BlockSpec((queries, LANE), by_column),
                pl.BlockSpec((2, keys, queries), lambda i, *_: (i, 0, 0)),
            ],
            scratch_shapes=[pltpu.VMEM((keys, queries), F32)],
        ),
        compiler_params=params(60),
        cost_estimate=cost(4 * queries * keys * D, 24 * queries * keys, 12 * queries * keys),
        name="attend",
    )(places, q, k, v)


def hidden_kernel(
    tokens, att, og, w_out, w_up, w_down, vec,
    result, grad_resid, resid_low, grad_att, d_up, d_down, vec_grad,
    resid, hat, n2, rate, acc, acc_grad, flat_up, flat_down,
):
    step = pl.program_id(0)
    per_row = D // LANE
    wide = FF // LANE

    @pl.when(step == 0)
    def _():
        base = tokens[...].astype(F32) + mm(att[...], w_out[...]) + vec_part(vec, 5)
        resid[...] = base
        unit, scale = normed(base)
        hat[...] = unit
        rate[...] = scale
        n2[...] = (unit * vec_part(vec, 2) + vec_part(vec, 3)).astype(BF16)
        vec_grad[...] = jnp.zeros_like(vec_grad)
        acc[...] = jnp.zeros_like(acc)
        acc_grad[...] = jnp.zeros_like(acc_grad)

    start = pl.multiple_of(7 * D + HV + step * FF_STEP, LANE)
    pre = mm(n2[...], w_up[...]) + vec[:, pl.ds(start, FF_STEP)]
    square = pre * pre
    bent = jnp.tanh(0.7978845608028654 * (pre + 0.044715 * square * pre))
    half = 0.5 * (1.0 + bent)
    act = (pre * half).astype(BF16)
    slope = half + (0.5 * 0.7978845608028654) * pre * (1.0 - bent * bent) * (1.0 + 0.134145 * square)
    grad_pre32 = mm(og[...], w_down[...], NT) * slope
    grad_pre = grad_pre32.astype(BF16)
    vec_grad[:, pl.ds(start, FF_STEP)] = jnp.sum(grad_pre.astype(F32), axis=0, keepdims=True)
    acc[...] += mm(act, w_down[...])
    acc_grad[...] += mm(grad_pre, w_up[...], NT)
    down = mm(act, og[...], TN)
    for j in range(per_row):
        flat_down[pl.ds(j, FF_STEP, stride=per_row), :] = down[:, j * LANE : (j + 1) * LANE]
    d_down[...] = flat_down[...].astype(BF16)
    up = mm(n2[...], grad_pre, TN)
    for j in range(FF_STEP // LANE):
        flat_up[pl.ds(step * (FF_STEP // LANE) + j, D, stride=wide), :] = up[
            :, j * LANE : (j + 1) * LANE
        ]

    @pl.when(step == FF // FF_STEP - 1)
    def _():
        d_up[...] = flat_up[...].astype(BF16)
        result[...] = (resid[...] + acc[...] + vec_part(vec, 6)).astype(BF16)
        grad = acc_grad[...]
        unit = hat[...]
        vec_grad[:, 2 * D : 3 * D] = jnp.sum(grad * unit, axis=0, keepdims=True)
        vec_grad[:, 3 * D : 4 * D] = jnp.sum(grad, axis=0, keepdims=True)
        given = og[...].astype(F32)
        back = given + norm_back(grad, unit, rate[...], vec_part(vec, 2))
        grad_resid[...] = back
        low = back.astype(BF16)
        resid_low[...] = low
        vec_grad[:, 5 * D : 6 * D] = jnp.sum(low.astype(F32), axis=0, keepdims=True)
        vec_grad[:, 6 * D : 7 * D] = jnp.sum(given, axis=0, keepdims=True)
        grad_att[...] = mm(low, w_out[...], NT).astype(BF16)


def hidden(tokens, att, og, w_out, w_up, w_down, vec):
    rows = tokens.shape[0]
    line = (rows, D)
    flat_rows = FF * D // LANE
    return pl.pallas_call(
        hidden_kernel,
        out_shape=[
            jax.ShapeDtypeStruct(line, BF16),
            jax.ShapeDtypeStruct(line, F32),
            jax.ShapeDtypeStruct(line, BF16),
            jax.ShapeDtypeStruct(line, BF16),
            jax.ShapeDtypeStruct((flat_rows, LANE), BF16),
            jax.ShapeDtypeStruct((flat_rows, LANE), BF16),
            jax.ShapeDtypeStruct((1, VEC), F32),
        ],
        grid=(FF // FF_STEP,),
        in_specs=[
            whole(line),
            whole(line),
            whole(line),
            whole((D, D)),
            pl.BlockSpec((D, FF_STEP), lambda i: (0, i)),
            pl.BlockSpec((FF_STEP, D), lambda i: (i, 0)),
            whole((1, VEC)),
        ],
        out_specs=[
            whole(line),
            whole(line),
            whole(line),
            whole(line),
            whole((flat_rows, LANE)),
            pl.BlockSpec((FF_STEP * D // LANE, LANE), lambda i: (i, 0)),
            whole((1, VEC)),
        ],
        scratch_shapes=[
            pltpu.VMEM(line, F32),
            pltpu.VMEM(line, F32),
            pltpu.VMEM(line, BF16),
            pltpu.VMEM((rows, 1), F32),
            pltpu.VMEM(line, F32),
            pltpu.VMEM(line, F32),
            pltpu.VMEM((flat_rows, LANE), F32),
            pltpu.VMEM((FF_STEP * D // LANE, LANE), F32),
        ],
        compiler_params=params(62),
        cost_estimate=cost(2 * rows * D * (6 * FF + 2 * D), 8 * D * FF + 20 * rows * D, rows * FF),
        name="hidden",
    )(tokens, att, og, w_out, w_up, w_down, vec)


def attend_back_kernel(q, k, v, att, grad_att, chance, d_q, d_k, d_fresh, d_first):
    pair = pl.program_id(0)
    for head in range(2):
        cols = slice(head * HD, (head + 1) * HD)
        grad = grad_att[:, cols]
        weights = chance[head]
        shared = grad.astype(F32) * att[:, cols].astype(F32)
        delta = jnp.sum(shared.T, axis=0, keepdims=True)
        grad_chance = mm(v[:, cols], grad, NT)
        grad_scores = (weights.astype(F32) * (grad_chance - delta)).astype(BF16)
        grad_value = mm(weights, grad)

        @pl.when(pair < 3)
        def _(grad_value=grad_value, cols=cols):
            d_fresh[:, cols] = grad_value.astype(BF16)

        @pl.when(pair >= 3)
        def _(grad_value=grad_value, cols=cols):
            d_first[:, cols] = grad_value

        d_k[:, cols] = mm(grad_scores, q[:, cols]).astype(BF16)
        d_q[:, cols] = (mm(k[:, cols], grad_scores, TN).T * HD ** (-0.5)).astype(BF16)


def attend_back(q, k, v, att, grad_att, chance):
    queries, keys = q.shape[0], k.shape[0]
    pairs = D // LANE
    by_column = lambda i: (0, i)
    return pl.pallas_call(
        attend_back_kernel,
        out_shape=[
            jax.ShapeDtypeStruct((queries, D), BF16),
            jax.ShapeDtypeStruct((keys, D), BF16),
            jax.ShapeDtypeStruct((keys, HV), BF16),
            jax.ShapeDtypeStruct((keys, HV), F32),
        ],
        grid=(pairs,),
        in_specs=[
            pl.BlockSpec((queries, LANE), by_column),
            pl.BlockSpec((keys, LANE), by_column),
            pl.BlockSpec((keys, LANE), by_column),
            pl.BlockSpec((queries, LANE), by_column),
            pl.BlockSpec((queries, LANE), by_column),
            pl.BlockSpec((2, keys, queries), lambda i: (i, 0, 0)),
        ],
        out_specs=[
            pl.BlockSpec((queries, LANE), by_column),
            pl.BlockSpec((keys, LANE), by_column),
            pl.BlockSpec((keys, LANE), lambda i: (0, jnp.minimum(i, 2))),
            pl.BlockSpec((keys, LANE), lambda i: (0, jnp.maximum(i - 3, 0))),
        ],
        compiler_params=params(60),
        cost_estimate=cost(8 * queries * keys * D, 24 * queries * keys),
        name="attend_back",
    )(q, k, v, att, grad_att, chance)


def project_back_kernel(
    tokens, n1, d_q, d_k, d_fresh, att, resid_low, w_qkv, vec, vec_one,
    grad_near, grad_far, d_rest, vec_grad, flat,
):
    rows = n1.shape[0] // 2
    per_row = D // LANE
    grads = mm(d_k[...], w_qkv[:, D : 2 * D], NT) + mm(d_fresh[...], w_qkv[:, 2 * D :], NT)
    near = grads[:rows] + mm(d_q[...], w_qkv[:, :D], NT)
    far = grads[rows:]
    grad_near[...] = near
    grad_far[...] = far.astype(BF16)
    hat, _ = normed(tokens[...].astype(F32))
    vec_grad[...] = vec_one[...]
    vec_grad[:, :D] = jnp.sum(near * hat[:rows], axis=0, keepdims=True) + jnp.sum(
        far * hat[rows:], axis=0, keepdims=True
    )
    vec_grad[:, D : 2 * D] = jnp.sum(near, axis=0, keepdims=True) + jnp.sum(
        far, axis=0, keepdims=True
    )
    vec_grad[:, 4 * D : 5 * D] = jnp.sum(d_q[...].astype(F32), axis=0, keepdims=True)
    vec_grad[:, 7 * D : 7 * D + HV] = jnp.sum(d_fresh[...].astype(F32), axis=0, keepdims=True)
    pieces = (
        (n1, d_q, rows, 0, per_row),
        (n1, d_k, 2 * rows, D * per_row, per_row),
        (n1, d_fresh, 2 * rows, 2 * D * per_row, HV // LANE),
        (att, resid_low, rows, 2 * D * per_row + D * HV // LANE, per_row),
    )
    for left, right, count, start, columns in pieces:
        product = mm(left[:count], right[:count], TN)
        size = D * columns
        for j in range(columns):
            flat[pl.ds(j, D, stride=columns), :] = product[:, j * LANE : (j + 1) * LANE]
        d_rest[start : start + size] = flat[:size].astype(BF16)
    flat[: 2 * LANE] = jnp.zeros((2 * LANE, LANE), F32)
    for j in range(VEC // LANE):
        flat[j : j + 1] = vec_grad[:, j * LANE : (j + 1) * LANE]
    d_rest[REST:] = flat[: 2 * LANE].astype(BF16)


def project_back(tokens, n1, d_q, d_k, d_fresh, att, resid_low, w_qkv, vec, vec_one):
    rows = n1.shape[0] // 2
    vm = pl.BlockSpec(memory_space=pltpu.VMEM)
    return pl.pallas_call(
        project_back_kernel,
        out_shape=[
            jax.ShapeDtypeStruct((rows, D), F32),
            jax.ShapeDtypeStruct((rows, D), BF16),
            jax.ShapeDtypeStruct((128 * LANE, LANE), BF16),
        ],
        in_specs=[vm] * 10,
        out_specs=[vm] * 3,
        scratch_shapes=[pltpu.VMEM((1, VEC), F32), pltpu.VMEM((D * D // LANE, LANE), F32)],
        compiler_params=params(58),
        cost_estimate=cost(2 * rows * D * (7 * D), 14 * MIB),
        name="project_back",
    )(tokens, n1, d_q, d_k, d_fresh, att, resid_low, w_qkv, vec, vec_one)


def finish_kernel(
    places, grads, weight, one, two,
    resid, near, far, tokens, vec, firsts, firsts_far, vec_weight, vec_one, vec_two,
    new, new_one, new_two, low, tokens_grad, first_grad, new_vec, new_vec_one, new_vec_two,
    stage, flat, vec_stage, v_weight, v_one, v_two, v_low,
    v_resid, v_near, v_far, v_tokens, v_firsts, v_firsts_far,
    slot_sems, in_sems, out_sems, side_sems, vec_sem,
):
    capacity = weight.shape[0]
    rows = flat.shape[0] // LANE
    steps = capacity // rows

    def span(s):
        return pl.ds(s * rows, rows)

    vec_copy = pltpu.make_async_copy(grads.at[pl.ds(REST, vec_stage.shape[0])], vec_stage, vec_sem)
    vec_copy.start()
    brought = []
    for s in range(steps):
        for i, (source, target) in enumerate(((weight, v_weight), (one, v_one), (two, v_two))):
            brought.append(
                pltpu.make_async_copy(source.at[span(s)], target.at[span(s)], in_sems.at[3 * s + i])
            )
            brought[-1].start()

        @pl.loop(0, rows)
        def _(i, s=s):
            slot = s * rows + i
            pltpu.make_async_copy(
                grads.at[pl.ds(pl.multiple_of(jnp.maximum(places[slot], 0) * LANE, LANE), LANE)],
                stage.at[pl.ds(pl.multiple_of(slot * LANE, LANE), LANE)],
                slot_sems.at[s],
            ).start()

    sides = [
        pltpu.make_async_copy(source, target, side_sems.at[i])
        for i, (source, target) in enumerate(
            (
                (resid, v_resid),
                (near, v_near),
                (far, v_far),
                (tokens, v_tokens),
                (firsts, v_firsts),
                (firsts_far, v_firsts_far),
            )
        )
    ]
    for copy in sides:
        copy.start()
    sent = []
    for s in range(steps):
        for copy in brought[3 * s : 3 * s + 3]:
            copy.wait()
        tile = pl.ds(s * rows * LANE, rows * LANE)
        pltpu.make_async_copy(stage.at[tile], stage.at[tile], slot_sems.at[s]).wait()
        flat[...] = stage[tile, :].astype(F32)
        line = lax.broadcasted_iota(jnp.int32, (rows, LANE), 0)
        taken = jnp.zeros((rows, LANE), jnp.int32)
        for i in range(rows):
            taken = jnp.where(line == i, places[s * rows + i], taken)
        keep = taken >= 0
        for c in range(LANE):
            columns = slice(c * LANE, (c + 1) * LANE)
            gradient = jnp.where(keep, flat[pl.ds(c, rows, stride=LANE), :], 0.0)
            after, after_one, after_two = adam_step(
                v_weight[span(s), columns], v_one[span(s), columns], v_two[span(s), columns],
                gradient, RATE_MATRIX, DECAY_MATRIX,
            )
            v_weight[span(s), columns] = after
            v_one[span(s), columns] = after_one
            v_two[span(s), columns] = after_two
            v_low[s, :, columns] = after.astype(BF16)
        for i, (source, target) in enumerate(
            (
                (v_weight.at[span(s)], new.at[span(s)]),
                (v_one.at[span(s)], new_one.at[span(s)]),
                (v_two.at[span(s)], new_two.at[span(s)]),
            )
        ):
            sent.append(pltpu.make_async_copy(source, target, out_sems.at[3 * s + i]))
            sent[-1].start()
    for s in range(steps):
        low[span(s), :] = v_low[s]
    vec_copy.wait()
    count = vec_weight.shape[0]
    after, after_one, after_two = adam_step(
        vec_weight[...], vec_one[...], vec_two[...],
        vec_stage[...].astype(F32)[:count], RATE_VECTOR, 0.0,
    )
    new_vec[...] = after
    new_vec_one[...] = after_one
    new_vec_two[...] = after_two
    for copy in sides:
        copy.wait()
    grad = v_near[...] + v_far[...].astype(F32)
    hat, rate = normed(v_tokens[...].astype(F32))
    v_resid[...] += norm_back(grad, hat, rate, vec_part(vec, 0))
    for i in range(HV // LANE):
        columns = slice(i * LANE, (i + 1) * LANE)
        v_firsts[:, columns] += v_firsts_far[i].astype(F32)
    for i, (source, target) in enumerate(((v_resid, tokens_grad), (v_firsts, first_grad))):
        sent.append(pltpu.make_async_copy(source, target, side_sems.at[i]))
        sent[-1].start()
    for copy in sent:
        copy.wait()


def finish(places, grads, weight, one, two, resid, near, far, tokens, vec, firsts, firsts_far, vectors):
    capacity, tile_len = weight.shape
    rows = 8 if capacity % 8 == 0 else capacity
    steps = capacity // rows
    flat_vec = vectors[0].shape
    any_space = pl.BlockSpec(memory_space=pl.ANY)
    sides = [resid, near, far, tokens, firsts, firsts_far]
    return pl.pallas_call(
        finish_kernel,
        out_shape=[jax.ShapeDtypeStruct(weight.shape, F32)] * 3
        + [jax.ShapeDtypeStruct(weight.shape, BF16)]
        + [jax.ShapeDtypeStruct(resid.shape, F32), jax.ShapeDtypeStruct(firsts.shape, F32)]
        + [jax.ShapeDtypeStruct(flat_vec, F32)] * 3,
        grid_spec=pltpu.PrefetchScalarGridSpec(
            num_scalar_prefetch=1,
            grid=(1,),
            in_specs=[any_space] * 8
            + [whole((1, VEC))]
            + [any_space] * 2
            + [whole(flat_vec)] * 3,
            out_specs=[any_space] * 3 + [whole(weight.shape)] + [any_space] * 2 + [whole(flat_vec)] * 3,
            scratch_shapes=[
                pltpu.VMEM((capacity * LANE, LANE), BF16),
                pltpu.VMEM((rows * LANE, LANE), F32),
                pltpu.VMEM((80, LANE), BF16),
                pltpu.VMEM(weight.shape, F32),
                pltpu.VMEM(weight.shape, F32),
                pltpu.VMEM(weight.shape, F32),
                pltpu.VMEM((steps, rows, tile_len), BF16),
            ]
            + [pltpu.VMEM(side.shape, side.dtype) for side in sides]
            + [
                pltpu.SemaphoreType.DMA((steps,)),
                pltpu.SemaphoreType.DMA((3 * steps,)),
                pltpu.SemaphoreType.DMA((3 * steps,)),
                pltpu.SemaphoreType.DMA((len(sides),)),
                pltpu.SemaphoreType.DMA,
            ],
        ),
        compiler_params=params(60),
        cost_estimate=cost(20 * capacity * tile_len, 28 * capacity * tile_len, 2 * capacity * tile_len),
        name="finish",
    )(places, grads, weight, one, two, resid, near, far, tokens, vec, firsts, firsts_far, *vectors)


class Links:
    def __init__(self, line, send_sems, recv_sems):
        dp = lax.axis_index("dp")
        self.line = line
        self.y = lax.axis_index("seq")
        self.z = dp // 4
        self.x = (dp // 2) % 2
        self.c = dp % 2
        self.send_sems, self.recv_sems = send_sems, recv_sems
        self.to = {
            "core": {"dp": self.z * 4 + self.x * 2 + (1 - self.c)},
            "x": {"dp": self.z * 4 + (1 - self.x) * 2 + self.c},
            "y": {"seq": 1 - self.y},
            "up": {"dp": dp + 4},
            "down": {"dp": dp - 4},
        }
        self.sent = []

    def greet(self, whole_line, meanwhile=lambda: None):
        barrier = pltpu.get_barrier_semaphore()
        for name in ("core", "x", "y"):
            pl.semaphore_signal(barrier, inc=1, device_id=self.to[name])
        if whole_line:
            for d in range(1, self.line):
                z = (self.z + d) % self.line
                pl.semaphore_signal(barrier, inc=1, device_id={"dp": z * 4 + self.x * 2 + self.c})
            meanwhile()
            pl.semaphore_wait(barrier, 2 + self.line)
            return

        @pl.when(self.z > 0)
        def _():
            pl.semaphore_signal(barrier, inc=1, device_id=self.to["down"])

        @pl.when(self.z < self.line - 1)
        def _():
            pl.semaphore_signal(barrier, inc=1, device_id=self.to["up"])

        meanwhile()
        pl.semaphore_wait(
            barrier,
            3 + jnp.where(self.z > 0, 1, 0) + jnp.where(self.z < self.line - 1, 1, 0),
        )

    def copy(self, source, target, index, way):
        sender, receiver = index if isinstance(index, tuple) else (index, index)
        to = self.to[way] if isinstance(way, str) else {"dp": way * 4 + self.x * 2 + self.c}
        return pltpu.make_async_remote_copy(
            src_ref=source,
            dst_ref=target,
            send_sem=self.send_sems.at[sender],
            recv_sem=self.recv_sems.at[receiver],
            device_id=to,
        )

    def send(self, describe):
        source, target, index, way, when = describe()
        if when is None:
            self.copy(source, target, index, way).start()
        else:

            @pl.when(when)
            def _():
                self.copy(source, target, index, way).start()

        self.sent.append(describe)

    def arrive(self, target, index, way):
        self.copy(target, target, index, way).wait_recv()

    def finish(self):
        for describe in self.sent:
            source, target, index, way, when = describe()
            if when is None:
                self.copy(source, target, index, way).wait_send()
            else:

                @pl.when(when)
                def _(source=source, target=target, index=index, way=way):
                    self.copy(source, target, index, way).wait_send()


def add_into(place, *others):
    total = place[...].astype(F32)
    for other in others:
        total = total + other[...].astype(F32)
    place[...] = total.astype(BF16)


class Scatter:
    KINDS = ("core", "xa", "yb", "ya", "xb", "to", "from")

    def __init__(self, links, base, source, offset, rows, cut, buffers, load_sems):
        self.k, self.base, self.source, self.offset, self.rows = links, base, source, offset, rows
        self.held, self.r_core, self.r_xa, self.r_yb, self.r_ya, self.r_xb, self.r_line = buffers
        self.load_sems = load_sems
        self.halves = (pl.ds(0, cut), pl.ds(cut, rows - cut))

    @staticmethod
    def buffers_of(rows, cut, line):
        return [
            pltpu.VMEM((line, 2, 2, rows, LANE), BF16),
            pltpu.VMEM((line, 4 * rows, LANE), BF16),
            pltpu.VMEM((line, 2, cut, LANE), BF16),
            pltpu.VMEM((line, 2, rows - cut, LANE), BF16),
            pltpu.VMEM((line, cut, LANE), BF16),
            pltpu.VMEM((line, rows - cut, LANE), BF16),
            pltpu.VMEM((line, rows, LANE), BF16),
        ]

    def at(self, kind, z):
        return self.base + self.KINDS.index(kind) * self.k.line + z

    def load(self, z):
        start = self.offset + (self.k.c * self.k.line + z) * 4 * self.rows
        return [
            pltpu.make_async_copy(
                self.source.at[pl.ds(pl.multiple_of(start + i * self.rows, 16), self.rows)],
                self.held.at[z, i // 2, i % 2],
                self.load_sems.at[4 * z + i],
            )
            for i in range(4)
        ]

    def begin(self):
        k = self.k

        def describe(z):
            start = self.offset + ((1 - k.c) * k.line + z) * 4 * self.rows
            source = self.source.at[pl.ds(pl.multiple_of(start, 16), 4 * self.rows)]
            return source, self.r_core.at[z], self.at("core", z), "core", None

        for z in range(k.line):
            k.send(functools.partial(describe, z))
            for copy in self.load(z):
                copy.start()

    def first(self, z):
        k, (a, b) = self.k, self.halves
        for copy in self.load(z):
            copy.wait()
        k.arrive(self.r_core.at[z], self.at("core", z), "core")
        for i in range(4):
            add_into(self.held.at[z, i // 2, i % 2], self.r_core.at[z, pl.ds(i * self.rows, self.rows)])
        k.send(lambda: (self.held.at[z, 1 - k.x, :, a], self.r_xa.at[z], self.at("xa", z), "x", None))
        k.send(lambda: (self.held.at[z, :, 1 - k.y, b], self.r_yb.at[z], self.at("yb", z), "y", None))

    def second(self, z):
        k, (a, b) = self.k, self.halves
        k.arrive(self.r_xa.at[z], self.at("xa", z), "x")
        for y in range(2):
            add_into(self.held.at[z, k.x, y, a], self.r_xa.at[z, y])
        k.send(lambda: (self.held.at[z, k.x, 1 - k.y, a], self.r_ya.at[z], self.at("ya", z), "y", None))
        k.arrive(self.r_yb.at[z], self.at("yb", z), "y")
        for x in range(2):
            add_into(self.held.at[z, x, k.y, b], self.r_yb.at[z, x])
        k.send(lambda: (self.held.at[z, 1 - k.x, k.y, b], self.r_xb.at[z], self.at("xb", z), "x", None))

    def third(self, z):
        k, (a, b) = self.k, self.halves
        k.arrive(self.r_ya.at[z], self.at("ya", z), "y")
        add_into(self.held.at[z, k.x, k.y, a], self.r_ya.at[z])
        k.arrive(self.r_xb.at[z], self.at("xb", z), "x")
        add_into(self.held.at[z, k.x, k.y, b], self.r_xb.at[z])

        def describe():
            index = (self.at("to", z), self.at("from", k.z))
            return self.held.at[z, k.x, k.y], self.r_line.at[k.z], index, z, k.z != z

        k.send(describe)

    def last(self):
        k = self.k
        others = [(k.z + d) % k.line for d in range(1, k.line)]
        for z in others:
            k.arrive(self.r_line.at[z], (self.at("to", z), self.at("from", z)), z)
        add_into(self.held.at[k.z, k.x, k.y], *[self.r_line.at[z] for z in others])


class Spread:
    KINDS = ("xa", "yb", "ya", "xb", "ya2", "xb2") + tuple(
        f"{way}{i}" for way in ("to", "from", "c") for i in range(4)
    )

    def __init__(self, links, base, piece, out, index, first, rows, cut):
        self.k, self.base, self.piece, self.out, self.index = links, base, piece, out, index
        self.parts = {None: (first, rows), 0: (first, cut), 1: (first + cut, rows - cut)}

    def own(self, half):
        first, count = self.parts[half]
        return self.piece(pl.ds(first, count))

    def at(self, kind, z):
        return self.base + self.KINDS.index(kind) * self.k.line + z

    def spot(self, z, other_x, other_y, half=None, core=None):
        k = self.k
        c = k.c if core is None else core
        x = 1 - k.x if other_x else k.x
        y = 1 - k.y if other_y else k.y
        first, count = self.parts[half]
        return self.out.at[pl.ds(pl.multiple_of(self.index(c, z, x, y) + first, 16), count)]

    def place(self, d):
        return (self.k.z + d) % self.k.line

    def give(self, kind, way, d, other_x=False, other_y=False, half=None, own=False):
        def describe():
            z = self.place(d)
            target = self.spot(z, other_x, other_y, half)
            source = self.own(half) if own else target
            return source, target, self.at(kind, z), way, None

        self.k.send(describe)

    def get(self, kind, way, d, other_x=False, other_y=False, half=None):
        z = self.place(d)
        self.k.arrive(self.spot(z, other_x, other_y, half), self.at(kind, z), way)

    def lift(self, i, own=False):
        k = self.k
        place = dict(other_x=i >= 2, other_y=i % 2 == 1)

        def describe(d):
            z = self.place(d)
            target = self.spot(k.z, **place)
            source = self.own(None) if own else target
            return source, target, (self.at(f"to{i}", z), self.at(f"from{i}", k.z)), z, None

        for d in (k.line - 1, 1, 2):
            k.send(functools.partial(describe, d))

    def land(self, d, i):
        z = self.place(d)
        place = dict(other_x=i >= 2, other_y=i % 2 == 1)
        self.k.arrive(self.spot(z, **place), (self.at(f"to{i}", z), self.at(f"from{i}", z)), z)

    def cross(self, d):
        own = d == 0
        self.give("xa", "x", d, half=0, own=own)
        self.give("yb", "y", d, half=1, own=own)
        self.give("ya", "y", d, half=0, own=own)
        self.give("xb", "x", d, half=1, own=own)
        self.give("c0", "core", d, own=own)

    def start(self):
        self.lift(0, True)
        self.cross(0)

    def along(self, d):
        self.land(d, 0)
        self.cross(d)

    def turn(self, d):
        self.get("xa", "x", d, other_x=True, half=0)
        self.give("ya2", "y", d, other_x=True, half=0)
        self.get("yb", "y", d, other_y=True, half=1)
        self.give("xb2", "x", d, other_y=True, half=1)

    def share(self, d, late=False):
        self.get("ya", "y", d, other_y=True, half=0)
        self.give("c1", "core", d, other_y=True)
        if late:
            self.lift(1)
        self.get("xb", "x", d, other_x=True, half=1)
        self.give("c2", "core", d, other_x=True)
        if late:
            self.lift(2)
        self.get("ya2", "y", d, other_x=True, other_y=True, half=0)
        self.get("xb2", "x", d, other_x=True, other_y=True, half=1)
        self.give("c3", "core", d, other_x=True, other_y=True)
        if late:
            self.lift(3)

    def along_late(self, d):
        for i in range(4):
            self.land(d, i)
            self.give(f"c{i}", "core", d, other_x=i >= 2, other_y=i % 2 == 1)

    def end(self):
        k = self.k
        for z in range(k.line):
            for i in range(4):
                k.arrive(self.spot(z, i >= 2, i % 2 == 1, core=1 - k.c), self.at(f"c{i}", z), "core")


RS_SEMS = len(Scatter.KINDS)
AR_SEMS = RS_SEMS + 2 * len(Spread.KINDS)


class Total:
    def __init__(self, links, base, source, offset, kind, out, top, buffers, load_sems, copy_sem):
        line = links.line
        size, cut, turn, plain = kind
        rows = size // (8 * line)
        held = buffers[0]

        def index(c, z, x, y):
            return top + (((c * line + z) * 2 + x) * 2 + y) * rows

        def piece(span):
            return held.at[links.z, links.x, links.y, span]

        self.k, self.piece, self.out, self.index, self.rows = links, piece, out, index, rows
        self.scatter = Scatter(links, base, source, offset, rows, cut, buffers, load_sems)
        base = base + RS_SEMS * line
        self.spread = Spread(links, base, piece, out, index, 0, plain, turn)
        self.late = None
        if plain < rows:
            base = base + len(Spread.KINDS) * line
            rest = rows - plain
            self.late = Spread(links, base, piece, out, index, plain, rest, rest // 32 * 16)
        self.copy_sem = copy_sem

    def keep(self):
        k = self.k
        start = pl.multiple_of(self.index(k.c, k.z, k.x, k.y), 16)
        return pltpu.make_async_copy(
            self.piece(pl.ds(0, self.rows)), self.out.at[pl.ds(start, self.rows)], self.copy_sem
        )

    def run(self, stage, part):
        scatter, spread, late = self.scatter, self.spread, self.late
        if stage == 0:
            scatter.begin()
        elif stage < 4:
            (scatter.first, scatter.second, scatter.third)[stage - 1](part)
        elif stage == 4:
            scatter.last()
            self.keep().start()
            spread.start()
            if late is not None:
                late.start()
        elif stage == 5 and part < 3:
            spread.along(part + 1)
        elif stage == 5 and part == 3:
            late.turn(0)
        elif stage == 5 and part == 4:
            late.share(0, True)
        elif stage == 5:
            late.along_late(part - 4)
        elif stage < 8:
            (spread.turn, spread.share)[stage - 6](part)
        else:
            self.keep().wait()
            spread.end()
            if late is not None:
                late.end()


class Gather:
    KINDS = ("up", "down", "xa", "yb", "ya", "xb", "ya2", "xb2", "x2") + tuple(
        f"{way}{i}" for way in ("u", "d", "c") for i in range(4)
    )

    def __init__(self, links, base, own, out, index, first, rows, cut, z_first, twice):
        self.k, self.base, self.own, self.out, self.index = links, base, own, out, index
        self.parts = {None: (first, rows), 0: (first, cut), 1: (first + cut, rows - cut)}
        self.z_first, self.twice = z_first, twice

    def at(self, kind, z):
        return self.base + self.KINDS.index(kind) * self.k.line + z

    def spot(self, z, other_x, other_y, half=None, core=None):
        k = self.k
        c = k.c if core is None else core
        x = 1 - k.x if other_x else k.x
        y = 1 - k.y if other_y else k.y
        first, count = self.parts[half]
        return self.out.at[pl.ds(pl.multiple_of(self.index(c, z, x, y) + first, 16), count)]

    def give(self, kind, way, z, other_x=False, other_y=False, half=None, when=None, own=False):
        def describe():
            place = self.spot(z(), other_x, other_y, half)
            source = self.own(other_y, half) if own else place
            return source, place, self.at(kind, z()), way, None if when is None else when()

        self.k.send(describe)

    def get(self, kind, way, z, other_x=False, other_y=False, half=None):
        self.k.arrive(self.spot(z, other_x, other_y, half), self.at(kind, z), way)

    def near(self):
        k = self.k
        found = []
        for r in range(1, k.line):
            found.append(
                (
                    lambda r=r: k.z - r,
                    lambda r=r: k.z >= r,
                    "u",
                    "up",
                    lambda r=r: (k.z >= r) & (k.z < k.line - 1),
                )
            )
            found.append(
                (
                    lambda r=r: k.z + r,
                    lambda r=r: k.z + r < k.line,
                    "d",
                    "down",
                    lambda r=r: (k.z + r < k.line) & (k.z > 0),
                )
            )
        return found

    def here(self):
        return self.k.z

    def lower(self):
        return self.k.z < self.k.line - 1

    def upper(self):
        return self.k.z > 0

    def cross(self, z, when, own):
        self.give("xa", "x", z, half=0, when=when, own=own)
        self.give("yb", "y", z, half=1, when=when, own=own)
        self.give("ya", "y", z, half=0, when=when, own=own)
        self.give("xb", "x", z, half=1, when=when, own=own)
        self.give("c0", "core", z, when=when, own=own)

    def start(self):
        self.give("up", "up", self.here, when=self.lower, own=True)
        self.give("down", "down", self.here, when=self.upper, own=True)
        if self.twice:
            for other, kind in ((False, "xa"), (True, "x2")):
                self.give(kind, "x", self.here, other_y=other, own=True)
                self.give("c1" if other else "c0", "core", self.here, other_y=other, own=True)
        else:
            self.cross(self.here, None, True)

    def along(self, number):
        z, exists, _, way, goes_on = self.near()[number]

        @pl.when(exists())
        def _():
            self.get(way, way, z())

        self.give(way, way, z, when=goes_on)
        self.cross(z, exists, False)

    def turn(self, z, when):
        def waits():
            self.get("xa", "x", z(), other_x=True, half=0)

        def waits_too():
            self.get("yb", "y", z(), other_y=True, half=1)

        waits() if when is None else pl.when(when())(waits)
        self.give("ya2", "y", z, other_x=True, half=0, when=when)
        waits_too() if when is None else pl.when(when())(waits_too)
        self.give("xb2", "x", z, other_y=True, half=1, when=when)

    def share(self, z, when):
        def waits(kind, way, **place):
            def wait():
                self.get(kind, way, z(), **place)

            wait() if when is None else pl.when(when())(wait)

        waits("ya", "y", other_y=True, half=0)
        self.give("c1", "core", z, other_y=True, when=when)
        waits("xb", "x", other_x=True, half=1)
        self.give("c2", "core", z, other_x=True, when=when)
        waits("ya2", "y", other_x=True, other_y=True, half=0)
        waits("xb2", "x", other_x=True, other_y=True, half=1)
        self.give("c3", "core", z, other_x=True, other_y=True, when=when)

    def share_twice(self):
        for other, kind in ((False, "xa"), (True, "x2")):
            self.get(kind, "x", self.k.z, other_x=True, other_y=other)
            self.give("c3" if other else "c2", "core", self.here, other_x=True, other_y=other)

    def lift(self, i, own=False):
        place = dict(other_x=i >= 2, other_y=i % 2 == 1)
        self.give(f"u{i}", "up", self.here, when=self.lower, own=own, **place)
        self.give(f"d{i}", "down", self.here, when=self.upper, own=own, **place)
        self.give(f"c{i}", "core", self.here, own=own, **place)

    def start_plane(self):
        if self.twice:
            for other, kind in ((False, "xa"), (True, "x2")):
                self.give(kind, "x", self.here, other_y=other, own=True)
            self.lift(0, True)
            self.lift(1, True)
        else:
            self.give("xa", "x", self.here, half=0, own=True)
            self.give("yb", "y", self.here, half=1, own=True)
            self.give("ya", "y", self.here, half=0, own=True)
            self.give("xb", "x", self.here, half=1, own=True)
            self.lift(0, True)

    def turn_plane(self):
        if self.twice:
            for other, kind in ((False, "xa"), (True, "x2")):
                self.get(kind, "x", self.k.z, other_x=True, other_y=other)
                self.lift(3 if other else 2)
        else:
            self.turn(self.here, None)

    def lift_plane(self):
        if not self.twice:
            z = self.k.z
            self.get("ya", "y", z, other_y=True, half=0)
            self.lift(1)
            self.get("xb", "x", z, other_x=True, half=1)
            self.lift(2)
            self.get("ya2", "y", z, other_x=True, other_y=True, half=0)
            self.get("xb2", "x", z, other_x=True, other_y=True, half=1)
            self.lift(3)

    def along_plane(self, number, i):
        z, exists, letter, way, goes_on = self.near()[number]
        place = dict(other_x=i >= 2, other_y=i % 2 == 1)

        @pl.when(exists())
        def _():
            self.get(f"{letter}{i}", way, z(), **place)

        self.give(f"{letter}{i}", way, z, when=goes_on, **place)
        self.give(f"c{i}", "core", z, when=exists, **place)

    def steps(self):
        count = 2 * (self.k.line - 1)
        if self.z_first:
            one = [self.start]
            two = [lambda n=n: self.along(n) for n in range(count)]
            spots = [(z, exists) for z, exists, _, _, _ in self.near()]
            if not self.twice:
                spots = [(self.here, None)] + spots
            three = [lambda z=z, e=e: self.turn(z, e) for z, e in spots]
            four = [lambda z=z, e=e: self.share(z, e) for z, e in spots]
            if self.twice:
                four = [self.share_twice] + four
            return [one, two, three, four]
        one = [self.start_plane]
        two = [self.turn_plane]
        three = [self.lift_plane]
        four = [lambda n=n, i=i: self.along_plane(n, i) for n in range(count) for i in range(4)]
        return [one, two, three, four]

    def end(self):
        k = self.k
        for z in range(k.line):
            for i in range(4):
                k.arrive(
                    self.spot(z, i >= 2, i % 2 == 1, core=1 - k.c), self.at(f"c{i}", z), "core"
                )


AG_SEMS = len(Gather.KINDS)


def all_gather_kernel(line, swaps, cuts, masters, *refs):
    near, out, far = refs[:swaps], refs[swaps], refs[swaps + 1 : 2 * swaps + 1]
    piece, flat, send_sems, recv_sems, copy_sem = refs[2 * swaps + 1 :]
    links = Links(line, send_sems, recv_sems)

    def pack():
        rows = flat.shape[0] // LANE
        for top in range(0, masters.shape[0], rows):
            pack_rows(masters.at[pl.ds(top, rows)], flat)
            piece[top * LANE : (top + rows) * LANE] = flat[...].astype(BF16)

    links.greet(False, pack)
    rows = piece.shape[0] // 2
    first_rows, second_rows = cuts
    spare = 2 * AG_SEMS * line

    def index(c, z, x, y):
        return (((z * 2 + x) * 2 + c) * 2 + y) * rows

    def keep():
        start = index(links.c, links.z, links.x, 0)
        return pltpu.make_async_copy(
            piece, out.at[pl.ds(pl.multiple_of(start, 16), 2 * rows)], copy_sem
        )

    gathers = []

    def own_of(first, count, cut):
        def own(other, half):
            begin, size = {None: (0, count), 0: (0, cut), 1: (cut, count - cut)}[half]
            y = 1 - links.y if other else links.y
            return piece.at[pl.ds(pl.multiple_of(y * rows + first + begin, 16), size)]

        return own

    last = rows - first_rows - second_rows
    spans = ((0, first_rows + second_rows, first_rows, True), (first_rows + second_rows, last, last // 32 * 16, False))
    for number, (first, count, cut, z_first) in enumerate(spans):
        gathers.append(
            Gather(
                links, number * AG_SEMS * line, own_of(first, count, cut), out, index,
                first, count, cut, z_first, True,
            )
        )
    flat, tall = gathers[0].steps(), gathers[1].steps()
    for step in flat[0] + tall[0]:
        step()
    keep().start()
    for i in range(swaps):
        links.send(lambda i=i: (near[i], far[i], spare + i, "y", None))
    along, rise = flat[1], tall[1] + tall[2]
    turn, share, climb = flat[2], flat[3], tall[3]
    for step in along[:2] + rise + turn[:2] + along[2:4] + climb[:8] + turn[2:4] + along[4:]:
        step()
    for step in climb[8:16] + turn[4:] + share[:3] + climb[16:] + share[3:]:
        step()
    for gather in gathers:
        gather.end()
    keep().wait()
    for i in range(swaps):
        links.arrive(far[i], spare + i, "y")
    links.finish()


def all_gather(masters, swaps, line, collective_id):
    any_space = pl.BlockSpec(memory_space=pl.ANY)
    sems = 2 * AG_SEMS * line + len(swaps)
    count = masters.shape[0] * LANE
    rows = count // 2
    cuts = (rows * 2 // 5 // 16 * 16, rows * 2 // 5 // 16 * 16)
    return pl.pallas_call(
        functools.partial(all_gather_kernel, line, len(swaps), cuts),
        out_shape=[jax.ShapeDtypeStruct((4 * line * count, LANE), BF16)]
        + [jax.ShapeDtypeStruct(s.shape, s.dtype) for s in swaps],
        in_specs=[pl.BlockSpec(memory_space=pltpu.VMEM)] + [any_space] * len(swaps),
        out_specs=[any_space] * (1 + len(swaps)),
        scratch_shapes=[
            pltpu.VMEM((count, LANE), BF16),
            pltpu.VMEM((8 * LANE, LANE), F32),
            pltpu.SemaphoreType.DMA((sems,)),
            pltpu.SemaphoreType.DMA((sems,)),
            pltpu.SemaphoreType.DMA,
        ],
        compiler_params=params(60, collective_id=collective_id, has_side_effects=True),
        cost_estimate=cost(0, 100 * MIB),
        name="all_gather",
    )(masters, *swaps)


PAIRS = D // LANE
UP_ROWS = FF * D // LANE
REST_ROWS = 128 * LANE
HEAD, NORM, LAST = 900, 901, 902
ORDER = (
    100, 0, HEAD, HEAD, 110, 111, 112, 113, 10, 11, 120, HEAD, HEAD, 121, HEAD, HEAD, 122, HEAD,
    HEAD, 123, 12, 13, HEAD, HEAD, HEAD, HEAD, NORM, 130, 20, 21, 131, 132, 133, LAST, 200, 22,
    23, 210, 211, 212, 213, 140, 150, 30, 31, 32, 33, 220, 221, 222, 40, 223, 160, 161, 153, 50,
    51, 52, 230, 231, 232, 233, 53, 170, 171, 154, 151, 152, 60, 61, 240, 155, 54, 62, 63, 250,
    156, 157, 162, 163, 70, 253, 251, 252, 260, 71, 72, 73, 172, 173, 180, 55, 254, 56, 261,
    262, 57, 80, 270, 271, 263, 272, 273, 255, 256, 257, 280,
)


def segments():
    found = [[]]
    for step in ORDER:
        if step >= HEAD:
            found.append([])
        else:
            found[-1].append((step // 100, step // 10 % 10, step % 10))
    return found


def total_kinds(line):
    kinds = []
    for size, late in ((UP_ROWS, 15), (UP_ROWS, 15), (REST_ROWS, 20)):
        rows = size // (8 * line)
        plain = rows - rows * late // 100 // 32 * 32
        kinds.append((size, rows * 72 // 100 // 16 * 16, plain * 30 // 100 // 16 * 16, plain))
    return kinds


def back_kernel(
    line,
    q, k, v, att, grad_att, chance, tokens, tokens_far, n1, att_all, resid_low, w_qkv, vec, vec_one, d_up, d_down,
    d_first, grad_near, out, grad_back, first_back,
    d_q, d_k, d_v, far, d_rest, vec_grad, flat, *scratch,
):
    step = pl.program_id(0)
    sources = (tokens, tokens_far, n1, att_all, resid_low, w_qkv)
    late, late_sems, scratch = scratch[:6], scratch[6], scratch[7:]
    copies = [
        pltpu.make_async_copy(source, target, late_sems.at[i])
        for i, (source, target) in enumerate(zip(sources, late))
    ]
    buffers, (send_sems, recv_sems, load_sems, copy_sems) = scratch[:-4], scratch[-4:]
    links = Links(line, send_sems, recv_sems)
    tops = (REST_ROWS + UP_ROWS, REST_ROWS, 0)
    totals = [
        Total(
            links, g * AR_SEMS * line, source, 0, kind, out, top,
            buffers[7 * g : 7 * g + 7], load_sems.at[g], copy_sems.at[g],
        )
        for g, (source, kind, top) in enumerate(zip((d_down, d_up, d_rest), total_kinds(line), tops))
    ]
    spare = len(totals) * AR_SEMS * line
    plan = segments()

    def run(number):
        for g, stage, part in plan[number]:
            totals[g].run(stage, part)

    queries = q.shape[0]
    for head in range(2):
        for s in range(PAIRS):

            @pl.when(step == s)
            def _(s=s, head=head):
                if s == 0 and head == 0:
                    links.greet(True)
                    for copy in copies:
                        copy.start()
                run(2 * s + head)

        @pl.when(step < PAIRS)
        def _(head=head):
            cols = slice(head * HD, (head + 1) * HD)
            grad = grad_att[:, cols]
            weights = chance[head]
            shared = grad.astype(F32) * att[:, cols].astype(F32)
            delta = jnp.sum(shared.T, axis=0, keepdims=True)
            grad_chance = mm(v[:, cols], grad, NT)
            grad_scores = (weights.astype(F32) * (grad_chance - delta)).astype(BF16)
            grad_value = mm(weights, grad)

            d_v[step, :, cols] = grad_value.astype(BF16)
            d_first[:, cols] = grad_value[:queries]
            d_k[step, :, cols] = mm(grad_scores, q[:, cols]).astype(BF16)
            d_q[step, :, cols] = (mm(k[:, cols], grad_scores, TN).T * HD ** (-0.5)).astype(BF16)

    @pl.when(step == PAIRS)
    def _():
        for copy in copies:
            copy.wait()
        tokens, tokens_far, n1, att_all, resid_low, w_qkv = late
        rows = n1.shape[0] // 2
        per_row = D // LANE
        rows = n1.shape[0] // 2
        first_far = d_v.at[pl.ds(PAIRS // 2, PAIRS // 2), pl.ds(rows, rows)]
        links.send(lambda: (first_far, first_back, spare, "y", None))
        run(2 * PAIRS)
        dq = jnp.concatenate([d_q[i] for i in range(PAIRS)], axis=1)
        dk = jnp.concatenate([d_k[i] for i in range(PAIRS)], axis=1)
        dv = jnp.concatenate([d_v[i] for i in range(PAIRS // 2)], axis=1)
        grads = mm(dk, w_qkv[:, D : 2 * D], NT) + mm(dv, w_qkv[:, 2 * D :], NT)
        beside = grads[rows:]
        far[...] = beside.astype(BF16)
        links.send(lambda: (far, grad_back, spare + 1, "y", None))
        near = grads[:rows] + mm(dq, w_qkv[:, :D], NT)
        grad_near[...] = near
        hat, _ = normed(tokens[...].astype(F32))
        hat_far, _ = normed(tokens_far[...].astype(F32))
        vec_grad[...] = vec_one[...]
        vec_grad[:, :D] = jnp.sum(near * hat, axis=0, keepdims=True) + jnp.sum(
            beside * hat_far, axis=0, keepdims=True
        )
        vec_grad[:, D : 2 * D] = jnp.sum(near, axis=0, keepdims=True) + jnp.sum(
            beside, axis=0, keepdims=True
        )
        vec_grad[:, 4 * D : 5 * D] = jnp.sum(dq.astype(F32), axis=0, keepdims=True)
        vec_grad[:, 7 * D : 7 * D + HV] = jnp.sum(dv.astype(F32), axis=0, keepdims=True)
        run(2 * PAIRS + 1)
        pieces = (
            (n1[:rows], dq, 0, per_row),
            (n1[...], dk, D * per_row, per_row),
            (n1[...], dv, 2 * D * per_row, HV // LANE),
            (att_all[...], resid_low[...], 2 * D * per_row + D * HV // LANE, per_row),
        )
        for left, right, start, columns in pieces:
            product = mm(left, right, TN)
            size = D * columns
            for j in range(columns):
                flat[pl.ds(j, D, stride=columns), :] = product[:, j * LANE : (j + 1) * LANE]
            d_rest[start : start + size] = flat[:size].astype(BF16)
        flat[: 2 * LANE] = jnp.zeros((2 * LANE, LANE), F32)
        for j in range(VEC // LANE):
            flat[j : j + 1] = vec_grad[:, j * LANE : (j + 1) * LANE]
        d_rest[REST:] = flat[: 2 * LANE].astype(BF16)
        run(2 * PAIRS + 2)
        links.arrive(first_back, spare, "y")
        links.arrive(grad_back, spare + 1, "y")
        links.finish()


def back(q, k, v, att, grad_att, chance, tokens, tokens_far, n1, resid_low, w_qkv, vec, vec_one, d_up, d_down, line):
    rows, keys = q.shape[0], k.shape[0]
    any_space = pl.BlockSpec(memory_space=pl.ANY)

    def column(count):
        return pl.BlockSpec((count, LANE), lambda i: (0, jnp.minimum(i, PAIRS - 1)))

    def once(array):
        return pl.BlockSpec(array.shape, lambda i: (0,) * array.ndim, pipeline_mode=pl.Buffered(1))

    kinds = total_kinds(line)
    scratch = []
    for size, cut, _, _ in kinds:
        scratch += Scatter.buffers_of(size // (8 * line), cut, line)
    sems = len(kinds) * AR_SEMS * line + 2
    return pl.pallas_call(
        functools.partial(back_kernel, line),
        out_shape=[
            jax.ShapeDtypeStruct((rows, HV), F32),
            jax.ShapeDtypeStruct((rows, D), F32),
            jax.ShapeDtypeStruct((REST_ROWS + 2 * UP_ROWS, LANE), BF16),
            jax.ShapeDtypeStruct((rows, D), BF16),
            jax.ShapeDtypeStruct((PAIRS // 2, rows, LANE), BF16),
        ],
        grid=(PAIRS + 1,),
        in_specs=[
            column(rows),
            column(keys),
            column(keys),
            column(rows),
            column(rows),
            pl.BlockSpec((2, keys, rows), lambda i: (jnp.minimum(i, PAIRS - 1), 0, 0)),
            any_space,
            any_space,
            any_space,
            any_space,
            any_space,
            any_space,
            once(vec),
            once(vec_one),
            any_space,
            any_space,
        ],
        out_specs=[
            pl.BlockSpec((rows, LANE), lambda i: (0, jnp.clip(i - 3, 0, 2))),
            pl.BlockSpec((rows, D), lambda i: (0, 0), pipeline_mode=pl.Buffered(1)),
            any_space,
            any_space,
            any_space,
        ],
        scratch_shapes=[
            pltpu.VMEM((PAIRS, rows, LANE), BF16),
            pltpu.VMEM((PAIRS, keys, LANE), BF16),
            pltpu.VMEM((PAIRS, keys, LANE), BF16),
            pltpu.VMEM((rows, D), BF16),
            pltpu.VMEM((REST_ROWS, LANE), BF16),
            pltpu.VMEM((1, VEC), F32),
            pltpu.VMEM((D * D // LANE, LANE), F32),
        ]
        + [pltpu.VMEM(a.shape, a.dtype) for a in (tokens, tokens_far, n1, att, resid_low, w_qkv)]
        + [pltpu.SemaphoreType.DMA((6,))]
        + scratch
        + [
            pltpu.SemaphoreType.DMA((sems,)),
            pltpu.SemaphoreType.DMA((sems,)),
            pltpu.SemaphoreType.DMA((len(kinds), 4 * line)),
            pltpu.SemaphoreType.DMA((len(kinds),)),
        ],
        compiler_params=params(62, collective_id=0, has_side_effects=True),
        cost_estimate=cost(8 * rows * keys * D + 14 * rows * D * D, 100 * MIB),
        name="back",
    )(q, k, v, att, grad_att, chance, tokens, tokens_far, n1, att, resid_low, w_qkv, vec, vec_one, d_up, d_down)


def swap(value):
    return lax.ppermute(value, "seq", [(0, 1), (1, 0)])


def shards(
    tokens,
    first_values,
    out_grad,
    block_place,
    owners,
    masters,
    moment_one,
    moment_two,
    vector_master,
    vector_moment_one,
    vector_moment_two,
):
    capacity = masters.shape[0]
    dp_count = lax.axis_size("dp")
    tile_count = owners.shape[0]
    dp_here = lax.axis_index("dp")
    seq_here = lax.axis_index("seq")
    _, half_len, _ = tokens.shape

    tokens = tokens.reshape(half_len, D)
    firsts = first_values.reshape(half_len, HV)
    given = out_grad.reshape(half_len, D)
    line = dp_count // 4
    if line == LINE and capacity % 8 == 0:
        slots, tokens_far, firsts_far = all_gather(masters, [tokens, firsts], line, 1)
    else:
        tokens_far, firsts_far = swap(tokens), swap(firsts)
        slots = lax.all_gather(pack_slots(masters), "dp", axis=0, tiled=True)

    slot_index = slot_numbers(owners)
    slot_rows = owners * capacity + slot_index
    mine = (owners == dp_here)[None, :] & (
        slot_index[None, :] == jnp.arange(capacity, dtype=jnp.int32)[:, None]
    )
    tile_order = jnp.arange(tile_count, dtype=jnp.int32)
    gap = REST_ROWS // LANE - 126
    tile_place = tile_order + jnp.where(tile_order >= 126, gap, 0)
    places = jnp.sum(jnp.where(mine, tile_place[None, :] + 1, 0), axis=1) - 1

    vec = vector_master.reshape(1, VEC)
    w_qkv, w_out, w_up, w_down = unpack_weights(slot_rows, slots)
    n1, q, k, v = project(tokens, tokens_far, firsts, firsts_far, w_qkv, vec)
    att, chance = attend(block_place, q, k, v)
    result, grad_resid, resid_low, grad_att, d_up, d_down, vec_one = hidden(
        tokens, att, given, w_out, w_up, w_down, vec
    )
    if line == LINE:
        first_near, grad_near, grads, grad_back, first_back = back(
            q, k, v, att, grad_att, chance, tokens, tokens_far, n1, resid_low, w_qkv, vec, vec_one, d_up, d_down, line
        )
    else:
        d_q, d_k, d_fresh, d_first = attend_back(q, k, v, att, grad_att, chance)
        grad_near, grad_far, d_rest = project_back(
            jnp.concatenate([tokens, tokens_far], axis=0), n1, d_q, d_k, d_fresh, att, resid_low, w_qkv, vec, vec_one
        )
        first_near = d_first[:half_len]
        grad_back, first_back = swap(grad_far), swap(d_first[half_len:].astype(BF16))
        first_back = first_back.reshape(half_len, HV // LANE, LANE).transpose(1, 0, 2)
        grads = lax.psum(jnp.concatenate([d_rest, d_up, d_down], axis=0), ("seq", "dp"))
    vectors = [
        v.reshape(VEC // LANE, LANE) for v in (vector_master, vector_moment_one, vector_moment_two)
    ]
    new_master, new_one, new_two, new_low, tokens_grad, first_grad, *new_vectors = finish(
        places, grads, masters, moment_one, moment_two,
        grad_resid, grad_near, grad_back, tokens, vec, first_near, first_back, vectors,
    )
    return (
        result.reshape(1, half_len, D),
        tokens_grad.reshape(1, half_len, D),
        first_grad.reshape(1, half_len, HV),
        new_master,
        new_one,
        new_two,
        new_low,
        *(v.reshape(VEC) for v in new_vectors),
    )


def solution(mesh):
    rows = P("dp", "seq", None)
    slots = P("dp", None)
    return jax.shard_map(
        shards,
        mesh=mesh,
        in_specs=(rows, rows, rows, slots, P(), slots, slots, slots, P(), P(), P()),
        out_specs=(rows, rows, rows, slots, slots, slots, slots, P(), P(), P()),
        check_vma=False,
    )
```

```python
import functools

import jax
import jax.numpy as jnp
from jax import lax
from jax.experimental import pallas as pl
from jax.experimental.pallas import tpu as pltpu
from jax.sharding import PartitionSpec as P

D = 768
HD = 64
FF = 3072
STEP = 10
HV = 384
LANE = 128
QKV = 2 * D + HV
FF_STEP = 768
VEC = 7 * D + HV + FF
MIB = 1024 * 1024
LINE = 4
REST = 126 * LANE

EPS_NORM = 1e-05
EPS_ADAM = 1e-08
BETA_ONE = 0.5
BETA_TWO = 0.5
RATE_MATRIX = 0.03
RATE_VECTOR = 0.25
DECAY_MATRIX = 0.1
FAR = -1e30

BF16 = jnp.bfloat16
F32 = jnp.float32

NN = (((1,), (0,)), ((), ()))
NT = (((1,), (1,)), ((), ()))
TN = (((0,), (0,)), ((), ()))


def mm(left, right, dims=NN):
    return lax.dot_general(left, right, dims, preferred_element_type=F32)


def vec_part(vec_ref, index):
    if index < 7:
        return vec_ref[:, index * D : (index + 1) * D]
    if index == 7:
        return vec_ref[:, 7 * D : 7 * D + HV]
    return vec_ref[:, 7 * D + HV :]


def params(mib, **more):
    return pltpu.CompilerParams(vmem_limit_bytes=mib * MIB, **more)


def whole(shape):
    return pl.BlockSpec(shape, lambda *_: (0,) * len(shape))


def cost(flops, bytes_accessed, transcendentals=0):
    return pl.CostEstimate(
        flops=int(flops), bytes_accessed=int(bytes_accessed), transcendentals=int(transcendentals)
    )


def adam_step(weight, first_moment, second_moment, gradient, step_rate, weight_decay):
    first_new = BETA_ONE * first_moment + (1.0 - BETA_ONE) * gradient
    second_new = BETA_TWO * second_moment + (1.0 - BETA_TWO) * gradient * gradient
    first_fix = 1.0 - BETA_ONE**STEP
    second_fix = 1.0 - BETA_TWO**STEP
    update = (first_new * (1.0 / first_fix)) / (jnp.sqrt(second_new * (1.0 / second_fix)) + EPS_ADAM)
    return (weight - step_rate * (update + weight_decay * weight), first_new, second_new)


def slot_numbers(owners):
    tile_order = jnp.arange(owners.shape[0], dtype=jnp.int32)
    earlier = (owners[None, :] == owners[:, None]) & (tile_order[None, :] < tile_order[:, None])
    return jnp.sum(earlier.astype(jnp.int32), axis=1)


def normed(values):
    center = jnp.mean(values, axis=-1, keepdims=True)
    centred = values - center
    spread = jnp.mean(centred * centred, axis=-1, keepdims=True)
    rate = lax.rsqrt(spread + EPS_NORM)
    return centred * rate, rate


def norm_back(grad, hat, rate, gain):
    g = grad * gain
    return rate * (
        g - jnp.mean(g, axis=-1, keepdims=True) - hat * jnp.mean(g * hat, axis=-1, keepdims=True)
    )


def pack_rows(src, flat):
    rows = src.shape[0]
    for c in range(LANE):
        flat[pl.ds(c, rows, stride=LANE), :] = src[:, c * LANE : (c + 1) * LANE]


def pack_kernel(src, dst, flat):
    pack_rows(src, flat)
    dst[...] = flat[...].astype(BF16)


def pack_slots(masters):
    capacity, tile_len = masters.shape
    rows = 8 if capacity % 8 == 0 else capacity
    return pl.pallas_call(
        pack_kernel,
        out_shape=jax.ShapeDtypeStruct((capacity * LANE, LANE), BF16),
        grid=(capacity // rows,),
        in_specs=[pl.BlockSpec((rows, tile_len), lambda i: (i, 0))],
        out_specs=pl.BlockSpec((rows * LANE, LANE), lambda i: (i, 0)),
        scratch_shapes=[pltpu.VMEM((rows * LANE, LANE), F32)],
        compiler_params=params(60),
        cost_estimate=cost(0, capacity * tile_len * 6),
        name="pack_slots",
    )(masters)


def weight_chunks():
    chunks = [
        (0, 36, 6, 0, 0, 0),
        (36, 36, 6, 0, D, 0),
        (72, 18, 3, 0, 2 * D, 0),
        (90, 36, 6, 1, 0, 0),
    ]
    for i in range(4):
        chunks.append((126 + 36 * i, 36, 24, 2, 0, 192 * i))
    for i in range(4):
        chunks.append((270 + 36 * i, 36, 6, 3, 0, 768 * i))
    return chunks


def unpack_kernel(slot_rows, slots, w_qkv, w_out, w_up, w_down, stage, o_qkv, o_out, o_up, o_down, flat, sems, out_sems):
    chunks = weight_chunks()
    places = (o_qkv, o_out, o_up, o_down)
    ends = (w_qkv, w_out, w_up, w_down)

    for number, (first, tiles, _, _, _, _) in enumerate(chunks):

        @pl.loop(0, tiles)
        def _(i, first=first, number=number):
            t = first + i
            pltpu.make_async_copy(
                slots.at[pl.ds(pl.multiple_of(slot_rows[t] * LANE, LANE), LANE)],
                stage.at[pl.ds(pl.multiple_of(t * LANE, LANE), LANE)],
                sems.at[number],
            ).start()

    copies = []
    for number, (first, tiles, per_row, matrix, column, row) in enumerate(chunks):
        span = pl.ds(first * LANE, tiles * LANE)
        pltpu.make_async_copy(stage.at[span], stage.at[span], sems.at[number]).wait()
        place = places[matrix]
        lines = 3 * LANE // per_row

        @pl.loop(0, tiles // 6)
        def _(g, first=first, per_row=per_row, place=place, column=column, row=row, lines=lines):
            for half in range(2):
                base = pl.multiple_of(first * LANE + (2 * g + half) * 3 * LANE, LANE)
                flat[half] = stage[pl.ds(base, 3 * LANE), :].astype(F32)
            for half in range(2):
                top = pl.multiple_of(row + (2 * g + half) * lines, 16)
                for j in range(per_row):
                    place[pl.ds(top, lines), column + j * LANE : column + (j + 1) * LANE] = flat[
                        half, pl.ds(j, lines, stride=per_row), :
                    ].astype(BF16)

        rows = tiles * LANE // per_row
        columns = pl.ds(column, per_row * LANE)
        copy = pltpu.make_async_copy(
            place.at[pl.ds(row, rows), columns],
            ends[matrix].at[pl.ds(row, rows), columns],
            out_sems.at[number],
        )
        copy.start()
        copies.append(copy)
    for copy in copies:
        copy.wait()


def unpack_weights(slot_rows, slots):
    tile_count = slot_rows.shape[0]
    shapes = [(D, QKV), (D, D), (D, FF), (FF, D)]
    any_space = pl.BlockSpec(memory_space=pl.ANY)
    return pl.pallas_call(
        unpack_kernel,
        out_shape=[jax.ShapeDtypeStruct(s, BF16) for s in shapes],
        grid_spec=pltpu.PrefetchScalarGridSpec(
            num_scalar_prefetch=1,
            grid=(1,),
            in_specs=[any_space],
            out_specs=[any_space] * 4,
            scratch_shapes=[pltpu.VMEM((tile_count * LANE, LANE), BF16)]
            + [pltpu.VMEM(s, BF16) for s in shapes]
            + [
                pltpu.VMEM((2, 3 * LANE, LANE), F32),
                pltpu.SemaphoreType.DMA((12,)),
                pltpu.SemaphoreType.DMA((12,)),
            ],
        ),
        compiler_params=params(60),
        cost_estimate=cost(0, 4 * tile_count * LANE * LANE),
        name="unpack_weights",
    )(slot_rows, slots)


def project_kernel(near, far, firsts, firsts_far, w_qkv, vec, n1, q, k, v):
    first = pl.program_id(0) == 0
    tokens = jnp.where(first, near[...], far[...])
    hat, _ = normed(tokens.astype(F32))
    low = (hat * vec_part(vec, 0) + vec_part(vec, 1)).astype(BF16)
    n1[...] = low
    k[...] = mm(low, w_qkv[:, D : 2 * D]).astype(BF16)
    v[:, :HV] = (mm(low, w_qkv[:, 2 * D :]) + vec_part(vec, 7)).astype(BF16)
    v[:, HV:] = jnp.where(first, firsts[...], firsts_far[...])

    @pl.when(first)
    def _():
        query = mm(low, w_qkv[:, :D]) + vec_part(vec, 4)
        q[...] = (query.astype(BF16).astype(F32) * HD ** (-0.5)).astype(BF16)


def project(near, far, firsts, firsts_far, w_qkv, vec):
    rows = near.shape[0]
    by_row = pl.BlockSpec((rows, D), lambda i: (i, 0))
    return pl.pallas_call(
        project_kernel,
        out_shape=[
            jax.ShapeDtypeStruct((2 * rows, D), BF16),
            jax.ShapeDtypeStruct((rows, D), BF16),
            jax.ShapeDtypeStruct((2 * rows, D), BF16),
            jax.ShapeDtypeStruct((2 * rows, D), BF16),
        ],
        grid=(2,),
        in_specs=[
            whole((rows, D)),
            whole((rows, D)),
            whole((rows, HV)),
            whole((rows, HV)),
            whole((D, QKV)),
            whole((1, VEC)),
        ],
        out_specs=[by_row, whole((rows, D)), by_row, by_row],
        compiler_params=params(60),
        cost_estimate=cost(4 * rows * D * QKV, 2 * D * QKV + rows * D * 20),
        name="project",
    )(near, far, firsts, firsts_far, w_qkv, vec)


def attend_kernel(places, q, k, v, out, chance, bias):
    @pl.when(pl.program_id(0) == 0)
    def _():
        here = lax.axis_index("seq")
        count = places.shape[1] // 2
        size = q.shape[0] // count
        ahead = lax.broadcasted_iota(jnp.int32, (size, size), 0) - lax.broadcasted_iota(
            jnp.int32, (size, size), 1
        )
        for i in range(2 * count):
            side = here if i < count else 1 - here
            key_place = places[0, side * count + i % count]
            for j in range(count):
                shift = (places[0, here * count + j] - key_place) * size
                bias[i * size : (i + 1) * size, j * size : (j + 1) * size] = jnp.where(
                    ahead <= shift, 0.0, FAR
                )

    heads = [slice(head * HD, (head + 1) * HD) for head in range(2)]
    scores = [mm(k[:, cols], q[:, cols], NT) + bias[...] for cols in heads]
    for head in range(2):
        top = jnp.max(scores[head], axis=0, keepdims=True)
        power = jnp.exp(scores[head] - top)
        total = jnp.sum(power, axis=0, keepdims=True)
        chance[head] = (power * (1.0 / total)).astype(BF16)
    for head, cols in enumerate(heads):
        out[:, cols] = mm(v[:, cols], chance[head], TN).T.astype(BF16)


def attend(places, q, k, v):
    queries, keys = q.shape[0], k.shape[0]
    pairs = D // LANE
    by_column = lambda i, *_: (0, i)
    return pl.pallas_call(
        attend_kernel,
        out_shape=[
            jax.ShapeDtypeStruct((queries, D), BF16),
            jax.ShapeDtypeStruct((2 * pairs, keys, queries), BF16),
        ],
        grid_spec=pltpu.PrefetchScalarGridSpec(
            num_scalar_prefetch=1,
            grid=(pairs,),
            in_specs=[
                pl.BlockSpec((queries, LANE), by_column),
                pl.BlockSpec((keys, LANE), by_column),
                pl.BlockSpec((keys, LANE), by_column),
            ],
            out_specs=[
                pl.BlockSpec((queries, LANE), by_column),
                pl.BlockSpec((2, keys, queries), lambda i, *_: (i, 0, 0)),
            ],
            scratch_shapes=[pltpu.VMEM((keys, queries), F32)],
        ),
        compiler_params=params(60),
        cost_estimate=cost(4 * queries * keys * D, 24 * queries * keys, 12 * queries * keys),
        name="attend",
    )(places, q, k, v)


def hidden_kernel(
    tokens, att, og, w_out, w_up, w_down, vec,
    result, grad_resid, resid_low, grad_att, d_up, d_down, vec_grad,
    resid, hat, n2, rate, acc, acc_grad, flat_up, flat_down,
):
    step = pl.program_id(0)
    per_row = D // LANE
    wide = FF // LANE

    @pl.when(step == 0)
    def _():
        base = tokens[...].astype(F32) + mm(att[...], w_out[...]) + vec_part(vec, 5)
        resid[...] = base
        unit, scale = normed(base)
        hat[...] = unit
        rate[...] = scale
        n2[...] = (unit * vec_part(vec, 2) + vec_part(vec, 3)).astype(BF16)
        vec_grad[...] = jnp.zeros_like(vec_grad)
        acc[...] = jnp.zeros_like(acc)
        acc_grad[...] = jnp.zeros_like(acc_grad)

    start = pl.multiple_of(7 * D + HV + step * FF_STEP, LANE)
    pre = mm(n2[...], w_up[...]) + vec[:, pl.ds(start, FF_STEP)]
    square = pre * pre
    bent = jnp.tanh(0.7978845608028654 * (pre + 0.044715 * square * pre))
    half = 0.5 * (1.0 + bent)
    act = (pre * half).astype(BF16)
    slope = half + (0.5 * 0.7978845608028654) * pre * (1.0 - bent * bent) * (1.0 + 0.134145 * square)
    grad_pre32 = mm(og[...], w_down[...], NT) * slope
    grad_pre = grad_pre32.astype(BF16)
    vec_grad[:, pl.ds(start, FF_STEP)] = jnp.sum(grad_pre.astype(F32), axis=0, keepdims=True)
    acc[...] += mm(act, w_down[...])
    acc_grad[...] += mm(grad_pre, w_up[...], NT)
    down = mm(act, og[...], TN)
    for j in range(per_row):
        flat_down[pl.ds(j, FF_STEP, stride=per_row), :] = down[:, j * LANE : (j + 1) * LANE]
    d_down[...] = flat_down[...].astype(BF16)
    up = mm(n2[...], grad_pre, TN)
    for j in range(FF_STEP // LANE):
        flat_up[pl.ds(step * (FF_STEP // LANE) + j, D, stride=wide), :] = up[
            :, j * LANE : (j + 1) * LANE
        ]

    @pl.when(step == FF // FF_STEP - 1)
    def _():
        d_up[...] = flat_up[...].astype(BF16)
        result[...] = (resid[...] + acc[...] + vec_part(vec, 6)).astype(BF16)
        grad = acc_grad[...]
        unit = hat[...]
        vec_grad[:, 2 * D : 3 * D] = jnp.sum(grad * unit, axis=0, keepdims=True)
        vec_grad[:, 3 * D : 4 * D] = jnp.sum(grad, axis=0, keepdims=True)
        given = og[...].astype(F32)
        back = given + norm_back(grad, unit, rate[...], vec_part(vec, 2))
        grad_resid[...] = back
        low = back.astype(BF16)
        resid_low[...] = low
        vec_grad[:, 5 * D : 6 * D] = jnp.sum(low.astype(F32), axis=0, keepdims=True)
        vec_grad[:, 6 * D : 7 * D] = jnp.sum(given, axis=0, keepdims=True)
        grad_att[...] = mm(low, w_out[...], NT).astype(BF16)


def hidden(tokens, att, og, w_out, w_up, w_down, vec):
    rows = tokens.shape[0]
    line = (rows, D)
    flat_rows = FF * D // LANE
    return pl.pallas_call(
        hidden_kernel,
        out_shape=[
            jax.ShapeDtypeStruct(line, BF16),
            jax.ShapeDtypeStruct(line, F32),
            jax.ShapeDtypeStruct(line, BF16),
            jax.ShapeDtypeStruct(line, BF16),
            jax.ShapeDtypeStruct((flat_rows, LANE), BF16),
            jax.ShapeDtypeStruct((flat_rows, LANE), BF16),
            jax.ShapeDtypeStruct((1, VEC), F32),
        ],
        grid=(FF // FF_STEP,),
        in_specs=[
            whole(line),
            whole(line),
            whole(line),
            whole((D, D)),
            pl.BlockSpec((D, FF_STEP), lambda i: (0, i)),
            pl.BlockSpec((FF_STEP, D), lambda i: (i, 0)),
            whole((1, VEC)),
        ],
        out_specs=[
            whole(line),
            whole(line),
            whole(line),
            whole(line),
            whole((flat_rows, LANE)),
            pl.BlockSpec((FF_STEP * D // LANE, LANE), lambda i: (i, 0)),
            whole((1, VEC)),
        ],
        scratch_shapes=[
            pltpu.VMEM(line, F32),
            pltpu.VMEM(line, F32),
            pltpu.VMEM(line, BF16),
            pltpu.VMEM((rows, 1), F32),
            pltpu.VMEM(line, F32),
            pltpu.VMEM(line, F32),
            pltpu.VMEM((flat_rows, LANE), F32),
            pltpu.VMEM((FF_STEP * D // LANE, LANE), F32),
        ],
        compiler_params=params(62),
        cost_estimate=cost(2 * rows * D * (6 * FF + 2 * D), 8 * D * FF + 20 * rows * D, rows * FF),
        name="hidden",
    )(tokens, att, og, w_out, w_up, w_down, vec)


def attend_back_kernel(q, k, v, att, grad_att, chance, d_q, d_k, d_fresh, d_first):
    pair = pl.program_id(0)
    for head in range(2):
        cols = slice(head * HD, (head + 1) * HD)
        grad = grad_att[:, cols]
        weights = chance[head]
        shared = grad.astype(F32) * att[:, cols].astype(F32)
        delta = jnp.sum(shared.T, axis=0, keepdims=True)
        grad_chance = mm(v[:, cols], grad, NT)
        grad_scores = (weights.astype(F32) * (grad_chance - delta)).astype(BF16)
        grad_value = mm(weights, grad)

        @pl.when(pair < 3)
        def _(grad_value=grad_value, cols=cols):
            d_fresh[:, cols] = grad_value.astype(BF16)

        @pl.when(pair >= 3)
        def _(grad_value=grad_value, cols=cols):
            d_first[:, cols] = grad_value

        d_k[:, cols] = mm(grad_scores, q[:, cols]).astype(BF16)
        d_q[:, cols] = (mm(k[:, cols], grad_scores, TN).T * HD ** (-0.5)).astype(BF16)


def attend_back(q, k, v, att, grad_att, chance):
    queries, keys = q.shape[0], k.shape[0]
    pairs = D // LANE
    by_column = lambda i: (0, i)
    return pl.pallas_call(
        attend_back_kernel,
        out_shape=[
            jax.ShapeDtypeStruct((queries, D), BF16),
            jax.ShapeDtypeStruct((keys, D), BF16),
            jax.ShapeDtypeStruct((keys, HV), BF16),
            jax.ShapeDtypeStruct((keys, HV), F32),
        ],
        grid=(pairs,),
        in_specs=[
            pl.BlockSpec((queries, LANE), by_column),
            pl.BlockSpec((keys, LANE), by_column),
            pl.BlockSpec((keys, LANE), by_column),
            pl.BlockSpec((queries, LANE), by_column),
            pl.BlockSpec((queries, LANE), by_column),
            pl.BlockSpec((2, keys, queries), lambda i: (i, 0, 0)),
        ],
        out_specs=[
            pl.BlockSpec((queries, LANE), by_column),
            pl.BlockSpec((keys, LANE), by_column),
            pl.BlockSpec((keys, LANE), lambda i: (0, jnp.minimum(i, 2))),
            pl.BlockSpec((keys, LANE), lambda i: (0, jnp.maximum(i - 3, 0))),
        ],
        compiler_params=params(60),
        cost_estimate=cost(8 * queries * keys * D, 24 * queries * keys),
        name="attend_back",
    )(q, k, v, att, grad_att, chance)


def project_back_kernel(
    tokens, n1, d_q, d_k, d_fresh, att, resid_low, w_qkv, vec, vec_one,
    grad_near, grad_far, d_rest, vec_grad, flat,
):
    rows = n1.shape[0] // 2
    per_row = D // LANE
    grads = mm(d_k[...], w_qkv[:, D : 2 * D], NT) + mm(d_fresh[...], w_qkv[:, 2 * D :], NT)
    near = grads[:rows] + mm(d_q[...], w_qkv[:, :D], NT)
    far = grads[rows:]
    grad_near[...] = near
    grad_far[...] = far.astype(BF16)
    hat, _ = normed(tokens[...].astype(F32))
    vec_grad[...] = vec_one[...]
    vec_grad[:, :D] = jnp.sum(near * hat[:rows], axis=0, keepdims=True) + jnp.sum(
        far * hat[rows:], axis=0, keepdims=True
    )
    vec_grad[:, D : 2 * D] = jnp.sum(near, axis=0, keepdims=True) + jnp.sum(
        far, axis=0, keepdims=True
    )
    vec_grad[:, 4 * D : 5 * D] = jnp.sum(d_q[...].astype(F32), axis=0, keepdims=True)
    vec_grad[:, 7 * D : 7 * D + HV] = jnp.sum(d_fresh[...].astype(F32), axis=0, keepdims=True)
    pieces = (
        (n1, d_q, rows, 0, per_row),
        (n1, d_k, 2 * rows, D * per_row, per_row),
        (n1, d_fresh, 2 * rows, 2 * D * per_row, HV // LANE),
        (att, resid_low, rows, 2 * D * per_row + D * HV // LANE, per_row),
    )
    for left, right, count, start, columns in pieces:
        product = mm(left[:count], right[:count], TN)
        size = D * columns
        for j in range(columns):
            flat[pl.ds(j, D, stride=columns), :] = product[:, j * LANE : (j + 1) * LANE]
        d_rest[start : start + size] = flat[:size].astype(BF16)
    flat[: 2 * LANE] = jnp.zeros((2 * LANE, LANE), F32)
    for j in range(VEC // LANE):
        flat[j : j + 1] = vec_grad[:, j * LANE : (j + 1) * LANE]
    d_rest[REST:] = flat[: 2 * LANE].astype(BF16)


def project_back(tokens, n1, d_q, d_k, d_fresh, att, resid_low, w_qkv, vec, vec_one):
    rows = n1.shape[0] // 2
    vm = pl.BlockSpec(memory_space=pltpu.VMEM)
    return pl.pallas_call(
        project_back_kernel,
        out_shape=[
            jax.ShapeDtypeStruct((rows, D), F32),
            jax.ShapeDtypeStruct((rows, D), BF16),
            jax.ShapeDtypeStruct((128 * LANE, LANE), BF16),
        ],
        in_specs=[vm] * 10,
        out_specs=[vm] * 3,
        scratch_shapes=[pltpu.VMEM((1, VEC), F32), pltpu.VMEM((D * D // LANE, LANE), F32)],
        compiler_params=params(58),
        cost_estimate=cost(2 * rows * D * (7 * D), 14 * MIB),
        name="project_back",
    )(tokens, n1, d_q, d_k, d_fresh, att, resid_low, w_qkv, vec, vec_one)


def finish_kernel(
    places, grads, weight, one, two,
    resid, near, far, tokens, vec, firsts, firsts_far, vec_weight, vec_one, vec_two,
    new, new_one, new_two, low, tokens_grad, first_grad, new_vec, new_vec_one, new_vec_two,
    stage, flat, vec_stage, v_weight, v_one, v_two, v_low,
    v_resid, v_near, v_far, v_tokens, v_firsts, v_firsts_far,
    slot_sems, in_sems, out_sems, side_sems, vec_sem,
):
    capacity = weight.shape[0]
    rows = flat.shape[0] // LANE
    steps = capacity // rows

    def span(s):
        return pl.ds(s * rows, rows)

    vec_copy = pltpu.make_async_copy(grads.at[pl.ds(REST, vec_stage.shape[0])], vec_stage, vec_sem)
    vec_copy.start()
    brought = []
    for s in range(steps):
        for i, (source, target) in enumerate(((weight, v_weight), (one, v_one), (two, v_two))):
            brought.append(
                pltpu.make_async_copy(source.at[span(s)], target.at[span(s)], in_sems.at[3 * s + i])
            )
            brought[-1].start()

        @pl.loop(0, rows)
        def _(i, s=s):
            slot = s * rows + i
            pltpu.make_async_copy(
                grads.at[pl.ds(pl.multiple_of(jnp.maximum(places[slot], 0) * LANE, LANE), LANE)],
                stage.at[pl.ds(pl.multiple_of(slot * LANE, LANE), LANE)],
                slot_sems.at[s],
            ).start()

    sides = [
        pltpu.make_async_copy(source, target, side_sems.at[i])
        for i, (source, target) in enumerate(
            (
                (resid, v_resid),
                (near, v_near),
                (far, v_far),
                (tokens, v_tokens),
                (firsts, v_firsts),
                (firsts_far, v_firsts_far),
            )
        )
    ]
    for copy in sides:
        copy.start()
    sent = []
    for s in range(steps):
        for copy in brought[3 * s : 3 * s + 3]:
            copy.wait()
        tile = pl.ds(s * rows * LANE, rows * LANE)
        pltpu.make_async_copy(stage.at[tile], stage.at[tile], slot_sems.at[s]).wait()
        flat[...] = stage[tile, :].astype(F32)
        line = lax.broadcasted_iota(jnp.int32, (rows, LANE), 0)
        taken = jnp.zeros((rows, LANE), jnp.int32)
        for i in range(rows):
            taken = jnp.where(line == i, places[s * rows + i], taken)
        keep = taken >= 0
        for c in range(LANE):
            columns = slice(c * LANE, (c + 1) * LANE)
            gradient = jnp.where(keep, flat[pl.ds(c, rows, stride=LANE), :], 0.0)
            after, after_one, after_two = adam_step(
                v_weight[span(s), columns], v_one[span(s), columns], v_two[span(s), columns],
                gradient, RATE_MATRIX, DECAY_MATRIX,
            )
            v_weight[span(s), columns] = after
            v_one[span(s), columns] = after_one
            v_two[span(s), columns] = after_two
            v_low[s, :, columns] = after.astype(BF16)
        for i, (source, target) in enumerate(
            (
                (v_weight.at[span(s)], new.at[span(s)]),
                (v_one.at[span(s)], new_one.at[span(s)]),
                (v_two.at[span(s)], new_two.at[span(s)]),
            )
        ):
            sent.append(pltpu.make_async_copy(source, target, out_sems.at[3 * s + i]))
            sent[-1].start()
    for s in range(steps):
        low[span(s), :] = v_low[s]
    vec_copy.wait()
    count = vec_weight.shape[0]
    after, after_one, after_two = adam_step(
        vec_weight[...], vec_one[...], vec_two[...],
        vec_stage[...].astype(F32)[:count], RATE_VECTOR, 0.0,
    )
    new_vec[...] = after
    new_vec_one[...] = after_one
    new_vec_two[...] = after_two
    for copy in sides:
        copy.wait()
    grad = v_near[...] + v_far[...].astype(F32)
    hat, rate = normed(v_tokens[...].astype(F32))
    v_resid[...] += norm_back(grad, hat, rate, vec_part(vec, 0))
    for i in range(HV // LANE):
        columns = slice(i * LANE, (i + 1) * LANE)
        v_firsts[:, columns] += v_firsts_far[i].astype(F32)
    for i, (source, target) in enumerate(((v_resid, tokens_grad), (v_firsts, first_grad))):
        sent.append(pltpu.make_async_copy(source, target, side_sems.at[i]))
        sent[-1].start()
    for copy in sent:
        copy.wait()


def finish(places, grads, weight, one, two, resid, near, far, tokens, vec, firsts, firsts_far, vectors):
    capacity, tile_len = weight.shape
    rows = 8 if capacity % 8 == 0 else capacity
    steps = capacity // rows
    flat_vec = vectors[0].shape
    any_space = pl.BlockSpec(memory_space=pl.ANY)
    sides = [resid, near, far, tokens, firsts, firsts_far]
    return pl.pallas_call(
        finish_kernel,
        out_shape=[jax.ShapeDtypeStruct(weight.shape, F32)] * 3
        + [jax.ShapeDtypeStruct(weight.shape, BF16)]
        + [jax.ShapeDtypeStruct(resid.shape, F32), jax.ShapeDtypeStruct(firsts.shape, F32)]
        + [jax.ShapeDtypeStruct(flat_vec, F32)] * 3,
        grid_spec=pltpu.PrefetchScalarGridSpec(
            num_scalar_prefetch=1,
            grid=(1,),
            in_specs=[any_space] * 8
            + [whole((1, VEC))]
            + [any_space] * 2
            + [whole(flat_vec)] * 3,
            out_specs=[any_space] * 3 + [whole(weight.shape)] + [any_space] * 2 + [whole(flat_vec)] * 3,
            scratch_shapes=[
                pltpu.VMEM((capacity * LANE, LANE), BF16),
                pltpu.VMEM((rows * LANE, LANE), F32),
                pltpu.VMEM((80, LANE), BF16),
                pltpu.VMEM(weight.shape, F32),
                pltpu.VMEM(weight.shape, F32),
                pltpu.VMEM(weight.shape, F32),
                pltpu.VMEM((steps, rows, tile_len), BF16),
            ]
            + [pltpu.VMEM(side.shape, side.dtype) for side in sides]
            + [
                pltpu.SemaphoreType.DMA((steps,)),
                pltpu.SemaphoreType.DMA((3 * steps,)),
                pltpu.SemaphoreType.DMA((3 * steps,)),
                pltpu.SemaphoreType.DMA((len(sides),)),
                pltpu.SemaphoreType.DMA,
            ],
        ),
        compiler_params=params(60),
        cost_estimate=cost(20 * capacity * tile_len, 28 * capacity * tile_len, 2 * capacity * tile_len),
        name="finish",
    )(places, grads, weight, one, two, resid, near, far, tokens, vec, firsts, firsts_far, *vectors)


class Links:
    def __init__(self, line, send_sems, recv_sems):
        dp = lax.axis_index("dp")
        self.line = line
        self.y = lax.axis_index("seq")
        self.z = dp // 4
        self.x = (dp // 2) % 2
        self.c = dp % 2
        self.send_sems, self.recv_sems = send_sems, recv_sems
        self.to = {
            "core": {"dp": self.z * 4 + self.x * 2 + (1 - self.c)},
            "x": {"dp": self.z * 4 + (1 - self.x) * 2 + self.c},
            "y": {"seq": 1 - self.y},
            "up": {"dp": dp + 4},
            "down": {"dp": dp - 4},
        }
        self.sent = []

    def greet(self, whole_line, meanwhile=lambda: None):
        barrier = pltpu.get_barrier_semaphore()
        for name in ("core", "x", "y"):
            pl.semaphore_signal(barrier, inc=1, device_id=self.to[name])
        if whole_line:
            for d in range(1, self.line):
                z = (self.z + d) % self.line
                pl.semaphore_signal(barrier, inc=1, device_id={"dp": z * 4 + self.x * 2 + self.c})
            meanwhile()
            pl.semaphore_wait(barrier, 2 + self.line)
            return

        @pl.when(self.z > 0)
        def _():
            pl.semaphore_signal(barrier, inc=1, device_id=self.to["down"])

        @pl.when(self.z < self.line - 1)
        def _():
            pl.semaphore_signal(barrier, inc=1, device_id=self.to["up"])

        meanwhile()
        pl.semaphore_wait(
            barrier,
            3 + jnp.where(self.z > 0, 1, 0) + jnp.where(self.z < self.line - 1, 1, 0),
        )

    def copy(self, source, target, index, way):
        sender, receiver = index if isinstance(index, tuple) else (index, index)
        to = self.to[way] if isinstance(way, str) else {"dp": way * 4 + self.x * 2 + self.c}
        return pltpu.make_async_remote_copy(
            src_ref=source,
            dst_ref=target,
            send_sem=self.send_sems.at[sender],
            recv_sem=self.recv_sems.at[receiver],
            device_id=to,
        )

    def send(self, describe):
        source, target, index, way, when = describe()
        if when is None:
            self.copy(source, target, index, way).start()
        else:

            @pl.when(when)
            def _():
                self.copy(source, target, index, way).start()

        self.sent.append(describe)

    def arrive(self, target, index, way):
        self.copy(target, target, index, way).wait_recv()

    def finish(self):
        for describe in self.sent:
            source, target, index, way, when = describe()
            if when is None:
                self.copy(source, target, index, way).wait_send()
            else:

                @pl.when(when)
                def _(source=source, target=target, index=index, way=way):
                    self.copy(source, target, index, way).wait_send()


def add_into(place, *others):
    total = place[...].astype(F32)
    for other in others:
        total = total + other[...].astype(F32)
    place[...] = total.astype(BF16)


class Scatter:
    KINDS = ("core", "xa", "yb", "ya", "xb", "to", "from")

    def __init__(self, links, base, source, offset, rows, cut, buffers, load_sems):
        self.k, self.base, self.source, self.offset, self.rows = links, base, source, offset, rows
        self.held, self.r_core, self.r_xa, self.r_yb, self.r_ya, self.r_xb, self.r_line = buffers
        self.load_sems = load_sems
        self.halves = (pl.ds(0, cut), pl.ds(cut, rows - cut))

    @staticmethod
    def buffers_of(rows, cut, line):
        return [
            pltpu.VMEM((line, 2, 2, rows, LANE), BF16),
            pltpu.VMEM((line, 4 * rows, LANE), BF16),
            pltpu.VMEM((line, 2, cut, LANE), BF16),
            pltpu.VMEM((line, 2, rows - cut, LANE), BF16),
            pltpu.VMEM((line, cut, LANE), BF16),
            pltpu.VMEM((line, rows - cut, LANE), BF16),
            pltpu.VMEM((line, rows, LANE), BF16),
        ]

    def at(self, kind, z):
        return self.base + self.KINDS.index(kind) * self.k.line + z

    def load(self, z):
        start = self.offset + (self.k.c * self.k.line + z) * 4 * self.rows
        return [
            pltpu.make_async_copy(
                self.source.at[pl.ds(pl.multiple_of(start + i * self.rows, 16), self.rows)],
                self.held.at[z, i // 2, i % 2],
                self.load_sems.at[4 * z + i],
            )
            for i in range(4)
        ]

    def begin(self):
        k = self.k

        def describe(z):
            start = self.offset + ((1 - k.c) * k.line + z) * 4 * self.rows
            source = self.source.at[pl.ds(pl.multiple_of(start, 16), 4 * self.rows)]
            return source, self.r_core.at[z], self.at("core", z), "core", None

        for z in range(k.line):
            k.send(functools.partial(describe, z))
            for copy in self.load(z):
                copy.start()

    def first(self, z):
        k, (a, b) = self.k, self.halves
        for copy in self.load(z):
            copy.wait()
        k.arrive(self.r_core.at[z], self.at("core", z), "core")
        for i in range(4):
            add_into(self.held.at[z, i // 2, i % 2], self.r_core.at[z, pl.ds(i * self.rows, self.rows)])
        k.send(lambda: (self.held.at[z, 1 - k.x, :, a], self.r_xa.at[z], self.at("xa", z), "x", None))
        k.send(lambda: (self.held.at[z, :, 1 - k.y, b], self.r_yb.at[z], self.at("yb", z), "y", None))

    def second(self, z):
        k, (a, b) = self.k, self.halves
        k.arrive(self.r_xa.at[z], self.at("xa", z), "x")
        for y in range(2):
            add_into(self.held.at[z, k.x, y, a], self.r_xa.at[z, y])
        k.send(lambda: (self.held.at[z, k.x, 1 - k.y, a], self.r_ya.at[z], self.at("ya", z), "y", None))
        k.arrive(self.r_yb.at[z], self.at("yb", z), "y")
        for x in range(2):
            add_into(self.held.at[z, x, k.y, b], self.r_yb.at[z, x])
        k.send(lambda: (self.held.at[z, 1 - k.x, k.y, b], self.r_xb.at[z], self.at("xb", z), "x", None))

    def third(self, z):
        k, (a, b) = self.k, self.halves
        k.arrive(self.r_ya.at[z], self.at("ya", z), "y")
        add_into(self.held.at[z, k.x, k.y, a], self.r_ya.at[z])
        k.arrive(self.r_xb.at[z], self.at("xb", z), "x")
        add_into(self.held.at[z, k.x, k.y, b], self.r_xb.at[z])

        def describe():
            index = (self.at("to", z), self.at("from", k.z))
            return self.held.at[z, k.x, k.y], self.r_line.at[k.z], index, z, k.z != z

        k.send(describe)

    def last(self):
        k = self.k
        others = [(k.z + d) % k.line for d in range(1, k.line)]
        for z in others:
            k.arrive(self.r_line.at[z], (self.at("to", z), self.at("from", z)), z)
        add_into(self.held.at[k.z, k.x, k.y], *[self.r_line.at[z] for z in others])


class Spread:
    KINDS = ("xa", "yb", "ya", "xb", "ya2", "xb2") + tuple(
        f"{way}{i}" for way in ("to", "from", "c") for i in range(4)
    )

    def __init__(self, links, base, piece, out, index, first, rows, cut):
        self.k, self.base, self.piece, self.out, self.index = links, base, piece, out, index
        self.parts = {None: (first, rows), 0: (first, cut), 1: (first + cut, rows - cut)}

    def own(self, half):
        first, count = self.parts[half]
        return self.piece(pl.ds(first, count))

    def at(self, kind, z):
        return self.base + self.KINDS.index(kind) * self.k.line + z

    def spot(self, z, other_x, other_y, half=None, core=None):
        k = self.k
        c = k.c if core is None else core
        x = 1 - k.x if other_x else k.x
        y = 1 - k.y if other_y else k.y
        first, count = self.parts[half]
        return self.out.at[pl.ds(pl.multiple_of(self.index(c, z, x, y) + first, 16), count)]

    def place(self, d):
        return (self.k.z + d) % self.k.line

    def give(self, kind, way, d, other_x=False, other_y=False, half=None, own=False):
        def describe():
            z = self.place(d)
            target = self.spot(z, other_x, other_y, half)
            source = self.own(half) if own else target
            return source, target, self.at(kind, z), way, None

        self.k.send(describe)

    def get(self, kind, way, d, other_x=False, other_y=False, half=None):
        z = self.place(d)
        self.k.arrive(self.spot(z, other_x, other_y, half), self.at(kind, z), way)

    def lift(self, i, own=False):
        k = self.k
        place = dict(other_x=i >= 2, other_y=i % 2 == 1)

        def describe(d):
            z = self.place(d)
            target = self.spot(k.z, **place)
            source = self.own(None) if own else target
            return source, target, (self.at(f"to{i}", z), self.at(f"from{i}", k.z)), z, None

        for d in (k.line - 1, 1, 2):
            k.send(functools.partial(describe, d))

    def land(self, d, i):
        z = self.place(d)
        place = dict(other_x=i >= 2, other_y=i % 2 == 1)
        self.k.arrive(self.spot(z, **place), (self.at(f"to{i}", z), self.at(f"from{i}", z)), z)

    def cross(self, d):
        own = d == 0
        self.give("xa", "x", d, half=0, own=own)
        self.give("yb", "y", d, half=1, own=own)
        self.give("ya", "y", d, half=0, own=own)
        self.give("xb", "x", d, half=1, own=own)
        self.give("c0", "core", d, own=own)

    def start(self):
        self.lift(0, True)
        self.cross(0)

    def along(self, d):
        self.land(d, 0)
        self.cross(d)

    def turn(self, d):
        self.get("xa", "x", d, other_x=True, half=0)
        self.give("ya2", "y", d, other_x=True, half=0)
        self.get("yb", "y", d, other_y=True, half=1)
        self.give("xb2", "x", d, other_y=True, half=1)

    def share(self, d, late=False):
        self.get("ya", "y", d, other_y=True, half=0)
        self.give("c1", "core", d, other_y=True)
        if late:
            self.lift(1)
        self.get("xb", "x", d, other_x=True, half=1)
        self.give("c2", "core", d, other_x=True)
        if late:
            self.lift(2)
        self.get("ya2", "y", d, other_x=True, other_y=True, half=0)
        self.get("xb2", "x", d, other_x=True, other_y=True, half=1)
        self.give("c3", "core", d, other_x=True, other_y=True)
        if late:
            self.lift(3)

    def along_late(self, d):
        for i in range(4):
            self.land(d, i)
            self.give(f"c{i}", "core", d, other_x=i >= 2, other_y=i % 2 == 1)

    def end(self):
        k = self.k
        for z in range(k.line):
            for i in range(4):
                k.arrive(self.spot(z, i >= 2, i % 2 == 1, core=1 - k.c), self.at(f"c{i}", z), "core")


RS_SEMS = len(Scatter.KINDS)
AR_SEMS = RS_SEMS + 2 * len(Spread.KINDS)


class Total:
    def __init__(self, links, base, source, offset, kind, out, top, buffers, load_sems, copy_sem):
        line = links.line
        size, cut, turn, plain = kind
        rows = size // (8 * line)
        held = buffers[0]

        def index(c, z, x, y):
            return top + (((c * line + z) * 2 + x) * 2 + y) * rows

        def piece(span):
            return held.at[links.z, links.x, links.y, span]

        self.k, self.piece, self.out, self.index, self.rows = links, piece, out, index, rows
        self.scatter = Scatter(links, base, source, offset, rows, cut, buffers, load_sems)
        base = base + RS_SEMS * line
        self.spread = Spread(links, base, piece, out, index, 0, plain, turn)
        self.late = None
        if plain < rows:
            base = base + len(Spread.KINDS) * line
            rest = rows - plain
            self.late = Spread(links, base, piece, out, index, plain, rest, rest // 32 * 16)
        self.copy_sem = copy_sem

    def keep(self):
        k = self.k
        start = pl.multiple_of(self.index(k.c, k.z, k.x, k.y), 16)
        return pltpu.make_async_copy(
            self.piece(pl.ds(0, self.rows)), self.out.at[pl.ds(start, self.rows)], self.copy_sem
        )

    def run(self, stage, part):
        scatter, spread, late = self.scatter, self.spread, self.late
        if stage == 0:
            scatter.begin()
        elif stage < 4:
            (scatter.first, scatter.second, scatter.third)[stage - 1](part)
        elif stage == 4:
            scatter.last()
            self.keep().start()
            spread.start()
            if late is not None:
                late.start()
        elif stage == 5 and part < 3:
            spread.along(part + 1)
        elif stage == 5 and part == 3:
            late.turn(0)
        elif stage == 5 and part == 4:
            late.share(0, True)
        elif stage == 5:
            late.along_late(part - 4)
        elif stage < 8:
            (spread.turn, spread.share)[stage - 6](part)
        else:
            self.keep().wait()
            spread.end()
            if late is not None:
                late.end()


class Gather:
    KINDS = ("up", "down", "xa", "yb", "ya", "xb", "ya2", "xb2", "x2") + tuple(
        f"{way}{i}" for way in ("u", "d", "c") for i in range(4)
    )

    def __init__(self, links, base, own, out, index, first, rows, cut, z_first, twice):
        self.k, self.base, self.own, self.out, self.index = links, base, own, out, index
        self.parts = {None: (first, rows), 0: (first, cut), 1: (first + cut, rows - cut)}
        self.z_first, self.twice = z_first, twice

    def at(self, kind, z):
        return self.base + self.KINDS.index(kind) * self.k.line + z

    def spot(self, z, other_x, other_y, half=None, core=None):
        k = self.k
        c = k.c if core is None else core
        x = 1 - k.x if other_x else k.x
        y = 1 - k.y if other_y else k.y
        first, count = self.parts[half]
        return self.out.at[pl.ds(pl.multiple_of(self.index(c, z, x, y) + first, 16), count)]

    def give(self, kind, way, z, other_x=False, other_y=False, half=None, when=None, own=False):
        def describe():
            place = self.spot(z(), other_x, other_y, half)
            source = self.own(other_y, half) if own else place
            return source, place, self.at(kind, z()), way, None if when is None else when()

        self.k.send(describe)

    def get(self, kind, way, z, other_x=False, other_y=False, half=None):
        self.k.arrive(self.spot(z, other_x, other_y, half), self.at(kind, z), way)

    def near(self):
        k = self.k
        found = []
        for r in range(1, k.line):
            found.append(
                (
                    lambda r=r: k.z - r,
                    lambda r=r: k.z >= r,
                    "u",
                    "up",
                    lambda r=r: (k.z >= r) & (k.z < k.line - 1),
                )
            )
            found.append(
                (
                    lambda r=r: k.z + r,
                    lambda r=r: k.z + r < k.line,
                    "d",
                    "down",
                    lambda r=r: (k.z + r < k.line) & (k.z > 0),
                )
            )
        return found

    def here(self):
        return self.k.z

    def lower(self):
        return self.k.z < self.k.line - 1

    def upper(self):
        return self.k.z > 0

    def cross(self, z, when, own):
        self.give("xa", "x", z, half=0, when=when, own=own)
        self.give("yb", "y", z, half=1, when=when, own=own)
        self.give("ya", "y", z, half=0, when=when, own=own)
        self.give("xb", "x", z, half=1, when=when, own=own)
        self.give("c0", "core", z, when=when, own=own)

    def start(self):
        self.give("up", "up", self.here, when=self.lower, own=True)
        self.give("down", "down", self.here, when=self.upper, own=True)
        if self.twice:
            for other, kind in ((False, "xa"), (True, "x2")):
                self.give(kind, "x", self.here, other_y=other, own=True)
                self.give("c1" if other else "c0", "core", self.here, other_y=other, own=True)
        else:
            self.cross(self.here, None, True)

    def along(self, number):
        z, exists, _, way, goes_on = self.near()[number]

        @pl.when(exists())
        def _():
            self.get(way, way, z())

        self.give(way, way, z, when=goes_on)
        self.cross(z, exists, False)

    def turn(self, z, when):
        def waits():
            self.get("xa", "x", z(), other_x=True, half=0)

        def waits_too():
            self.get("yb", "y", z(), other_y=True, half=1)

        waits() if when is None else pl.when(when())(waits)
        self.give("ya2", "y", z, other_x=True, half=0, when=when)
        waits_too() if when is None else pl.when(when())(waits_too)
        self.give("xb2", "x", z, other_y=True, half=1, when=when)

    def share(self, z, when):
        def waits(kind, way, **place):
            def wait():
                self.get(kind, way, z(), **place)

            wait() if when is None else pl.when(when())(wait)

        waits("ya", "y", other_y=True, half=0)
        self.give("c1", "core", z, other_y=True, when=when)
        waits("xb", "x", other_x=True, half=1)
        self.give("c2", "core", z, other_x=True, when=when)
        waits("ya2", "y", other_x=True, other_y=True, half=0)
        waits("xb2", "x", other_x=True, other_y=True, half=1)
        self.give("c3", "core", z, other_x=True, other_y=True, when=when)

    def share_twice(self):
        for other, kind in ((False, "xa"), (True, "x2")):
            self.get(kind, "x", self.k.z, other_x=True, other_y=other)
            self.give("c3" if other else "c2", "core", self.here, other_x=True, other_y=other)

    def lift(self, i, own=False):
        place = dict(other_x=i >= 2, other_y=i % 2 == 1)
        self.give(f"u{i}", "up", self.here, when=self.lower, own=own, **place)
        self.give(f"d{i}", "down", self.here, when=self.upper, own=own, **place)
        self.give(f"c{i}", "core", self.here, own=own, **place)

    def start_plane(self):
        if self.twice:
            for other, kind in ((False, "xa"), (True, "x2")):
                self.give(kind, "x", self.here, other_y=other, own=True)
            self.lift(0, True)
            self.lift(1, True)
        else:
            self.give("xa", "x", self.here, half=0, own=True)
            self.give("yb", "y", self.here, half=1, own=True)
            self.give("ya", "y", self.here, half=0, own=True)
            self.give("xb", "x", self.here, half=1, own=True)
            self.lift(0, True)

    def turn_plane(self):
        if self.twice:
            for other, kind in ((False, "xa"), (True, "x2")):
                self.get(kind, "x", self.k.z, other_x=True, other_y=other)
                self.lift(3 if other else 2)
        else:
            self.turn(self.here, None)

    def lift_plane(self):
        if not self.twice:
            z = self.k.z
            self.get("ya", "y", z, other_y=True, half=0)
            self.lift(1)
            self.get("xb", "x", z, other_x=True, half=1)
            self.lift(2)
            self.get("ya2", "y", z, other_x=True, other_y=True, half=0)
            self.get("xb2", "x", z, other_x=True, other_y=True, half=1)
            self.lift(3)

    def along_plane(self, number, i):
        z, exists, letter, way, goes_on = self.near()[number]
        place = dict(other_x=i >= 2, other_y=i % 2 == 1)

        @pl.when(exists())
        def _():
            self.get(f"{letter}{i}", way, z(), **place)

        self.give(f"{letter}{i}", way, z, when=goes_on, **place)
        self.give(f"c{i}", "core", z, when=exists, **place)

    def steps(self):
        count = 2 * (self.k.line - 1)
        if self.z_first:
            one = [self.start]
            two = [lambda n=n: self.along(n) for n in range(count)]
            spots = [(z, exists) for z, exists, _, _, _ in self.near()]
            if not self.twice:
                spots = [(self.here, None)] + spots
            three = [lambda z=z, e=e: self.turn(z, e) for z, e in spots]
            four = [lambda z=z, e=e: self.share(z, e) for z, e in spots]
            if self.twice:
                four = [self.share_twice] + four
            return [one, two, three, four]
        one = [self.start_plane]
        two = [self.turn_plane]
        three = [self.lift_plane]
        four = [lambda n=n, i=i: self.along_plane(n, i) for n in range(count) for i in range(4)]
        return [one, two, three, four]

    def end(self):
        k = self.k
        for z in range(k.line):
            for i in range(4):
                k.arrive(
                    self.spot(z, i >= 2, i % 2 == 1, core=1 - k.c), self.at(f"c{i}", z), "core"
                )


AG_SEMS = len(Gather.KINDS)


def all_gather_kernel(line, swaps, cuts, masters, *refs):
    near, out, far = refs[:swaps], refs[swaps], refs[swaps + 1 : 2 * swaps + 1]
    piece, flat, send_sems, recv_sems, copy_sem = refs[2 * swaps + 1 :]
    links = Links(line, send_sems, recv_sems)

    def pack():
        rows = flat.shape[0] // LANE
        for top in range(0, masters.shape[0], rows):
            pack_rows(masters.at[pl.ds(top, rows)], flat)
            piece[top * LANE : (top + rows) * LANE] = flat[...].astype(BF16)

    links.greet(False, pack)
    rows = piece.shape[0] // 2
    first_rows, second_rows = cuts
    spare = 2 * AG_SEMS * line

    def index(c, z, x, y):
        return (((z * 2 + x) * 2 + c) * 2 + y) * rows

    def keep():
        start = index(links.c, links.z, links.x, 0)
        return pltpu.make_async_copy(
            piece, out.at[pl.ds(pl.multiple_of(start, 16), 2 * rows)], copy_sem
        )

    gathers = []

    def own_of(first, count, cut):
        def own(other, half):
            begin, size = {None: (0, count), 0: (0, cut), 1: (cut, count - cut)}[half]
            y = 1 - links.y if other else links.y
            return piece.at[pl.ds(pl.multiple_of(y * rows + first + begin, 16), size)]

        return own

    last = rows - first_rows - second_rows
    spans = ((0, first_rows + second_rows, first_rows, True), (first_rows + second_rows, last, last // 32 * 16, False))
    for number, (first, count, cut, z_first) in enumerate(spans):
        gathers.append(
            Gather(
                links, number * AG_SEMS * line, own_of(first, count, cut), out, index,
                first, count, cut, z_first, True,
            )
        )
    flat, tall = gathers[0].steps(), gathers[1].steps()
    for step in flat[0] + tall[0]:
        step()
    keep().start()
    for i in range(swaps):
        links.send(lambda i=i: (near[i], far[i], spare + i, "y", None))
    along, rise = flat[1], tall[1] + tall[2]
    turn, share, climb = flat[2], flat[3], tall[3]
    for step in along[:2] + rise + turn[:2] + along[2:4] + climb[:8] + turn[2:4] + along[4:]:
        step()
    for step in climb[8:16] + turn[4:] + share[:3] + climb[16:] + share[3:]:
        step()
    for gather in gathers:
        gather.end()
    keep().wait()
    for i in range(swaps):
        links.arrive(far[i], spare + i, "y")
    links.finish()


def all_gather(masters, swaps, line, collective_id):
    any_space = pl.BlockSpec(memory_space=pl.ANY)
    sems = 2 * AG_SEMS * line + len(swaps)
    count = masters.shape[0] * LANE
    rows = count // 2
    cuts = (rows * 2 // 5 // 16 * 16, rows * 2 // 5 // 16 * 16)
    return pl.pallas_call(
        functools.partial(all_gather_kernel, line, len(swaps), cuts),
        out_shape=[jax.ShapeDtypeStruct((4 * line * count, LANE), BF16)]
        + [jax.ShapeDtypeStruct(s.shape, s.dtype) for s in swaps],
        in_specs=[pl.BlockSpec(memory_space=pltpu.VMEM)] + [any_space] * len(swaps),
        out_specs=[any_space] * (1 + len(swaps)),
        scratch_shapes=[
            pltpu.VMEM((count, LANE), BF16),
            pltpu.VMEM((8 * LANE, LANE), F32),
            pltpu.SemaphoreType.DMA((sems,)),
            pltpu.SemaphoreType.DMA((sems,)),
            pltpu.SemaphoreType.DMA,
        ],
        compiler_params=params(60, collective_id=collective_id, has_side_effects=True),
        cost_estimate=cost(0, 100 * MIB),
        name="all_gather",
    )(masters, *swaps)


PAIRS = D // LANE
UP_ROWS = FF * D // LANE
REST_ROWS = 128 * LANE
HEAD, NORM, LAST = 900, 901, 902
ORDER = (
    100, 0, HEAD, HEAD, 110, 111, 112, 113, 10, 11, 120, HEAD, HEAD, 121, HEAD, HEAD, 122, HEAD,
    HEAD, 123, 12, 13, HEAD, HEAD, HEAD, HEAD, NORM, 130, 20, 21, 131, 132, 133, LAST, 200, 22,
    23, 210, 211, 212, 213, 140, 150, 30, 31, 32, 33, 220, 221, 222, 40, 223, 160, 161, 153, 50,
    51, 52, 230, 231, 232, 233, 53, 170, 171, 154, 151, 152, 60, 61, 240, 155, 54, 62, 63, 250,
    156, 157, 162, 163, 70, 253, 251, 252, 260, 71, 72, 73, 172, 173, 180, 55, 254, 56, 261,
    262, 57, 80, 270, 271, 263, 272, 273, 255, 256, 257, 280,
)


def segments():
    found = [[]]
    for step in ORDER:
        if step >= HEAD:
            found.append([])
        else:
            found[-1].append((step // 100, step // 10 % 10, step % 10))
    return found


def total_kinds(line):
    kinds = []
    for size, late in ((UP_ROWS, 10), (UP_ROWS, 10), (REST_ROWS, 15)):
        rows = size // (8 * line)
        plain = rows - rows * late // 100 // 32 * 32
        kinds.append((size, rows * 72 // 100 // 16 * 16, plain * 30 // 100 // 16 * 16, plain))
    return kinds


def back_kernel(
    line,
    q, k, v, att, grad_att, chance, tokens, tokens_far, n1, att_all, resid_low, w_qkv, vec, vec_one, d_up, d_down,
    d_first, grad_near, out, grad_back, first_back,
    d_q, d_k, d_v, far, d_rest, vec_grad, flat, *scratch,
):
    step = pl.program_id(0)
    sources = (tokens, tokens_far, n1, att_all, resid_low, w_qkv)
    late, late_sems, scratch = scratch[:6], scratch[6], scratch[7:]
    copies = [
        pltpu.make_async_copy(source, target, late_sems.at[i])
        for i, (source, target) in enumerate(zip(sources, late))
    ]
    buffers, (send_sems, recv_sems, load_sems, copy_sems) = scratch[:-4], scratch[-4:]
    links = Links(line, send_sems, recv_sems)
    tops = (REST_ROWS + UP_ROWS, REST_ROWS, 0)
    totals = [
        Total(
            links, g * AR_SEMS * line, source, 0, kind, out, top,
            buffers[7 * g : 7 * g + 7], load_sems.at[g], copy_sems.at[g],
        )
        for g, (source, kind, top) in enumerate(zip((d_down, d_up, d_rest), total_kinds(line), tops))
    ]
    spare = len(totals) * AR_SEMS * line
    plan = segments()

    def run(number):
        for g, stage, part in plan[number]:
            totals[g].run(stage, part)

    queries = q.shape[0]
    for head in range(2):
        for s in range(PAIRS):

            @pl.when(step == s)
            def _(s=s, head=head):
                if s == 0 and head == 0:
                    links.greet(True)
                    for copy in copies:
                        copy.start()
                run(2 * s + head)

        @pl.when(step < PAIRS)
        def _(head=head):
            cols = slice(head * HD, (head + 1) * HD)
            grad = grad_att[:, cols]
            weights = chance[head]
            shared = grad.astype(F32) * att[:, cols].astype(F32)
            delta = jnp.sum(shared.T, axis=0, keepdims=True)
            grad_chance = mm(v[:, cols], grad, NT)
            grad_scores = (weights.astype(F32) * (grad_chance - delta)).astype(BF16)
            grad_value = mm(weights, grad)

            d_v[step, :, cols] = grad_value.astype(BF16)
            d_first[:, cols] = grad_value[:queries]
            d_k[step, :, cols] = mm(grad_scores, q[:, cols]).astype(BF16)
            d_q[step, :, cols] = (mm(k[:, cols], grad_scores, TN).T * HD ** (-0.5)).astype(BF16)

    @pl.when(step == PAIRS)
    def _():
        for copy in copies:
            copy.wait()
        tokens, tokens_far, n1, att_all, resid_low, w_qkv = late
        rows = n1.shape[0] // 2
        per_row = D // LANE
        rows = n1.shape[0] // 2
        first_far = d_v.at[pl.ds(PAIRS // 2, PAIRS // 2), pl.ds(rows, rows)]
        links.send(lambda: (first_far, first_back, spare, "y", None))
        run(2 * PAIRS)
        dq = jnp.concatenate([d_q[i] for i in range(PAIRS)], axis=1)
        dk = jnp.concatenate([d_k[i] for i in range(PAIRS)], axis=1)
        dv = jnp.concatenate([d_v[i] for i in range(PAIRS // 2)], axis=1)
        grads = mm(dk, w_qkv[:, D : 2 * D], NT) + mm(dv, w_qkv[:, 2 * D :], NT)
        beside = grads[rows:]
        far[...] = beside.astype(BF16)
        links.send(lambda: (far, grad_back, spare + 1, "y", None))
        near = grads[:rows] + mm(dq, w_qkv[:, :D], NT)
        grad_near[...] = near
        hat, _ = normed(tokens[...].astype(F32))
        hat_far, _ = normed(tokens_far[...].astype(F32))
        vec_grad[...] = vec_one[...]
        vec_grad[:, :D] = jnp.sum(near * hat, axis=0, keepdims=True) + jnp.sum(
            beside * hat_far, axis=0, keepdims=True
        )
        vec_grad[:, D : 2 * D] = jnp.sum(near, axis=0, keepdims=True) + jnp.sum(
            beside, axis=0, keepdims=True
        )
        vec_grad[:, 4 * D : 5 * D] = jnp.sum(dq.astype(F32), axis=0, keepdims=True)
        vec_grad[:, 7 * D : 7 * D + HV] = jnp.sum(dv.astype(F32), axis=0, keepdims=True)
        run(2 * PAIRS + 1)
        pieces = (
            (n1[:rows], dq, 0, per_row),
            (n1[...], dk, D * per_row, per_row),
            (n1[...], dv, 2 * D * per_row, HV // LANE),
            (att_all[...], resid_low[...], 2 * D * per_row + D * HV // LANE, per_row),
        )
        for left, right, start, columns in pieces:
            product = mm(left, right, TN)
            size = D * columns
            for j in range(columns):
                flat[pl.ds(j, D, stride=columns), :] = product[:, j * LANE : (j + 1) * LANE]
            d_rest[start : start + size] = flat[:size].astype(BF16)
        flat[: 2 * LANE] = jnp.zeros((2 * LANE, LANE), F32)
        for j in range(VEC // LANE):
            flat[j : j + 1] = vec_grad[:, j * LANE : (j + 1) * LANE]
        d_rest[REST:] = flat[: 2 * LANE].astype(BF16)
        run(2 * PAIRS + 2)
        links.arrive(first_back, spare, "y")
        links.arrive(grad_back, spare + 1, "y")
        links.finish()


def back(q, k, v, att, grad_att, chance, tokens, tokens_far, n1, resid_low, w_qkv, vec, vec_one, d_up, d_down, line):
    rows, keys = q.shape[0], k.shape[0]
    any_space = pl.BlockSpec(memory_space=pl.ANY)

    def column(count):
        return pl.BlockSpec((count, LANE), lambda i: (0, jnp.minimum(i, PAIRS - 1)))

    def once(array):
        return pl.BlockSpec(array.shape, lambda i: (0,) * array.ndim, pipeline_mode=pl.Buffered(1))

    kinds = total_kinds(line)
    scratch = []
    for size, cut, _, _ in kinds:
        scratch += Scatter.buffers_of(size // (8 * line), cut, line)
    sems = len(kinds) * AR_SEMS * line + 2
    return pl.pallas_call(
        functools.partial(back_kernel, line),
        out_shape=[
            jax.ShapeDtypeStruct((rows, HV), F32),
            jax.ShapeDtypeStruct((rows, D), F32),
            jax.ShapeDtypeStruct((REST_ROWS + 2 * UP_ROWS, LANE), BF16),
            jax.ShapeDtypeStruct((rows, D), BF16),
            jax.ShapeDtypeStruct((PAIRS // 2, rows, LANE), BF16),
        ],
        grid=(PAIRS + 1,),
        in_specs=[
            column(rows),
            column(keys),
            column(keys),
            column(rows),
            column(rows),
            pl.BlockSpec((2, keys, rows), lambda i: (jnp.minimum(i, PAIRS - 1), 0, 0)),
            any_space,
            any_space,
            any_space,
            any_space,
            any_space,
            any_space,
            once(vec),
            once(vec_one),
            any_space,
            any_space,
        ],
        out_specs=[
            pl.BlockSpec((rows, LANE), lambda i: (0, jnp.clip(i - 3, 0, 2))),
            pl.BlockSpec((rows, D), lambda i: (0, 0), pipeline_mode=pl.Buffered(1)),
            any_space,
            any_space,
            any_space,
        ],
        scratch_shapes=[
            pltpu.VMEM((PAIRS, rows, LANE), BF16),
            pltpu.VMEM((PAIRS, keys, LANE), BF16),
            pltpu.VMEM((PAIRS, keys, LANE), BF16),
            pltpu.VMEM((rows, D), BF16),
            pltpu.VMEM((REST_ROWS, LANE), BF16),
            pltpu.VMEM((1, VEC), F32),
            pltpu.VMEM((D * D // LANE, LANE), F32),
        ]
        + [pltpu.VMEM(a.shape, a.dtype) for a in (tokens, tokens_far, n1, att, resid_low, w_qkv)]
        + [pltpu.SemaphoreType.DMA((6,))]
        + scratch
        + [
            pltpu.SemaphoreType.DMA((sems,)),
            pltpu.SemaphoreType.DMA((sems,)),
            pltpu.SemaphoreType.DMA((len(kinds), 4 * line)),
            pltpu.SemaphoreType.DMA((len(kinds),)),
        ],
        compiler_params=params(62, collective_id=0, has_side_effects=True),
        cost_estimate=cost(8 * rows * keys * D + 14 * rows * D * D, 100 * MIB),
        name="back",
    )(q, k, v, att, grad_att, chance, tokens, tokens_far, n1, att, resid_low, w_qkv, vec, vec_one, d_up, d_down)


def swap(value):
    return lax.ppermute(value, "seq", [(0, 1), (1, 0)])


def shards(
    tokens,
    first_values,
    out_grad,
    block_place,
    owners,
    masters,
    moment_one,
    moment_two,
    vector_master,
    vector_moment_one,
    vector_moment_two,
):
    capacity = masters.shape[0]
    dp_count = lax.axis_size("dp")
    tile_count = owners.shape[0]
    dp_here = lax.axis_index("dp")
    seq_here = lax.axis_index("seq")
    _, half_len, _ = tokens.shape

    tokens = tokens.reshape(half_len, D)
    firsts = first_values.reshape(half_len, HV)
    given = out_grad.reshape(half_len, D)
    line = dp_count // 4
    if line == LINE and capacity % 8 == 0:
        slots, tokens_far, firsts_far = all_gather(masters, [tokens, firsts], line, 1)
    else:
        tokens_far, firsts_far = swap(tokens), swap(firsts)
        slots = lax.all_gather(pack_slots(masters), "dp", axis=0, tiled=True)

    slot_index = slot_numbers(owners)
    slot_rows = owners * capacity + slot_index
    mine = (owners == dp_here)[None, :] & (
        slot_index[None, :] == jnp.arange(capacity, dtype=jnp.int32)[:, None]
    )
    tile_order = jnp.arange(tile_count, dtype=jnp.int32)
    gap = REST_ROWS // LANE - 126
    tile_place = tile_order + jnp.where(tile_order >= 126, gap, 0)
    places = jnp.sum(jnp.where(mine, tile_place[None, :] + 1, 0), axis=1) - 1

    vec = vector_master.reshape(1, VEC)
    w_qkv, w_out, w_up, w_down = unpack_weights(slot_rows, slots)
    n1, q, k, v = project(tokens, tokens_far, firsts, firsts_far, w_qkv, vec)
    att, chance = attend(block_place, q, k, v)
    result, grad_resid, resid_low, grad_att, d_up, d_down, vec_one = hidden(
        tokens, att, given, w_out, w_up, w_down, vec
    )
    if line == LINE:
        first_near, grad_near, grads, grad_back, first_back = back(
            q, k, v, att, grad_att, chance, tokens, tokens_far, n1, resid_low, w_qkv, vec, vec_one, d_up, d_down, line
        )
    else:
        d_q, d_k, d_fresh, d_first = attend_back(q, k, v, att, grad_att, chance)
        grad_near, grad_far, d_rest = project_back(
            jnp.concatenate([tokens, tokens_far], axis=0), n1, d_q, d_k, d_fresh, att, resid_low, w_qkv, vec, vec_one
        )
        first_near = d_first[:half_len]
        grad_back, first_back = swap(grad_far), swap(d_first[half_len:].astype(BF16))
        first_back = first_back.reshape(half_len, HV // LANE, LANE).transpose(1, 0, 2)
        grads = lax.psum(jnp.concatenate([d_rest, d_up, d_down], axis=0), ("seq", "dp"))
    vectors = [
        v.reshape(VEC // LANE, LANE) for v in (vector_master, vector_moment_one, vector_moment_two)
    ]
    new_master, new_one, new_two, new_low, tokens_grad, first_grad, *new_vectors = finish(
        places, grads, masters, moment_one, moment_two,
        grad_resid, grad_near, grad_back, tokens, vec, first_near, first_back, vectors,
    )
    return (
        result.reshape(1, half_len, D),
        tokens_grad.reshape(1, half_len, D),
        first_grad.reshape(1, half_len, HV),
        new_master,
        new_one,
        new_two,
        new_low,
        *(v.reshape(VEC) for v in new_vectors),
    )


def solution(mesh):
    rows = P("dp", "seq", None)
    slots = P("dp", None)
    return jax.shard_map(
        shards,
        mesh=mesh,
        in_specs=(rows, rows, rows, slots, P(), slots, slots, slots, P(), P(), P()),
        out_specs=(rows, rows, rows, slots, slots, slots, slots, P(), P(), P()),
        check_vma=False,
    )
```
